32 devices in a mesh: grp: 4 (over y, x), emb: 8 (over z, core).
Axes of the slice: x: 2, y: 2, z: 4, core: 2. Of those that a mesh axis runs over, the one named last changes fastest.
Arguments:
- pooled: bfloat16 [384, 256, 192], P(('grp', 'emb')), may hold values from -6 to 6
- upstream: bfloat16 [384, 256, 192], P(('grp', 'emb')), may hold values from -6 to 6
- ids_now: int32 [384, 256], P(('grp', 'emb')), may hold values from 0 to 127
- ids_next: int32 [384, 256], P(('grp', 'emb')), may hold values from 0 to 127
- tables: bfloat16 [256, 128, 192], P('emb'), may hold values from -6 to 6
- w_fm: bfloat16 [256, 128], replicated, may hold values from -0.02734375 to 0.02734375
- w_proj: bfloat16 [128, 192], replicated, may hold values from -0.5 to 0.5
- w_lcb: bfloat16 [256, 256], replicated, may hold values from -0.375 to 0.375
- gain: float32 [192], replicated, may hold values from 0.5 to 1.5
Outputs:
- next_rows: bfloat16 [384, 256, 192], P(('grp', 'emb'))
- table_grad: float32 [256, 128, 192], P('emb', 'grp')
- grad_fm: float32 [256, 128], replicated
- grad_proj: float32 [128, 192], replicated
- grad_lcb: float32 [256, 256], replicated
- grad_gain: float32 [192], replicated
The draws below stay inside these ranges and needn't reach their ends.
All inputs are finite; a program needn't handle non-finite values.
Results may differ from the reference program's by a relative error of at most 0.017.
Values may be sent and summed in bfloat16 or wider, within the bound.
No kernel may reach another device: no remote copies, remote signals or barrier semaphores. Data moves between devices by JAX's collectives and lax.ppermute only.
A program may use at most 64 MiB of HBM per device.

```python
import math
import jax
import jax.numpy as jnp
import numpy as np
from jax import lax

NF = 256
D = 192
K = 128
B_DEV = 12
BATCH = 384
ROWS = 128
N_GRP = 4
N_EMB = 8


def touch_ends(drawn, key, low, top_value):
    longest = drawn.shape.index(max(drawn.shape))
    spots = []
    for shift in (0, 1):
        where = [jax.random.randint(jax.random.fold_in(key, axis), (), 0, length) for axis, length in enumerate(drawn.shape)]
        where[longest] = (where[longest] + shift) % drawn.shape[longest]
        spots.append(tuple(where))
    return drawn.at[spots[0]].set(low).at[spots[1]].set(top_value)


def level_of(stream_key, shape, pieces, least, high):
    level, own = 1.0, jax.random.fold_in(stream_key, 6)
    for dim, shards_of in pieces:
        draws = jnp.exp(jax.random.uniform(jax.random.fold_in(own, dim), (shards_of,), jnp.float32, least / len(pieces), high / len(pieces)))
        level = level * jnp.repeat(draws, shape[dim] // shards_of).reshape([-1 if axis == dim else 1 for axis in range(len(shape))])
    return level


def rank_table(number_of, lean):
    weights = [(1 << 20) // math.isqrt(grade ** lean) + 1 for grade in range(1, number_of + 1)]
    scale = 1 + sum(weights) // (1 << 30)
    return np.cumsum(np.array([max(1, weight // scale) for weight in weights]))


def ranked_ids(stream_key, extent, count, skew):
    table = rank_table(count, skew)
    lot = jax.random.randint(jax.random.fold_in(stream_key, 1), extent, 0, int(table[count - 1]))
    standing = jnp.searchsorted(jnp.asarray(table, jnp.int32), lot, side="right")
    return jax.random.permutation(jax.random.fold_in(stream_key, 2), count)[standing].astype(jnp.int32)


def normal_values(key, shape, width, bound, cuts=(), dtype=jnp.bfloat16):
    values = jax.random.normal(key, shape, jnp.float32) * width
    if len(cuts) > 0:
        values = level_of(key, shape, cuts, -0.22, 0.18) * values
    return jnp.clip(values, min=-bound, max=bound).astype(dtype)


def setup_inputs(seed: int = 0) -> dict:
    arg_keys = jax.random.split(jax.random.key(seed), 10)
    pooled = normal_values(arg_keys[0], (BATCH, NF, D), 1.0, 6.0, ((0, 32),))
    upstream = normal_values(arg_keys[1], (BATCH, NF, D), 1.0, 6.0, ((0, 32),))
    ids_now = touch_ends(ranked_ids(arg_keys[2], (BATCH, NF), ROWS, 2), jax.random.fold_in(arg_keys[2], 3), 0, ROWS - 1).astype(jnp.int32)
    ids_next = touch_ends(ranked_ids(arg_keys[3], (BATCH, NF), ROWS, 2), jax.random.fold_in(arg_keys[3], 3), 0, ROWS - 1).astype(jnp.int32)
    tables = normal_values(arg_keys[4], (NF, ROWS, D), 1.0, 6.0, ((0, 8),))
    w_fm = normal_values(arg_keys[5], (NF, K), (NF * D) ** -0.5, 0.02734375)
    w_proj = normal_values(arg_keys[6], (K, D), K ** -0.5, 0.5)
    w_lcb = normal_values(arg_keys[7], (NF, NF), NF ** -0.5, 0.375)
    gain = jnp.clip(1.0 + 0.1 * jax.random.normal(arg_keys[8], (D,), jnp.float32), 0.5, 1.5)
    return dict(pooled=pooled, upstream=upstream, ids_now=ids_now, ids_next=ids_next, tables=tables, w_fm=w_fm, w_proj=w_proj, w_lcb=w_lcb, gain=gain)


def product(form, left, right):
    return jnp.einsum(form, left.astype(jnp.float32), right.astype(jnp.float32))

def layer_backward(embeds, cotangent, w_fm, w_proj, w_lcb, gain):
    fm_proj = product('bfc,fj->bcj', embeds, w_fm).astype(jnp.bfloat16)
    fm_rows = product('bfc,bcj->bfj', embeds, fm_proj).astype(jnp.bfloat16)
    projected = product('bfj,jc->bfc', fm_rows, w_proj)
    compressed = product('fi,bfc->bic', w_lcb, embeds)
    summed = embeds.astype(jnp.float32) + projected + compressed
    centre = lax.optimization_barrier(jnp.mean(summed, axis=2, keepdims=True))
    spread = lax.optimization_barrier(jnp.mean((summed - centre) ** 2, axis=2, keepdims=True))
    inverse = lax.rsqrt(spread + 1e-05)
    normed = (summed - centre) * inverse
    upper = cotangent.astype(jnp.float32)
    scaled = upper * gain
    grad_sum = inverse * (scaled - lax.optimization_barrier(jnp.mean(scaled, axis=2, keepdims=True)) - normed * lax.optimization_barrier(jnp.mean(scaled * normed, axis=2, keepdims=True)))
    grad_sum = grad_sum.astype(jnp.bfloat16)
    grad_gain = lax.optimization_barrier(jnp.sum(upper * normed, axis=(0, 1)))
    grad_proj = product('bfj,bfc->jc', fm_rows, grad_sum)
    grad_rows = product('bfc,jc->bfj', grad_sum, w_proj).astype(jnp.bfloat16)
    grad_p = product('bfc,bfj->bcj', embeds, grad_rows).astype(jnp.bfloat16)
    grad_fm = product('bfc,bcj->fj', embeds, grad_p)
    grad_lcb = product('bfc,bic->fi', embeds, grad_sum)
    grad_in = grad_sum.astype(jnp.float32) + product('bfj,bcj->bfc', grad_rows, fm_proj) + product('fj,bcj->bfc', w_fm, grad_p) + product('fi,bic->bfc', w_lcb, grad_sum)
    return (grad_in.astype(jnp.bfloat16), (grad_fm, grad_proj, grad_lcb, grad_gain))

def reference(pooled, upstream, ids_now, ids_next, tables, w_fm, w_proj, w_lcb, gain):
    features = jnp.arange(NF)[None, :]
    next_rows = tables[features, ids_next]
    group_size = B_DEV * N_EMB
    embeds_all = pooled.reshape(N_GRP, group_size, NF, D)
    upper_all = upstream.reshape(N_GRP, group_size, NF, D)
    ids_all = ids_now.reshape(N_GRP, group_size, NF)
    row_index = jnp.arange(ROWS)

    def group_step(carry, inputs):
        embeds, cotangent, ids_group = inputs
        grad_in, partials = layer_backward(embeds, cotangent, w_fm, w_proj, w_lcb, gain)
        indicator = (ids_group.T[:, None, :] == row_index[None, :, None]).astype(jnp.bfloat16)
        part = product('frs,sfc->frc', indicator, grad_in).astype(jnp.bfloat16)
        part = lax.optimization_barrier(part)
        table_total = carry[0] + part.astype(jnp.float32)
        dense = tuple((old + new for old, new in zip(carry[1], partials)))
        return ((table_total, dense), None)
    start = (jnp.zeros((NF, ROWS, D), jnp.float32), (jnp.zeros((NF, K), jnp.float32), jnp.zeros((K, D), jnp.float32), jnp.zeros((NF, NF), jnp.float32), jnp.zeros((D,), jnp.float32)))
    (table_grad, dense), unused = lax.scan(group_step, start, (embeds_all, upper_all, ids_all))
    samples = 1.0 / (B_DEV * N_GRP * N_EMB)
    return (next_rows, table_grad, dense[0] * samples, dense[1] * samples, dense[2] * samples, dense[3] * samples)
```

```python
import jax
import jax.numpy as jnp
from jax import lax
from jax.sharding import PartitionSpec as P

BOTH = ("grp", "emb")


def product(form, left, right):
    return jnp.einsum(form, left, right, preferred_element_type=jnp.float32)


def layer_backward(embeds, cotangent, w_fm, w_proj, w_lcb, gain):
    fm_proj = product("bfc,fj->bcj", embeds, w_fm).astype(jnp.bfloat16)
    fm_rows = product("bfc,bcj->bfj", embeds, fm_proj).astype(jnp.bfloat16)
    projected = product("bfj,jc->bfc", fm_rows, w_proj)
    compressed = product("fi,bfc->bic", w_lcb, embeds)
    summed = embeds.astype(jnp.float32) + projected + compressed
    centre = jnp.mean(summed, axis=2, keepdims=True)
    spread = jnp.mean((summed - centre) ** 2, axis=2, keepdims=True)
    inverse = lax.rsqrt(spread + 1e-05)
    normed = (summed - centre) * inverse
    upper = cotangent.astype(jnp.float32)
    scaled = upper * gain
    grad_sum = inverse * (
        scaled
        - jnp.mean(scaled, axis=2, keepdims=True)
        - normed * jnp.mean(scaled * normed, axis=2, keepdims=True)
    )
    grad_sum = grad_sum.astype(jnp.bfloat16)
    grad_gain = jnp.sum(upper * normed, axis=(0, 1))
    grad_proj = product("bfj,bfc->jc", fm_rows, grad_sum)
    grad_rows = product("bfc,jc->bfj", grad_sum, w_proj).astype(jnp.bfloat16)
    grad_p = product("bfc,bfj->bcj", embeds, grad_rows).astype(jnp.bfloat16)
    grad_fm = product("bfc,bcj->fj", embeds, grad_p)
    grad_lcb = product("bfc,bic->fi", embeds, grad_sum)
    grad_in = (
        grad_sum.astype(jnp.float32)
        + product("bfj,bcj->bfc", grad_rows, fm_proj)
        + product("fj,bcj->bfc", w_fm, grad_p)
        + product("fi,bic->bfc", w_lcb, grad_sum)
    )
    return (grad_in.astype(jnp.bfloat16), (grad_fm, grad_proj, grad_lcb, grad_gain))


def exchange(blocks, axes):
    return lax.all_to_all(blocks, axes, split_axis=0, concat_axis=0, tiled=True)


def dense_sum(partials, factor):
    n = lax.axis_size("grp") * lax.axis_size("emb")
    shapes = [part.shape for part in partials]
    flat = jnp.concatenate([part.reshape(-1) for part in partials])
    unit = 128 * n
    padded = -(-flat.shape[0] // unit) * unit
    flat = jnp.pad(flat, (0, padded - flat.shape[0])).astype(jnp.bfloat16)
    seen = exchange(flat.reshape(n, padded // unit, 128), BOTH)
    share = (jnp.sum(seen.astype(jnp.float32), axis=0) * factor).astype(jnp.bfloat16)
    total = exchange(jnp.broadcast_to(share[None], (n,) + share.shape), BOTH).reshape(-1)
    total = total.astype(jnp.float32)
    outs, at = [], 0
    for shape in shapes:
        size = 1
        for extent in shape:
            size *= extent
        outs.append(total[at : at + size].reshape(shape))
        at += size
    return outs


def local(pooled, upstream, ids_now, ids_next, tables, w_fm, w_proj, w_lcb, gain):
    n_grp, n_emb = lax.axis_size("grp"), lax.axis_size("emb")
    count, features, width = pooled.shape
    owned, rows = tables.shape[:2]
    ids = jnp.stack([ids_now, ids_next]).reshape(2, count, n_emb, owned)
    ids = exchange(ids.transpose(2, 0, 1, 3), "emb")
    row_index = jnp.arange(rows)
    wanted = (ids[:, 1, :, :, None] == row_index).astype(jnp.bfloat16)
    fetched = product("esfr,frc->esfc", wanted, tables).astype(jnp.bfloat16)
    next_rows = exchange(fetched, "emb")
    next_rows = next_rows.transpose(1, 0, 2, 3).reshape(count, features, width)
    grad_in, partials = layer_backward(pooled, upstream, w_fm, w_proj, w_lcb, gain)
    grad_in = grad_in.reshape(count, n_emb, owned, width).transpose(1, 0, 2, 3)
    grads = exchange(grad_in, "emb")
    hit = (ids[:, 0, :, :, None] == row_index).astype(jnp.bfloat16)
    part = product("esfr,esfc->frc", hit, grads).astype(jnp.bfloat16)
    part = part.reshape(owned, n_grp, rows // n_grp, width).transpose(1, 0, 2, 3)
    table_grad = jnp.sum(exchange(part, "grp").astype(jnp.float32), axis=0)
    dense = dense_sum(partials, 1.0 / (count * n_grp * n_emb))
    return (next_rows, table_grad, *dense)


def solution(mesh):
    return jax.shard_map(
        local,
        mesh=mesh,
        in_specs=(
            P(BOTH, None, None),
            P(BOTH, None, None),
            P(BOTH, None),
            P(BOTH, None),
            P("emb", None, None),
            P(),
            P(),
            P(),
            P(),
        ),
        out_specs=(P(BOTH, None, None), P("emb", "grp", None), P(), P(), P(), P()),
        check_vma=False,
    )
```

```python
import functools

import jax
import jax.numpy as jnp
from jax import lax
from jax.experimental import pallas as pl
from jax.experimental.pallas import tpu as pltpu
from jax.sharding import Mesh, PartitionSpec as P

F32, BF16 = jnp.float32, jnp.bfloat16
VMEM = pl.BlockSpec(memory_space=pltpu.VMEM)
LANES = 128
TILE = 8
STEP = 4
LIMIT = 40 * 1024 * 1024
PEER = ("grp", "lane")


BOTH = ("grp", "emb")


def product(form, left, right):
    return jnp.einsum(form, left, right, preferred_element_type=jnp.float32)


def layer_backward(embeds, cotangent, w_fm, w_proj, w_lcb, gain):
    fm_proj = product("bfc,fj->bcj", embeds, w_fm).astype(jnp.bfloat16)
    fm_rows = product("bfc,bcj->bfj", embeds, fm_proj).astype(jnp.bfloat16)
    projected = product("bfj,jc->bfc", fm_rows, w_proj)
    compressed = product("fi,bfc->bic", w_lcb, embeds)
    summed = embeds.astype(jnp.float32) + projected + compressed
    centre = jnp.mean(summed, axis=2, keepdims=True)
    spread = jnp.mean((summed - centre) ** 2, axis=2, keepdims=True)
    inverse = lax.rsqrt(spread + 1e-05)
    normed = (summed - centre) * inverse
    upper = cotangent.astype(jnp.float32)
    scaled = upper * gain
    grad_sum = inverse * (
        scaled
        - jnp.mean(scaled, axis=2, keepdims=True)
        - normed * jnp.mean(scaled * normed, axis=2, keepdims=True)
    )
    grad_sum = grad_sum.astype(jnp.bfloat16)
    grad_gain = jnp.sum(upper * normed, axis=(0, 1))
    grad_proj = product("bfj,bfc->jc", fm_rows, grad_sum)
    grad_rows = product("bfc,jc->bfj", grad_sum, w_proj).astype(jnp.bfloat16)
    grad_p = product("bfc,bfj->bcj", embeds, grad_rows).astype(jnp.bfloat16)
    grad_fm = product("bfc,bcj->fj", embeds, grad_p)
    grad_lcb = product("bfc,bic->fi", embeds, grad_sum)
    grad_in = (
        grad_sum.astype(jnp.float32)
        + product("bfj,bcj->bfc", grad_rows, fm_proj)
        + product("fj,bcj->bfc", w_fm, grad_p)
        + product("fi,bic->bfc", w_lcb, grad_sum)
    )
    return (grad_in.astype(jnp.bfloat16), (grad_fm, grad_proj, grad_lcb, grad_gain))


def exchange(blocks, axes):
    return lax.all_to_all(blocks, axes, split_axis=0, concat_axis=0, tiled=True)


def dense_sum(partials, factor):
    n = lax.axis_size("grp") * lax.axis_size("emb")
    shapes = [part.shape for part in partials]
    flat = jnp.concatenate([part.reshape(-1) for part in partials])
    unit = 128 * n
    padded = -(-flat.shape[0] // unit) * unit
    flat = jnp.pad(flat, (0, padded - flat.shape[0])).astype(jnp.bfloat16)
    seen = exchange(flat.reshape(n, padded // unit, 128), BOTH)
    share = (jnp.sum(seen.astype(jnp.float32), axis=0) * factor).astype(jnp.bfloat16)
    total = exchange(jnp.broadcast_to(share[None], (n,) + share.shape), BOTH).reshape(-1)
    total = total.astype(jnp.float32)
    outs, at = [], 0
    for shape in shapes:
        size = 1
        for extent in shape:
            size *= extent
        outs.append(total[at : at + size].reshape(shape))
        at += size
    return outs


def local(pooled, upstream, ids_now, ids_next, tables, w_fm, w_proj, w_lcb, gain):
    n_grp, n_emb = lax.axis_size("grp"), lax.axis_size("emb")
    count, features, width = pooled.shape
    owned, rows = tables.shape[:2]
    ids = jnp.stack([ids_now, ids_next]).reshape(2, count, n_emb, owned)
    ids = exchange(ids.transpose(2, 0, 1, 3), "emb")
    row_index = jnp.arange(rows)
    wanted = (ids[:, 1, :, :, None] == row_index).astype(jnp.bfloat16)
    fetched = product("esfr,frc->esfc", wanted, tables).astype(jnp.bfloat16)
    next_rows = exchange(fetched, "emb")
    next_rows = next_rows.transpose(1, 0, 2, 3).reshape(count, features, width)
    grad_in, partials = layer_backward(pooled, upstream, w_fm, w_proj, w_lcb, gain)
    grad_in = grad_in.reshape(count, n_emb, owned, width).transpose(1, 0, 2, 3)
    grads = exchange(grad_in, "emb")
    hit = (ids[:, 0, :, :, None] == row_index).astype(jnp.bfloat16)
    part = product("esfr,esfc->frc", hit, grads).astype(jnp.bfloat16)
    part = part.reshape(owned, n_grp, rows // n_grp, width).transpose(1, 0, 2, 3)
    table_grad = jnp.sum(exchange(part, "grp").astype(jnp.float32), axis=0)
    dense = dense_sum(partials, 1.0 / (count * n_grp * n_emb))
    return (next_rows, table_grad, *dense)


def mm(left, right, dims=((1,), (0,))):
    return lax.dot_general(left, right, (dims, ((), ())), preferred_element_type=F32)


def low_lanes(shape):
    return lax.broadcasted_iota(jnp.int32, shape, 1) < LANES // 2


def turn(tile):
    return pltpu.roll(tile, LANES // 2, 1)


def pair_up(first, second):
    return jnp.where(low_lanes(first.shape), first, turn(second))


class Wire:
    def __init__(self, count, peers):
        self.left = count * TILE
        self.half = self.left + self.left // 2
        self.dense = 2 * self.half
        self.dense_rows = 1024 // peers
        self.ids = self.dense + self.dense_rows
        self.out_rows = self.ids + 16


def pack_tables_kernel(place, tables, out):
    for f in range(TILE):
        whole = tables[f].astype(F32)
        out[f, 0:128] = whole[:, 0:128].astype(BF16)
        right = jnp.concatenate([whole[:, 128:192], whole[:, 128:192]], axis=1)
        out[f, 128:192] = jnp.where(low_lanes((64, LANES)), right[0:64], right[64:128]).astype(BF16)


def pack_tables(tables, place):
    rows, width = tables.shape[1:]
    return pl.pallas_call(
        pack_tables_kernel,
        grid_spec=pltpu.PrefetchScalarGridSpec(
            num_scalar_prefetch=1,
            grid=(1,),
            in_specs=[pl.BlockSpec((TILE, rows, width), lambda i, place: (place[0], 0, 0))],
            out_specs=pl.BlockSpec((TILE, 192, LANES), lambda i, place: (0, 0, 0)),
        ),
        out_shape=jax.ShapeDtypeStruct((TILE, 192, LANES), BF16),
        compiler_params=pltpu.CompilerParams(vmem_limit_bytes=LIMIT),
        name="pack_tables",
    )(place, tables)


def backward_kernel(
    n_grp, n_lane, wire,
    x_ref, u_ref, now_ref, next_ref, fm_ref, proj_ref, lcb_ref, gain_ref,
    out_ref,
    fm_t, lcb_t, grad, sum_fm, sum_proj, sum_lcb, sum_gain, ids,
):
    step = pl.program_id(0)
    width = x_ref.shape[2]
    scale = 1.0 / width

    @pl.when(step == 0)
    def _():
        fm_t[...] = fm_ref[...].astype(F32).T.astype(BF16)
        lcb_t[...] = lcb_ref[...].astype(F32).T.astype(BF16)
        sum_fm[...] = jnp.zeros_like(sum_fm)
        sum_proj[...] = jnp.zeros_like(sum_proj)
        sum_lcb[...] = jnp.zeros_like(sum_lcb)
        sum_gain[...] = jnp.zeros_like(sum_gain)

    fm, proj, lcb = fm_ref[...], proj_ref[...], lcb_ref[...]
    gain = gain_ref[...]
    for s in range(STEP):
        x = x_ref[s]
        p_t = mm(fm_t[...], x).astype(BF16)
        g = mm(x, p_t, ((1,), (1,))).astype(BF16)
        summed = x.astype(F32) + mm(g, proj) + mm(lcb_t[...], x)
        centre = jnp.sum(summed, axis=1, keepdims=True) * scale
        summed = summed - centre
        spread = jnp.sum(summed * summed, axis=1, keepdims=True) * scale
        inverse = lax.rsqrt(spread + 1e-05)
        normed = summed * inverse
        upper = u_ref[s].astype(F32)
        scaled = upper * gain
        first = jnp.sum(scaled, axis=1, keepdims=True) * scale
        second = jnp.sum(scaled * normed, axis=1, keepdims=True) * scale
        d_sum = (inverse * (scaled - first - normed * second)).astype(BF16)
        sum_gain[...] += jnp.sum((upper * normed).reshape(-1, 8, width), axis=0)
        d_g = mm(d_sum, proj, ((1,), (1,))).astype(BF16)
        d_p_t = mm(d_g, x, ((0,), (0,))).astype(BF16)
        grad[s, :, 0:width] = (
            d_sum.astype(F32) + mm(d_g, p_t) + mm(fm, d_p_t) + mm(lcb, d_sum)
        )
        sum_fm[...] += mm(x, d_p_t, ((1,), (1,)))
        sum_proj[:, 0:width] += mm(g, d_sum, ((0,), (0,)))
        sum_lcb[...] += mm(x, d_sum, ((1,), (1,)))

    for half in range(2):
        for peer in range(n_grp * n_lane):
            at = half * (n_grp * n_lane * TILE) + (peer % n_lane) * n_grp * TILE + (peer // n_lane) * TILE
            rows = [grad[s, at : at + TILE, 0:128] for s in range(STEP)]
            row = pl.multiple_of(half * wire.half + step * (STEP * TILE), 16)
            out_ref[peer, pl.ds(row, STEP * TILE)] = jnp.concatenate(rows, axis=0).astype(BF16)
            rest = [grad[s, at : at + TILE, 128:256] for s in range(STEP)]
            packed = pair_up(jnp.concatenate(rest[:2], axis=0), jnp.concatenate(rest[2:], axis=0))
            row = pl.multiple_of(half * wire.half + wire.left + step * (STEP * TILE // 2), 16)
            out_ref[peer, pl.ds(row, STEP * TILE // 2)] = packed.astype(BF16)

    @pl.when(step == pl.num_programs(0) - 1)
    def _():
        peers = n_grp * n_lane
        part = 256 // peers
        total = jnp.sum(sum_gain[...], axis=0, keepdims=True)
        high = total.astype(BF16).astype(F32)
        low = total - high
        both = [piece[:, 64 * c : 64 * c + 64] for piece in (high, low) for c in range(3)]
        column = jnp.concatenate(both + [jnp.zeros((2, 64), F32)], axis=0)
        column = jnp.concatenate([column, column], axis=1)
        for peer in range(peers):
            at = wire.dense
            here = slice(peer * part, (peer + 1) * part)
            out_ref[peer, at : at + part] = sum_fm[here].astype(BF16)
            out_ref[peer, at + part : at + 2 * part] = sum_lcb[here, 0:128].astype(BF16)
            out_ref[peer, at + 2 * part : at + 3 * part] = sum_lcb[here, 128:256].astype(BF16)
            here = slice(peer * part // 2, (peer + 1) * part // 2)
            right = jnp.where(low_lanes((part // 2, LANES)), sum_proj[here, 128:256], column)
            both = jnp.concatenate([sum_proj[here, 0:128], right], axis=0)
            out_ref[peer, at + 3 * part : at + 4 * part] = both.astype(BF16)

        count = now_ref.shape[0]
        lane = lax.broadcasted_iota(jnp.int32, (16, LANES), 1)
        sample = lax.broadcasted_iota(jnp.int32, (16, LANES), 0)
        mine = (lane // TILE == sample) & (sample < count)
        for which, ref in enumerate((now_ref, next_ref)):
            ids[which] = jnp.zeros_like(ids[which])
            ids[which, 0:count] = ref[...].astype(F32)
        for peer in range(peers):
            at = (peer % n_lane) * n_grp * TILE + (peer // n_lane) * TILE
            rows = []
            for which in range(2):
                for half in range(2):
                    line = ids[which, :, half * 128 : half * 128 + 128]
                    if at:
                        line = pltpu.roll(line, LANES - at, 1)
                    line = pltpu.roll(line, 0, 1, stride=TILE, stride_axis=0)
                    rows.append(jnp.sum(jnp.where(mine, line, 0.0), axis=0, keepdims=True))
            rows.append(jnp.zeros((12, LANES), F32))
            out_ref[peer, wire.ids : wire.ids + 16] = jnp.concatenate(rows, axis=0).astype(BF16)


def backward(n_grp, n_lane, wire, pooled, upstream, ids_now, ids_next, w_fm, w_proj, w_lcb, gain):
    count, features, width = pooled.shape
    rank = w_fm.shape[1]
    peers = n_grp * n_lane
    block = pl.BlockSpec((STEP, features, width), lambda i: (i, 0, 0))

    def whole(array):
        return pl.BlockSpec(array.shape, lambda i: (0,) * array.ndim)

    gain = gain.reshape(1, width)
    rest = (ids_now, ids_next, w_fm, w_proj, w_lcb, gain)
    return pl.pallas_call(
        functools.partial(backward_kernel, n_grp, n_lane, wire),
        grid=(count // STEP,),
        in_specs=[block, block] + [whole(array) for array in rest],
        out_specs=pl.BlockSpec((peers, wire.out_rows, LANES), lambda i: (0, 0, 0)),
        out_shape=jax.ShapeDtypeStruct((peers, wire.out_rows, LANES), BF16),
        scratch_shapes=[
            pltpu.VMEM((rank, features), BF16),
            pltpu.VMEM((features, features), BF16),
            pltpu.VMEM((STEP, features, 256), F32),
            pltpu.VMEM((features, rank), F32),
            pltpu.VMEM((rank, 256), F32),
            pltpu.VMEM((features, features), F32),
            pltpu.VMEM((8, width), F32),
            pltpu.VMEM((2, 16, features), F32),
        ],
        compiler_params=pltpu.CompilerParams(vmem_limit_bytes=LIMIT),
        cost_estimate=pl.CostEstimate(flops=6 * 10**9, bytes_accessed=4 * 10**6, transcendentals=0),
        name="layer_backward",
    )(pooled, upstream, *rest)


def part_kernel(n_grp, wire, other, half_ref, seen, *refs):
    out, held = refs[0], refs[-1]
    peers = seen.shape[0]
    half = 1 - half_ref[0] if other else half_ref[0]
    if other:
        dense = refs[1]
        total = seen[0, wire.dense : wire.ids].astype(F32)
        for peer in range(1, peers):
            total = total + seen[peer, wire.dense : wire.ids].astype(F32)
        dense[...] = total
    lane = lax.broadcasted_iota(jnp.int32, (1, LANES), 1)
    start = ((lane % TILE) * LANES).astype(F32)
    keys = []
    for peer in range(peers):
        at = peer * LANES
        base = pl.multiple_of(half * wire.half, 16)
        held[at : at + wire.left, 0:128] = seen[peer, pl.ds(base, wire.left)]
        base = pl.multiple_of(half * wire.half + wire.left, 16)
        right = seen[peer, pl.ds(base, wire.left // 2)]
        turned = turn(right.astype(F32)).astype(BF16)
        for i in range(wire.left // 32):
            held[at + 32 * i : at + 32 * i + 16, 128:256] = right[16 * i : 16 * i + 16]
            held[at + 32 * i + 16 : at + 32 * i + 32, 128:256] = turned[16 * i : 16 * i + 16]
        if wire.left < LANES:
            held[at + wire.left : at + LANES] = jnp.zeros((LANES - wire.left, 256), BF16)
        ids = seen[peer, wire.ids : wire.ids + 16].astype(F32)
        key = jnp.where(half == 0, ids[0:1], ids[1:2]) + start
        keys.append(jnp.where(lane < wire.left, key, -1.0))
    keys = jnp.concatenate(keys, axis=1)
    piece = LANES // n_grp
    for pair in range(TILE // 2):
        row = lax.broadcasted_iota(jnp.int32, (256, 1), 0).astype(F32) + 256.0 * pair
        hit = jnp.where(keys == row, 1.0, 0.0).astype(BF16)
        part = mm(hit, held[...])
        for f in range(2):
            for g in range(n_grp):
                at = f * LANES + g * piece
                rows = part[at : at + piece]
                out[g, 2 * pair + f, 0:piece] = rows[:, 0:128].astype(out.dtype)
                packed = pair_up(rows[: piece // 2, 128:256], rows[piece // 2 :, 128:256])
                out[g, 2 * pair + f, piece : piece + piece // 2] = packed.astype(out.dtype)


def part_sums(n_grp, wire, other, half, seen):
    peers = seen.shape[0]
    piece = LANES // n_grp
    shape = (n_grp, TILE, piece + piece // 2, LANES)
    out_shape = [jax.ShapeDtypeStruct(shape, BF16 if other else F32)]
    if other:
        out_shape.append(jax.ShapeDtypeStruct((wire.dense_rows, LANES), F32))
    return pl.pallas_call(
        functools.partial(part_kernel, n_grp, wire, other),
        in_specs=[pl.BlockSpec(memory_space=pltpu.SMEM), VMEM],
        out_specs=[VMEM] * len(out_shape),
        out_shape=out_shape,
        scratch_shapes=[pltpu.VMEM((peers * LANES, 256), BF16)],
        compiler_params=pltpu.CompilerParams(vmem_limit_bytes=LIMIT),
        cost_estimate=pl.CostEstimate(flops=2 * 10**9, bytes_accessed=2 * 10**6, transcendentals=0),
        name="part_other" if other else "part_own",
    )(half, seen)


def lookup_kernel(wire, factor, place, tables, crossed, ids_ref, dense_own, dense_seen, out, held):
    peers = ids_ref.shape[0]
    half = place[1]
    rows = tables.shape[1]
    for f in range(TILE):
        at = f * rows
        held[half, at : at + rows, 0:192] = tables[f]
        held[1 - half, at : at + rows, 0:128] = crossed[f, 0:128]
        right = crossed[f, 128:192]
        held[1 - half, at : at + 64, 128:256] = right
        held[1 - half, at + 64 : at + 128, 128:256] = turn(right.astype(F32)).astype(BF16)
    ids = ids_ref[...].astype(F32).reshape(peers * 16, LANES)
    lane = lax.broadcasted_iota(jnp.int32, (1, LANES), 1)
    keys = (ids + ((lane % TILE) * LANES).astype(F32)).T
    column = lax.broadcasted_iota(jnp.int32, (1, TILE * rows), 1).astype(F32)
    total = ((dense_own[...] + dense_seen[...]) * factor).astype(BF16)
    for which in range(2):
        for pair in range(peers // 2):
            mine = []
            for peer in (2 * pair, 2 * pair + 1):
                at = peer * 16 + 2 + which
                mine.append(keys[0 : wire.left, at : at + 1])
            hit = jnp.where(jnp.concatenate(mine, axis=0) == column, 1.0, 0.0).astype(BF16)
            both = mm(hit, held[which])
            for k in range(2):
                got = both[k * wire.left : (k + 1) * wire.left]
                peer, base = 2 * pair + k, which * wire.half
                out[peer, base : base + wire.left] = got[:, 0:128].astype(BF16)
                for i in range(wire.left // 32):
                    packed = pair_up(got[32 * i : 32 * i + 16, 128:256], got[32 * i + 16 : 32 * i + 32, 128:256])
                    at = base + wire.left + 16 * i
                    out[peer, at : at + 16] = packed.astype(BF16)
    for peer in range(peers):
        out[peer, wire.dense : wire.ids] = total


def lookup(wire, factor, place, tables, crossed, seen, dense_own, dense_seen):
    peers = seen.shape[0]
    rows, width = tables.shape[1:]

    def whole(array):
        return pl.BlockSpec(array.shape, lambda i, place: (0,) * array.ndim)

    at = wire.ids // 16
    return pl.pallas_call(
        functools.partial(lookup_kernel, wire, factor),
        grid_spec=pltpu.PrefetchScalarGridSpec(
            num_scalar_prefetch=1,
            grid=(1,),
            in_specs=[
                pl.BlockSpec((TILE, rows, width), lambda i, place: (place[0], 0, 0)),
                whole(crossed),
                pl.BlockSpec((peers, 16, LANES), lambda i, place: (0, at, 0)),
                whole(dense_own),
                whole(dense_seen),
            ],
            out_specs=pl.BlockSpec((peers, wire.ids, LANES), lambda i, place: (0, 0, 0)),
            scratch_shapes=[pltpu.VMEM((2, TILE * rows, 256), BF16)],
        ),
        out_shape=jax.ShapeDtypeStruct((peers, wire.ids, LANES), BF16),
        compiler_params=pltpu.CompilerParams(vmem_limit_bytes=LIMIT),
        cost_estimate=pl.CostEstimate(flops=2 * 10**9, bytes_accessed=4 * 10**6, transcendentals=0),
        name="lookup",
    )(place, tables, crossed, seen, dense_own, dense_seen)


def unpack_kernel(n_grp, n_lane, wire, seen, rows_out, fm, proj, lcb, gain):
    step = pl.program_id(0)
    peers = n_grp * n_lane
    for half in range(2):
        for q in range(n_lane):
            for gg in range(n_grp // 2):
                left, right = [], []
                for g in (2 * gg, 2 * gg + 1):
                    peer = g * n_lane + q
                    row = pl.multiple_of(half * wire.half + step * 32, 16)
                    left.append(seen[peer, pl.ds(row, 32)].astype(F32))
                    row = pl.multiple_of(half * wire.half + wire.left + step * 16, 16)
                    packed = seen[peer, pl.ds(row, 16)].astype(F32)
                    right.append(jnp.concatenate([packed, turn(packed)], axis=0))
                at = half * 128 + q * n_grp * TILE + gg * 16
                for s in range(STEP):
                    here = slice(s * TILE, s * TILE + TILE)
                    rows_out[s, at : at + 16, 0:128] = jnp.concatenate(
                        [left[0][here], left[1][here]], axis=0
                    ).astype(BF16)
                    rows_out[s, at : at + 16, 128:192] = jnp.concatenate(
                        [right[0][here], right[1][here]], axis=0
                    )[:, 0:64].astype(BF16)

    @pl.when(step == 0)
    def _():
        part = 256 // peers
        for peer in range(peers):
            dense = seen[peer, wire.dense : wire.ids].astype(F32)
            here = slice(peer * part, (peer + 1) * part)
            fm[here] = dense[0:part]
            lcb[here, 0:128] = dense[part : 2 * part]
            lcb[here, 128:256] = dense[2 * part : 3 * part]
            here = slice(peer * part // 2, (peer + 1) * part // 2)
            proj[here, 0:128] = dense[3 * part : 3 * part + part // 2]
            last = dense[3 * part + part // 2 :]
            proj[here, 128:192] = last[:, 0:64]
            if peer == 0:
                total = turn(last)
                total = total[0:3] + total[3:6]
                gain[:, 0:128] = jnp.where(low_lanes((1, LANES)), total[0:1], turn(total)[1:2])
                gain[:, 128:192] = total[2:3, 0:64]


def unpack(n_grp, n_lane, wire, count, seen):
    def whole(*shape):
        return pl.BlockSpec(shape, lambda i: (0,) * len(shape))

    shapes = [(256, 128), (128, 192), (256, 256), (1, 192)]
    return pl.pallas_call(
        functools.partial(unpack_kernel, n_grp, n_lane, wire),
        grid=(count // STEP,),
        in_specs=[whole(*seen.shape)],
        out_specs=[pl.BlockSpec((STEP, 256, 192), lambda i: (i, 0, 0))] + [whole(*shape) for shape in shapes],
        out_shape=[jax.ShapeDtypeStruct((count, 256, 192), BF16)]
        + [jax.ShapeDtypeStruct(shape, F32) for shape in shapes],
        compiler_params=pltpu.CompilerParams(vmem_limit_bytes=LIMIT),
        cost_estimate=pl.CostEstimate(flops=0, bytes_accessed=4 * 10**6, transcendentals=0),
        name="unpack_rows",
    )(seen)


def finish_kernel(seen, out):
    piece = out.shape[1]
    for f in range(TILE):
        out[f, :, 0:128] = seen[0, f, 0:piece].astype(F32)
        packed = seen[0, f, piece : piece + piece // 2].astype(F32)
        out[f, 0 : piece // 2, 128:192] = packed[:, 0:64]
        out[f, piece // 2 : piece, 128:192] = turn(packed)[:, 0:64]


def finish(seen):
    n_grp, _, packed, _ = seen.shape
    piece = packed * 2 // 3
    return pl.pallas_call(
        finish_kernel,
        grid=(n_grp,),
        in_specs=[pl.BlockSpec((1, TILE, packed, LANES), lambda i: (i, 0, 0, 0))],
        out_specs=pl.BlockSpec((TILE, piece, 192), lambda i: (i, 0, 0)),
        out_shape=jax.ShapeDtypeStruct((n_grp * TILE, piece, 192), F32),
        compiler_params=pltpu.CompilerParams(vmem_limit_bytes=LIMIT),
        name="finish_tables",
    )(seen)


def cross(array):
    return lax.ppermute(array, "half", [(0, 1), (1, 0)])


def halves(pooled, upstream, ids_now, ids_next, tables, w_fm, w_proj, w_lcb, gain):
    n_grp, n_lane = lax.axis_size("grp"), lax.axis_size("lane")
    count = pooled.shape[0]
    wire = Wire(count, n_grp * n_lane)
    factor = 1.0 / (count * n_grp * 2 * n_lane)
    half = lax.axis_index("half").astype(jnp.int32)
    place = jnp.stack([lax.axis_index("grp").astype(jnp.int32), half])
    crossed = cross(pack_tables(tables, place))
    sent = backward(n_grp, n_lane, wire, pooled, upstream, ids_now, ids_next, w_fm, w_proj, w_lcb, gain)
    seen = exchange(sent, PEER)
    part, dense = part_sums(n_grp, wire, True, half[None], seen)
    dense_seen = cross(dense)
    part_seen = cross(part)
    (own,) = part_sums(n_grp, wire, False, half[None], seen)
    rows = exchange(lookup(wire, factor, place, tables, crossed, seen, dense, dense_seen), PEER)
    next_rows, grad_fm, grad_proj, grad_lcb, grad_gain = unpack(n_grp, n_lane, wire, count, rows)
    both = (own + part_seen.astype(F32)).astype(BF16)
    table_grad = finish(exchange(both, "grp"))
    return next_rows, table_grad, grad_fm, grad_proj, grad_lcb, grad_gain.reshape(-1)


def solution(mesh):
    n_grp, n_emb = mesh.shape["grp"], mesh.shape["emb"]
    split = n_emb % 2 == 0 and n_grp * (n_emb // 2) == 16 and n_grp % 2 == 0

    def run(*args):
        pooled, _, _, _, tables, w_fm = args[:6]
        count = pooled.shape[0] // (n_grp * n_emb)
        fits = (
            split
            and pooled.shape[1:] == (256, 192)
            and tables.shape[1] == 128
            and w_fm.shape[1] == 128
            and pooled.shape[1] == n_grp * n_emb * TILE
            and count % STEP == 0
            and count <= 16
        )
        if fits:
            devices = mesh.devices.reshape(n_grp, 2, n_emb // 2)
            where, emb, body = Mesh(devices, ("grp", "half", "lane")), ("half", "lane"), halves
        else:
            where, emb, body = mesh, ("emb",), local
        both = ("grp",) + emb
        return jax.shard_map(
            body,
            mesh=where,
            in_specs=(
                P(both, None, None),
                P(both, None, None),
                P(both, None),
                P(both, None),
                P(emb, None, None),
                P(),
                P(),
                P(),
                P(),
            ),
            out_specs=(P(both, None, None), P(emb, "grp", None), P(), P(), P(), P()),
            check_vma=False,
        )(*args)

    return run
```

```python
import functools

import jax
import jax.numpy as jnp
from jax import lax
from jax.experimental import pallas as pl
from jax.experimental.pallas import tpu as pltpu
from jax.sharding import Mesh, PartitionSpec as P

F32, BF16 = jnp.float32, jnp.bfloat16
SMEM = pl.BlockSpec(memory_space=pltpu.SMEM)
VMEM = pl.BlockSpec(memory_space=pltpu.VMEM)
LANES = 128
TILE = 8
STEP = 4
LIMIT = 40 * 1024 * 1024
PEER = ("grp", "lane")


BOTH = ("grp", "emb")


def product(form, left, right):
    return jnp.einsum(form, left, right, preferred_element_type=jnp.float32)


def layer_backward(embeds, cotangent, w_fm, w_proj, w_lcb, gain):
    fm_proj = product("bfc,fj->bcj", embeds, w_fm).astype(jnp.bfloat16)
    fm_rows = product("bfc,bcj->bfj", embeds, fm_proj).astype(jnp.bfloat16)
    projected = product("bfj,jc->bfc", fm_rows, w_proj)
    compressed = product("fi,bfc->bic", w_lcb, embeds)
    summed = embeds.astype(jnp.float32) + projected + compressed
    centre = jnp.mean(summed, axis=2, keepdims=True)
    spread = jnp.mean((summed - centre) ** 2, axis=2, keepdims=True)
    inverse = lax.rsqrt(spread + 1e-05)
    normed = (summed - centre) * inverse
    upper = cotangent.astype(jnp.float32)
    scaled = upper * gain
    grad_sum = inverse * (
        scaled
        - jnp.mean(scaled, axis=2, keepdims=True)
        - normed * jnp.mean(scaled * normed, axis=2, keepdims=True)
    )
    grad_sum = grad_sum.astype(jnp.bfloat16)
    grad_gain = jnp.sum(upper * normed, axis=(0, 1))
    grad_proj = product("bfj,bfc->jc", fm_rows, grad_sum)
    grad_rows = product("bfc,jc->bfj", grad_sum, w_proj).astype(jnp.bfloat16)
    grad_p = product("bfc,bfj->bcj", embeds, grad_rows).astype(jnp.bfloat16)
    grad_fm = product("bfc,bcj->fj", embeds, grad_p)
    grad_lcb = product("bfc,bic->fi", embeds, grad_sum)
    grad_in = (
        grad_sum.astype(jnp.float32)
        + product("bfj,bcj->bfc", grad_rows, fm_proj)
        + product("fj,bcj->bfc", w_fm, grad_p)
        + product("fi,bic->bfc", w_lcb, grad_sum)
    )
    return (grad_in.astype(jnp.bfloat16), (grad_fm, grad_proj, grad_lcb, grad_gain))


def exchange(blocks, axes):
    return lax.all_to_all(blocks, axes, split_axis=0, concat_axis=0, tiled=True)


def dense_sum(partials, factor):
    n = lax.axis_size("grp") * lax.axis_size("emb")
    shapes = [part.shape for part in partials]
    flat = jnp.concatenate([part.reshape(-1) for part in partials])
    unit = 128 * n
    padded = -(-flat.shape[0] // unit) * unit
    flat = jnp.pad(flat, (0, padded - flat.shape[0])).astype(jnp.bfloat16)
    seen = exchange(flat.reshape(n, padded // unit, 128), BOTH)
    share = (jnp.sum(seen.astype(jnp.float32), axis=0) * factor).astype(jnp.bfloat16)
    total = exchange(jnp.broadcast_to(share[None], (n,) + share.shape), BOTH).reshape(-1)
    total = total.astype(jnp.float32)
    outs, at = [], 0
    for shape in shapes:
        size = 1
        for extent in shape:
            size *= extent
        outs.append(total[at : at + size].reshape(shape))
        at += size
    return outs


def local(pooled, upstream, ids_now, ids_next, tables, w_fm, w_proj, w_lcb, gain):
    n_grp, n_emb = lax.axis_size("grp"), lax.axis_size("emb")
    count, features, width = pooled.shape
    owned, rows = tables.shape[:2]
    ids = jnp.stack([ids_now, ids_next]).reshape(2, count, n_emb, owned)
    ids = exchange(ids.transpose(2, 0, 1, 3), "emb")
    row_index = jnp.arange(rows)
    wanted = (ids[:, 1, :, :, None] == row_index).astype(jnp.bfloat16)
    fetched = product("esfr,frc->esfc", wanted, tables).astype(jnp.bfloat16)
    next_rows = exchange(fetched, "emb")
    next_rows = next_rows.transpose(1, 0, 2, 3).reshape(count, features, width)
    grad_in, partials = layer_backward(pooled, upstream, w_fm, w_proj, w_lcb, gain)
    grad_in = grad_in.reshape(count, n_emb, owned, width).transpose(1, 0, 2, 3)
    grads = exchange(grad_in, "emb")
    hit = (ids[:, 0, :, :, None] == row_index).astype(jnp.bfloat16)
    part = product("esfr,esfc->frc", hit, grads).astype(jnp.bfloat16)
    part = part.reshape(owned, n_grp, rows // n_grp, width).transpose(1, 0, 2, 3)
    table_grad = jnp.sum(exchange(part, "grp").astype(jnp.float32), axis=0)
    dense = dense_sum(partials, 1.0 / (count * n_grp * n_emb))
    return (next_rows, table_grad, *dense)


def params(**more):
    return pltpu.CompilerParams(vmem_limit_bytes=LIMIT, **more)


def mm(left, right, dims=((1,), (0,))):
    return lax.dot_general(left, right, (dims, ((), ())), preferred_element_type=F32)


def mm_nt(left, right):
    return mm(left, right, ((1,), (1,)))


def low_lanes(shape):
    return lax.broadcasted_iota(jnp.int32, shape, 1) < LANES // 2


def turn(tile):
    return pltpu.roll(tile, LANES // 2, 1)


def identity(rows, lanes):
    row = lax.broadcasted_iota(jnp.int32, (rows, lanes), 0)
    return jnp.where(row == lax.broadcasted_iota(jnp.int32, (rows, lanes), 1), 1.0, 0.0).astype(BF16)


class Wire:
    def __init__(self, count, peers):
        self.left = count * TILE
        self.half = self.left + self.left // 2
        self.ids = 16
        self.dense = 1024 // peers


def place_of(n_grp, n_lane, peer):
    return (peer % n_lane) * n_grp * TILE + (peer // n_lane) * TILE


def backward_kernel(
    n_grp, n_lane, wire,
    half_ref, x_ref, u_ref, now_ref, next_ref, fm_ref, proj_t_ref, lcb_ref, gain_ref,
    other_ref, own_ref,
    fm_t, proj, lcb_t, gains, eye, left_in, right_in, grads, turned, sum_fm_t, sum_proj_t, sum_lcb, sum_gain, ids,
):
    step = pl.program_id(0)
    width, features = x_ref.shape[1:]
    rank = fm_ref.shape[1]
    peers = n_grp * n_lane
    scale = 1.0 / width

    @pl.when(step == 0)
    def _():
        turned_fm = fm_ref[...].astype(F32).T.astype(BF16)
        fm_t[...] = turned_fm
        for s in range(STEP):
            right_in[s, rank : 2 * rank] = turned_fm
        proj[...] = proj_t_ref[...].astype(F32).T.astype(BF16)
        lcb_t[...] = lcb_ref[...].astype(F32).T.astype(BF16)
        column = jnp.broadcast_to(gain_ref[...], (LANES, width)).T
        gains[:, 0:128] = column
        gains[:, 128:256] = column
        eye[...] = identity(features, features)
        sum_fm_t[...] = jnp.zeros_like(sum_fm_t)
        sum_proj_t[...] = jnp.zeros_like(sum_proj_t)
        sum_lcb[...] = jnp.zeros_like(sum_lcb)
        sum_gain[...] = jnp.zeros_like(sum_gain)

    x_all = x_ref[...].reshape(STEP * width, features)
    p_all = mm(x_all, fm_ref[...]).astype(BF16)
    mixed = mm(x_all, lcb_ref[...])
    d_sums = []
    add_fm, add_proj, add_gain = 0.0, 0.0, 0.0
    for s in range(STEP):
        here = slice(s * width, (s + 1) * width)
        x = x_ref[s]
        left_in[s, :, 0:rank] = p_all[here]
        p_t = mm_nt(fm_t[...], x).astype(BF16)
        g_t = mm(p_t, x).astype(BF16)
        summed = x.astype(F32) + mm(proj_t_ref[...], g_t) + mixed[here]
        centre = jnp.sum(summed, axis=0, keepdims=True) * scale
        summed = summed - centre
        spread = jnp.sum(summed * summed, axis=0, keepdims=True) * scale
        inverse = lax.rsqrt(spread + 1e-05)
        normed = summed * inverse
        upper = u_ref[s].astype(F32)
        scaled = upper * gains[...]
        first = jnp.sum(scaled, axis=0, keepdims=True) * scale
        second = jnp.sum(scaled * normed, axis=0, keepdims=True) * scale
        d_sum = (inverse * (scaled - first - normed * second)).astype(BF16)
        add_gain += upper * normed
        d_g_t = mm(proj[...], d_sum).astype(BF16)
        right_in[s, 0:rank] = d_g_t
        left_in[s, :, rank : 2 * rank] = mm_nt(x, d_g_t).astype(BF16)
        d_p_t = mm_nt(d_g_t, x).astype(BF16)
        add_fm += mm(d_p_t, x)
        add_proj += mm_nt(d_sum, g_t)
        d_sums.append(d_sum)
    d_all = jnp.concatenate(d_sums, axis=0)
    back = mm(d_all, lcb_t[...])
    sum_lcb[...] += mm(x_all, d_all, ((0,), (0,)))
    sum_fm_t[...] += add_fm
    sum_proj_t[...] += add_proj
    sum_gain[...] += add_gain
    for s in range(STEP):
        here = slice(s * width, (s + 1) * width)
        grad = d_sums[s].astype(F32) + mm(left_in[s], right_in[s]) + back[here]
        grad = grad.astype(BF16)
        grads[s * 128 : s * 128 + 128] = grad[0:128]
        at = 512 + 64 * (2 * (s % 2) + s // 2)
        grads[at : at + 64] = grad[128:192]
    rows = mm_nt(eye[...], grads[...])
    turned[0] = rows[0:128]
    turned[1] = rows[128:256]

    half = half_ref[0]
    for out_ref, which in ((other_ref, 1 - half), (own_ref, half)):
        for peer in range(peers):
            at = place_of(n_grp, n_lane, peer)
            line = turned[which, at : at + TILE]
            left = jnp.concatenate([line[:, s * 128 : s * 128 + 128] for s in range(STEP)], axis=0)
            row = pl.multiple_of(step * 32, 16)
            out_ref[peer, pl.ds(row, 32)] = left.astype(BF16)
            right = jnp.concatenate([line[:, 512:640], line[:, 640:768]], axis=0)
            row = pl.multiple_of(wire.left + step * 16, 16)
            out_ref[peer, pl.ds(row, 16)] = right.astype(BF16)

    @pl.when(step == pl.num_programs(0) - 1)
    def _():
        part = features // peers
        third = width // peers
        total = jnp.sum((sum_gain[:, 0:128] + sum_gain[:, 128:256]).T, axis=0, keepdims=True)
        high = total.astype(BF16).astype(F32)
        low = total - high
        middle = jnp.concatenate([high[:, 128:192], low[:, 128:192]], axis=1)
        gain_rows = [high[:, 0:128], middle, low[:, 0:128], jnp.zeros((1, LANES), F32)]
        total_fm = sum_fm_t[...].T
        for peer in range(peers):
            at = wire.half
            here = slice(peer * part, (peer + 1) * part)
            own_ref[peer, at : at + part] = total_fm[here].astype(BF16)
            own_ref[peer, at + part : at + 2 * part] = sum_lcb[here, 0:128].astype(BF16)
            own_ref[peer, at + 2 * part : at + 3 * part] = sum_lcb[here, 128:256].astype(BF16)
            last = [sum_proj_t[peer * third : (peer + 1) * third]] + gain_rows
            own_ref[peer, at + 3 * part : at + 4 * part] = jnp.concatenate(last, axis=0).astype(BF16)

        count = now_ref.shape[0]
        lane = lax.broadcasted_iota(jnp.int32, (16, LANES), 1)
        sample = lax.broadcasted_iota(jnp.int32, (16, LANES), 0)
        mine = (lane // TILE == sample) & (sample < count)
        for which, ref in enumerate((now_ref, next_ref)):
            ids[which] = jnp.zeros_like(ids[which])
            ids[which, 0:count] = ref[...].astype(F32)
        for peer in range(peers):
            at = place_of(n_grp, n_lane, peer)
            lines = []
            for which in range(2):
                for side in range(2):
                    line = ids[which, :, side * 128 : side * 128 + 128]
                    if at:
                        line = pltpu.roll(line, LANES - at, 1)
                    line = pltpu.roll(line, 0, 1, stride=TILE, stride_axis=0)
                    lines.append(jnp.sum(jnp.where(mine, line, 0.0), axis=0, keepdims=True))
            lines.append(jnp.zeros((12, LANES), F32))
            other_ref[peer, wire.half : wire.half + 16] = jnp.concatenate(lines, axis=0).astype(BF16)


def backward(n_grp, n_lane, wire, half, pooled_t, upstream_t, ids_now, ids_next, w_fm, w_proj_t, w_lcb, gain):
    count, width, features = pooled_t.shape
    rank = w_fm.shape[1]
    peers = n_grp * n_lane
    block = pl.BlockSpec((STEP, width, features), lambda i: (i, 0, 0))

    def whole(shape):
        return pl.BlockSpec(shape, lambda i: (0,) * len(shape))

    rest = (ids_now, ids_next, w_fm, w_proj_t, w_lcb, gain.reshape(1, width))
    shapes = [(peers, wire.half + wire.ids, LANES), (peers, wire.half + wire.dense, LANES)]
    return pl.pallas_call(
        functools.partial(backward_kernel, n_grp, n_lane, wire),
        grid=(count // STEP,),
        in_specs=[SMEM, block, block] + [whole(array.shape) for array in rest],
        out_specs=[whole(shape) for shape in shapes],
        out_shape=[jax.ShapeDtypeStruct(shape, BF16) for shape in shapes],
        scratch_shapes=[
            pltpu.VMEM((rank, features), BF16),
            pltpu.VMEM((rank, width), BF16),
            pltpu.VMEM((features, features), BF16),
            pltpu.VMEM((width, features), F32),
            pltpu.VMEM((features, features), BF16),
            pltpu.VMEM((STEP, width, 2 * rank), BF16),
            pltpu.VMEM((STEP, 2 * rank, features), BF16),
            pltpu.VMEM((STEP * width, features), BF16),
            pltpu.VMEM((2, features // 2, STEP * width), F32),
            pltpu.VMEM((rank, features), F32),
            pltpu.VMEM((width, rank), F32),
            pltpu.VMEM((features, features), F32),
            pltpu.VMEM((width, features), F32),
            pltpu.VMEM((2, 16, features), F32),
        ],
        compiler_params=params(),
        cost_estimate=pl.CostEstimate(flops=10**9, bytes_accessed=4 * 10**6, transcendentals=0),
        name="layer_backward",
    )(half, pooled_t, upstream_t, *rest)


def part_kernel(n_grp, wire, other, half_ref, seen, ids_ref, *refs):
    out, held = refs[0], refs[-1]
    peers = seen.shape[0]
    half = 1 - half_ref[0] if other else half_ref[0]
    if not other:
        dense = refs[1]
        total = seen[0, wire.half : wire.half + wire.dense].astype(F32)
        for peer in range(1, peers):
            total = total + seen[peer, wire.half : wire.half + wire.dense].astype(F32)
        dense[...] = total
    lane = lax.broadcasted_iota(jnp.int32, (1, LANES), 1)
    start = ((lane % TILE) * LANES).astype(F32)
    keys = []
    for peer in range(peers):
        at = peer * LANES
        held[at : at + wire.left, 0:128] = seen[peer, 0 : wire.left]
        right = seen[peer, wire.left : wire.half]
        turned = turn(right.astype(F32)).astype(BF16)
        for i in range(wire.left // 32):
            held[at + 32 * i : at + 32 * i + 16, 128:256] = right[16 * i : 16 * i + 16]
            held[at + 32 * i + 16 : at + 32 * i + 32, 128:256] = turned[16 * i : 16 * i + 16]
        if wire.left < LANES:
            held[at + wire.left : at + LANES] = jnp.zeros((LANES - wire.left, 256), BF16)
        ids = ids_ref[peer].astype(F32)
        key = jnp.where(half == 0, ids[0:1], ids[1:2]) + start
        keys.append(jnp.where(lane < wire.left, key, -1.0))
    keys = jnp.concatenate(keys, axis=1)
    piece = LANES // n_grp
    for pair in range(TILE // 2):
        row = lax.broadcasted_iota(jnp.int32, (256, 1), 0).astype(F32) + 256.0 * pair
        hit = jnp.where(keys == row, 1.0, 0.0).astype(BF16)
        part = mm(hit, held[...])
        for f in range(2):
            for g in range(n_grp):
                at = f * LANES + g * piece
                rows = part[at : at + piece]
                out[g, 2 * pair + f, 0:piece] = rows[:, 0:128].astype(out.dtype)
                second = turn(rows[piece // 2 :, 128:256])
                packed = jnp.where(low_lanes(second.shape), rows[: piece // 2, 128:256], second)
                out[g, 2 * pair + f, piece : piece + piece // 2] = packed.astype(out.dtype)


def part_sums(n_grp, wire, other, half, seen, ids):
    peers = seen.shape[0]
    piece = LANES // n_grp
    shapes = [jax.ShapeDtypeStruct((n_grp, TILE, piece + piece // 2, LANES), BF16 if other else F32)]
    if not other:
        shapes.append(jax.ShapeDtypeStruct((wire.dense, LANES), F32))

    def whole(shape):
        return pl.BlockSpec(shape, lambda i: (0,) * len(shape))

    at = wire.half // 16
    return pl.pallas_call(
        functools.partial(part_kernel, n_grp, wire, other),
        grid=(1,),
        in_specs=[SMEM, whole(seen.shape), pl.BlockSpec((peers, 16, LANES), lambda i: (0, at, 0))],
        out_specs=[whole(shape.shape) for shape in shapes],
        out_shape=shapes,
        scratch_shapes=[pltpu.VMEM((peers * LANES, 256), BF16)],
        compiler_params=params(),
        cost_estimate=pl.CostEstimate(flops=10**9, bytes_accessed=10**6, transcendentals=0),
        name="part_other" if other else "part_own",
    )(half, seen, ids)


def lookup_kernel(wire, factor, half_ref, mine_t, crossed_t, ids_ref, dense_own, dense_seen, out, held):
    peers = ids_ref.shape[0]
    half = half_ref[0]
    for f in range(TILE):
        at = f * LANES
        for side, ref in ((half, mine_t), (1 - half, crossed_t)):
            held[side, 0:192, at : at + LANES] = ref[f]
            held[side, 192:256, at : at + LANES] = ref[f, 128:192]
    ids = ids_ref[...].astype(F32).reshape(peers * 16, LANES)
    lane = lax.broadcasted_iota(jnp.int32, (1, LANES), 1)
    keys = (ids + ((lane % TILE) * LANES).astype(F32)).T
    column = lax.broadcasted_iota(jnp.int32, (1, TILE * LANES), 1).astype(F32)
    total = ((dense_own[...] + dense_seen[...]) * factor).astype(BF16)
    for which in range(2):
        for pair in range(peers // 2):
            mine = []
            for peer in (2 * pair, 2 * pair + 1):
                at = peer * 16 + 2 + which
                mine.append(keys[0 : wire.left, at : at + 1])
            hit = jnp.where(jnp.concatenate(mine, axis=0) == column, 1.0, 0.0).astype(BF16)
            both = mm_nt(hit, held[which])
            for k in range(2):
                got = both[k * wire.left : (k + 1) * wire.left]
                peer, base = 2 * pair + k, which * wire.half
                out[peer, base : base + wire.left] = got[:, 0:128].astype(BF16)
                for i in range(wire.left // 32):
                    first, second = got[32 * i : 32 * i + 16, 128:256], got[32 * i + 16 : 32 * i + 32, 128:256]
                    at = base + wire.left + 16 * i
                    out[peer, at : at + 16] = jnp.where(low_lanes(first.shape), first, second).astype(BF16)
    for peer in range(peers):
        out[peer, 2 * wire.half :] = total


def lookup(wire, factor, half, mine_t, crossed_t, ids, dense_own, dense_seen):
    peers = ids.shape[0]
    rows = 2 * wire.half + wire.dense

    def whole(shape):
        return pl.BlockSpec(shape, lambda i: (0,) * len(shape))

    at = wire.half // 16
    return pl.pallas_call(
        functools.partial(lookup_kernel, wire, factor),
        grid=(1,),
        in_specs=[
            SMEM,
            whole(mine_t.shape),
            whole(crossed_t.shape),
            pl.BlockSpec((peers, 16, LANES), lambda i: (0, at, 0)),
            whole(dense_own.shape),
            whole(dense_seen.shape),
        ],
        out_specs=whole((peers, rows, LANES)),
        out_shape=jax.ShapeDtypeStruct((peers, rows, LANES), BF16),
        scratch_shapes=[pltpu.VMEM((2, 256, TILE * LANES), BF16)],
        compiler_params=params(),
        cost_estimate=pl.CostEstimate(flops=10**9, bytes_accessed=10**6, transcendentals=0),
        name="lookup",
    )(half, mine_t, crossed_t, ids, dense_own, dense_seen)


def unpack_kernel(n_grp, n_lane, wire, seen, rows_out, fm, proj_t, lcb, gain, held):
    step = pl.program_id(0)
    peers = n_grp * n_lane
    for side in range(2):
        for q in range(n_lane):
            for gg in range(n_grp // 2):
                left, right = [], []
                for g in (2 * gg, 2 * gg + 1):
                    peer = g * n_lane + q
                    row = pl.multiple_of(side * wire.half + step * 32, 16)
                    left.append(seen[peer, pl.ds(row, 32)].astype(F32))
                    row = pl.multiple_of(side * wire.half + wire.left + step * 16, 16)
                    packed = seen[peer, pl.ds(row, 16)].astype(F32)
                    right.append(jnp.concatenate([packed, turn(packed)], axis=0))
                at = side * 128 + q * n_grp * TILE + gg * 16
                for s in range(STEP):
                    here = slice(s * TILE, s * TILE + TILE)
                    both = jnp.concatenate([left[0][here], left[1][here]], axis=0)
                    held[s, at : at + 16, 0:128] = both.astype(BF16)
                    both = jnp.concatenate([right[0][here], right[1][here]], axis=0)
                    held[s, at : at + 16, 128:256] = both.astype(BF16)
    eye = identity(192, 256)
    for s in range(STEP):
        rows_out[s] = mm_nt(eye, held[s]).astype(BF16)

    @pl.when(step == 0)
    def _():
        part, third = 256 // peers, 192 // peers
        for peer in range(peers):
            dense = seen[peer, 2 * wire.half :].astype(F32)
            here = slice(peer * part, (peer + 1) * part)
            fm[here] = dense[0:part]
            lcb[here, 0:128] = dense[part : 2 * part]
            lcb[here, 128:256] = dense[2 * part : 3 * part]
            last = dense[3 * part : 4 * part]
            proj_t[peer * third : (peer + 1) * third] = last[0:third]
            if peer == 0:
                last = last[third : third + 3]
                gain[:, 0:128] = last[0:1] + last[2:3]
                gain[:, 128:192] = (last + turn(last))[1:2, 0:64]


def unpack(n_grp, n_lane, wire, count, seen):
    def whole(*shape):
        return pl.BlockSpec(shape, lambda i: (0,) * len(shape))

    shapes = [(256, 128), (192, 128), (256, 256), (1, 192)]
    return pl.pallas_call(
        functools.partial(unpack_kernel, n_grp, n_lane, wire),
        grid=(count // STEP,),
        in_specs=[whole(*seen.shape)],
        out_specs=[pl.BlockSpec((STEP, 192, 256), lambda i: (i, 0, 0))] + [whole(*shape) for shape in shapes],
        out_shape=[jax.ShapeDtypeStruct((count, 192, 256), BF16)]
        + [jax.ShapeDtypeStruct(shape, F32) for shape in shapes],
        scratch_shapes=[pltpu.VMEM((STEP, 256, 256), BF16)],
        compiler_params=params(),
        cost_estimate=pl.CostEstimate(flops=0, bytes_accessed=10**6, transcendentals=0),
        name="unpack_rows",
    )(seen)


def combine_kernel(place, own, seen, *outs):
    for k, out in enumerate(outs):
        g = jnp.bitwise_xor(place[0], k)
        out[...] = (own[g] + seen[g].astype(F32)).astype(BF16)


def combine(place, own, seen):
    n_grp = own.shape[0]
    shape = jax.ShapeDtypeStruct(own.shape[1:], BF16)
    return pl.pallas_call(
        combine_kernel,
        in_specs=[SMEM, VMEM, VMEM],
        out_specs=[VMEM] * n_grp,
        out_shape=[shape] * n_grp,
        compiler_params=params(),
        cost_estimate=pl.CostEstimate(flops=0, bytes_accessed=10**6, transcendentals=0),
        name="combine",
    )(place, own, seen)


def finish_kernel(place, *refs):
    out = refs[-1]
    piece = out.shape[1]
    for k, seen in enumerate(refs[:-1]):
        base = jnp.bitwise_xor(place[0], k) * TILE
        for f in range(TILE):
            out[base + f, :, 0:128] = seen[f, 0:piece].astype(F32)
            packed = seen[f, piece : piece + piece // 2].astype(F32)
            out[base + f, 0 : piece // 2, 128:192] = packed[:, 0:64]
            out[base + f, piece // 2 : piece, 128:192] = turn(packed)[:, 0:64]


def finish(place, pieces):
    n_grp = len(pieces)
    piece = pieces[0].shape[1] * 2 // 3
    return pl.pallas_call(
        finish_kernel,
        in_specs=[SMEM] + [VMEM] * n_grp,
        out_specs=VMEM,
        out_shape=jax.ShapeDtypeStruct((n_grp * TILE, piece, 192), F32),
        compiler_params=params(),
        cost_estimate=pl.CostEstimate(flops=0, bytes_accessed=10**6, transcendentals=0),
        name="finish_tables",
    )(place, *pieces)


def cross(array):
    return lax.ppermute(array, "half", [(0, 1), (1, 0)])


def halves(pooled, upstream, ids_now, ids_next, tables, w_fm, w_proj, w_lcb, gain):
    n_grp, n_lane = lax.axis_size("grp"), lax.axis_size("lane")
    count = pooled.shape[0]
    wire = Wire(count, n_grp * n_lane)
    factor = 1.0 / (count * n_grp * 2 * n_lane)
    half = lax.axis_index("half").astype(jnp.int32)[None]
    grp = lax.axis_index("grp").astype(jnp.int32)
    mine_t = lax.dynamic_slice_in_dim(tables.transpose(0, 2, 1), grp * TILE, TILE, 0)
    mine_t, pooled = lax.optimization_barrier((mine_t, pooled))
    crossed_t = cross(mine_t)
    other_wire, own_wire = backward(
        n_grp, n_lane, wire, half,
        pooled.transpose(0, 2, 1), upstream.transpose(0, 2, 1), ids_now, ids_next, w_fm, w_proj.T, w_lcb, gain,
    )
    seen_other = exchange(other_wire, PEER)
    crossed_t, seen_other = lax.optimization_barrier((crossed_t, seen_other))
    seen_own = exchange(own_wire, PEER)
    (part,) = part_sums(n_grp, wire, True, half, seen_other, seen_other)
    part_seen = cross(part)
    own, dense = part_sums(n_grp, wire, False, half, seen_own, seen_other)
    dense_seen = cross(dense)
    rows_wire = lookup(wire, factor, half, mine_t, crossed_t, seen_other, dense, dense_seen)
    rows = exchange(rows_wire, PEER)
    next_rows, grad_fm, grad_proj_t, grad_lcb, grad_gain = unpack(n_grp, n_lane, wire, count, rows)
    own, _ = lax.optimization_barrier((own, rows_wire))
    pieces = combine(grp[None], own, part_seen)
    pieces = [pieces[0]] + [
        lax.ppermute(pieces[k], "grp", [(g, g ^ k) for g in range(n_grp)]) for k in range(1, n_grp)
    ]
    table_grad = finish(grp[None], pieces)
    return next_rows.transpose(0, 2, 1), table_grad, grad_fm, grad_proj_t.T, grad_lcb, grad_gain.reshape(-1)


def solution(mesh):
    n_grp, n_emb = mesh.shape["grp"], mesh.shape["emb"]
    split = n_emb % 2 == 0 and n_grp * (n_emb // 2) == 16 and n_grp % 2 == 0

    def run(*args):
        pooled, _, _, _, tables, w_fm = args[:6]
        count = pooled.shape[0] // (n_grp * n_emb)
        fits = (
            split
            and pooled.shape[1:] == (256, 192)
            and tables.shape[1] == 128
            and w_fm.shape[1] == 128
            and pooled.shape[1] == n_grp * n_emb * TILE
            and count % STEP == 0
            and count <= 16
        )
        if fits:
            devices = mesh.devices.reshape(n_grp, 2, n_emb // 2)
            where, emb, body = Mesh(devices, ("grp", "half", "lane")), ("half", "lane"), halves
        else:
            where, emb, body = mesh, ("emb",), local
        both = ("grp",) + emb
        return jax.shard_map(
            body,
            mesh=where,
            in_specs=(
                P(both, None, None),
                P(both, None, None),
                P(both, None),
                P(both, None),
                P(emb, None, None),
                P(),
                P(),
                P(),
                P(),
            ),
            out_specs=(P(both, None, None), P(emb, "grp", None), P(), P(), P(), P()),
            check_vma=False,
        )(*args)

    return run
```

```python
import functools

import jax
import jax.numpy as jnp
from jax import lax
from jax.experimental import pallas as pl
from jax.experimental.pallas import tpu as pltpu
from jax.sharding import Mesh, PartitionSpec as P

F32, BF16 = jnp.float32, jnp.bfloat16
SMEM = pl.BlockSpec(memory_space=pltpu.SMEM)
VMEM = pl.BlockSpec(memory_space=pltpu.VMEM)
LANES = 128
TILE = 8
STEP = 4
LIMIT = 40 * 1024 * 1024
PEER = ("grp", "lane")


BOTH = ("grp", "emb")


def product(form, left, right):
    return jnp.einsum(form, left, right, preferred_element_type=jnp.float32)


def layer_backward(embeds, cotangent, w_fm, w_proj, w_lcb, gain):
    fm_proj = product("bfc,fj->bcj", embeds, w_fm).astype(jnp.bfloat16)
    fm_rows = product("bfc,bcj->bfj", embeds, fm_proj).astype(jnp.bfloat16)
    projected = product("bfj,jc->bfc", fm_rows, w_proj)
    compressed = product("fi,bfc->bic", w_lcb, embeds)
    summed = embeds.astype(jnp.float32) + projected + compressed
    centre = jnp.mean(summed, axis=2, keepdims=True)
    spread = jnp.mean((summed - centre) ** 2, axis=2, keepdims=True)
    inverse = lax.rsqrt(spread + 1e-05)
    normed = (summed - centre) * inverse
    upper = cotangent.astype(jnp.float32)
    scaled = upper * gain
    grad_sum = inverse * (
        scaled
        - jnp.mean(scaled, axis=2, keepdims=True)
        - normed * jnp.mean(scaled * normed, axis=2, keepdims=True)
    )
    grad_sum = grad_sum.astype(jnp.bfloat16)
    grad_gain = jnp.sum(upper * normed, axis=(0, 1))
    grad_proj = product("bfj,bfc->jc", fm_rows, grad_sum)
    grad_rows = product("bfc,jc->bfj", grad_sum, w_proj).astype(jnp.bfloat16)
    grad_p = product("bfc,bfj->bcj", embeds, grad_rows).astype(jnp.bfloat16)
    grad_fm = product("bfc,bcj->fj", embeds, grad_p)
    grad_lcb = product("bfc,bic->fi", embeds, grad_sum)
    grad_in = (
        grad_sum.astype(jnp.float32)
        + product("bfj,bcj->bfc", grad_rows, fm_proj)
        + product("fj,bcj->bfc", w_fm, grad_p)
        + product("fi,bic->bfc", w_lcb, grad_sum)
    )
    return (grad_in.astype(jnp.bfloat16), (grad_fm, grad_proj, grad_lcb, grad_gain))


def exchange(blocks, axes):
    return lax.all_to_all(blocks, axes, split_axis=0, concat_axis=0, tiled=True)


def dense_sum(partials, factor):
    n = lax.axis_size("grp") * lax.axis_size("emb")
    shapes = [part.shape for part in partials]
    flat = jnp.concatenate([part.reshape(-1) for part in partials])
    unit = 128 * n
    padded = -(-flat.shape[0] // unit) * unit
    flat = jnp.pad(flat, (0, padded - flat.shape[0])).astype(jnp.bfloat16)
    seen = exchange(flat.reshape(n, padded // unit, 128), BOTH)
    share = (jnp.sum(seen.astype(jnp.float32), axis=0) * factor).astype(jnp.bfloat16)
    total = exchange(jnp.broadcast_to(share[None], (n,) + share.shape), BOTH).reshape(-1)
    total = total.astype(jnp.float32)
    outs, at = [], 0
    for shape in shapes:
        size = 1
        for extent in shape:
            size *= extent
        outs.append(total[at : at + size].reshape(shape))
        at += size
    return outs


def local(pooled, upstream, ids_now, ids_next, tables, w_fm, w_proj, w_lcb, gain):
    n_grp, n_emb = lax.axis_size("grp"), lax.axis_size("emb")
    count, features, width = pooled.shape
    owned, rows = tables.shape[:2]
    ids = jnp.stack([ids_now, ids_next]).reshape(2, count, n_emb, owned)
    ids = exchange(ids.transpose(2, 0, 1, 3), "emb")
    row_index = jnp.arange(rows)
    wanted = (ids[:, 1, :, :, None] == row_index).astype(jnp.bfloat16)
    fetched = product("esfr,frc->esfc", wanted, tables).astype(jnp.bfloat16)
    next_rows = exchange(fetched, "emb")
    next_rows = next_rows.transpose(1, 0, 2, 3).reshape(count, features, width)
    grad_in, partials = layer_backward(pooled, upstream, w_fm, w_proj, w_lcb, gain)
    grad_in = grad_in.reshape(count, n_emb, owned, width).transpose(1, 0, 2, 3)
    grads = exchange(grad_in, "emb")
    hit = (ids[:, 0, :, :, None] == row_index).astype(jnp.bfloat16)
    part = product("esfr,esfc->frc", hit, grads).astype(jnp.bfloat16)
    part = part.reshape(owned, n_grp, rows // n_grp, width).transpose(1, 0, 2, 3)
    table_grad = jnp.sum(exchange(part, "grp").astype(jnp.float32), axis=0)
    dense = dense_sum(partials, 1.0 / (count * n_grp * n_emb))
    return (next_rows, table_grad, *dense)


def params(**more):
    return pltpu.CompilerParams(vmem_limit_bytes=LIMIT, **more)


def mm(left, right, dims=((1,), (0,))):
    return lax.dot_general(left, right, (dims, ((), ())), preferred_element_type=F32)


def mm_nt(left, right):
    return mm(left, right, ((1,), (1,)))


def low_lanes(shape):
    return lax.broadcasted_iota(jnp.int32, shape, 1) < LANES // 2


def turn(tile):
    return pltpu.roll(tile, LANES // 2, 1)


def identity(rows, lanes):
    row = lax.broadcasted_iota(jnp.int32, (rows, lanes), 0)
    return jnp.where(row == lax.broadcasted_iota(jnp.int32, (rows, lanes), 1), 1.0, 0.0).astype(BF16)


class Wire:
    def __init__(self, count, peers):
        self.left = count * TILE
        self.half = self.left + self.left // 2
        self.dense = 2 * self.half
        self.ids = self.dense + 1024 // peers


def place_of(n_grp, n_lane, peer):
    return (peer % n_lane) * n_grp * TILE + (peer // n_lane) * TILE


def backward_kernel(
    n_grp, n_lane, wire,
    half_ref, x_ref, u_ref, now_ref, next_ref, fm_ref, proj_t_ref, lcb_ref, gain_ref,
    out_ref,
    fm_t, proj, lcb_t, gains, eye, mixed, p_t, g_t, d_sum, d_p_t, left_in, right_in, grads, turned, ids,
):
    count, width, features = x_ref.shape
    rank = fm_ref.shape[1]
    peers = n_grp * n_lane
    scale = 1.0 / width
    samples = range(count)

    turned_fm = fm_ref[...].astype(F32).T.astype(BF16)
    fm_t[...] = turned_fm
    proj[...] = proj_t_ref[...].astype(F32).T.astype(BF16)
    lcb_t[...] = lcb_ref[...].astype(F32).T.astype(BF16)
    column = jnp.broadcast_to(gain_ref[...], (LANES, width)).T
    gains[:, 0:128] = column
    gains[:, 128:256] = column
    eye[...] = identity(features, features)

    x_all = x_ref[...].reshape(count * width, features)
    left_in[:, :, 0:rank] = mm(x_all, fm_ref[...]).astype(BF16).reshape(count, width, rank)
    mixed[...] = mm(x_all, lcb_ref[...]).reshape(count, width, features)
    for s in samples:
        p_t[s] = mm_nt(fm_t[...], x_ref[s]).astype(BF16)
        right_in[s, rank : 2 * rank] = turned_fm
    for s in samples:
        g_t[s] = mm(p_t[s], x_ref[s]).astype(BF16)
    for s in samples:
        mixed[s] = mixed[s] + mm(proj_t_ref[...], g_t[s])
    sum_gain = 0.0
    for s in samples:
        summed = x_ref[s].astype(F32) + mixed[s]
        centre = jnp.sum(summed, axis=0, keepdims=True) * scale
        summed = summed - centre
        spread = jnp.sum(summed * summed, axis=0, keepdims=True) * scale
        inverse = lax.rsqrt(spread + 1e-05)
        normed = summed * inverse
        upper = u_ref[s].astype(F32)
        scaled = upper * gains[...]
        first = jnp.sum(scaled, axis=0, keepdims=True) * scale
        second = jnp.sum(scaled * normed, axis=0, keepdims=True) * scale
        d_sum[s] = (inverse * (scaled - first - normed * second)).astype(BF16)
        product_gain = upper * normed
        sum_gain += product_gain[:, 0:128] + product_gain[:, 128:256]
    for s in samples:
        right_in[s, 0:rank] = mm(proj[...], d_sum[s]).astype(BF16)
    for s in samples:
        left_in[s, :, rank : 2 * rank] = mm_nt(x_ref[s], right_in[s, 0:rank]).astype(BF16)
        d_p_t[s] = mm_nt(right_in[s, 0:rank], x_ref[s]).astype(BF16)
    d_all = d_sum[...].reshape(count * width, features)
    mixed[...] = mm(d_all, lcb_t[...]).reshape(count, width, features)
    for s in samples:
        grad = d_sum[s].astype(F32) + mixed[s] + mm(left_in[s], right_in[s])
        grad = grad.astype(BF16)
        group, k = s // STEP, s % STEP
        grads[group, k * 128 : k * 128 + 128] = grad[0:128]
        at = 512 + 64 * (2 * (k % 2) + k // 2)
        grads[group, at : at + 64] = grad[128:192]
    sum_lcb = mm(x_all, d_all, ((0,), (0,)))
    sum_fm_t, sum_proj_t = 0.0, 0.0
    for s in samples:
        sum_fm_t += mm(d_p_t[s], x_ref[s])
        sum_proj_t += mm_nt(d_sum[s], g_t[s])

    half = half_ref[0]
    for group in range(count // STEP):
        rows = mm_nt(eye[...], grads[group])
        turned[group, 0] = rows[0:128]
        turned[group, 1] = rows[128:256]
    for group in range(count // STEP):
        for which in range(2):
            side = half if which else 1 - half
            for peer in range(peers):
                at = place_of(n_grp, n_lane, peer)
                line = turned[group, side, at : at + TILE]
                left = jnp.concatenate([line[:, k * 128 : k * 128 + 128] for k in range(STEP)], axis=0)
                row = which * wire.half + group * 32
                out_ref[peer, row : row + 32] = left.astype(BF16)
                right = jnp.concatenate([line[:, 512:640], line[:, 640:768]], axis=0)
                row = which * wire.half + wire.left + group * 16
                out_ref[peer, row : row + 16] = right.astype(BF16)

    part = features // peers
    third = width // peers
    total = jnp.sum(sum_gain.T, axis=0, keepdims=True)
    high = total.astype(BF16).astype(F32)
    low = total - high
    middle = jnp.concatenate([high[:, 128:192], low[:, 128:192]], axis=1)
    gain_rows = [high[:, 0:128], middle, low[:, 0:128], jnp.zeros((1, LANES), F32)]
    sum_fm = sum_fm_t.T
    for peer in range(peers):
        at = wire.dense
        here = slice(peer * part, (peer + 1) * part)
        out_ref[peer, at : at + part] = sum_fm[here].astype(BF16)
        out_ref[peer, at + part : at + 2 * part] = sum_lcb[here, 0:128].astype(BF16)
        out_ref[peer, at + 2 * part : at + 3 * part] = sum_lcb[here, 128:256].astype(BF16)
        last = [sum_proj_t[peer * third : (peer + 1) * third]] + gain_rows
        out_ref[peer, at + 3 * part : at + 4 * part] = jnp.concatenate(last, axis=0).astype(BF16)

    lane = lax.broadcasted_iota(jnp.int32, (16, LANES), 1)
    sample = lax.broadcasted_iota(jnp.int32, (16, LANES), 0)
    mine = (lane // TILE == sample) & (sample < count)
    spread_ids = []
    for which, ref in enumerate((now_ref, next_ref)):
        ids[which] = jnp.zeros_like(ids[which])
        ids[which, 0:count] = ref[...].astype(F32)
        for side in range(2):
            line = ids[which, :, side * 128 : side * 128 + 128]
            spread_ids.append(pltpu.roll(line, 0, 1, stride=TILE, stride_axis=0))
    for peer in range(peers):
        at = place_of(n_grp, n_lane, peer)
        lines = []
        for line in spread_ids:
            line = pltpu.roll(line, LANES - at, 1) if at else line
            lines.append(jnp.sum(jnp.where(mine, line, 0.0), axis=0, keepdims=True))
        lines.append(jnp.zeros((12, LANES), F32))
        out_ref[peer, wire.ids : wire.ids + 16] = jnp.concatenate(lines, axis=0).astype(BF16)


def backward(n_grp, n_lane, wire, half, pooled_t, upstream_t, ids_now, ids_next, w_fm, w_proj_t, w_lcb, gain):
    count, width, features = pooled_t.shape
    rank = w_fm.shape[1]
    peers = n_grp * n_lane

    def whole(shape):
        return pl.BlockSpec(shape, lambda i: (0,) * len(shape))

    operands = (pooled_t, upstream_t, ids_now, ids_next, w_fm, w_proj_t, w_lcb, gain.reshape(1, width))
    shape = (peers, wire.ids + 16, LANES)
    return pl.pallas_call(
        functools.partial(backward_kernel, n_grp, n_lane, wire),
        grid=(1,),
        in_specs=[SMEM] + [whole(array.shape) for array in operands],
        out_specs=whole(shape),
        out_shape=jax.ShapeDtypeStruct(shape, BF16),
        scratch_shapes=[
            pltpu.VMEM((rank, features), BF16),
            pltpu.VMEM((rank, width), BF16),
            pltpu.VMEM((features, features), BF16),
            pltpu.VMEM((width, features), F32),
            pltpu.VMEM((features, features), BF16),
            pltpu.VMEM((count, width, features), F32),
            pltpu.VMEM((count, rank, width), BF16),
            pltpu.VMEM((count, rank, features), BF16),
            pltpu.VMEM((count, width, features), BF16),
            pltpu.VMEM((count, rank, width), BF16),
            pltpu.VMEM((count, width, 2 * rank), BF16),
            pltpu.VMEM((count, 2 * rank, features), BF16),
            pltpu.VMEM((count // STEP, STEP * width, features), BF16),
            pltpu.VMEM((count // STEP, 2, features // 2, STEP * width), F32),
            pltpu.VMEM((2, 16, features), F32),
        ],
        compiler_params=pltpu.CompilerParams(vmem_limit_bytes=60 * 1024 * 1024),
        cost_estimate=pl.CostEstimate(flops=10**9, bytes_accessed=4 * 10**6, transcendentals=0),
        name="layer_backward",
    )(half, *operands)


def part_kernel(n_grp, wire, other, half_ref, seen, *refs):
    out, held = refs[0], refs[-1]
    peers = seen.shape[0]
    half = 1 - half_ref[0] if other else half_ref[0]
    base = 0 if other else wire.half
    if other:
        dense = refs[1]
        total = seen[0, wire.dense : wire.ids].astype(F32)
        for peer in range(1, peers):
            total = total + seen[peer, wire.dense : wire.ids].astype(F32)
        dense[...] = total
    lane = lax.broadcasted_iota(jnp.int32, (1, LANES), 1)
    start = ((lane % TILE) * LANES).astype(F32)
    keys = []
    for peer in range(peers):
        at = peer * LANES
        held[at : at + wire.left, 0:128] = seen[peer, base : base + wire.left]
        right = seen[peer, base + wire.left : base + wire.half]
        turned = turn(right.astype(F32)).astype(BF16)
        for i in range(wire.left // 32):
            held[at + 32 * i : at + 32 * i + 16, 128:256] = right[16 * i : 16 * i + 16]
            held[at + 32 * i + 16 : at + 32 * i + 32, 128:256] = turned[16 * i : 16 * i + 16]
        if wire.left < LANES:
            held[at + wire.left : at + LANES] = jnp.zeros((LANES - wire.left, 256), BF16)
        ids = seen[peer, wire.ids : wire.ids + 16].astype(F32)
        key = jnp.where(half == 0, ids[0:1], ids[1:2]) + start
        keys.append(jnp.where(lane < wire.left, key, -1.0))
    keys = jnp.concatenate(keys, axis=1)
    piece = LANES // n_grp
    for pair in range(TILE // 2):
        row = lax.broadcasted_iota(jnp.int32, (256, 1), 0).astype(F32) + 256.0 * pair
        hit = jnp.where(keys == row, 1.0, 0.0).astype(BF16)
        part = mm(hit, held[...])
        for f in range(2):
            for g in range(n_grp):
                at = f * LANES + g * piece
                rows = part[at : at + piece]
                out[g, 2 * pair + f, 0:piece] = rows[:, 0:128].astype(out.dtype)
                second = turn(rows[piece // 2 :, 128:256])
                packed = jnp.where(low_lanes(second.shape), rows[: piece // 2, 128:256], second)
                out[g, 2 * pair + f, piece : piece + piece // 2] = packed.astype(out.dtype)


def part_sums(n_grp, wire, other, half, seen):
    peers = seen.shape[0]
    piece = LANES // n_grp
    shapes = [jax.ShapeDtypeStruct((n_grp, TILE, piece + piece // 2, LANES), BF16 if other else F32)]
    if other:
        shapes.append(jax.ShapeDtypeStruct((wire.ids - wire.dense, LANES), F32))
    return pl.pallas_call(
        functools.partial(part_kernel, n_grp, wire, other),
        in_specs=[SMEM, VMEM],
        out_specs=[VMEM] * len(shapes),
        out_shape=shapes,
        scratch_shapes=[pltpu.VMEM((peers * LANES, 256), BF16)],
        compiler_params=params(),
        cost_estimate=pl.CostEstimate(flops=10**9, bytes_accessed=10**6, transcendentals=0),
        name="part_other" if other else "part_own",
    )(half, seen)


def lookup_kernel(wire, factor, half_ref, mine_t, crossed_t, ids_ref, dense_own, dense_seen, out, held):
    peers = out.shape[0]
    half = half_ref[0]
    for f in range(TILE):
        at = f * LANES
        for side, ref in ((half, mine_t), (1 - half, crossed_t)):
            held[side, 0:192, at : at + LANES] = ref[f]
            held[side, 192:256, at : at + LANES] = ref[f, 128:192]
    ids = ids_ref[...].astype(F32).reshape(peers * 16, LANES)
    lane = lax.broadcasted_iota(jnp.int32, (1, LANES), 1)
    keys = (ids + ((lane % TILE) * LANES).astype(F32)).T
    column = lax.broadcasted_iota(jnp.int32, (1, TILE * LANES), 1).astype(F32)
    total = ((dense_own[...] + dense_seen[...]) * factor).astype(BF16)
    for which in range(2):
        for pair in range(peers // 2):
            mine = []
            for peer in (2 * pair, 2 * pair + 1):
                at = peer * 16 + 2 + which
                mine.append(keys[0 : wire.left, at : at + 1])
            hit = jnp.where(jnp.concatenate(mine, axis=0) == column, 1.0, 0.0).astype(BF16)
            both = mm_nt(hit, held[which])
            for k in range(2):
                got = both[k * wire.left : (k + 1) * wire.left]
                peer, base = 2 * pair + k, which * wire.half
                out[peer, base : base + wire.left] = got[:, 0:128].astype(BF16)
                for i in range(wire.left // 32):
                    first, second = got[32 * i : 32 * i + 16, 128:256], got[32 * i + 16 : 32 * i + 32, 128:256]
                    at = base + wire.left + 16 * i
                    out[peer, at : at + 16] = jnp.where(low_lanes(first.shape), first, second).astype(BF16)
    for peer in range(peers):
        out[peer, wire.dense : wire.ids] = total


def lookup(wire, factor, half, mine_t, crossed_t, ids, dense_own, dense_seen):
    peers = ids.shape[0]
    rows = wire.ids

    def whole(shape):
        return pl.BlockSpec(shape, lambda i: (0,) * len(shape))

    at = wire.ids // 16
    return pl.pallas_call(
        functools.partial(lookup_kernel, wire, factor),
        grid=(1,),
        in_specs=[
            SMEM,
            whole(mine_t.shape),
            whole(crossed_t.shape),
            pl.BlockSpec((peers, 16, LANES), lambda i: (0, at, 0)),
            whole(dense_own.shape),
            whole(dense_seen.shape),
        ],
        out_specs=whole((peers, rows, LANES)),
        out_shape=jax.ShapeDtypeStruct((peers, rows, LANES), BF16),
        scratch_shapes=[pltpu.VMEM((2, 256, TILE * LANES), BF16)],
        compiler_params=params(),
        cost_estimate=pl.CostEstimate(flops=10**9, bytes_accessed=10**6, transcendentals=0),
        name="lookup",
    )(half, mine_t, crossed_t, ids, dense_own, dense_seen)


def unpack_kernel(n_grp, n_lane, wire, seen, rows_out, fm, proj_t, lcb, gain, held):
    step = pl.program_id(0)
    peers = n_grp * n_lane
    for side in range(2):
        for q in range(n_lane):
            for gg in range(n_grp // 2):
                left, right = [], []
                for g in (2 * gg, 2 * gg + 1):
                    peer = g * n_lane + q
                    row = pl.multiple_of(side * wire.half + step * 32, 16)
                    left.append(seen[peer, pl.ds(row, 32)].astype(F32))
                    row = pl.multiple_of(side * wire.half + wire.left + step * 16, 16)
                    packed = seen[peer, pl.ds(row, 16)].astype(F32)
                    right.append(jnp.concatenate([packed, turn(packed)], axis=0))
                at = side * 128 + q * n_grp * TILE + gg * 16
                for s in range(STEP):
                    here = slice(s * TILE, s * TILE + TILE)
                    both = jnp.concatenate([left[0][here], left[1][here]], axis=0)
                    held[s, at : at + 16, 0:128] = both.astype(BF16)
                    both = jnp.concatenate([right[0][here], right[1][here]], axis=0)
                    held[s, at : at + 16, 128:256] = both.astype(BF16)
    eye = identity(192, 256)
    for s in range(STEP):
        rows_out[s] = mm_nt(eye, held[s]).astype(BF16)

    @pl.when(step == 0)
    def _():
        part, third = 256 // peers, 192 // peers
        for peer in range(peers):
            dense = seen[peer, wire.dense : wire.ids].astype(F32)
            here = slice(peer * part, (peer + 1) * part)
            fm[here] = dense[0:part]
            lcb[here, 0:128] = dense[part : 2 * part]
            lcb[here, 128:256] = dense[2 * part : 3 * part]
            last = dense[3 * part : 4 * part]
            proj_t[peer * third : (peer + 1) * third] = last[0:third]
            if peer == 0:
                last = last[third : third + 3]
                gain[:, 0:128] = last[0:1] + last[2:3]
                gain[:, 128:192] = (last + turn(last))[1:2, 0:64]


def unpack(n_grp, n_lane, wire, count, seen):
    def whole(*shape):
        return pl.BlockSpec(shape, lambda i: (0,) * len(shape))

    shapes = [(256, 128), (192, 128), (256, 256), (1, 192)]
    return pl.pallas_call(
        functools.partial(unpack_kernel, n_grp, n_lane, wire),
        grid=(count // STEP,),
        in_specs=[whole(*seen.shape)],
        out_specs=[pl.BlockSpec((STEP, 192, 256), lambda i: (i, 0, 0))] + [whole(*shape) for shape in shapes],
        out_shape=[jax.ShapeDtypeStruct((count, 192, 256), BF16)]
        + [jax.ShapeDtypeStruct(shape, F32) for shape in shapes],
        scratch_shapes=[pltpu.VMEM((STEP, 256, 256), BF16)],
        compiler_params=params(),
        cost_estimate=pl.CostEstimate(flops=0, bytes_accessed=10**6, transcendentals=0),
        name="unpack_rows",
    )(seen)


def combine_kernel(place, own, seen, *outs):
    for k, out in enumerate(outs):
        g = jnp.bitwise_xor(place[0], k)
        out[...] = (own[g] + seen[g].astype(F32)).astype(BF16)


def combine(place, own, seen):
    n_grp = own.shape[0]
    shape = jax.ShapeDtypeStruct(own.shape[1:], BF16)
    return pl.pallas_call(
        combine_kernel,
        in_specs=[SMEM, VMEM, VMEM],
        out_specs=[VMEM] * n_grp,
        out_shape=[shape] * n_grp,
        compiler_params=params(),
        cost_estimate=pl.CostEstimate(flops=0, bytes_accessed=10**6, transcendentals=0),
        name="combine",
    )(place, own, seen)


def finish_kernel(place, *refs):
    out = refs[-1]
    piece = out.shape[1]
    for k, seen in enumerate(refs[:-1]):
        base = jnp.bitwise_xor(place[0], k) * TILE
        for f in range(TILE):
            out[base + f, :, 0:128] = seen[f, 0:piece].astype(F32)
            packed = seen[f, piece : piece + piece // 2].astype(F32)
            out[base + f, 0 : piece // 2, 128:192] = packed[:, 0:64]
            out[base + f, piece // 2 : piece, 128:192] = turn(packed)[:, 0:64]


def finish(place, pieces):
    n_grp = len(pieces)
    piece = pieces[0].shape[1] * 2 // 3
    return pl.pallas_call(
        finish_kernel,
        in_specs=[SMEM] + [VMEM] * n_grp,
        out_specs=VMEM,
        out_shape=jax.ShapeDtypeStruct((n_grp * TILE, piece, 192), F32),
        compiler_params=params(),
        cost_estimate=pl.CostEstimate(flops=0, bytes_accessed=10**6, transcendentals=0),
        name="finish_tables",
    )(place, *pieces)


def cross(array):
    return lax.ppermute(array, "half", [(0, 1), (1, 0)])


def halves(pooled, upstream, ids_now, ids_next, tables, w_fm, w_proj, w_lcb, gain):
    n_grp, n_lane = lax.axis_size("grp"), lax.axis_size("lane")
    count = pooled.shape[0]
    wire = Wire(count, n_grp * n_lane)
    factor = 1.0 / (count * n_grp * 2 * n_lane)
    half = lax.axis_index("half").astype(jnp.int32)[None]
    grp = lax.axis_index("grp").astype(jnp.int32)
    mine_t = lax.dynamic_slice_in_dim(tables.transpose(0, 2, 1), grp * TILE, TILE, 0)
    crossed_t = cross(mine_t)
    sent = backward(
        n_grp, n_lane, wire, half,
        pooled.transpose(0, 2, 1), upstream.transpose(0, 2, 1), ids_now, ids_next, w_fm, w_proj.T, w_lcb, gain,
    )
    seen = exchange(sent, PEER)
    crossed_t, seen = lax.optimization_barrier((crossed_t, seen))
    part, dense = part_sums(n_grp, wire, True, half, seen)
    dense_seen = cross(dense)
    part_seen = cross(part)
    (own,) = part_sums(n_grp, wire, False, half, seen)
    rows_wire = lookup(wire, factor, half, mine_t, crossed_t, seen, dense, dense_seen)
    rows = exchange(rows_wire, PEER)
    next_rows, grad_fm, grad_proj_t, grad_lcb, grad_gain = unpack(n_grp, n_lane, wire, count, rows)
    own, _ = lax.optimization_barrier((own, rows_wire))
    pieces = combine(grp[None], own, part_seen)
    pieces = [pieces[0]] + [
        lax.ppermute(pieces[k], "grp", [(g, g ^ k) for g in range(n_grp)]) for k in range(1, n_grp)
    ]
    table_grad = finish(grp[None], pieces)
    return next_rows.transpose(0, 2, 1), table_grad, grad_fm, grad_proj_t.T, grad_lcb, grad_gain.reshape(-1)


def solution(mesh):
    n_grp, n_emb = mesh.shape["grp"], mesh.shape["emb"]
    split = n_emb % 2 == 0 and n_grp * (n_emb // 2) == 16 and n_grp % 2 == 0

    def run(*args):
        pooled, _, _, _, tables, w_fm = args[:6]
        count = pooled.shape[0] // (n_grp * n_emb)
        fits = (
            split
            and pooled.shape[1:] == (256, 192)
            and tables.shape[1] == 128
            and w_fm.shape[1] == 128
            and pooled.shape[1] == n_grp * n_emb * TILE
            and count % STEP == 0
            and count <= 16
        )
        if fits:
            devices = mesh.devices.reshape(n_grp, 2, n_emb // 2)
            where, emb, body = Mesh(devices, ("grp", "half", "lane")), ("half", "lane"), halves
        else:
            where, emb, body = mesh, ("emb",), local
        both = ("grp",) + emb
        return jax.shard_map(
            body,
            mesh=where,
            in_specs=(
                P(both, None, None),
                P(both, None, None),
                P(both, None),
                P(both, None),
                P(emb, None, None),
                P(),
                P(),
                P(),
                P(),
            ),
            out_specs=(P(both, None, None), P(emb, "grp", None), P(), P(), P(), P()),
            check_vma=False,
        )(*args)

    return run
```

```python
import functools

import jax
import jax.numpy as jnp
from jax import lax
from jax.experimental import pallas as pl
from jax.experimental.pallas import tpu as pltpu
from jax.sharding import Mesh, PartitionSpec as P

F32, BF16 = jnp.float32, jnp.bfloat16
SMEM = pl.BlockSpec(memory_space=pltpu.SMEM)
VMEM = pl.BlockSpec(memory_space=pltpu.VMEM)
LANES = 128
TILE = 8
STEP = 4
LIMIT = 40 * 1024 * 1024
PEER = ("grp", "lane")


BOTH = ("grp", "emb")


def product(form, left, right):
    return jnp.einsum(form, left, right, preferred_element_type=jnp.float32)


def layer_backward(embeds, cotangent, w_fm, w_proj, w_lcb, gain):
    fm_proj = product("bfc,fj->bcj", embeds, w_fm).astype(jnp.bfloat16)
    fm_rows = product("bfc,bcj->bfj", embeds, fm_proj).astype(jnp.bfloat16)
    projected = product("bfj,jc->bfc", fm_rows, w_proj)
    compressed = product("fi,bfc->bic", w_lcb, embeds)
    summed = embeds.astype(jnp.float32) + projected + compressed
    centre = jnp.mean(summed, axis=2, keepdims=True)
    spread = jnp.mean((summed - centre) ** 2, axis=2, keepdims=True)
    inverse = lax.rsqrt(spread + 1e-05)
    normed = (summed - centre) * inverse
    upper = cotangent.astype(jnp.float32)
    scaled = upper * gain
    grad_sum = inverse * (
        scaled
        - jnp.mean(scaled, axis=2, keepdims=True)
        - normed * jnp.mean(scaled * normed, axis=2, keepdims=True)
    )
    grad_sum = grad_sum.astype(jnp.bfloat16)
    grad_gain = jnp.sum(upper * normed, axis=(0, 1))
    grad_proj = product("bfj,bfc->jc", fm_rows, grad_sum)
    grad_rows = product("bfc,jc->bfj", grad_sum, w_proj).astype(jnp.bfloat16)
    grad_p = product("bfc,bfj->bcj", embeds, grad_rows).astype(jnp.bfloat16)
    grad_fm = product("bfc,bcj->fj", embeds, grad_p)
    grad_lcb = product("bfc,bic->fi", embeds, grad_sum)
    grad_in = (
        grad_sum.astype(jnp.float32)
        + product("bfj,bcj->bfc", grad_rows, fm_proj)
        + product("fj,bcj->bfc", w_fm, grad_p)
        + product("fi,bic->bfc", w_lcb, grad_sum)
    )
    return (grad_in.astype(jnp.bfloat16), (grad_fm, grad_proj, grad_lcb, grad_gain))


def exchange(blocks, axes):
    return lax.all_to_all(blocks, axes, split_axis=0, concat_axis=0, tiled=True)


def dense_sum(partials, factor):
    n = lax.axis_size("grp") * lax.axis_size("emb")
    shapes = [part.shape for part in partials]
    flat = jnp.concatenate([part.reshape(-1) for part in partials])
    unit = 128 * n
    padded = -(-flat.shape[0] // unit) * unit
    flat = jnp.pad(flat, (0, padded - flat.shape[0])).astype(jnp.bfloat16)
    seen = exchange(flat.reshape(n, padded // unit, 128), BOTH)
    share = (jnp.sum(seen.astype(jnp.float32), axis=0) * factor).astype(jnp.bfloat16)
    total = exchange(jnp.broadcast_to(share[None], (n,) + share.shape), BOTH).reshape(-1)
    total = total.astype(jnp.float32)
    outs, at = [], 0
    for shape in shapes:
        size = 1
        for extent in shape:
            size *= extent
        outs.append(total[at : at + size].reshape(shape))
        at += size
    return outs


def local(pooled, upstream, ids_now, ids_next, tables, w_fm, w_proj, w_lcb, gain):
    n_grp, n_emb = lax.axis_size("grp"), lax.axis_size("emb")
    count, features, width = pooled.shape
    owned, rows = tables.shape[:2]
    ids = jnp.stack([ids_now, ids_next]).reshape(2, count, n_emb, owned)
    ids = exchange(ids.transpose(2, 0, 1, 3), "emb")
    row_index = jnp.arange(rows)
    wanted = (ids[:, 1, :, :, None] == row_index).astype(jnp.bfloat16)
    fetched = product("esfr,frc->esfc", wanted, tables).astype(jnp.bfloat16)
    next_rows = exchange(fetched, "emb")
    next_rows = next_rows.transpose(1, 0, 2, 3).reshape(count, features, width)
    grad_in, partials = layer_backward(pooled, upstream, w_fm, w_proj, w_lcb, gain)
    grad_in = grad_in.reshape(count, n_emb, owned, width).transpose(1, 0, 2, 3)
    grads = exchange(grad_in, "emb")
    hit = (ids[:, 0, :, :, None] == row_index).astype(jnp.bfloat16)
    part = product("esfr,esfc->frc", hit, grads).astype(jnp.bfloat16)
    part = part.reshape(owned, n_grp, rows // n_grp, width).transpose(1, 0, 2, 3)
    table_grad = jnp.sum(exchange(part, "grp").astype(jnp.float32), axis=0)
    dense = dense_sum(partials, 1.0 / (count * n_grp * n_emb))
    return (next_rows, table_grad, *dense)


def params(**more):
    return pltpu.CompilerParams(vmem_limit_bytes=LIMIT, **more)


def mm(left, right, dims=((1,), (0,))):
    return lax.dot_general(left, right, (dims, ((), ())), preferred_element_type=F32)


def mm_nt(left, right):
    return mm(left, right, ((1,), (1,)))


def low_lanes(shape):
    return lax.broadcasted_iota(jnp.int32, shape, 1) < LANES // 2


def turn(tile):
    return pltpu.roll(tile, LANES // 2, 1)


def identity(rows, lanes):
    row = lax.broadcasted_iota(jnp.int32, (rows, lanes), 0)
    return jnp.where(row == lax.broadcasted_iota(jnp.int32, (rows, lanes), 1), 1.0, 0.0).astype(BF16)


class Wire:
    def __init__(self, count, peers):
        self.left = count * TILE
        self.half = self.left + self.left // 2
        self.dense = 2 * self.half
        self.ids = self.dense + 1024 // peers


def place_of(n_grp, n_lane, peer):
    return (peer % n_lane) * n_grp * TILE + (peer // n_lane) * TILE


def backward_kernel(
    n_grp, n_lane, wire,
    place_ref, x_ref, u_ref, now_ref, next_ref, fm_ref, proj_t_ref, lcb_ref, gain_ref,
    *refs,
):
    out_refs, refs = refs[: n_grp * n_lane], refs[n_grp * n_lane :]
    fm_t, proj, lcb_t, gains, eye, mixed, p_t, g_t, d_sum, d_p_t, left_in, right_in = refs[:12]
    grads, turned, ids, sum_fm, sum_lcb, sum_rest = refs[12:]
    count, width, features = x_ref.shape
    rank = fm_ref.shape[1]
    peers = n_grp * n_lane
    scale = 1.0 / width
    samples = range(count)

    turned_fm = fm_ref[...].astype(F32).T.astype(BF16)
    fm_t[...] = turned_fm
    proj[...] = proj_t_ref[...].astype(F32).T.astype(BF16)
    lcb_t[...] = lcb_ref[...].astype(F32).T.astype(BF16)
    column = jnp.broadcast_to(gain_ref[...], (LANES, width)).T
    gains[:, 0:128] = column
    gains[:, 128:256] = column
    eye[...] = identity(features, features)

    x_all = x_ref[...].reshape(count * width, features)
    left_in[:, :, 0:rank] = mm(x_all, fm_ref[...]).astype(BF16).reshape(count, width, rank)
    mixed[...] = mm(x_all, lcb_ref[...]).reshape(count, width, features)
    for s in samples:
        p_t[s] = mm_nt(fm_t[...], x_ref[s]).astype(BF16)
        right_in[s, rank : 2 * rank] = turned_fm
    for s in samples:
        g_t[s] = mm(p_t[s], x_ref[s]).astype(BF16)
    for s in samples:
        mixed[s] = mixed[s] + mm(proj_t_ref[...], g_t[s])
    sum_gain = 0.0
    for s in samples:
        summed = x_ref[s].astype(F32) + mixed[s]
        centre = jnp.sum(summed, axis=0, keepdims=True) * scale
        summed = summed - centre
        spread = jnp.sum(summed * summed, axis=0, keepdims=True) * scale
        inverse = lax.rsqrt(spread + 1e-05)
        normed = summed * inverse
        upper = u_ref[s].astype(F32)
        scaled = upper * gains[...]
        first = jnp.sum(scaled, axis=0, keepdims=True) * scale
        second = jnp.sum(scaled * normed, axis=0, keepdims=True) * scale
        d_sum[s] = (inverse * (scaled - first - normed * second)).astype(BF16)
        product_gain = upper * normed
        sum_gain += product_gain[:, 0:128] + product_gain[:, 128:256]
    for s in samples:
        right_in[s, 0:rank] = mm(proj[...], d_sum[s]).astype(BF16)
    for s in samples:
        left_in[s, :, rank : 2 * rank] = mm_nt(x_ref[s], right_in[s, 0:rank]).astype(BF16)
        d_p_t[s] = mm_nt(right_in[s, 0:rank], x_ref[s]).astype(BF16)
    d_all = d_sum[...].reshape(count * width, features)
    mixed[...] = mm(d_all, lcb_t[...]).reshape(count, width, features)
    for s in samples:
        grad = d_sum[s].astype(F32) + mixed[s] + mm(left_in[s], right_in[s])
        grad = grad.astype(BF16)
        group, k = s // STEP, s % STEP
        grads[group, k * 128 : k * 128 + 128] = grad[0:128]
        at = 512 + 64 * (2 * (k % 2) + k // 2)
        grads[group, at : at + 64] = grad[128:192]
    sum_lcb[...] = mm(x_all, d_all, ((0,), (0,)))
    sum_fm_t, sum_proj_t = 0.0, 0.0
    for s in samples:
        sum_fm_t += mm(d_p_t[s], x_ref[s])
        sum_proj_t += mm_nt(d_sum[s], g_t[s])

    half, me = place_ref[0], place_ref[1]
    for group in range(count // STEP):
        rows = mm_nt(eye[...], grads[group])
        turned[group, 0] = rows[0:128]
        turned[group, 1] = rows[128:256]
    part = features // peers
    third = width // peers
    total = jnp.sum(sum_gain.T, axis=0, keepdims=True)
    high = total.astype(BF16).astype(F32)
    low = total - high
    middle = jnp.concatenate([high[:, 128:192], low[:, 128:192]], axis=1)
    gain_rows = [high[:, 0:128], middle, low[:, 0:128], jnp.zeros((1, LANES), F32)]
    sum_fm[...] = sum_fm_t.T
    for peer in range(peers):
        last = [sum_proj_t[peer * third : (peer + 1) * third]] + gain_rows
        sum_rest[peer] = jnp.concatenate(last, axis=0)

    lane = lax.broadcasted_iota(jnp.int32, (16, LANES), 1)
    sample = lax.broadcasted_iota(jnp.int32, (16, LANES), 0)
    mine = (lane // TILE == sample) & (sample < count)
    spread_ids = []
    for which, ref in enumerate((now_ref, next_ref)):
        ids[which] = jnp.zeros_like(ids[which])
        ids[which, 0:count] = ref[...].astype(F32)
        for side in range(2):
            line = ids[which, :, side * 128 : side * 128 + 128]
            spread_ids.append(pltpu.roll(line, 0, 1, stride=TILE, stride_axis=0))

    for k, out_ref in enumerate(out_refs):
        peer = jnp.bitwise_xor(me, k)
        place = place_of(n_grp, n_lane, peer)
        at = pl.multiple_of(place, TILE)
        for group in range(count // STEP):
            for which in range(2):
                side = half if which else 1 - half
                line = turned[group, side, pl.ds(at, TILE)]
                left = jnp.concatenate([line[:, j * 128 : j * 128 + 128] for j in range(STEP)], axis=0)
                row = which * wire.half + group * 32
                out_ref[row : row + 32] = left.astype(BF16)
                right = jnp.concatenate([line[:, 512:640], line[:, 640:768]], axis=0)
                row = which * wire.half + wire.left + group * 16
                out_ref[row : row + 16] = right.astype(BF16)
        here = pl.ds(pl.multiple_of(peer * part, part), part)
        row = wire.dense
        out_ref[row : row + part] = sum_fm[here].astype(BF16)
        out_ref[row + part : row + 2 * part] = sum_lcb[here, 0:128].astype(BF16)
        out_ref[row + 2 * part : row + 3 * part] = sum_lcb[here, 128:256].astype(BF16)
        out_ref[row + 3 * part : row + 4 * part] = sum_rest[peer].astype(BF16)
        lines = []
        for line in spread_ids:
            line = pltpu.roll(line, (LANES - place) % LANES, 1)
            lines.append(jnp.sum(jnp.where(mine, line, 0.0), axis=0, keepdims=True))
        lines.append(jnp.zeros((12, LANES), F32))
        out_ref[wire.ids : wire.ids + 16] = jnp.concatenate(lines, axis=0).astype(BF16)


def backward(n_grp, n_lane, wire, place, pooled_t, upstream_t, ids_now, ids_next, w_fm, w_proj_t, w_lcb, gain):
    count, width, features = pooled_t.shape
    rank = w_fm.shape[1]
    peers = n_grp * n_lane

    def whole(shape):
        return pl.BlockSpec(shape, lambda i: (0,) * len(shape))

    operands = (pooled_t, upstream_t, ids_now, ids_next, w_fm, w_proj_t, w_lcb, gain.reshape(1, width))
    shape = (wire.ids + 16, LANES)
    return pl.pallas_call(
        functools.partial(backward_kernel, n_grp, n_lane, wire),
        grid=(1,),
        in_specs=[SMEM] + [whole(array.shape) for array in operands],
        out_specs=[whole(shape)] * peers,
        out_shape=[jax.ShapeDtypeStruct(shape, BF16)] * peers,
        scratch_shapes=[
            pltpu.VMEM((rank, features), BF16),
            pltpu.VMEM((rank, width), BF16),
            pltpu.VMEM((features, features), BF16),
            pltpu.VMEM((width, features), F32),
            pltpu.VMEM((features, features), BF16),
            pltpu.VMEM((count, width, features), F32),
            pltpu.VMEM((count, rank, width), BF16),
            pltpu.VMEM((count, rank, features), BF16),
            pltpu.VMEM((count, width, features), BF16),
            pltpu.VMEM((count, rank, width), BF16),
            pltpu.VMEM((count, width, 2 * rank), BF16),
            pltpu.VMEM((count, 2 * rank, features), BF16),
            pltpu.VMEM((count // STEP, STEP * width, features), BF16),
            pltpu.VMEM((count // STEP, 2, features // 2, STEP * width), F32),
            pltpu.VMEM((2, 16, features), F32),
            pltpu.VMEM((features, rank), F32),
            pltpu.VMEM((features, features), F32),
            pltpu.VMEM((peers, width // peers + 4, rank), F32),
        ],
        compiler_params=pltpu.CompilerParams(vmem_limit_bytes=60 * 1024 * 1024),
        cost_estimate=pl.CostEstimate(flops=10**9, bytes_accessed=4 * 10**6, transcendentals=0),
        name="layer_backward",
    )(place, *operands)


def part_kernel(n_grp, peers, wire, other, place_ref, *refs):
    seen, refs = refs[:peers], refs[peers:]
    out, held = refs[0], refs[-1]
    half = 1 - place_ref[0] if other else place_ref[0]
    base = 0 if other else wire.half
    if other:
        dense, all_ids = refs[1:3]
        total = seen[0][wire.dense : wire.ids].astype(F32)
        for peer in range(1, peers):
            total = total + seen[peer][wire.dense : wire.ids].astype(F32)
        dense[...] = total
    lane = lax.broadcasted_iota(jnp.int32, (1, LANES), 1)
    start = ((lane % TILE) * LANES).astype(F32)
    keys = []
    for peer in range(peers):
        at = peer * LANES
        held[at : at + wire.left, 0:128] = seen[peer][base : base + wire.left]
        right = seen[peer][base + wire.left : base + wire.half]
        turned = turn(right.astype(F32)).astype(BF16)
        for i in range(wire.left // 32):
            held[at + 32 * i : at + 32 * i + 16, 128:256] = right[16 * i : 16 * i + 16]
            held[at + 32 * i + 16 : at + 32 * i + 32, 128:256] = turned[16 * i : 16 * i + 16]
        if wire.left < LANES:
            held[at + wire.left : at + LANES] = jnp.zeros((LANES - wire.left, 256), BF16)
        ids = seen[peer][wire.ids : wire.ids + 16].astype(F32)
        if other:
            all_ids[peer] = ids
        key = jnp.where(half == 0, ids[0:1], ids[1:2]) + start
        keys.append(jnp.where(lane < wire.left, key, -1.0))
    keys = jnp.concatenate(keys, axis=1)
    piece = LANES // n_grp
    for pair in range(TILE // 2):
        row = lax.broadcasted_iota(jnp.int32, (256, 1), 0).astype(F32) + 256.0 * pair
        hit = jnp.where(keys == row, 1.0, 0.0).astype(BF16)
        part = mm(hit, held[...])
        for f in range(2):
            for g in range(n_grp):
                at = f * LANES + g * piece
                rows = part[at : at + piece]
                out[g, 2 * pair + f, 0:piece] = rows[:, 0:128].astype(out.dtype)
                second = turn(rows[piece // 2 :, 128:256])
                packed = jnp.where(low_lanes(second.shape), rows[: piece // 2, 128:256], second)
                out[g, 2 * pair + f, piece : piece + piece // 2] = packed.astype(out.dtype)


def part_sums(n_grp, wire, other, place, seen):
    peers = len(seen)
    piece = LANES // n_grp
    shapes = [jax.ShapeDtypeStruct((n_grp, TILE, piece + piece // 2, LANES), BF16 if other else F32)]
    if other:
        shapes.append(jax.ShapeDtypeStruct((wire.ids - wire.dense, LANES), F32))
        shapes.append(jax.ShapeDtypeStruct((peers, 16, LANES), F32))
    return pl.pallas_call(
        functools.partial(part_kernel, n_grp, peers, wire, other),
        in_specs=[SMEM] + [VMEM] * peers,
        out_specs=[VMEM] * len(shapes),
        out_shape=shapes,
        scratch_shapes=[pltpu.VMEM((peers * LANES, 256), BF16)],
        compiler_params=params(),
        cost_estimate=pl.CostEstimate(flops=10**9, bytes_accessed=10**6, transcendentals=0),
        name="part_other" if other else "part_own",
    )(place, *seen)


def lookup_kernel(wire, factor, place_ref, mine_t, crossed_t, ids_ref, dense_own, dense_seen, *refs):
    out, held = refs[:-1], refs[-1]
    peers = len(out)
    half = place_ref[0]
    for f in range(TILE):
        at = f * LANES
        for side, ref in ((half, mine_t), (1 - half, crossed_t)):
            held[side, 0:192, at : at + LANES] = ref[f]
            held[side, 192:256, at : at + LANES] = ref[f, 128:192]
    ids = ids_ref[...].reshape(peers * 16, LANES)
    lane = lax.broadcasted_iota(jnp.int32, (1, LANES), 1)
    keys = (ids + ((lane % TILE) * LANES).astype(F32)).T
    column = lax.broadcasted_iota(jnp.int32, (1, TILE * LANES), 1).astype(F32)
    total = ((dense_own[...] + dense_seen[...]) * factor).astype(BF16)
    for which in range(2):
        for pair in range(peers // 2):
            mine = []
            for peer in (2 * pair, 2 * pair + 1):
                at = peer * 16 + 2 + which
                mine.append(keys[0 : wire.left, at : at + 1])
            hit = jnp.where(jnp.concatenate(mine, axis=0) == column, 1.0, 0.0).astype(BF16)
            both = mm_nt(hit, held[which])
            for k in range(2):
                got = both[k * wire.left : (k + 1) * wire.left]
                peer, base = 2 * pair + k, which * wire.half
                out[peer][base : base + wire.left] = got[:, 0:128].astype(BF16)
                for i in range(wire.left // 32):
                    first, second = got[32 * i : 32 * i + 16, 128:256], got[32 * i + 16 : 32 * i + 32, 128:256]
                    at = base + wire.left + 16 * i
                    out[peer][at : at + 16] = jnp.where(low_lanes(first.shape), first, second).astype(BF16)
    for peer in range(peers):
        out[peer][wire.dense : wire.ids] = total


def lookup(wire, factor, place, mine_t, crossed_t, ids, dense_own, dense_seen):
    peers = ids.shape[0]
    return pl.pallas_call(
        functools.partial(lookup_kernel, wire, factor),
        in_specs=[SMEM] + [VMEM] * 5,
        out_specs=[VMEM] * peers,
        out_shape=[jax.ShapeDtypeStruct((wire.ids, LANES), BF16)] * peers,
        scratch_shapes=[pltpu.VMEM((2, 256, TILE * LANES), BF16)],
        compiler_params=params(),
        cost_estimate=pl.CostEstimate(flops=10**9, bytes_accessed=10**6, transcendentals=0),
        name="lookup",
    )(place, mine_t, crossed_t, ids, dense_own, dense_seen)


def unpack_kernel(n_grp, n_lane, wire, place_ref, *refs):
    peers = n_grp * n_lane
    seen, refs = refs[:peers], refs[peers:]
    rows_out, fm, proj_t, lcb, gain, held, rest = refs
    step = pl.program_id(0)
    me = place_ref[1]
    for k in range(peers):
        place = place_of(n_grp, n_lane, jnp.bitwise_xor(me, k))
        for side in range(2):
            row = pl.multiple_of(side * wire.half + step * 32, 16)
            left = seen[k][pl.ds(row, 32)].astype(F32)
            row = pl.multiple_of(side * wire.half + wire.left + step * 16, 16)
            right = seen[k][pl.ds(row, 16)].astype(F32)
            turned = turn(right)
            at = pl.ds(pl.multiple_of(side * 128 + place, TILE), TILE)
            for s in range(STEP):
                held[s, at, 0:128] = left[s * TILE : s * TILE + TILE]
                base = (s % 2) * TILE
                held[s, at, 128:256] = (turned if s // 2 else right)[base : base + TILE]
    eye = identity(192, 256)
    for s in range(STEP):
        rows_out[s] = mm_nt(eye, held[s].astype(BF16)).astype(BF16)

    @pl.when(step == 0)
    def _():
        part, third = 256 // peers, 192 // peers
        for k in range(peers):
            peer = jnp.bitwise_xor(me, k)
            dense = seen[k][wire.dense : wire.ids].astype(F32)
            here = pl.ds(pl.multiple_of(peer * part, part), part)
            fm[here] = dense[0:part]
            lcb[here, 0:128] = dense[part : 2 * part]
            lcb[here, 128:256] = dense[2 * part : 3 * part]
            rest[peer] = dense[3 * part : 4 * part]
        for peer in range(peers):
            proj_t[peer * third : (peer + 1) * third] = rest[peer, 0:third]
        last = rest[0, third : third + 3]
        gain[:, 0:128] = last[0:1] + last[2:3]
        gain[:, 128:192] = (last + turn(last))[1:2, 0:64]


def unpack(n_grp, n_lane, wire, count, place, seen):
    def whole(*shape):
        return pl.BlockSpec(shape, lambda i: (0,) * len(shape))

    peers = len(seen)
    shapes = [(256, 128), (192, 128), (256, 256), (1, 192)]
    return pl.pallas_call(
        functools.partial(unpack_kernel, n_grp, n_lane, wire),
        grid=(count // STEP,),
        in_specs=[SMEM] + [whole(*seen[0].shape)] * peers,
        out_specs=[pl.BlockSpec((STEP, 192, 256), lambda i: (i, 0, 0))] + [whole(*shape) for shape in shapes],
        out_shape=[jax.ShapeDtypeStruct((count, 192, 256), BF16)]
        + [jax.ShapeDtypeStruct(shape, F32) for shape in shapes],
        scratch_shapes=[pltpu.VMEM((STEP, 256, 256), F32), pltpu.VMEM((peers, 256 // peers, LANES), F32)],
        compiler_params=params(),
        cost_estimate=pl.CostEstimate(flops=0, bytes_accessed=10**6, transcendentals=0),
        name="unpack_rows",
    )(place, *seen)


def combine_kernel(place, own, seen, *outs):
    for k, out in enumerate(outs):
        g = jnp.bitwise_xor(place[0], k)
        out[...] = (own[g] + seen[g].astype(F32)).astype(BF16)


def combine(place, own, seen):
    n_grp = own.shape[0]
    shape = jax.ShapeDtypeStruct(own.shape[1:], BF16)
    return pl.pallas_call(
        combine_kernel,
        in_specs=[SMEM, VMEM, VMEM],
        out_specs=[VMEM] * n_grp,
        out_shape=[shape] * n_grp,
        compiler_params=params(),
        cost_estimate=pl.CostEstimate(flops=0, bytes_accessed=10**6, transcendentals=0),
        name="combine",
    )(place, own, seen)


def finish_kernel(place, *refs):
    out = refs[-1]
    piece = out.shape[1]
    for k, seen in enumerate(refs[:-1]):
        base = jnp.bitwise_xor(place[0], k) * TILE
        for f in range(TILE):
            out[base + f, :, 0:128] = seen[f, 0:piece].astype(F32)
            packed = seen[f, piece : piece + piece // 2].astype(F32)
            out[base + f, 0 : piece // 2, 128:192] = packed[:, 0:64]
            out[base + f, piece // 2 : piece, 128:192] = turn(packed)[:, 0:64]


def finish(place, pieces):
    n_grp = len(pieces)
    piece = pieces[0].shape[1] * 2 // 3
    return pl.pallas_call(
        finish_kernel,
        in_specs=[SMEM] + [VMEM] * n_grp,
        out_specs=VMEM,
        out_shape=jax.ShapeDtypeStruct((n_grp * TILE, piece, 192), F32),
        compiler_params=params(),
        cost_estimate=pl.CostEstimate(flops=0, bytes_accessed=10**6, transcendentals=0),
        name="finish_tables",
    )(place, *pieces)


def swap(blocks, axes):
    n = len(blocks)
    return [blocks[0]] + [lax.ppermute(blocks[k], axes, [(i, i ^ k) for i in range(n)]) for k in range(1, n)]


def cross(array):
    return lax.ppermute(array, "half", [(0, 1), (1, 0)])


def halves(pooled, upstream, ids_now, ids_next, tables, w_fm, w_proj, w_lcb, gain):
    n_grp, n_lane = lax.axis_size("grp"), lax.axis_size("lane")
    count = pooled.shape[0]
    wire = Wire(count, n_grp * n_lane)
    factor = 1.0 / (count * n_grp * 2 * n_lane)
    half = lax.axis_index("half").astype(jnp.int32)
    grp = lax.axis_index("grp").astype(jnp.int32)
    place = jnp.stack([half, lax.axis_index(PEER).astype(jnp.int32)])
    mine_t = lax.dynamic_slice_in_dim(tables.transpose(0, 2, 1), grp * TILE, TILE, 0)
    crossed_t = cross(mine_t)
    sent = backward(
        n_grp, n_lane, wire, place,
        pooled.transpose(0, 2, 1), upstream.transpose(0, 2, 1), ids_now, ids_next, w_fm, w_proj.T, w_lcb, gain,
    )
    seen = swap(sent, PEER)
    part, dense, ids = part_sums(n_grp, wire, True, place, seen)
    dense_seen = cross(dense)
    part_seen = cross(part)
    (own,) = part_sums(n_grp, wire, False, place, seen)
    own, ids = lax.optimization_barrier((own, ids))
    rows_wire = lookup(wire, factor, place, mine_t, crossed_t, ids, dense, dense_seen)
    rows = swap(rows_wire, PEER)
    next_rows, grad_fm, grad_proj_t, grad_lcb, grad_gain = unpack(n_grp, n_lane, wire, count, place, rows)
    pieces = swap(combine(grp[None], own, part_seen), "grp")
    table_grad = finish(grp[None], pieces)
    return next_rows.transpose(0, 2, 1), table_grad, grad_fm, grad_proj_t.T, grad_lcb, grad_gain.reshape(-1)


def solution(mesh):
    n_grp, n_emb = mesh.shape["grp"], mesh.shape["emb"]
    split = n_emb % 2 == 0 and n_grp * (n_emb // 2) == 16 and n_grp % 2 == 0

    def run(*args):
        pooled, _, _, _, tables, w_fm = args[:6]
        count = pooled.shape[0] // (n_grp * n_emb)
        fits = (
            split
            and pooled.shape[1:] == (256, 192)
            and tables.shape[1] == 128
            and w_fm.shape[1] == 128
            and pooled.shape[1] == n_grp * n_emb * TILE
            and count % STEP == 0
            and count <= 16
        )
        if fits:
            devices = mesh.devices.reshape(n_grp, 2, n_emb // 2)
            where, emb, body = Mesh(devices, ("grp", "half", "lane")), ("half", "lane"), halves
        else:
            where, emb, body = mesh, ("emb",), local
        both = ("grp",) + emb
        return jax.shard_map(
            body,
            mesh=where,
            in_specs=(
                P(both, None, None),
                P(both, None, None),
                P(both, None),
                P(both, None),
                P(emb, None, None),
                P(),
                P(),
                P(),
                P(),
            ),
            out_specs=(P(both, None, None), P(emb, "grp", None), P(), P(), P(), P()),
            check_vma=False,
        )(*args)

    return run
```

```python
import functools

import jax
import jax.numpy as jnp
from jax import lax
from jax.experimental import pallas as pl
from jax.experimental.pallas import tpu as pltpu
from jax.sharding import Mesh, PartitionSpec as P

F32, BF16 = jnp.float32, jnp.bfloat16
SMEM = pl.BlockSpec(memory_space=pltpu.SMEM)
VMEM = pl.BlockSpec(memory_space=pltpu.VMEM)
LANES = 128
TILE = 8
STEP = 4
LIMIT = 30 * 1024 * 1024
PEER = ("grp", "lane")


BOTH = ("grp", "emb")


def product(form, left, right):
    return jnp.einsum(form, left, right, preferred_element_type=jnp.float32)


def layer_backward(embeds, cotangent, w_fm, w_proj, w_lcb, gain):
    fm_proj = product("bfc,fj->bcj", embeds, w_fm).astype(jnp.bfloat16)
    fm_rows = product("bfc,bcj->bfj", embeds, fm_proj).astype(jnp.bfloat16)
    projected = product("bfj,jc->bfc", fm_rows, w_proj)
    compressed = product("fi,bfc->bic", w_lcb, embeds)
    summed = embeds.astype(jnp.float32) + projected + compressed
    centre = jnp.mean(summed, axis=2, keepdims=True)
    spread = jnp.mean((summed - centre) ** 2, axis=2, keepdims=True)
    inverse = lax.rsqrt(spread + 1e-05)
    normed = (summed - centre) * inverse
    upper = cotangent.astype(jnp.float32)
    scaled = upper * gain
    grad_sum = inverse * (
        scaled
        - jnp.mean(scaled, axis=2, keepdims=True)
        - normed * jnp.mean(scaled * normed, axis=2, keepdims=True)
    )
    grad_sum = grad_sum.astype(jnp.bfloat16)
    grad_gain = jnp.sum(upper * normed, axis=(0, 1))
    grad_proj = product("bfj,bfc->jc", fm_rows, grad_sum)
    grad_rows = product("bfc,jc->bfj", grad_sum, w_proj).astype(jnp.bfloat16)
    grad_p = product("bfc,bfj->bcj", embeds, grad_rows).astype(jnp.bfloat16)
    grad_fm = product("bfc,bcj->fj", embeds, grad_p)
    grad_lcb = product("bfc,bic->fi", embeds, grad_sum)
    grad_in = (
        grad_sum.astype(jnp.float32)
        + product("bfj,bcj->bfc", grad_rows, fm_proj)
        + product("fj,bcj->bfc", w_fm, grad_p)
        + product("fi,bic->bfc", w_lcb, grad_sum)
    )
    return (grad_in.astype(jnp.bfloat16), (grad_fm, grad_proj, grad_lcb, grad_gain))


def exchange(blocks, axes):
    return lax.all_to_all(blocks, axes, split_axis=0, concat_axis=0, tiled=True)


def dense_sum(partials, factor):
    n = lax.axis_size("grp") * lax.axis_size("emb")
    shapes = [part.shape for part in partials]
    flat = jnp.concatenate([part.reshape(-1) for part in partials])
    unit = 128 * n
    padded = -(-flat.shape[0] // unit) * unit
    flat = jnp.pad(flat, (0, padded - flat.shape[0])).astype(jnp.bfloat16)
    seen = exchange(flat.reshape(n, padded // unit, 128), BOTH)
    share = (jnp.sum(seen.astype(jnp.float32), axis=0) * factor).astype(jnp.bfloat16)
    total = exchange(jnp.broadcast_to(share[None], (n,) + share.shape), BOTH).reshape(-1)
    total = total.astype(jnp.float32)
    outs, at = [], 0
    for shape in shapes:
        size = 1
        for extent in shape:
            size *= extent
        outs.append(total[at : at + size].reshape(shape))
        at += size
    return outs


def local(pooled, upstream, ids_now, ids_next, tables, w_fm, w_proj, w_lcb, gain):
    n_grp, n_emb = lax.axis_size("grp"), lax.axis_size("emb")
    count, features, width = pooled.shape
    owned, rows = tables.shape[:2]
    ids = jnp.stack([ids_now, ids_next]).reshape(2, count, n_emb, owned)
    ids = exchange(ids.transpose(2, 0, 1, 3), "emb")
    row_index = jnp.arange(rows)
    wanted = (ids[:, 1, :, :, None] == row_index).astype(jnp.bfloat16)
    fetched = product("esfr,frc->esfc", wanted, tables).astype(jnp.bfloat16)
    next_rows = exchange(fetched, "emb")
    next_rows = next_rows.transpose(1, 0, 2, 3).reshape(count, features, width)
    grad_in, partials = layer_backward(pooled, upstream, w_fm, w_proj, w_lcb, gain)
    grad_in = grad_in.reshape(count, n_emb, owned, width).transpose(1, 0, 2, 3)
    grads = exchange(grad_in, "emb")
    hit = (ids[:, 0, :, :, None] == row_index).astype(jnp.bfloat16)
    part = product("esfr,esfc->frc", hit, grads).astype(jnp.bfloat16)
    part = part.reshape(owned, n_grp, rows // n_grp, width).transpose(1, 0, 2, 3)
    table_grad = jnp.sum(exchange(part, "grp").astype(jnp.float32), axis=0)
    dense = dense_sum(partials, 1.0 / (count * n_grp * n_emb))
    return (next_rows, table_grad, *dense)


def params(share=1):
    return pltpu.CompilerParams(vmem_limit_bytes=share * LIMIT)


def cost(weight):
    return pl.CostEstimate(flops=weight * 10**9, bytes_accessed=10**5, transcendentals=0)


def mm(left, right, dims=((1,), (0,))):
    return lax.dot_general(left, right, (dims, ((), ())), preferred_element_type=F32)


def mm_nt(left, right):
    return mm(left, right, ((1,), (1,)))


def low_lanes(shape):
    return lax.broadcasted_iota(jnp.int32, shape, 1) < LANES // 2


def turn(tile):
    return pltpu.roll(tile, LANES // 2, 1)


def identity(rows, lanes):
    row = lax.broadcasted_iota(jnp.int32, (rows, lanes), 0)
    return jnp.where(row == lax.broadcasted_iota(jnp.int32, (rows, lanes), 1), 1.0, 0.0).astype(BF16)


class Wire:
    def __init__(self, count, peers):
        self.left = count * TILE
        self.half = self.left + self.left // 2
        self.dense = 2 * self.half
        self.share = 1024 // peers
        self.ids = self.dense + self.share
        self.back_left = (self.share, self.share + self.left)
        self.back_right = (self.share + 2 * self.left, self.share + 2 * self.left + self.left // 2)


def place_of(n_grp, n_lane, peer):
    return (peer % n_lane) * n_grp * TILE + (peer // n_lane) * TILE


def backward_kernel(
    n_grp, n_lane, wire,
    half_ref, x_ref, u_ref, now_ref, next_ref, fm_ref, proj_t_ref, lcb_ref, gain_ref,
    out_ref,
    fm_t, proj, lcb_t, gains, eye, mixed, p_t, g_t, d_sum, d_p_t, left_in, right_in, grads, turned, ids,
):
    count, width, features = x_ref.shape
    rank = fm_ref.shape[1]
    peers = n_grp * n_lane
    scale = 1.0 / width
    samples = range(count)

    turned_fm = fm_ref[...].astype(F32).T.astype(BF16)
    fm_t[...] = turned_fm
    proj[...] = proj_t_ref[...].astype(F32).T.astype(BF16)
    lcb_t[...] = lcb_ref[...].astype(F32).T.astype(BF16)
    column = jnp.broadcast_to(gain_ref[...], (LANES, width)).T
    gains[:, 0:128] = column
    gains[:, 128:256] = column
    eye[...] = identity(features, features)

    x_all = x_ref[...].reshape(count * width, features)
    left_in[:, :, 0:rank] = mm(x_all, fm_ref[...]).astype(BF16).reshape(count, width, rank)
    mixed[...] = mm(x_all, lcb_ref[...]).reshape(count, width, features)
    for s in samples:
        p_t[s] = mm_nt(fm_t[...], x_ref[s]).astype(BF16)
        right_in[s, rank : 2 * rank] = turned_fm
    for s in samples:
        g_t[s] = mm(p_t[s], x_ref[s]).astype(BF16)
    for s in samples:
        mixed[s] = mixed[s] + mm(proj_t_ref[...], g_t[s])
    sum_gain = 0.0
    for s in samples:
        summed = x_ref[s].astype(F32) + mixed[s]
        centre = jnp.sum(summed, axis=0, keepdims=True) * scale
        summed = summed - centre
        spread = jnp.sum(summed * summed, axis=0, keepdims=True) * scale
        inverse = lax.rsqrt(spread + 1e-05)
        normed = summed * inverse
        upper = u_ref[s].astype(F32)
        scaled = upper * gains[...]
        first = jnp.sum(scaled, axis=0, keepdims=True) * scale
        second = jnp.sum(scaled * normed, axis=0, keepdims=True) * scale
        d_sum[s] = (inverse * (scaled - first - normed * second)).astype(BF16)
        product_gain = upper * normed
        sum_gain += product_gain[:, 0:128] + product_gain[:, 128:256]
    for s in samples:
        right_in[s, 0:rank] = mm(proj[...], d_sum[s]).astype(BF16)
    for s in samples:
        left_in[s, :, rank : 2 * rank] = mm_nt(x_ref[s], right_in[s, 0:rank]).astype(BF16)
        d_p_t[s] = mm_nt(right_in[s, 0:rank], x_ref[s]).astype(BF16)
    d_all = d_sum[...].reshape(count * width, features)
    mixed[...] = mm(d_all, lcb_t[...]).reshape(count, width, features)
    for s in samples:
        grad = d_sum[s].astype(F32) + mixed[s] + mm(left_in[s], right_in[s])
        grad = grad.astype(BF16)
        group, k = s // STEP, s % STEP
        grads[group, k * 128 : k * 128 + 128] = grad[0:128]
        at = 512 + 64 * (2 * (k % 2) + k // 2)
        grads[group, at : at + 64] = grad[128:192]
    sum_lcb = mm(x_all, d_all, ((0,), (0,)))
    sum_fm_t, sum_proj_t = 0.0, 0.0
    for s in samples:
        sum_fm_t += mm(d_p_t[s], x_ref[s])
        sum_proj_t += mm_nt(d_sum[s], g_t[s])

    half = half_ref[0]
    for group in range(count // STEP):
        rows = mm_nt(eye[...], grads[group])
        turned[group, 0] = rows[0:128]
        turned[group, 1] = rows[128:256]
    for group in range(count // STEP):
        for which in range(2):
            side = half if which else 1 - half
            for peer in range(peers):
                at = place_of(n_grp, n_lane, peer)
                line = turned[group, side, at : at + TILE]
                left = jnp.concatenate([line[:, k * 128 : k * 128 + 128] for k in range(STEP)], axis=0)
                row = which * wire.half + group * 32
                out_ref[peer, row : row + 32] = left.astype(BF16)
                right = jnp.concatenate([line[:, 512:640], line[:, 640:768]], axis=0)
                row = which * wire.half + wire.left + group * 16
                out_ref[peer, row : row + 16] = right.astype(BF16)

    part = features // peers
    third = width // peers
    total = jnp.sum(sum_gain.T, axis=0, keepdims=True)
    high = total.astype(BF16).astype(F32)
    low = total - high
    middle = jnp.concatenate([high[:, 128:192], low[:, 128:192]], axis=1)
    gain_rows = [high[:, 0:128], middle, low[:, 0:128], jnp.zeros((1, LANES), F32)]
    sum_fm = sum_fm_t.T
    for peer in range(peers):
        at = wire.dense
        here = slice(peer * part, (peer + 1) * part)
        out_ref[peer, at : at + part] = sum_fm[here].astype(BF16)
        out_ref[peer, at + part : at + 2 * part] = sum_lcb[here, 0:128].astype(BF16)
        out_ref[peer, at + 2 * part : at + 3 * part] = sum_lcb[here, 128:256].astype(BF16)
        last = [sum_proj_t[peer * third : (peer + 1) * third]] + gain_rows
        out_ref[peer, at + 3 * part : at + 4 * part] = jnp.concatenate(last, axis=0).astype(BF16)

    lane = lax.broadcasted_iota(jnp.int32, (16, LANES), 1)
    sample = lax.broadcasted_iota(jnp.int32, (16, LANES), 0)
    mine = (lane // TILE == sample) & (sample < count)
    spread_ids = []
    for which, ref in enumerate((now_ref, next_ref)):
        ids[which] = jnp.zeros_like(ids[which])
        ids[which, 0:count] = ref[...].astype(F32)
        for side in range(2):
            line = ids[which, :, side * 128 : side * 128 + 128]
            spread_ids.append(pltpu.roll(line, 0, 1, stride=TILE, stride_axis=0))
    for peer in range(peers):
        at = place_of(n_grp, n_lane, peer)
        lines = []
        for line in spread_ids:
            line = pltpu.roll(line, LANES - at, 1) if at else line
            lines.append(jnp.sum(jnp.where(mine, line, 0.0), axis=0, keepdims=True))
        lines.append(jnp.zeros((12, LANES), F32))
        out_ref[peer, wire.ids : wire.ids + 16] = jnp.concatenate(lines, axis=0).astype(BF16)


def backward(n_grp, n_lane, wire, half, pooled_t, upstream_t, ids_now, ids_next, w_fm, w_proj_t, w_lcb, gain):
    count, width, features = pooled_t.shape
    rank = w_fm.shape[1]
    peers = n_grp * n_lane

    def whole(shape):
        return pl.BlockSpec(shape, lambda i: (0,) * len(shape))

    operands = (pooled_t, upstream_t, ids_now, ids_next, w_fm, w_proj_t, w_lcb, gain.reshape(1, width))
    shape = (peers, wire.ids + 16, LANES)
    return pl.pallas_call(
        functools.partial(backward_kernel, n_grp, n_lane, wire),
        grid=(1,),
        in_specs=[SMEM] + [whole(array.shape) for array in operands],
        out_specs=whole(shape),
        out_shape=jax.ShapeDtypeStruct(shape, BF16),
        scratch_shapes=[
            pltpu.VMEM((rank, features), BF16),
            pltpu.VMEM((rank, width), BF16),
            pltpu.VMEM((features, features), BF16),
            pltpu.VMEM((width, features), F32),
            pltpu.VMEM((features, features), BF16),
            pltpu.VMEM((count, width, features), F32),
            pltpu.VMEM((count, rank, width), BF16),
            pltpu.VMEM((count, rank, features), BF16),
            pltpu.VMEM((count, width, features), BF16),
            pltpu.VMEM((count, rank, width), BF16),
            pltpu.VMEM((count, width, 2 * rank), BF16),
            pltpu.VMEM((count, 2 * rank, features), BF16),
            pltpu.VMEM((count // STEP, STEP * width, features), BF16),
            pltpu.VMEM((count // STEP, 2, features // 2, STEP * width), F32),
            pltpu.VMEM((2, 16, features), F32),
        ],
        compiler_params=params(2),
        cost_estimate=cost(1),
        name="layer_backward",
    )(half, *operands)


def part_kernel(n_grp, wire, other, half_ref, seen, *refs):
    refs = refs if other else refs[1:]
    out, held = refs[0], refs[-1]
    peers = seen.shape[0]
    half = 1 - half_ref[0] if other else half_ref[0]
    base = 0 if other else wire.half
    if other:
        dense = refs[1]
        total = seen[0, wire.dense : wire.ids].astype(F32)
        for peer in range(1, peers):
            total = total + seen[peer, wire.dense : wire.ids].astype(F32)
        dense[...] = total
    lane = lax.broadcasted_iota(jnp.int32, (1, LANES), 1)
    start = ((lane % TILE) * LANES).astype(F32)
    keys = []
    for peer in range(peers):
        at = peer * LANES
        held[at : at + wire.left, 0:128] = seen[peer, base : base + wire.left]
        right = seen[peer, base + wire.left : base + wire.half]
        turned = turn(right.astype(F32)).astype(BF16)
        for i in range(wire.left // 32):
            held[at + 32 * i : at + 32 * i + 16, 128:256] = right[16 * i : 16 * i + 16]
            held[at + 32 * i + 16 : at + 32 * i + 32, 128:256] = turned[16 * i : 16 * i + 16]
        if wire.left < LANES:
            held[at + wire.left : at + LANES] = jnp.zeros((LANES - wire.left, 256), BF16)
        ids = seen[peer, wire.ids : wire.ids + 16].astype(F32)
        key = jnp.where(half == 0, ids[0:1], ids[1:2]) + start
        keys.append(jnp.where(lane < wire.left, key, -1.0))
    keys = jnp.concatenate(keys, axis=1)
    piece = LANES // n_grp
    for pair in range(TILE // 2):
        row = lax.broadcasted_iota(jnp.int32, (256, 1), 0).astype(F32) + 256.0 * pair
        hit = jnp.where(keys == row, 1.0, 0.0).astype(BF16)
        part = mm(hit, held[...])
        for f in range(2):
            for g in range(n_grp):
                at = f * LANES + g * piece
                rows = part[at : at + piece]
                out[g, 2 * pair + f, 0:piece] = rows[:, 0:128].astype(out.dtype)
                second = turn(rows[piece // 2 :, 128:256])
                packed = jnp.where(low_lanes(second.shape), rows[: piece // 2, 128:256], second)
                out[g, 2 * pair + f, piece : piece + piece // 2] = packed.astype(out.dtype)


def part_sums(n_grp, wire, other, half, seen, *after):
    peers = seen.shape[0]
    piece = LANES // n_grp
    shapes = [jax.ShapeDtypeStruct((n_grp, TILE, piece + piece // 2, LANES), BF16 if other else F32)]
    if other:
        shapes.append(jax.ShapeDtypeStruct((wire.share, LANES), F32))
    return pl.pallas_call(
        functools.partial(part_kernel, n_grp, wire, other),
        in_specs=[SMEM, VMEM] + [pl.BlockSpec(memory_space=pl.ANY)] * len(after),
        out_specs=[VMEM] * len(shapes),
        out_shape=shapes,
        scratch_shapes=[pltpu.VMEM((peers * LANES, 256), BF16)],
        compiler_params=params(),
        cost_estimate=cost(1),
        name="part_other" if other else "part_own",
    )(half, seen, *after)


def lookup_kernel(wire, half_ref, mine_t, crossed_t, ids_ref, out, held, hit):
    peers = out.shape[0]
    half = half_ref[0]
    for f in range(TILE):
        at = f * LANES
        for side, ref in ((half, mine_t), (1 - half, crossed_t)):
            held[side, 0:192, at : at + LANES] = ref[f]
            held[side, 192:256, at : at + LANES] = ref[f, 128:192]
    ids = ids_ref[...].astype(F32).reshape(peers * 16, LANES)
    lane = lax.broadcasted_iota(jnp.int32, (1, LANES), 1)
    keys = (ids + ((lane % TILE) * LANES).astype(F32)).T
    column = lax.broadcasted_iota(jnp.int32, (1, TILE * LANES), 1).astype(F32)
    for which in range(2):
        for peer in range(peers):
            at = peer * 16 + 2 + which
            mine = jnp.where(keys[0 : wire.left, at : at + 1] == column, 1.0, 0.0)
            hit[which, peer * wire.left : (peer + 1) * wire.left] = mine.astype(BF16)
    for which in range(2):
        rows = mm_nt(hit[which], held[which])
        for peer in range(peers):
            got = rows[peer * wire.left : (peer + 1) * wire.left]
            base = wire.back_left[which]
            out[peer, base : base + wire.left] = got[:, 0:128].astype(BF16)
            packed = []
            for i in range(wire.left // 32):
                first, second = got[32 * i : 32 * i + 16, 128:256], got[32 * i + 16 : 32 * i + 32, 128:256]
                packed.append(jnp.where(low_lanes(first.shape), first, second))
            base = wire.back_right[which]
            out[peer, base : base + wire.left // 2] = jnp.concatenate(packed, axis=0).astype(BF16)


def lookup(wire, half, mine_t, crossed_t, ids):
    peers = ids.shape[0]

    def whole(shape):
        return pl.BlockSpec(shape, lambda i: (0,) * len(shape))

    at = wire.ids // 16
    return pl.pallas_call(
        functools.partial(lookup_kernel, wire),
        grid=(1,),
        in_specs=[
            SMEM,
            whole(mine_t.shape),
            whole(crossed_t.shape),
            pl.BlockSpec((peers, 16, LANES), lambda i: (0, at, 0)),
        ],
        out_specs=whole((peers, wire.ids, LANES)),
        out_shape=jax.ShapeDtypeStruct((peers, wire.ids, LANES), BF16),
        scratch_shapes=[
            pltpu.VMEM((2, 256, TILE * LANES), BF16),
            pltpu.VMEM((2, peers * wire.left, TILE * LANES), BF16),
        ],
        compiler_params=params(2),
        cost_estimate=cost(100),
        name="lookup",
    )(half, mine_t, crossed_t, ids)


def fill_kernel(factor, rows, own, seen, out, token):
    token[...] = jnp.zeros_like(token)
    total = ((own[...] + seen[...]) * factor).astype(BF16)
    for peer in range(out.shape[0]):
        out[peer] = total


def fill(wire, factor, rows, own, seen):
    peers = rows.shape[0]

    def whole(shape):
        return pl.BlockSpec(shape, lambda i: (0,) * len(shape))

    return pl.pallas_call(
        functools.partial(fill_kernel, factor),
        grid=(1,),
        in_specs=[pl.BlockSpec(memory_space=pl.ANY), whole(own.shape), whole(seen.shape)],
        out_specs=[whole((peers, wire.share, LANES)), whole((8, LANES))],
        out_shape=[jax.ShapeDtypeStruct(rows.shape, BF16), jax.ShapeDtypeStruct((8, LANES), F32)],
        input_output_aliases={0: 0},
        compiler_params=params(2),
        cost_estimate=cost(1),
        name="fill_dense",
    )(rows, own, seen)


def unpack_kernel(n_grp, n_lane, dense_ref, left0, left1, right0, right1, rows_out, fm, proj_t, lcb, gain, held):
    step = pl.program_id(0)
    peers = n_grp * n_lane
    for side, (left_ref, right_ref) in enumerate(((left0, right0), (left1, right1))):
        for q in range(n_lane):
            for gg in range(n_grp // 2):
                left, right = [], []
                for g in (2 * gg, 2 * gg + 1):
                    peer = g * n_lane + q
                    left.append(left_ref[peer].astype(F32))
                    packed = right_ref[peer].astype(F32)
                    right.append(jnp.concatenate([packed, turn(packed)], axis=0))
                at = side * 128 + q * n_grp * TILE + gg * 16
                for s in range(STEP):
                    here = slice(s * TILE, s * TILE + TILE)
                    both = jnp.concatenate([left[0][here], left[1][here]], axis=0)
                    held[s, at : at + 16, 0:128] = both.astype(BF16)
                    both = jnp.concatenate([right[0][here], right[1][here]], axis=0)
                    held[s, at : at + 16, 128:256] = both.astype(BF16)
    eye = identity(192, 256)
    for s in range(STEP):
        rows_out[s] = mm_nt(eye, held[s]).astype(BF16)

    @pl.when(step == 0)
    def _():
        part, third = 256 // peers, 192 // peers
        for peer in range(peers):
            dense = dense_ref[peer].astype(F32)
            here = slice(peer * part, (peer + 1) * part)
            fm[here] = dense[0:part]
            lcb[here, 0:128] = dense[part : 2 * part]
            lcb[here, 128:256] = dense[2 * part : 3 * part]
            last = dense[3 * part : 4 * part]
            proj_t[peer * third : (peer + 1) * third] = last[0:third]
            if peer == 0:
                last = last[third : third + 3]
                gain[:, 0:128] = last[0:1] + last[2:3]
                gain[:, 128:192] = (last + turn(last))[1:2, 0:64]


def unpack(n_grp, n_lane, wire, count, seen):
    def whole(*shape):
        return pl.BlockSpec(shape, lambda i: (0,) * len(shape))

    def part(rows, start):
        return pl.BlockSpec((peers, rows, LANES), lambda i: (0, start // rows + i, 0))

    peers = n_grp * n_lane
    shapes = [(256, 128), (192, 128), (256, 256), (1, 192)]
    return pl.pallas_call(
        functools.partial(unpack_kernel, n_grp, n_lane),
        grid=(count // STEP,),
        in_specs=[pl.BlockSpec((peers, wire.share, LANES), lambda i: (0, 0, 0))]
        + [part(32, start) for start in wire.back_left]
        + [part(16, start) for start in wire.back_right],
        out_specs=[pl.BlockSpec((STEP, 192, 256), lambda i: (i, 0, 0))] + [whole(*shape) for shape in shapes],
        out_shape=[jax.ShapeDtypeStruct((count, 192, 256), BF16)]
        + [jax.ShapeDtypeStruct(shape, F32) for shape in shapes],
        scratch_shapes=[pltpu.VMEM((STEP, 256, 256), BF16)],
        compiler_params=params(),
        cost_estimate=cost(1),
        name="unpack_rows",
    )(seen, seen, seen, seen, seen)


def combine_kernel(place, own, seen, after, *outs):
    for k, out in enumerate(outs):
        g = jnp.bitwise_xor(place[0], k)
        out[...] = (own[g] + seen[g].astype(F32)).astype(BF16)


def combine(place, own, seen, after):
    n_grp = own.shape[0]
    shape = jax.ShapeDtypeStruct(own.shape[1:], BF16)
    return pl.pallas_call(
        combine_kernel,
        in_specs=[SMEM, VMEM, VMEM, pl.BlockSpec(memory_space=pl.ANY)],
        out_specs=[VMEM] * n_grp,
        out_shape=[shape] * n_grp,
        compiler_params=params(),
        cost_estimate=cost(100),
        name="combine",
    )(place, own, seen, after)


def finish_kernel(place, *refs):
    out = refs[-1]
    piece = out.shape[1]
    for k, seen in enumerate(refs[:-1]):
        base = jnp.bitwise_xor(place[0], k) * TILE
        for f in range(TILE):
            out[base + f, :, 0:128] = seen[f, 0:piece].astype(F32)
            packed = seen[f, piece : piece + piece // 2].astype(F32)
            out[base + f, 0 : piece // 2, 128:192] = packed[:, 0:64]
            out[base + f, piece // 2 : piece, 128:192] = turn(packed)[:, 0:64]


def finish(place, pieces):
    n_grp = len(pieces)
    piece = pieces[0].shape[1] * 2 // 3
    return pl.pallas_call(
        finish_kernel,
        in_specs=[SMEM] + [VMEM] * n_grp,
        out_specs=VMEM,
        out_shape=jax.ShapeDtypeStruct((n_grp * TILE, piece, 192), F32),
        compiler_params=params(),
        cost_estimate=cost(0),
        name="finish_tables",
    )(place, *pieces)


def cross(array):
    return lax.ppermute(array, "half", [(0, 1), (1, 0)])


def halves(pooled, upstream, ids_now, ids_next, tables, w_fm, w_proj, w_lcb, gain):
    n_grp, n_lane = lax.axis_size("grp"), lax.axis_size("lane")
    count = pooled.shape[0]
    wire = Wire(count, n_grp * n_lane)
    factor = 1.0 / (count * n_grp * 2 * n_lane)
    half = lax.axis_index("half").astype(jnp.int32)[None]
    grp = lax.axis_index("grp").astype(jnp.int32)
    mine_t = lax.dynamic_slice_in_dim(tables.transpose(0, 2, 1), grp * TILE, TILE, 0)
    crossed_t = cross(mine_t)
    sent = backward(
        n_grp, n_lane, wire, half,
        pooled.transpose(0, 2, 1), upstream.transpose(0, 2, 1), ids_now, ids_next, w_fm, w_proj.T, w_lcb, gain,
    )
    seen = exchange(sent, PEER)
    part, dense = part_sums(n_grp, wire, True, half, seen)
    dense_seen = cross(dense)
    part_seen = cross(part)
    rows_wire = lookup(wire, half, mine_t, crossed_t, seen)
    rows_wire, token = fill(wire, factor, rows_wire, dense, dense_seen)
    rows = exchange(rows_wire, PEER)
    (own,) = part_sums(n_grp, wire, False, half, seen, token)
    next_rows, grad_fm, grad_proj_t, grad_lcb, grad_gain = unpack(n_grp, n_lane, wire, count, rows)
    pieces = combine(grp[None], own, part_seen, token)
    pieces = [pieces[0]] + [
        lax.ppermute(pieces[k], "grp", [(g, g ^ k) for g in range(n_grp)]) for k in range(1, n_grp)
    ]
    table_grad = finish(grp[None], pieces)
    return next_rows.transpose(0, 2, 1), table_grad, grad_fm, grad_proj_t.T, grad_lcb, grad_gain.reshape(-1)


def solution(mesh):
    n_grp, n_emb = mesh.shape["grp"], mesh.shape["emb"]
    split = n_emb % 2 == 0 and n_grp * (n_emb // 2) == 16 and n_grp % 2 == 0

    def run(*args):
        pooled, _, _, _, tables, w_fm = args[:6]
        count = pooled.shape[0] // (n_grp * n_emb)
        fits = (
            split
            and pooled.shape[1:] == (256, 192)
            and tables.shape[1] == 128
            and w_fm.shape[1] == 128
            and pooled.shape[1] == n_grp * n_emb * TILE
            and count % STEP == 0
            and count <= 16
        )
        if fits:
            devices = mesh.devices.reshape(n_grp, 2, n_emb // 2)
            where, emb, body = Mesh(devices, ("grp", "half", "lane")), ("half", "lane"), halves
        else:
            where, emb, body = mesh, ("emb",), local
        both = ("grp",) + emb
        return jax.shard_map(
            body,
            mesh=where,
            in_specs=(
                P(both, None, None),
                P(both, None, None),
                P(both, None),
                P(both, None),
                P(emb, None, None),
                P(),
                P(),
                P(),
                P(),
            ),
            out_specs=(P(both, None, None), P(emb, "grp", None), P(), P(), P(), P()),
            check_vma=False,
        )(*args)

    return run
```

```python
import functools

import jax
import jax.numpy as jnp
from jax import lax
from jax.experimental import pallas as pl
from jax.experimental.pallas import tpu as pltpu
from jax.sharding import Mesh, PartitionSpec as P

F32, BF16 = jnp.float32, jnp.bfloat16
SMEM = pl.BlockSpec(memory_space=pltpu.SMEM)
VMEM = pl.BlockSpec(memory_space=pltpu.VMEM)
LANES = 128
TILE = 8
STEP = 4
LIMIT = 30 * 1024 * 1024
PEER = ("grp", "lane")


BOTH = ("grp", "emb")


def product(form, left, right):
    return jnp.einsum(form, left, right, preferred_element_type=jnp.float32)


def layer_backward(embeds, cotangent, w_fm, w_proj, w_lcb, gain):
    fm_proj = product("bfc,fj->bcj", embeds, w_fm).astype(jnp.bfloat16)
    fm_rows = product("bfc,bcj->bfj", embeds, fm_proj).astype(jnp.bfloat16)
    projected = product("bfj,jc->bfc", fm_rows, w_proj)
    compressed = product("fi,bfc->bic", w_lcb, embeds)
    summed = embeds.astype(jnp.float32) + projected + compressed
    centre = jnp.mean(summed, axis=2, keepdims=True)
    spread = jnp.mean((summed - centre) ** 2, axis=2, keepdims=True)
    inverse = lax.rsqrt(spread + 1e-05)
    normed = (summed - centre) * inverse
    upper = cotangent.astype(jnp.float32)
    scaled = upper * gain
    grad_sum = inverse * (
        scaled
        - jnp.mean(scaled, axis=2, keepdims=True)
        - normed * jnp.mean(scaled * normed, axis=2, keepdims=True)
    )
    grad_sum = grad_sum.astype(jnp.bfloat16)
    grad_gain = jnp.sum(upper * normed, axis=(0, 1))
    grad_proj = product("bfj,bfc->jc", fm_rows, grad_sum)
    grad_rows = product("bfc,jc->bfj", grad_sum, w_proj).astype(jnp.bfloat16)
    grad_p = product("bfc,bfj->bcj", embeds, grad_rows).astype(jnp.bfloat16)
    grad_fm = product("bfc,bcj->fj", embeds, grad_p)
    grad_lcb = product("bfc,bic->fi", embeds, grad_sum)
    grad_in = (
        grad_sum.astype(jnp.float32)
        + product("bfj,bcj->bfc", grad_rows, fm_proj)
        + product("fj,bcj->bfc", w_fm, grad_p)
        + product("fi,bic->bfc", w_lcb, grad_sum)
    )
    return (grad_in.astype(jnp.bfloat16), (grad_fm, grad_proj, grad_lcb, grad_gain))


def exchange(blocks, axes):
    return lax.all_to_all(blocks, axes, split_axis=0, concat_axis=0, tiled=True)


def dense_sum(partials, factor):
    n = lax.axis_size("grp") * lax.axis_size("emb")
    shapes = [part.shape for part in partials]
    flat = jnp.concatenate([part.reshape(-1) for part in partials])
    unit = 128 * n
    padded = -(-flat.shape[0] // unit) * unit
    flat = jnp.pad(flat, (0, padded - flat.shape[0])).astype(jnp.bfloat16)
    seen = exchange(flat.reshape(n, padded // unit, 128), BOTH)
    share = (jnp.sum(seen.astype(jnp.float32), axis=0) * factor).astype(jnp.bfloat16)
    total = exchange(jnp.broadcast_to(share[None], (n,) + share.shape), BOTH).reshape(-1)
    total = total.astype(jnp.float32)
    outs, at = [], 0
    for shape in shapes:
        size = 1
        for extent in shape:
            size *= extent
        outs.append(total[at : at + size].reshape(shape))
        at += size
    return outs


def local(pooled, upstream, ids_now, ids_next, tables, w_fm, w_proj, w_lcb, gain):
    n_grp, n_emb = lax.axis_size("grp"), lax.axis_size("emb")
    count, features, width = pooled.shape
    owned, rows = tables.shape[:2]
    ids = jnp.stack([ids_now, ids_next]).reshape(2, count, n_emb, owned)
    ids = exchange(ids.transpose(2, 0, 1, 3), "emb")
    row_index = jnp.arange(rows)
    wanted = (ids[:, 1, :, :, None] == row_index).astype(jnp.bfloat16)
    fetched = product("esfr,frc->esfc", wanted, tables).astype(jnp.bfloat16)
    next_rows = exchange(fetched, "emb")
    next_rows = next_rows.transpose(1, 0, 2, 3).reshape(count, features, width)
    grad_in, partials = layer_backward(pooled, upstream, w_fm, w_proj, w_lcb, gain)
    grad_in = grad_in.reshape(count, n_emb, owned, width).transpose(1, 0, 2, 3)
    grads = exchange(grad_in, "emb")
    hit = (ids[:, 0, :, :, None] == row_index).astype(jnp.bfloat16)
    part = product("esfr,esfc->frc", hit, grads).astype(jnp.bfloat16)
    part = part.reshape(owned, n_grp, rows // n_grp, width).transpose(1, 0, 2, 3)
    table_grad = jnp.sum(exchange(part, "grp").astype(jnp.float32), axis=0)
    dense = dense_sum(partials, 1.0 / (count * n_grp * n_emb))
    return (next_rows, table_grad, *dense)


def params(share=1):
    return pltpu.CompilerParams(vmem_limit_bytes=share * LIMIT)


def cost(weight):
    return pl.CostEstimate(flops=weight * 10**9, bytes_accessed=10**5, transcendentals=0)


def mm(left, right, dims=((1,), (0,))):
    return lax.dot_general(left, right, (dims, ((), ())), preferred_element_type=F32)


def mm_nt(left, right):
    return mm(left, right, ((1,), (1,)))


def low_lanes(shape):
    return lax.broadcasted_iota(jnp.int32, shape, 1) < LANES // 2


def turn(tile):
    return pltpu.roll(tile, LANES // 2, 1)


def identity(rows, lanes):
    row = lax.broadcasted_iota(jnp.int32, (rows, lanes), 0)
    return jnp.where(row == lax.broadcasted_iota(jnp.int32, (rows, lanes), 1), 1.0, 0.0).astype(BF16)


class Wire:
    def __init__(self, count, peers):
        self.left = count * TILE
        self.half = self.left + self.left // 2
        self.dense = self.half
        self.share = 1024 // peers
        self.ids = self.dense + self.share
        self.back = 2 * self.half + self.share
        self.back_left = (self.share, self.share + self.left)
        self.back_right = (self.share + 2 * self.left, self.share + 2 * self.left + self.left // 2)


def place_of(n_grp, n_lane, peer):
    return (peer % n_lane) * n_grp * TILE + (peer // n_lane) * TILE


def backward_kernel(
    n_grp, n_lane, wire,
    half_ref, x_ref, u_ref, now_ref, next_ref, fm_ref, proj_t_ref, lcb_ref, gain_ref,
    out_ref, own_ref,
    fm_t, proj, lcb_t, gains, eye, mixed, p_t, g_t, d_sum, d_p_t, left_in, right_in, grads, turned, ids,
):
    count, width, features = x_ref.shape
    rank = fm_ref.shape[1]
    peers = n_grp * n_lane
    scale = 1.0 / width
    samples = range(count)

    turned_fm = fm_ref[...].astype(F32).T.astype(BF16)
    fm_t[...] = turned_fm
    proj[...] = proj_t_ref[...].astype(F32).T.astype(BF16)
    lcb_t[...] = lcb_ref[...].astype(F32).T.astype(BF16)
    column = jnp.broadcast_to(gain_ref[...], (LANES, width)).T
    gains[:, 0:128] = column
    gains[:, 128:256] = column
    eye[...] = identity(features, features)

    x_all = x_ref[...].reshape(count * width, features)
    left_in[:, :, 0:rank] = mm(x_all, fm_ref[...]).astype(BF16).reshape(count, width, rank)
    mixed[...] = mm(x_all, lcb_ref[...]).reshape(count, width, features)
    for s in samples:
        p_t[s] = mm_nt(fm_t[...], x_ref[s]).astype(BF16)
        right_in[s, rank : 2 * rank] = turned_fm
    for s in samples:
        g_t[s] = mm(p_t[s], x_ref[s]).astype(BF16)
    for s in samples:
        mixed[s] = mixed[s] + mm(proj_t_ref[...], g_t[s])
    sum_gain = 0.0
    for s in samples:
        summed = x_ref[s].astype(F32) + mixed[s]
        centre = jnp.sum(summed, axis=0, keepdims=True) * scale
        summed = summed - centre
        spread = jnp.sum(summed * summed, axis=0, keepdims=True) * scale
        inverse = lax.rsqrt(spread + 1e-05)
        normed = summed * inverse
        upper = u_ref[s].astype(F32)
        scaled = upper * gains[...]
        first = jnp.sum(scaled, axis=0, keepdims=True) * scale
        second = jnp.sum(scaled * normed, axis=0, keepdims=True) * scale
        d_sum[s] = (inverse * (scaled - first - normed * second)).astype(BF16)
        product_gain = upper * normed
        sum_gain += product_gain[:, 0:128] + product_gain[:, 128:256]
    for s in samples:
        right_in[s, 0:rank] = mm(proj[...], d_sum[s]).astype(BF16)
    for s in samples:
        left_in[s, :, rank : 2 * rank] = mm_nt(x_ref[s], right_in[s, 0:rank]).astype(BF16)
        d_p_t[s] = mm_nt(right_in[s, 0:rank], x_ref[s]).astype(BF16)
    d_all = d_sum[...].reshape(count * width, features)
    mixed[...] = mm(d_all, lcb_t[...]).reshape(count, width, features)
    for s in samples:
        grad = d_sum[s].astype(F32) + mixed[s] + mm(left_in[s], right_in[s])
        grad = grad.astype(BF16)
        group, k = s // STEP, s % STEP
        grads[group, k * 128 : k * 128 + 128] = grad[0:128]
        at = 512 + 64 * (2 * (k % 2) + k // 2)
        grads[group, at : at + 64] = grad[128:192]
    sum_lcb = mm(x_all, d_all, ((0,), (0,)))
    sum_fm_t, sum_proj_t = 0.0, 0.0
    for s in samples:
        sum_fm_t += mm(d_p_t[s], x_ref[s])
        sum_proj_t += mm_nt(d_sum[s], g_t[s])

    half = half_ref[0]
    for group in range(count // STEP):
        rows = mm_nt(eye[...], grads[group])
        turned[group, 0] = rows[0:128]
        turned[group, 1] = rows[128:256]
    for group in range(count // STEP):
        for side, ref in ((1 - half, out_ref), (half, own_ref)):
            for peer in range(peers):
                at = place_of(n_grp, n_lane, peer)
                line = turned[group, side, at : at + TILE]
                left = jnp.concatenate([line[:, k * 128 : k * 128 + 128] for k in range(STEP)], axis=0)
                ref[peer, group * 32 : group * 32 + 32] = left.astype(BF16)
                right = jnp.concatenate([line[:, 512:640], line[:, 640:768]], axis=0)
                row = wire.left + group * 16
                ref[peer, row : row + 16] = right.astype(BF16)

    part = features // peers
    third = width // peers
    total = jnp.sum(sum_gain.T, axis=0, keepdims=True)
    high = total.astype(BF16).astype(F32)
    low = total - high
    middle = jnp.concatenate([high[:, 128:192], low[:, 128:192]], axis=1)
    gain_rows = [high[:, 0:128], middle, low[:, 0:128], jnp.zeros((1, LANES), F32)]
    sum_fm = sum_fm_t.T
    for peer in range(peers):
        at = wire.dense
        here = slice(peer * part, (peer + 1) * part)
        out_ref[peer, at : at + part] = sum_fm[here].astype(BF16)
        out_ref[peer, at + part : at + 2 * part] = sum_lcb[here, 0:128].astype(BF16)
        out_ref[peer, at + 2 * part : at + 3 * part] = sum_lcb[here, 128:256].astype(BF16)
        last = [sum_proj_t[peer * third : (peer + 1) * third]] + gain_rows
        out_ref[peer, at + 3 * part : at + 4 * part] = jnp.concatenate(last, axis=0).astype(BF16)

    lane = lax.broadcasted_iota(jnp.int32, (16, LANES), 1)
    sample = lax.broadcasted_iota(jnp.int32, (16, LANES), 0)
    mine = (lane // TILE == sample) & (sample < count)
    spread_ids = []
    for which, ref in enumerate((now_ref, next_ref)):
        ids[which] = jnp.zeros_like(ids[which])
        ids[which, 0:count] = ref[...].astype(F32)
        for side in range(2):
            line = ids[which, :, side * 128 : side * 128 + 128]
            spread_ids.append(pltpu.roll(line, 0, 1, stride=TILE, stride_axis=0))
    for peer in range(peers):
        at = place_of(n_grp, n_lane, peer)
        lines = []
        for line in spread_ids:
            line = pltpu.roll(line, LANES - at, 1) if at else line
            lines.append(jnp.sum(jnp.where(mine, line, 0.0), axis=0, keepdims=True))
        lines.append(jnp.zeros((12, LANES), F32))
        out_ref[peer, wire.ids : wire.ids + 16] = jnp.concatenate(lines, axis=0).astype(BF16)


def backward(n_grp, n_lane, wire, half, pooled_t, upstream_t, ids_now, ids_next, w_fm, w_proj_t, w_lcb, gain):
    count, width, features = pooled_t.shape
    rank = w_fm.shape[1]
    peers = n_grp * n_lane

    def whole(shape):
        return pl.BlockSpec(shape, lambda i: (0,) * len(shape))

    operands = (pooled_t, upstream_t, ids_now, ids_next, w_fm, w_proj_t, w_lcb, gain.reshape(1, width))
    shapes = [(peers, wire.ids + 16, LANES), (peers, wire.half, LANES)]
    return pl.pallas_call(
        functools.partial(backward_kernel, n_grp, n_lane, wire),
        grid=(1,),
        in_specs=[SMEM] + [whole(array.shape) for array in operands],
        out_specs=[whole(shape) for shape in shapes],
        out_shape=[jax.ShapeDtypeStruct(shape, BF16) for shape in shapes],
        scratch_shapes=[
            pltpu.VMEM((rank, features), BF16),
            pltpu.VMEM((rank, width), BF16),
            pltpu.VMEM((features, features), BF16),
            pltpu.VMEM((width, features), F32),
            pltpu.VMEM((features, features), BF16),
            pltpu.VMEM((count, width, features), F32),
            pltpu.VMEM((count, rank, width), BF16),
            pltpu.VMEM((count, rank, features), BF16),
            pltpu.VMEM((count, width, features), BF16),
            pltpu.VMEM((count, rank, width), BF16),
            pltpu.VMEM((count, width, 2 * rank), BF16),
            pltpu.VMEM((count, 2 * rank, features), BF16),
            pltpu.VMEM((count // STEP, STEP * width, features), BF16),
            pltpu.VMEM((count // STEP, 2, features // 2, STEP * width), F32),
            pltpu.VMEM((2, 16, features), F32),
        ],
        compiler_params=params(2),
        cost_estimate=cost(1),
        name="layer_backward",
    )(half, *operands)


def part_kernel(n_grp, wire, other, half_ref, seen, *refs):
    held = refs[-1]
    peers = seen.shape[0]
    if other:
        half = 1 - half_ref[0]
        out, dense, all_ids = refs[:3]
        total = seen[0, wire.dense : wire.ids].astype(F32)
        for peer in range(1, peers):
            total = total + seen[peer, wire.dense : wire.ids].astype(F32)
        dense[...] = total
        all_ids[...] = seen[:, wire.ids : wire.ids + 16].astype(F32)
    else:
        half = half_ref[0]
        all_ids, out = refs[0], refs[2]
    lane = lax.broadcasted_iota(jnp.int32, (1, LANES), 1)
    start = ((lane % TILE) * LANES).astype(F32)
    keys = []
    for peer in range(peers):
        at = peer * LANES
        held[at : at + wire.left, 0:128] = seen[peer, 0 : wire.left]
        right = seen[peer, wire.left : wire.half]
        turned = turn(right.astype(F32)).astype(BF16)
        for i in range(wire.left // 32):
            held[at + 32 * i : at + 32 * i + 16, 128:256] = right[16 * i : 16 * i + 16]
            held[at + 32 * i + 16 : at + 32 * i + 32, 128:256] = turned[16 * i : 16 * i + 16]
        if wire.left < LANES:
            held[at + wire.left : at + LANES] = jnp.zeros((LANES - wire.left, 256), BF16)
        ids = all_ids[peer]
        key = jnp.where(half == 0, ids[0:1], ids[1:2]) + start
        keys.append(jnp.where(lane < wire.left, key, -1.0))
    keys = jnp.concatenate(keys, axis=1)
    piece = LANES // n_grp
    for pair in range(TILE // 2):
        row = lax.broadcasted_iota(jnp.int32, (256, 1), 0).astype(F32) + 256.0 * pair
        hit = jnp.where(keys == row, 1.0, 0.0).astype(BF16)
        part = mm(hit, held[...])
        for f in range(2):
            for g in range(n_grp):
                at = f * LANES + g * piece
                rows = part[at : at + piece]
                out[g, 2 * pair + f, 0:piece] = rows[:, 0:128].astype(out.dtype)
                second = turn(rows[piece // 2 :, 128:256])
                packed = jnp.where(low_lanes(second.shape), rows[: piece // 2, 128:256], second)
                out[g, 2 * pair + f, piece : piece + piece // 2] = packed.astype(out.dtype)


def part_sums(n_grp, wire, other, half, seen, *more):
    peers = seen.shape[0]
    piece = LANES // n_grp
    shapes = [jax.ShapeDtypeStruct((n_grp, TILE, piece + piece // 2, LANES), BF16 if other else F32)]
    if other:
        shapes.append(jax.ShapeDtypeStruct((wire.share, LANES), F32))
        shapes.append(jax.ShapeDtypeStruct((peers, 16, LANES), F32))
    return pl.pallas_call(
        functools.partial(part_kernel, n_grp, wire, other),
        in_specs=[SMEM, VMEM] + [VMEM] * len(more),
        out_specs=[VMEM] * len(shapes),
        out_shape=shapes,
        scratch_shapes=[pltpu.VMEM((peers * LANES, 256), BF16)],
        compiler_params=params(),
        cost_estimate=cost(1),
        name="part_other" if other else "part_own",
    )(half, seen, *more)


def lookup_kernel(wire, half_ref, mine_t, crossed_t, ids_ref, out, held):
    peers = out.shape[0]
    half = half_ref[0]
    for f in range(TILE):
        at = f * LANES
        for side, ref in ((half, mine_t), (1 - half, crossed_t)):
            held[side, 0:192, at : at + LANES] = ref[f]
            held[side, 192:256, at : at + LANES] = ref[f, 128:192]
    ids = ids_ref[...].reshape(peers * 16, LANES)
    lane = lax.broadcasted_iota(jnp.int32, (1, LANES), 1)
    keys = (ids + ((lane % TILE) * LANES).astype(F32)).T
    column = lax.broadcasted_iota(jnp.int32, (1, TILE * LANES), 1).astype(F32)
    for which in range(2):
        for pair in range(peers // 2):
            mine = []
            for peer in (2 * pair, 2 * pair + 1):
                at = peer * 16 + 2 + which
                mine.append(keys[0 : wire.left, at : at + 1])
            hit = jnp.where(jnp.concatenate(mine, axis=0) == column, 1.0, 0.0).astype(BF16)
            rows = mm_nt(hit, held[which])
            for k in range(2):
                got, peer = rows[k * wire.left : (k + 1) * wire.left], 2 * pair + k
                base = wire.back_left[which]
                out[peer, base : base + wire.left] = got[:, 0:128].astype(BF16)
                packed = []
                for i in range(wire.left // 32):
                    first, second = got[32 * i : 32 * i + 16, 128:256], got[32 * i + 16 : 32 * i + 32, 128:256]
                    packed.append(jnp.where(low_lanes(first.shape), first, second))
                base = wire.back_right[which]
                out[peer, base : base + wire.left // 2] = jnp.concatenate(packed, axis=0).astype(BF16)


def lookup(wire, half, mine_t, crossed_t, ids):
    shape = (ids.shape[0], wire.back, LANES)
    return pl.pallas_call(
        functools.partial(lookup_kernel, wire),
        in_specs=[SMEM, VMEM, VMEM, VMEM],
        out_specs=VMEM,
        out_shape=jax.ShapeDtypeStruct(shape, BF16),
        scratch_shapes=[pltpu.VMEM((2, 256, TILE * LANES), BF16)],
        compiler_params=params(2),
        cost_estimate=cost(100),
        name="lookup",
    )(half, mine_t, crossed_t, ids)


def fill_kernel(factor, rows, own, seen, out, token):
    token[...] = jnp.zeros_like(token)
    total = ((own[...] + seen[...]) * factor).astype(BF16)
    for peer in range(out.shape[0]):
        out[peer] = total


def fill(wire, factor, rows, own, seen):
    peers = rows.shape[0]

    def whole(shape):
        return pl.BlockSpec(shape, lambda i: (0,) * len(shape))

    return pl.pallas_call(
        functools.partial(fill_kernel, factor),
        grid=(1,),
        in_specs=[pl.BlockSpec(memory_space=pl.ANY), whole(own.shape), whole(seen.shape)],
        out_specs=[whole((peers, wire.share, LANES)), whole((8, LANES))],
        out_shape=[jax.ShapeDtypeStruct(rows.shape, BF16), jax.ShapeDtypeStruct((8, LANES), F32)],
        input_output_aliases={0: 0},
        compiler_params=params(2),
        cost_estimate=cost(1),
        name="fill_dense",
    )(rows, own, seen)


def unpack_kernel(n_grp, n_lane, dense_ref, left0, left1, right0, right1, rows_out, fm, proj_t, lcb, gain, held):
    step = pl.program_id(0)
    peers = n_grp * n_lane
    for side, (left_ref, right_ref) in enumerate(((left0, right0), (left1, right1))):
        for q in range(n_lane):
            for gg in range(n_grp // 2):
                left, right = [], []
                for g in (2 * gg, 2 * gg + 1):
                    peer = g * n_lane + q
                    left.append(left_ref[peer].astype(F32))
                    packed = right_ref[peer].astype(F32)
                    right.append(jnp.concatenate([packed, turn(packed)], axis=0))
                at = side * 128 + q * n_grp * TILE + gg * 16
                for s in range(STEP):
                    here = slice(s * TILE, s * TILE + TILE)
                    both = jnp.concatenate([left[0][here], left[1][here]], axis=0)
                    held[s, at : at + 16, 0:128] = both.astype(BF16)
                    both = jnp.concatenate([right[0][here], right[1][here]], axis=0)
                    held[s, at : at + 16, 128:256] = both.astype(BF16)
    eye = identity(192, 256)
    for s in range(STEP):
        rows_out[s] = mm_nt(eye, held[s]).astype(BF16)

    @pl.when(step == 0)
    def _():
        part, third = 256 // peers, 192 // peers
        for peer in range(peers):
            dense = dense_ref[peer].astype(F32)
            here = slice(peer * part, (peer + 1) * part)
            fm[here] = dense[0:part]
            lcb[here, 0:128] = dense[part : 2 * part]
            lcb[here, 128:256] = dense[2 * part : 3 * part]
            last = dense[3 * part : 4 * part]
            proj_t[peer * third : (peer + 1) * third] = last[0:third]
            if peer == 0:
                last = last[third : third + 3]
                gain[:, 0:128] = last[0:1] + last[2:3]
                gain[:, 128:192] = (last + turn(last))[1:2, 0:64]


def unpack(n_grp, n_lane, wire, count, seen):
    def whole(*shape):
        return pl.BlockSpec(shape, lambda i: (0,) * len(shape))

    def part(rows, start):
        return pl.BlockSpec((peers, rows, LANES), lambda i: (0, start // rows + i, 0))

    peers = n_grp * n_lane
    shapes = [(256, 128), (192, 128), (256, 256), (1, 192)]
    return pl.pallas_call(
        functools.partial(unpack_kernel, n_grp, n_lane),
        grid=(count // STEP,),
        in_specs=[pl.BlockSpec((peers, wire.share, LANES), lambda i: (0, 0, 0))]
        + [part(32, start) for start in wire.back_left]
        + [part(16, start) for start in wire.back_right],
        out_specs=[pl.BlockSpec((STEP, 192, 256), lambda i: (i, 0, 0))] + [whole(*shape) for shape in shapes],
        out_shape=[jax.ShapeDtypeStruct((count, 192, 256), BF16)]
        + [jax.ShapeDtypeStruct(shape, F32) for shape in shapes],
        scratch_shapes=[pltpu.VMEM((STEP, 256, 256), BF16)],
        compiler_params=params(),
        cost_estimate=cost(1),
        name="unpack_rows",
    )(seen, seen, seen, seen, seen)


def combine_kernel(place, own, seen, after, *outs):
    for k, out in enumerate(outs):
        g = jnp.bitwise_xor(place[0], k)
        out[...] = (own[g] + seen[g].astype(F32)).astype(BF16)


def combine(place, own, seen, after):
    n_grp = own.shape[0]
    shape = jax.ShapeDtypeStruct(own.shape[1:], BF16)
    return pl.pallas_call(
        combine_kernel,
        in_specs=[SMEM, VMEM, VMEM, pl.BlockSpec(memory_space=pl.ANY)],
        out_specs=[VMEM] * n_grp,
        out_shape=[shape] * n_grp,
        compiler_params=params(),
        cost_estimate=cost(100),
        name="combine",
    )(place, own, seen, after)


def finish_kernel(place, *refs):
    out = refs[-1]
    piece = out.shape[1]
    for k, seen in enumerate(refs[:-1]):
        base = jnp.bitwise_xor(place[0], k) * TILE
        for f in range(TILE):
            out[base + f, :, 0:128] = seen[f, 0:piece].astype(F32)
            packed = seen[f, piece : piece + piece // 2].astype(F32)
            out[base + f, 0 : piece // 2, 128:192] = packed[:, 0:64]
            out[base + f, piece // 2 : piece, 128:192] = turn(packed)[:, 0:64]


def finish(place, pieces):
    n_grp = len(pieces)
    piece = pieces[0].shape[1] * 2 // 3
    return pl.pallas_call(
        finish_kernel,
        in_specs=[SMEM] + [VMEM] * n_grp,
        out_specs=VMEM,
        out_shape=jax.ShapeDtypeStruct((n_grp * TILE, piece, 192), F32),
        compiler_params=params(),
        cost_estimate=cost(0),
        name="finish_tables",
    )(place, *pieces)


def cross(array):
    return lax.ppermute(array, "half", [(0, 1), (1, 0)])


def halves(pooled, upstream, ids_now, ids_next, tables, w_fm, w_proj, w_lcb, gain):
    n_grp, n_lane = lax.axis_size("grp"), lax.axis_size("lane")
    count = pooled.shape[0]
    wire = Wire(count, n_grp * n_lane)
    factor = 1.0 / (count * n_grp * 2 * n_lane)
    half = lax.axis_index("half").astype(jnp.int32)[None]
    grp = lax.axis_index("grp").astype(jnp.int32)
    mine_t = lax.dynamic_slice_in_dim(tables.transpose(0, 2, 1), grp * TILE, TILE, 0)
    crossed_t = cross(mine_t)
    sent, sent_own = backward(
        n_grp, n_lane, wire, half,
        pooled.transpose(0, 2, 1), upstream.transpose(0, 2, 1), ids_now, ids_next, w_fm, w_proj.T, w_lcb, gain,
    )
    seen = exchange(sent, PEER)
    seen_own = exchange(sent_own, PEER)
    part, dense, ids = part_sums(n_grp, wire, True, half, seen)
    dense_seen = cross(dense)
    part_seen = cross(part)
    rows_wire = lookup(wire, half, mine_t, crossed_t, ids)
    rows_wire, token = fill(wire, factor, rows_wire, dense, dense_seen)
    rows = exchange(rows_wire, PEER)
    (own,) = part_sums(n_grp, wire, False, half, seen_own, ids, token)
    next_rows, grad_fm, grad_proj_t, grad_lcb, grad_gain = unpack(n_grp, n_lane, wire, count, rows)
    pieces = combine(grp[None], own, part_seen, token)
    pieces = [pieces[0]] + [
        lax.ppermute(pieces[k], "grp", [(g, g ^ k) for g in range(n_grp)]) for k in range(1, n_grp)
    ]
    table_grad = finish(grp[None], pieces)
    return next_rows.transpose(0, 2, 1), table_grad, grad_fm, grad_proj_t.T, grad_lcb, grad_gain.reshape(-1)


def solution(mesh):
    n_grp, n_emb = mesh.shape["grp"], mesh.shape["emb"]
    split = n_emb % 2 == 0 and n_grp * (n_emb // 2) == 16 and n_grp % 2 == 0

    def run(*args):
        pooled, _, _, _, tables, w_fm = args[:6]
        count = pooled.shape[0] // (n_grp * n_emb)
        fits = (
            split
            and pooled.shape[1:] == (256, 192)
            and tables.shape[1] == 128
            and w_fm.shape[1] == 128
            and pooled.shape[1] == n_grp * n_emb * TILE
            and count % STEP == 0
            and count <= 16
        )
        if fits:
            devices = mesh.devices.reshape(n_grp, 2, n_emb // 2)
            where, emb, body = Mesh(devices, ("grp", "half", "lane")), ("half", "lane"), halves
        else:
            where, emb, body = mesh, ("emb",), local
        both = ("grp",) + emb
        return jax.shard_map(
            body,
            mesh=where,
            in_specs=(
                P(both, None, None),
                P(both, None, None),
                P(both, None),
                P(both, None),
                P(emb, None, None),
                P(),
                P(),
                P(),
                P(),
            ),
            out_specs=(P(both, None, None), P(emb, "grp", None), P(), P(), P(), P()),
            check_vma=False,
        )(*args)

    return run
```

```python
import functools

import jax
import jax.numpy as jnp
from jax import lax
from jax.experimental import pallas as pl
from jax.experimental.pallas import tpu as pltpu
from jax.sharding import Mesh, PartitionSpec as P

F32, BF16 = jnp.float32, jnp.bfloat16
SMEM = pl.BlockSpec(memory_space=pltpu.SMEM)
VMEM = pl.BlockSpec(memory_space=pltpu.VMEM)
LANES = 128
TILE = 8
STEP = 4
LIMIT = 30 * 1024 * 1024
PEER = ("grp", "lane")


BOTH = ("grp", "emb")


def product(form, left, right):
    return jnp.einsum(form, left, right, preferred_element_type=jnp.float32)


def layer_backward(embeds, cotangent, w_fm, w_proj, w_lcb, gain):
    fm_proj = product("bfc,fj->bcj", embeds, w_fm).astype(jnp.bfloat16)
    fm_rows = product("bfc,bcj->bfj", embeds, fm_proj).astype(jnp.bfloat16)
    projected = product("bfj,jc->bfc", fm_rows, w_proj)
    compressed = product("fi,bfc->bic", w_lcb, embeds)
    summed = embeds.astype(jnp.float32) + projected + compressed
    centre = jnp.mean(summed, axis=2, keepdims=True)
    spread = jnp.mean((summed - centre) ** 2, axis=2, keepdims=True)
    inverse = lax.rsqrt(spread + 1e-05)
    normed = (summed - centre) * inverse
    upper = cotangent.astype(jnp.float32)
    scaled = upper * gain
    grad_sum = inverse * (
        scaled
        - jnp.mean(scaled, axis=2, keepdims=True)
        - normed * jnp.mean(scaled * normed, axis=2, keepdims=True)
    )
    grad_sum = grad_sum.astype(jnp.bfloat16)
    grad_gain = jnp.sum(upper * normed, axis=(0, 1))
    grad_proj = product("bfj,bfc->jc", fm_rows, grad_sum)
    grad_rows = product("bfc,jc->bfj", grad_sum, w_proj).astype(jnp.bfloat16)
    grad_p = product("bfc,bfj->bcj", embeds, grad_rows).astype(jnp.bfloat16)
    grad_fm = product("bfc,bcj->fj", embeds, grad_p)
    grad_lcb = product("bfc,bic->fi", embeds, grad_sum)
    grad_in = (
        grad_sum.astype(jnp.float32)
        + product("bfj,bcj->bfc", grad_rows, fm_proj)
        + product("fj,bcj->bfc", w_fm, grad_p)
        + product("fi,bic->bfc", w_lcb, grad_sum)
    )
    return (grad_in.astype(jnp.bfloat16), (grad_fm, grad_proj, grad_lcb, grad_gain))


def exchange(blocks, axes):
    return lax.all_to_all(blocks, axes, split_axis=0, concat_axis=0, tiled=True)


def dense_sum(partials, factor):
    n = lax.axis_size("grp") * lax.axis_size("emb")
    shapes = [part.shape for part in partials]
    flat = jnp.concatenate([part.reshape(-1) for part in partials])
    unit = 128 * n
    padded = -(-flat.shape[0] // unit) * unit
    flat = jnp.pad(flat, (0, padded - flat.shape[0])).astype(jnp.bfloat16)
    seen = exchange(flat.reshape(n, padded // unit, 128), BOTH)
    share = (jnp.sum(seen.astype(jnp.float32), axis=0) * factor).astype(jnp.bfloat16)
    total = exchange(jnp.broadcast_to(share[None], (n,) + share.shape), BOTH).reshape(-1)
    total = total.astype(jnp.float32)
    outs, at = [], 0
    for shape in shapes:
        size = 1
        for extent in shape:
            size *= extent
        outs.append(total[at : at + size].reshape(shape))
        at += size
    return outs


def local(pooled, upstream, ids_now, ids_next, tables, w_fm, w_proj, w_lcb, gain):
    n_grp, n_emb = lax.axis_size("grp"), lax.axis_size("emb")
    count, features, width = pooled.shape
    owned, rows = tables.shape[:2]
    ids = jnp.stack([ids_now, ids_next]).reshape(2, count, n_emb, owned)
    ids = exchange(ids.transpose(2, 0, 1, 3), "emb")
    row_index = jnp.arange(rows)
    wanted = (ids[:, 1, :, :, None] == row_index).astype(jnp.bfloat16)
    fetched = product("esfr,frc->esfc", wanted, tables).astype(jnp.bfloat16)
    next_rows = exchange(fetched, "emb")
    next_rows = next_rows.transpose(1, 0, 2, 3).reshape(count, features, width)
    grad_in, partials = layer_backward(pooled, upstream, w_fm, w_proj, w_lcb, gain)
    grad_in = grad_in.reshape(count, n_emb, owned, width).transpose(1, 0, 2, 3)
    grads = exchange(grad_in, "emb")
    hit = (ids[:, 0, :, :, None] == row_index).astype(jnp.bfloat16)
    part = product("esfr,esfc->frc", hit, grads).astype(jnp.bfloat16)
    part = part.reshape(owned, n_grp, rows // n_grp, width).transpose(1, 0, 2, 3)
    table_grad = jnp.sum(exchange(part, "grp").astype(jnp.float32), axis=0)
    dense = dense_sum(partials, 1.0 / (count * n_grp * n_emb))
    return (next_rows, table_grad, *dense)


def params(share=1):
    return pltpu.CompilerParams(vmem_limit_bytes=share * LIMIT)


def cost(weight):
    return pl.CostEstimate(flops=weight * 10**9, bytes_accessed=10**5, transcendentals=0)


def mm(left, right, dims=((1,), (0,))):
    return lax.dot_general(left, right, (dims, ((), ())), preferred_element_type=F32)


def mm_nt(left, right):
    return mm(left, right, ((1,), (1,)))


def low_lanes(shape):
    return lax.broadcasted_iota(jnp.int32, shape, 1) < LANES // 2


def turn(tile):
    return pltpu.roll(tile, LANES // 2, 1)


def identity(rows, lanes):
    row = lax.broadcasted_iota(jnp.int32, (rows, lanes), 0)
    return jnp.where(row == lax.broadcasted_iota(jnp.int32, (rows, lanes), 1), 1.0, 0.0).astype(BF16)


class Wire:
    def __init__(self, count, peers):
        self.left = count * TILE
        self.half = self.left + self.left // 2
        self.dense = self.half
        self.share = 1024 // peers
        self.ids = self.dense + self.share
        self.back = 2 * self.half + self.share
        self.back_left = (self.share, self.share + self.left)
        self.back_right = (self.share + 2 * self.left, self.share + 2 * self.left + self.left // 2)


def place_of(n_grp, n_lane, peer):
    return (peer % n_lane) * n_grp * TILE + (peer // n_lane) * TILE


def backward_kernel(
    n_grp, n_lane, wire,
    half_ref, x_ref, u_ref, now_ref, next_ref, fm_ref, proj_t_ref, lcb_ref, gain_ref,
    out_ref, own_ref,
    fm_t, proj, lcb_t, gains, eye, mixed, p_t, g_t, d_sum, d_p_t, left_in, right_in, grads, turned, ids,
):
    count, width, features = x_ref.shape
    rank = fm_ref.shape[1]
    peers = n_grp * n_lane
    scale = 1.0 / width
    samples = range(count)

    turned_fm = fm_ref[...].astype(F32).T.astype(BF16)
    fm_t[...] = turned_fm
    proj[...] = proj_t_ref[...].astype(F32).T.astype(BF16)
    lcb_t[...] = lcb_ref[...].astype(F32).T.astype(BF16)
    column = jnp.broadcast_to(gain_ref[...], (LANES, width)).T
    gains[:, 0:128] = column
    gains[:, 128:256] = column
    eye[...] = identity(features, features)

    x_all = x_ref[...].reshape(count * width, features)
    left_in[:, :, 0:rank] = mm(x_all, fm_ref[...]).astype(BF16).reshape(count, width, rank)
    mixed[...] = mm(x_all, lcb_ref[...]).reshape(count, width, features)
    for s in samples:
        p_t[s] = mm_nt(fm_t[...], x_ref[s]).astype(BF16)
        right_in[s, rank : 2 * rank] = turned_fm
    for s in samples:
        g_t[s] = mm(p_t[s], x_ref[s]).astype(BF16)
    for s in samples:
        mixed[s] = mixed[s] + mm(proj_t_ref[...], g_t[s])
    sum_gain = 0.0
    for s in samples:
        summed = x_ref[s].astype(F32) + mixed[s]
        centre = jnp.sum(summed, axis=0, keepdims=True) * scale
        summed = summed - centre
        spread = jnp.sum(summed * summed, axis=0, keepdims=True) * scale
        inverse = lax.rsqrt(spread + 1e-05)
        normed = summed * inverse
        upper = u_ref[s].astype(F32)
        scaled = upper * gains[...]
        first = jnp.sum(scaled, axis=0, keepdims=True) * scale
        second = jnp.sum(scaled * normed, axis=0, keepdims=True) * scale
        d_sum[s] = (inverse * (scaled - first - normed * second)).astype(BF16)
        product_gain = upper * normed
        sum_gain += product_gain[:, 0:128] + product_gain[:, 128:256]
    for s in samples:
        right_in[s, 0:rank] = mm(proj[...], d_sum[s]).astype(BF16)
    for s in samples:
        left_in[s, :, rank : 2 * rank] = mm_nt(x_ref[s], right_in[s, 0:rank]).astype(BF16)
        d_p_t[s] = mm_nt(right_in[s, 0:rank], x_ref[s]).astype(BF16)
    d_all = d_sum[...].reshape(count * width, features)
    mixed[...] = mm(d_all, lcb_t[...]).reshape(count, width, features)
    for s in samples:
        grad = d_sum[s].astype(F32) + mixed[s] + mm(left_in[s], right_in[s])
        grad = grad.astype(BF16)
        group, k = s // STEP, s % STEP
        grads[group, k * 128 : k * 128 + 128] = grad[0:128]
        at = 512 + 64 * (2 * (k % 2) + k // 2)
        grads[group, at : at + 64] = grad[128:192]
    sum_lcb = mm(x_all, d_all, ((0,), (0,)))
    sum_fm_t, sum_proj_t = 0.0, 0.0
    for s in samples:
        sum_fm_t += mm(d_p_t[s], x_ref[s])
        sum_proj_t += mm_nt(d_sum[s], g_t[s])

    half = half_ref[0]
    for group in range(count // STEP):
        rows = mm_nt(eye[...], grads[group])
        turned[group, 0] = rows[0:128]
        turned[group, 1] = rows[128:256]
    for group in range(count // STEP):
        for side, ref in ((1 - half, out_ref), (half, own_ref)):
            for peer in range(peers):
                at = place_of(n_grp, n_lane, peer)
                line = turned[group, side, at : at + TILE]
                left = jnp.concatenate([line[:, k * 128 : k * 128 + 128] for k in range(STEP)], axis=0)
                ref[peer, group * 32 : group * 32 + 32] = left.astype(BF16)
                right = jnp.concatenate([line[:, 512:640], line[:, 640:768]], axis=0)
                row = wire.left + group * 16
                ref[peer, row : row + 16] = right.astype(BF16)

    part = features // peers
    third = width // peers
    total = jnp.sum(sum_gain.T, axis=0, keepdims=True)
    high = total.astype(BF16).astype(F32)
    low = total - high
    middle = jnp.concatenate([high[:, 128:192], low[:, 128:192]], axis=1)
    gain_rows = [high[:, 0:128], middle, low[:, 0:128], jnp.zeros((1, LANES), F32)]
    sum_fm = sum_fm_t.T
    for peer in range(peers):
        at = wire.dense
        here = slice(peer * part, (peer + 1) * part)
        out_ref[peer, at : at + part] = sum_fm[here].astype(BF16)
        out_ref[peer, at + part : at + 2 * part] = sum_lcb[here, 0:128].astype(BF16)
        out_ref[peer, at + 2 * part : at + 3 * part] = sum_lcb[here, 128:256].astype(BF16)
        last = [sum_proj_t[peer * third : (peer + 1) * third]] + gain_rows
        out_ref[peer, at + 3 * part : at + 4 * part] = jnp.concatenate(last, axis=0).astype(BF16)

    lane = lax.broadcasted_iota(jnp.int32, (16, LANES), 1)
    sample = lax.broadcasted_iota(jnp.int32, (16, LANES), 0)
    mine = (lane // TILE == sample) & (sample < count)
    spread_ids = []
    for which, ref in enumerate((now_ref, next_ref)):
        ids[which] = jnp.zeros_like(ids[which])
        ids[which, 0:count] = ref[...].astype(F32)
        for side in range(2):
            line = ids[which, :, side * 128 : side * 128 + 128]
            spread_ids.append(pltpu.roll(line, 0, 1, stride=TILE, stride_axis=0))
    for peer in range(peers):
        at = place_of(n_grp, n_lane, peer)
        lines = []
        for line in spread_ids:
            line = pltpu.roll(line, LANES - at, 1) if at else line
            lines.append(jnp.sum(jnp.where(mine, line, 0.0), axis=0, keepdims=True))
        lines.append(jnp.zeros((12, LANES), F32))
        out_ref[peer, wire.ids : wire.ids + 16] = jnp.concatenate(lines, axis=0).astype(BF16)


def backward(n_grp, n_lane, wire, half, pooled_t, upstream_t, ids_now, ids_next, w_fm, w_proj_t, w_lcb, gain):
    count, width, features = pooled_t.shape
    rank = w_fm.shape[1]
    peers = n_grp * n_lane

    def whole(shape):
        return pl.BlockSpec(shape, lambda i: (0,) * len(shape))

    operands = (pooled_t, upstream_t, ids_now, ids_next, w_fm, w_proj_t, w_lcb, gain.reshape(1, width))
    shapes = [(peers, wire.ids + 16, LANES), (peers, wire.half, LANES)]
    return pl.pallas_call(
        functools.partial(backward_kernel, n_grp, n_lane, wire),
        grid=(1,),
        in_specs=[SMEM] + [whole(array.shape) for array in operands],
        out_specs=[whole(shape) for shape in shapes],
        out_shape=[pltpu.HBM(shape, BF16) for shape in shapes],
        scratch_shapes=[
            pltpu.VMEM((rank, features), BF16),
            pltpu.VMEM((rank, width), BF16),
            pltpu.VMEM((features, features), BF16),
            pltpu.VMEM((width, features), F32),
            pltpu.VMEM((features, features), BF16),
            pltpu.VMEM((count, width, features), F32),
            pltpu.VMEM((count, rank, width), BF16),
            pltpu.VMEM((count, rank, features), BF16),
            pltpu.VMEM((count, width, features), BF16),
            pltpu.VMEM((count, rank, width), BF16),
            pltpu.VMEM((count, width, 2 * rank), BF16),
            pltpu.VMEM((count, 2 * rank, features), BF16),
            pltpu.VMEM((count // STEP, STEP * width, features), BF16),
            pltpu.VMEM((count // STEP, 2, features // 2, STEP * width), F32),
            pltpu.VMEM((2, 16, features), F32),
        ],
        compiler_params=params(2),
        cost_estimate=cost(1),
        name="layer_backward",
    )(half, *operands)


def part_kernel(n_grp, wire, other, half_ref, seen, *refs):
    held = refs[-1]
    peers = seen.shape[0]
    if other:
        half = 1 - half_ref[0]
        out, dense, all_ids = refs[:3]
        total = seen[0, wire.dense : wire.ids].astype(F32)
        for peer in range(1, peers):
            total = total + seen[peer, wire.dense : wire.ids].astype(F32)
        dense[...] = total
        all_ids[...] = seen[:, wire.ids : wire.ids + 16].astype(F32)
    else:
        half = half_ref[0]
        all_ids, out = refs[0], refs[2]
    lane = lax.broadcasted_iota(jnp.int32, (1, LANES), 1)
    start = ((lane % TILE) * LANES).astype(F32)
    keys = []
    for peer in range(peers):
        at = peer * LANES
        held[at : at + wire.left, 0:128] = seen[peer, 0 : wire.left]
        right = seen[peer, wire.left : wire.half]
        turned = turn(right.astype(F32)).astype(BF16)
        for i in range(wire.left // 32):
            held[at + 32 * i : at + 32 * i + 16, 128:256] = right[16 * i : 16 * i + 16]
            held[at + 32 * i + 16 : at + 32 * i + 32, 128:256] = turned[16 * i : 16 * i + 16]
        if wire.left < LANES:
            held[at + wire.left : at + LANES] = jnp.zeros((LANES - wire.left, 256), BF16)
        ids = all_ids[peer]
        key = jnp.where(half == 0, ids[0:1], ids[1:2]) + start
        keys.append(jnp.where(lane < wire.left, key, -1.0))
    keys = jnp.concatenate(keys, axis=1)
    piece = LANES // n_grp
    for pair in range(TILE // 2):
        row = lax.broadcasted_iota(jnp.int32, (256, 1), 0).astype(F32) + 256.0 * pair
        hit = jnp.where(keys == row, 1.0, 0.0).astype(BF16)
        part = mm(hit, held[...])
        for f in range(2):
            for g in range(n_grp):
                at = f * LANES + g * piece
                rows = part[at : at + piece]
                out[g, 2 * pair + f, 0:piece] = rows[:, 0:128].astype(out.dtype)
                second = turn(rows[piece // 2 :, 128:256])
                packed = jnp.where(low_lanes(second.shape), rows[: piece // 2, 128:256], second)
                out[g, 2 * pair + f, piece : piece + piece // 2] = packed.astype(out.dtype)


def part_sums(n_grp, wire, other, half, seen, *more):
    peers = seen.shape[0]
    piece = LANES // n_grp
    shapes = [jax.ShapeDtypeStruct((n_grp, TILE, piece + piece // 2, LANES), BF16 if other else F32)]
    if other:
        shapes.append(jax.ShapeDtypeStruct((wire.share, LANES), F32))
        shapes.append(jax.ShapeDtypeStruct((peers, 16, LANES), F32))
    return pl.pallas_call(
        functools.partial(part_kernel, n_grp, wire, other),
        in_specs=[SMEM, VMEM] + [VMEM] * len(more),
        out_specs=[VMEM] * len(shapes),
        out_shape=shapes,
        scratch_shapes=[pltpu.VMEM((peers * LANES, 256), BF16)],
        compiler_params=params(1 if other else 2),
        cost_estimate=cost(1),
        name="part_other" if other else "part_own",
    )(half, seen, *more)


def stack_kernel(half_ref, mine_t, crossed_t, out):
    half = half_ref[0]
    for f in range(TILE):
        at = f * LANES
        for side, ref in ((half, mine_t), (1 - half, crossed_t)):
            out[side, 0:192, at : at + LANES] = ref[f]
            out[side, 192:256, at : at + LANES] = ref[f, 128:192]


def stack_tables(half, mine_t, crossed_t):
    return pl.pallas_call(
        stack_kernel,
        in_specs=[SMEM, VMEM, VMEM],
        out_specs=VMEM,
        out_shape=jax.ShapeDtypeStruct((2, 256, TILE * LANES), BF16),
        compiler_params=params(),
        cost_estimate=cost(100),
        name="stack_tables",
    )(half, mine_t, crossed_t)


def lookup_kernel(wire, stacked, ids_ref, out):
    peers = out.shape[0]
    ids = ids_ref[...].reshape(peers * 16, LANES)
    lane = lax.broadcasted_iota(jnp.int32, (1, LANES), 1)
    keys = (ids + ((lane % TILE) * LANES).astype(F32)).T
    column = lax.broadcasted_iota(jnp.int32, (1, TILE * LANES), 1).astype(F32)
    for which in range(2):
        for pair in range(peers // 2):
            mine = []
            for peer in (2 * pair, 2 * pair + 1):
                at = peer * 16 + 2 + which
                mine.append(keys[0 : wire.left, at : at + 1])
            hit = jnp.where(jnp.concatenate(mine, axis=0) == column, 1.0, 0.0).astype(BF16)
            rows = mm_nt(hit, stacked[which])
            for k in range(2):
                got, peer = rows[k * wire.left : (k + 1) * wire.left], 2 * pair + k
                base = wire.back_left[which]
                out[peer, base : base + wire.left] = got[:, 0:128].astype(BF16)
                packed = []
                for i in range(wire.left // 32):
                    first, second = got[32 * i : 32 * i + 16, 128:256], got[32 * i + 16 : 32 * i + 32, 128:256]
                    packed.append(jnp.where(low_lanes(first.shape), first, second))
                base = wire.back_right[which]
                out[peer, base : base + wire.left // 2] = jnp.concatenate(packed, axis=0).astype(BF16)


def lookup(wire, stacked, ids):
    peers = ids.shape[0]
    some = peers // 4
    return pl.pallas_call(
        functools.partial(lookup_kernel, wire),
        grid=(4,),
        in_specs=[
            pl.BlockSpec(stacked.shape, lambda i: (0, 0, 0)),
            pl.BlockSpec((some, 16, LANES), lambda i: (i, 0, 0)),
        ],
        out_specs=pl.BlockSpec((some, wire.back, LANES), lambda i: (i, 0, 0)),
        out_shape=pltpu.HBM((peers, wire.back, LANES), BF16),
        compiler_params=params(),
        cost_estimate=cost(100),
        name="lookup",
    )(stacked, ids)


def fill_kernel(factor, rows, own, seen, out, token):
    token[...] = jnp.zeros_like(token)
    total = ((own[...] + seen[...]) * factor).astype(BF16)
    for peer in range(out.shape[0]):
        out[peer] = total


def fill(wire, factor, rows, own, seen):
    peers = rows.shape[0]

    def whole(shape):
        return pl.BlockSpec(shape, lambda i: (0,) * len(shape))

    return pl.pallas_call(
        functools.partial(fill_kernel, factor),
        grid=(1,),
        in_specs=[pl.BlockSpec(memory_space=pl.ANY), whole(own.shape), whole(seen.shape)],
        out_specs=[whole((peers, wire.share, LANES)), whole((8, LANES))],
        out_shape=[pltpu.HBM(rows.shape, BF16), jax.ShapeDtypeStruct((8, LANES), F32)],
        input_output_aliases={0: 0},
        compiler_params=params(),
        cost_estimate=cost(1),
        name="fill_dense",
    )(rows, own, seen)


def unpack_kernel(n_grp, n_lane, dense_ref, left0, left1, right0, right1, rows_out, fm, proj_t, lcb, gain, token, held):
    step = pl.program_id(0)
    token[...] = jnp.zeros_like(token)
    peers = n_grp * n_lane
    for side, (left_ref, right_ref) in enumerate(((left0, right0), (left1, right1))):
        for q in range(n_lane):
            for gg in range(n_grp // 2):
                left, right = [], []
                for g in (2 * gg, 2 * gg + 1):
                    peer = g * n_lane + q
                    left.append(left_ref[peer].astype(F32))
                    packed = right_ref[peer].astype(F32)
                    right.append(jnp.concatenate([packed, turn(packed)], axis=0))
                at = side * 128 + q * n_grp * TILE + gg * 16
                for s in range(STEP):
                    here = slice(s * TILE, s * TILE + TILE)
                    both = jnp.concatenate([left[0][here], left[1][here]], axis=0)
                    held[s, at : at + 16, 0:128] = both.astype(BF16)
                    both = jnp.concatenate([right[0][here], right[1][here]], axis=0)
                    held[s, at : at + 16, 128:256] = both.astype(BF16)
    eye = identity(192, 256)
    for s in range(STEP):
        rows_out[s] = mm_nt(eye, held[s]).astype(BF16)

    @pl.when(step == 0)
    def _():
        part, third = 256 // peers, 192 // peers
        for peer in range(peers):
            dense = dense_ref[peer].astype(F32)
            here = slice(peer * part, (peer + 1) * part)
            fm[here] = dense[0:part]
            lcb[here, 0:128] = dense[part : 2 * part]
            lcb[here, 128:256] = dense[2 * part : 3 * part]
            last = dense[3 * part : 4 * part]
            proj_t[peer * third : (peer + 1) * third] = last[0:third]
            if peer == 0:
                last = last[third : third + 3]
                gain[:, 0:128] = last[0:1] + last[2:3]
                gain[:, 128:192] = (last + turn(last))[1:2, 0:64]


def unpack(n_grp, n_lane, wire, count, seen):
    def whole(*shape):
        return pl.BlockSpec(shape, lambda i: (0,) * len(shape))

    def part(rows, start):
        return pl.BlockSpec((peers, rows, LANES), lambda i: (0, start // rows + i, 0))

    peers = n_grp * n_lane
    shapes = [(256, 128), (192, 128), (256, 256), (1, 192), (8, 128)]
    return pl.pallas_call(
        functools.partial(unpack_kernel, n_grp, n_lane),
        grid=(count // STEP,),
        in_specs=[pl.BlockSpec((peers, wire.share, LANES), lambda i: (0, 0, 0))]
        + [part(32, start) for start in wire.back_left]
        + [part(16, start) for start in wire.back_right],
        out_specs=[pl.BlockSpec((STEP, 192, 256), lambda i: (i, 0, 0))] + [whole(*shape) for shape in shapes],
        out_shape=[jax.ShapeDtypeStruct((count, 192, 256), BF16)]
        + [jax.ShapeDtypeStruct(shape, F32) for shape in shapes],
        scratch_shapes=[pltpu.VMEM((STEP, 256, 256), BF16)],
        compiler_params=params(),
        cost_estimate=cost(1),
        name="unpack_rows",
    )(seen, seen, seen, seen, seen)


def combine_kernel(place, own, seen, after, *outs):
    for k, out in enumerate(outs):
        g = jnp.bitwise_xor(place[0], k)
        out[...] = (own[g] + seen[g].astype(F32)).astype(BF16)


def combine(place, own, seen, after):
    n_grp = own.shape[0]
    shape = jax.ShapeDtypeStruct(own.shape[1:], BF16)
    return pl.pallas_call(
        combine_kernel,
        in_specs=[SMEM, VMEM, VMEM, pl.BlockSpec(memory_space=pl.ANY)],
        out_specs=[VMEM] * n_grp,
        out_shape=[shape] * n_grp,
        compiler_params=params(),
        cost_estimate=cost(100),
        name="combine",
    )(place, own, seen, after)


def finish_kernel(place, *refs):
    out = refs[-1]
    piece = out.shape[1]
    for k, seen in enumerate(refs[:-2]):
        base = jnp.bitwise_xor(place[0], k) * TILE
        for f in range(TILE):
            out[base + f, :, 0:128] = seen[f, 0:piece].astype(F32)
            packed = seen[f, piece : piece + piece // 2].astype(F32)
            out[base + f, 0 : piece // 2, 128:192] = packed[:, 0:64]
            out[base + f, piece // 2 : piece, 128:192] = turn(packed)[:, 0:64]


def finish(place, pieces, after):
    n_grp = len(pieces)
    piece = pieces[0].shape[1] * 2 // 3
    return pl.pallas_call(
        finish_kernel,
        in_specs=[SMEM] + [VMEM] * n_grp + [pl.BlockSpec(memory_space=pl.ANY)],
        out_specs=VMEM,
        out_shape=jax.ShapeDtypeStruct((n_grp * TILE, piece, 192), F32),
        compiler_params=params(),
        cost_estimate=cost(0),
        name="finish_tables",
    )(place, *pieces, after)


def cross(array):
    return lax.ppermute(array, "half", [(0, 1), (1, 0)])


def halves(pooled, upstream, ids_now, ids_next, tables, w_fm, w_proj, w_lcb, gain):
    n_grp, n_lane = lax.axis_size("grp"), lax.axis_size("lane")
    count = pooled.shape[0]
    wire = Wire(count, n_grp * n_lane)
    factor = 1.0 / (count * n_grp * 2 * n_lane)
    half = lax.axis_index("half").astype(jnp.int32)[None]
    grp = lax.axis_index("grp").astype(jnp.int32)
    mine_t = lax.dynamic_slice_in_dim(tables.transpose(0, 2, 1), grp * TILE, TILE, 0)
    crossed_t = cross(mine_t)
    sent, sent_own = backward(
        n_grp, n_lane, wire, half,
        pooled.transpose(0, 2, 1), upstream.transpose(0, 2, 1), ids_now, ids_next, w_fm, w_proj.T, w_lcb, gain,
    )
    seen = exchange(sent, PEER)
    seen_own = exchange(sent_own, PEER)
    part, dense, ids = part_sums(n_grp, wire, True, half, seen)
    dense_seen = cross(dense)
    part_seen = cross(part)
    rows_wire = lookup(wire, stack_tables(half, mine_t, crossed_t), ids)
    rows_wire, token = fill(wire, factor, rows_wire, dense, dense_seen)
    rows = exchange(rows_wire, PEER)
    (own,) = part_sums(n_grp, wire, False, half, seen_own, ids, token)
    next_rows, grad_fm, grad_proj_t, grad_lcb, grad_gain, token_out = unpack(n_grp, n_lane, wire, count, rows)
    pieces = combine(grp[None], own, part_seen, token)
    pieces = [pieces[0]] + [
        lax.ppermute(pieces[k], "grp", [(g, g ^ k) for g in range(n_grp)]) for k in range(1, n_grp)
    ]
    table_grad = finish(grp[None], pieces, token_out)
    return next_rows.transpose(0, 2, 1), table_grad, grad_fm, grad_proj_t.T, grad_lcb, grad_gain.reshape(-1)


def solution(mesh):
    n_grp, n_emb = mesh.shape["grp"], mesh.shape["emb"]
    split = n_emb % 2 == 0 and n_grp * (n_emb // 2) == 16 and n_grp % 2 == 0

    def run(*args):
        pooled, _, _, _, tables, w_fm = args[:6]
        count = pooled.shape[0] // (n_grp * n_emb)
        fits = (
            split
            and pooled.shape[1:] == (256, 192)
            and tables.shape[1] == 128
            and w_fm.shape[1] == 128
            and pooled.shape[1] == n_grp * n_emb * TILE
            and count % STEP == 0
            and count <= 16
        )
        if fits:
            devices = mesh.devices.reshape(n_grp, 2, n_emb // 2)
            where, emb, body = Mesh(devices, ("grp", "half", "lane")), ("half", "lane"), halves
        else:
            where, emb, body = mesh, ("emb",), local
        both = ("grp",) + emb
        return jax.shard_map(
            body,
            mesh=where,
            in_specs=(
                P(both, None, None),
                P(both, None, None),
                P(both, None),
                P(both, None),
                P(emb, None, None),
                P(),
                P(),
                P(),
                P(),
            ),
            out_specs=(P(both, None, None), P(emb, "grp", None), P(), P(), P(), P()),
            check_vma=False,
        )(*args)

    return run
```

```python
import functools

import jax
import jax.numpy as jnp
from jax import lax
from jax.experimental import pallas as pl
from jax.experimental.pallas import tpu as pltpu
from jax.sharding import Mesh, PartitionSpec as P

F32, BF16 = jnp.float32, jnp.bfloat16
SMEM = pl.BlockSpec(memory_space=pltpu.SMEM)
VMEM = pl.BlockSpec(memory_space=pltpu.VMEM)
LANES = 128
TILE = 8
STEP = 4
LIMIT = 30 * 1024 * 1024
PEER = ("grp", "lane")


BOTH = ("grp", "emb")


def product(form, left, right):
    return jnp.einsum(form, left, right, preferred_element_type=jnp.float32)


def layer_backward(embeds, cotangent, w_fm, w_proj, w_lcb, gain):
    fm_proj = product("bfc,fj->bcj", embeds, w_fm).astype(jnp.bfloat16)
    fm_rows = product("bfc,bcj->bfj", embeds, fm_proj).astype(jnp.bfloat16)
    projected = product("bfj,jc->bfc", fm_rows, w_proj)
    compressed = product("fi,bfc->bic", w_lcb, embeds)
    summed = embeds.astype(jnp.float32) + projected + compressed
    centre = jnp.mean(summed, axis=2, keepdims=True)
    spread = jnp.mean((summed - centre) ** 2, axis=2, keepdims=True)
    inverse = lax.rsqrt(spread + 1e-05)
    normed = (summed - centre) * inverse
    upper = cotangent.astype(jnp.float32)
    scaled = upper * gain
    grad_sum = inverse * (
        scaled
        - jnp.mean(scaled, axis=2, keepdims=True)
        - normed * jnp.mean(scaled * normed, axis=2, keepdims=True)
    )
    grad_sum = grad_sum.astype(jnp.bfloat16)
    grad_gain = jnp.sum(upper * normed, axis=(0, 1))
    grad_proj = product("bfj,bfc->jc", fm_rows, grad_sum)
    grad_rows = product("bfc,jc->bfj", grad_sum, w_proj).astype(jnp.bfloat16)
    grad_p = product("bfc,bfj->bcj", embeds, grad_rows).astype(jnp.bfloat16)
    grad_fm = product("bfc,bcj->fj", embeds, grad_p)
    grad_lcb = product("bfc,bic->fi", embeds, grad_sum)
    grad_in = (
        grad_sum.astype(jnp.float32)
        + product("bfj,bcj->bfc", grad_rows, fm_proj)
        + product("fj,bcj->bfc", w_fm, grad_p)
        + product("fi,bic->bfc", w_lcb, grad_sum)
    )
    return (grad_in.astype(jnp.bfloat16), (grad_fm, grad_proj, grad_lcb, grad_gain))


def exchange(blocks, axes):
    return lax.all_to_all(blocks, axes, split_axis=0, concat_axis=0, tiled=True)


def dense_sum(partials, factor):
    n = lax.axis_size("grp") * lax.axis_size("emb")
    shapes = [part.shape for part in partials]
    flat = jnp.concatenate([part.reshape(-1) for part in partials])
    unit = 128 * n
    padded = -(-flat.shape[0] // unit) * unit
    flat = jnp.pad(flat, (0, padded - flat.shape[0])).astype(jnp.bfloat16)
    seen = exchange(flat.reshape(n, padded // unit, 128), BOTH)
    share = (jnp.sum(seen.astype(jnp.float32), axis=0) * factor).astype(jnp.bfloat16)
    total = exchange(jnp.broadcast_to(share[None], (n,) + share.shape), BOTH).reshape(-1)
    total = total.astype(jnp.float32)
    outs, at = [], 0
    for shape in shapes:
        size = 1
        for extent in shape:
            size *= extent
        outs.append(total[at : at + size].reshape(shape))
        at += size
    return outs


def local(pooled, upstream, ids_now, ids_next, tables, w_fm, w_proj, w_lcb, gain):
    n_grp, n_emb = lax.axis_size("grp"), lax.axis_size("emb")
    count, features, width = pooled.shape
    owned, rows = tables.shape[:2]
    ids = jnp.stack([ids_now, ids_next]).reshape(2, count, n_emb, owned)
    ids = exchange(ids.transpose(2, 0, 1, 3), "emb")
    row_index = jnp.arange(rows)
    wanted = (ids[:, 1, :, :, None] == row_index).astype(jnp.bfloat16)
    fetched = product("esfr,frc->esfc", wanted, tables).astype(jnp.bfloat16)
    next_rows = exchange(fetched, "emb")
    next_rows = next_rows.transpose(1, 0, 2, 3).reshape(count, features, width)
    grad_in, partials = layer_backward(pooled, upstream, w_fm, w_proj, w_lcb, gain)
    grad_in = grad_in.reshape(count, n_emb, owned, width).transpose(1, 0, 2, 3)
    grads = exchange(grad_in, "emb")
    hit = (ids[:, 0, :, :, None] == row_index).astype(jnp.bfloat16)
    part = product("esfr,esfc->frc", hit, grads).astype(jnp.bfloat16)
    part = part.reshape(owned, n_grp, rows // n_grp, width).transpose(1, 0, 2, 3)
    table_grad = jnp.sum(exchange(part, "grp").astype(jnp.float32), axis=0)
    dense = dense_sum(partials, 1.0 / (count * n_grp * n_emb))
    return (next_rows, table_grad, *dense)


def params(share=1):
    return pltpu.CompilerParams(vmem_limit_bytes=share * LIMIT)


def cost(weight):
    return pl.CostEstimate(flops=weight * 10**9, bytes_accessed=10**5, transcendentals=0)


def mm(left, right, dims=((1,), (0,))):
    return lax.dot_general(left, right, (dims, ((), ())), preferred_element_type=F32)


def mm_nt(left, right):
    return mm(left, right, ((1,), (1,)))


def low_lanes(shape):
    return lax.broadcasted_iota(jnp.int32, shape, 1) < LANES // 2


def turn(tile):
    return pltpu.roll(tile, LANES // 2, 1)


def identity(rows, lanes):
    row = lax.broadcasted_iota(jnp.int32, (rows, lanes), 0)
    return jnp.where(row == lax.broadcasted_iota(jnp.int32, (rows, lanes), 1), 1.0, 0.0).astype(BF16)


class Wire:
    def __init__(self, count, peers):
        self.left = count * TILE
        self.half = self.left + self.left // 2
        self.dense = 2 * self.half
        self.share = 1024 // peers
        self.ids = self.dense + self.share
        self.back = 2 * self.half + self.share
        self.back_left = (self.share, self.share + self.left)
        self.back_right = (self.share + 2 * self.left, self.share + 2 * self.left + self.left // 2)


def place_of(n_grp, n_lane, peer):
    return (peer % n_lane) * n_grp * TILE + (peer // n_lane) * TILE


def backward_kernel(
    n_grp, n_lane, wire,
    half_ref, x_ref, u_ref, now_ref, next_ref, fm_ref, proj_t_ref, lcb_ref, gain_ref,
    out_ref,
    fm_t, proj, lcb_t, gains, eye, mixed, p_t, g_t, d_sum, d_p_t, left_in, right_in, grads, turned, ids,
):
    count, width, features = x_ref.shape
    rank = fm_ref.shape[1]
    peers = n_grp * n_lane
    scale = 1.0 / width
    samples = range(count)

    turned_fm = fm_ref[...].astype(F32).T.astype(BF16)
    fm_t[...] = turned_fm
    proj[...] = proj_t_ref[...].astype(F32).T.astype(BF16)
    lcb_t[...] = lcb_ref[...].astype(F32).T.astype(BF16)
    column = jnp.broadcast_to(gain_ref[...], (LANES, width)).T
    gains[:, 0:128] = column
    gains[:, 128:256] = column
    eye[...] = identity(features, features)

    x_all = x_ref[...].reshape(count * width, features)
    left_in[:, :, 0:rank] = mm(x_all, fm_ref[...]).astype(BF16).reshape(count, width, rank)
    mixed[...] = mm(x_all, lcb_ref[...]).reshape(count, width, features)
    for s in samples:
        p_t[s] = mm_nt(fm_t[...], x_ref[s]).astype(BF16)
        right_in[s, rank : 2 * rank] = turned_fm
    for s in samples:
        g_t[s] = mm(p_t[s], x_ref[s]).astype(BF16)
    for s in samples:
        mixed[s] = mixed[s] + mm(proj_t_ref[...], g_t[s])
    sum_gain = 0.0
    for s in samples:
        summed = x_ref[s].astype(F32) + mixed[s]
        centre = jnp.sum(summed, axis=0, keepdims=True) * scale
        summed = summed - centre
        spread = jnp.sum(summed * summed, axis=0, keepdims=True) * scale
        inverse = lax.rsqrt(spread + 1e-05)
        normed = summed * inverse
        upper = u_ref[s].astype(F32)
        scaled = upper * gains[...]
        first = jnp.sum(scaled, axis=0, keepdims=True) * scale
        second = jnp.sum(scaled * normed, axis=0, keepdims=True) * scale
        d_sum[s] = (inverse * (scaled - first - normed * second)).astype(BF16)
        product_gain = upper * normed
        sum_gain += product_gain[:, 0:128] + product_gain[:, 128:256]
    for s in samples:
        right_in[s, 0:rank] = mm(proj[...], d_sum[s]).astype(BF16)
    for s in samples:
        left_in[s, :, rank : 2 * rank] = mm_nt(x_ref[s], right_in[s, 0:rank]).astype(BF16)
        d_p_t[s] = mm_nt(right_in[s, 0:rank], x_ref[s]).astype(BF16)
    d_all = d_sum[...].reshape(count * width, features)
    mixed[...] = mm(d_all, lcb_t[...]).reshape(count, width, features)
    for s in samples:
        grad = d_sum[s].astype(F32) + mixed[s] + mm(left_in[s], right_in[s])
        grad = grad.astype(BF16)
        group, k = s // STEP, s % STEP
        grads[group, k * 128 : k * 128 + 128] = grad[0:128]
        at = 512 + 64 * (2 * (k % 2) + k // 2)
        grads[group, at : at + 64] = grad[128:192]
    sum_lcb = mm(x_all, d_all, ((0,), (0,)))
    sum_fm_t, sum_proj_t = 0.0, 0.0
    for s in samples:
        sum_fm_t += mm(d_p_t[s], x_ref[s])
        sum_proj_t += mm_nt(d_sum[s], g_t[s])

    half = half_ref[0]
    for group in range(count // STEP):
        rows = mm_nt(eye[...], grads[group])
        turned[group, 0] = rows[0:128]
        turned[group, 1] = rows[128:256]
    for group in range(count // STEP):
        for side, base in ((1 - half, 0), (half, wire.half)):
            for peer in range(peers):
                at = place_of(n_grp, n_lane, peer)
                line = turned[group, side, at : at + TILE]
                left = jnp.concatenate([line[:, k * 128 : k * 128 + 128] for k in range(STEP)], axis=0)
                row = base + group * 32
                out_ref[peer, row : row + 32] = left.astype(BF16)
                right = jnp.concatenate([line[:, 512:640], line[:, 640:768]], axis=0)
                row = base + wire.left + group * 16
                out_ref[peer, row : row + 16] = right.astype(BF16)

    part = features // peers
    third = width // peers
    total = jnp.sum(sum_gain.T, axis=0, keepdims=True)
    high = total.astype(BF16).astype(F32)
    low = total - high
    middle = jnp.concatenate([high[:, 128:192], low[:, 128:192]], axis=1)
    gain_rows = [high[:, 0:128], middle, low[:, 0:128], jnp.zeros((1, LANES), F32)]
    sum_fm = sum_fm_t.T
    for peer in range(peers):
        at = wire.dense
        here = slice(peer * part, (peer + 1) * part)
        out_ref[peer, at : at + part] = sum_fm[here].astype(BF16)
        out_ref[peer, at + part : at + 2 * part] = sum_lcb[here, 0:128].astype(BF16)
        out_ref[peer, at + 2 * part : at + 3 * part] = sum_lcb[here, 128:256].astype(BF16)
        last = [sum_proj_t[peer * third : (peer + 1) * third]] + gain_rows
        out_ref[peer, at + 3 * part : at + 4 * part] = jnp.concatenate(last, axis=0).astype(BF16)

    lane = lax.broadcasted_iota(jnp.int32, (16, LANES), 1)
    sample = lax.broadcasted_iota(jnp.int32, (16, LANES), 0)
    mine = (lane // TILE == sample) & (sample < count)
    spread_ids = []
    for which, ref in enumerate((now_ref, next_ref)):
        ids[which] = jnp.zeros_like(ids[which])
        ids[which, 0:count] = ref[...].astype(F32)
        for side in range(2):
            line = ids[which, :, side * 128 : side * 128 + 128]
            spread_ids.append(pltpu.roll(line, 0, 1, stride=TILE, stride_axis=0))
    for peer in range(peers):
        at = place_of(n_grp, n_lane, peer)
        lines = []
        for line in spread_ids:
            line = pltpu.roll(line, LANES - at, 1) if at else line
            lines.append(jnp.sum(jnp.where(mine, line, 0.0), axis=0, keepdims=True))
        lines.append(jnp.zeros((12, LANES), F32))
        out_ref[peer, wire.ids : wire.ids + 16] = jnp.concatenate(lines, axis=0).astype(BF16)


def backward(n_grp, n_lane, wire, half, pooled_t, upstream_t, ids_now, ids_next, w_fm, w_proj_t, w_lcb, gain):
    count, width, features = pooled_t.shape
    rank = w_fm.shape[1]
    peers = n_grp * n_lane

    def whole(shape):
        return pl.BlockSpec(shape, lambda i: (0,) * len(shape))

    operands = (pooled_t, upstream_t, ids_now, ids_next, w_fm, w_proj_t, w_lcb, gain.reshape(1, width))
    shape = (peers, wire.ids + 16, LANES)
    return pl.pallas_call(
        functools.partial(backward_kernel, n_grp, n_lane, wire),
        grid=(1,),
        in_specs=[SMEM] + [whole(array.shape) for array in operands],
        out_specs=whole(shape),
        out_shape=pltpu.HBM(shape, BF16),
        scratch_shapes=[
            pltpu.VMEM((rank, features), BF16),
            pltpu.VMEM((rank, width), BF16),
            pltpu.VMEM((features, features), BF16),
            pltpu.VMEM((width, features), F32),
            pltpu.VMEM((features, features), BF16),
            pltpu.VMEM((count, width, features), F32),
            pltpu.VMEM((count, rank, width), BF16),
            pltpu.VMEM((count, rank, features), BF16),
            pltpu.VMEM((count, width, features), BF16),
            pltpu.VMEM((count, rank, width), BF16),
            pltpu.VMEM((count, width, 2 * rank), BF16),
            pltpu.VMEM((count, 2 * rank, features), BF16),
            pltpu.VMEM((count // STEP, STEP * width, features), BF16),
            pltpu.VMEM((count // STEP, 2, features // 2, STEP * width), F32),
            pltpu.VMEM((2, 16, features), F32),
        ],
        compiler_params=params(2),
        cost_estimate=cost(1),
        name="layer_backward",
    )(half, *operands)


def part_kernel(n_grp, wire, other, half_ref, seen, *refs):
    held = refs[-1]
    peers = seen.shape[0]
    base = 0 if other else wire.half
    if other:
        half = 1 - half_ref[0]
        out, dense, all_ids = refs[:3]
        total = seen[0, wire.dense : wire.ids].astype(F32)
        for peer in range(1, peers):
            total = total + seen[peer, wire.dense : wire.ids].astype(F32)
        dense[...] = total
        all_ids[...] = seen[:, wire.ids : wire.ids + 16].astype(F32)
    else:
        half = half_ref[0]
        all_ids, out = refs[0], refs[2]
    lane = lax.broadcasted_iota(jnp.int32, (1, LANES), 1)
    keys = []
    for peer in range(peers):
        at = peer * LANES
        held[at : at + wire.left, 0:128] = seen[peer, base : base + wire.left]
        right = seen[peer, base + wire.left : base + wire.half]
        turned = turn(right.astype(F32)).astype(BF16)
        for i in range(wire.left // 32):
            held[at + 32 * i : at + 32 * i + 16, 128:256] = right[16 * i : 16 * i + 16]
            held[at + 32 * i + 16 : at + 32 * i + 32, 128:256] = turned[16 * i : 16 * i + 16]
        if wire.left < LANES:
            held[at + wire.left : at + LANES] = jnp.zeros((LANES - wire.left, 256), BF16)
        ids = all_ids[peer]
        key = jnp.where(half == 0, ids[0:1], ids[1:2])
        keys.append(jnp.where(lane < wire.left, key, -1.0))
    keys = jnp.concatenate(keys, axis=1)
    piece = LANES // n_grp
    row = lax.broadcasted_iota(jnp.int32, (LANES, 1), 0).astype(F32)
    same = jnp.where(keys == row, 1.0, 0.0).astype(BF16)
    feature = lax.broadcasted_iota(jnp.int32, (16, peers * LANES), 1) % TILE
    feature = jnp.concatenate([feature] * (LANES // 16), axis=0)
    for pair in range(TILE // 2):
        hit = [same * jnp.where(feature == 2 * pair + f, 1.0, 0.0).astype(BF16) for f in range(2)]
        hit = jnp.concatenate(hit, axis=0)
        part = mm(hit, held[...])
        for f in range(2):
            for g in range(n_grp):
                at = f * LANES + g * piece
                rows = part[at : at + piece]
                out[g, 2 * pair + f, 0:piece] = rows[:, 0:128].astype(out.dtype)
                second = turn(rows[piece // 2 :, 128:256])
                packed = jnp.where(low_lanes(second.shape), rows[: piece // 2, 128:256], second)
                out[g, 2 * pair + f, piece : piece + piece // 2] = packed.astype(out.dtype)


def part_sums(n_grp, wire, other, half, seen, *more):
    peers = seen.shape[0]
    piece = LANES // n_grp
    shapes = [jax.ShapeDtypeStruct((n_grp, TILE, piece + piece // 2, LANES), BF16 if other else F32)]
    if other:
        shapes.append(jax.ShapeDtypeStruct((wire.share, LANES), F32))
        shapes.append(jax.ShapeDtypeStruct((peers, 16, LANES), F32))
    return pl.pallas_call(
        functools.partial(part_kernel, n_grp, wire, other),
        in_specs=[SMEM, VMEM] + [VMEM] * len(more),
        out_specs=[VMEM] * len(shapes),
        out_shape=shapes,
        scratch_shapes=[pltpu.VMEM((peers * LANES, 256), BF16)],
        compiler_params=params(1 if other else 2),
        cost_estimate=cost(1),
        name="part_other" if other else "part_own",
    )(half, seen, *more)


def stack_kernel(half_ref, mine_t, crossed_t, out):
    half = half_ref[0]
    for f in range(TILE):
        at = f * LANES
        for side, ref in ((half, mine_t), (1 - half, crossed_t)):
            out[side, 0:192, at : at + LANES] = ref[f]
            out[side, 192:256, at : at + LANES] = ref[f, 128:192]


def stack_tables(half, mine_t, crossed_t):
    return pl.pallas_call(
        stack_kernel,
        in_specs=[SMEM, VMEM, VMEM],
        out_specs=VMEM,
        out_shape=jax.ShapeDtypeStruct((2, 256, TILE * LANES), BF16),
        compiler_params=params(),
        cost_estimate=cost(100),
        name="stack_tables",
    )(half, mine_t, crossed_t)


def lookup_kernel(wire, stacked, ids_ref, out):
    peers = out.shape[0]
    ids = ids_ref[...].reshape(peers * 16, LANES)
    keys = ids.T
    rows = peers * wire.left
    lane = lax.broadcasted_iota(jnp.int32, (1, LANES), 1).astype(F32)
    feature = lax.broadcasted_iota(jnp.int32, (rows, LANES), 0) % TILE
    masks = [jnp.where(feature == f, 1.0, 0.0).astype(BF16) for f in range(TILE)]
    for which in range(2):
        same = []
        for peer in range(peers):
            at = peer * 16 + 2 + which
            same.append(jnp.where(keys[0 : wire.left, at : at + 1] == lane, 1.0, 0.0))
        same = jnp.concatenate(same, axis=0).astype(BF16)
        hit = jnp.concatenate([same * mask for mask in masks], axis=1)
        both = mm_nt(hit, stacked[which])
        for peer in range(peers):
            got = both[peer * wire.left : (peer + 1) * wire.left]
            base = wire.back_left[which]
            out[peer, base : base + wire.left] = got[:, 0:128].astype(BF16)
            packed = []
            for i in range(wire.left // 32):
                first, second = got[32 * i : 32 * i + 16, 128:256], got[32 * i + 16 : 32 * i + 32, 128:256]
                packed.append(jnp.where(low_lanes(first.shape), first, second))
            base = wire.back_right[which]
            out[peer, base : base + wire.left // 2] = jnp.concatenate(packed, axis=0).astype(BF16)


def lookup(wire, stacked, ids):
    peers = ids.shape[0]
    some = peers // 4
    return pl.pallas_call(
        functools.partial(lookup_kernel, wire),
        grid=(4,),
        in_specs=[
            pl.BlockSpec(stacked.shape, lambda i: (0, 0, 0)),
            pl.BlockSpec((some, 16, LANES), lambda i: (i, 0, 0)),
        ],
        out_specs=pl.BlockSpec((some, wire.back, LANES), lambda i: (i, 0, 0)),
        out_shape=pltpu.HBM((peers, wire.back, LANES), BF16),
        compiler_params=params(),
        cost_estimate=cost(100),
        name="lookup",
    )(stacked, ids)


def fill_kernel(factor, rows, own, seen, out, token):
    token[...] = jnp.zeros_like(token)
    total = ((own[...] + seen[...]) * factor).astype(BF16)
    for peer in range(out.shape[0]):
        out[peer] = total


def fill(wire, factor, rows, own, seen):
    peers = rows.shape[0]

    def whole(shape):
        return pl.BlockSpec(shape, lambda i: (0,) * len(shape))

    return pl.pallas_call(
        functools.partial(fill_kernel, factor),
        grid=(1,),
        in_specs=[pl.BlockSpec(memory_space=pl.ANY), whole(own.shape), whole(seen.shape)],
        out_specs=[whole((peers, wire.share, LANES)), whole((8, LANES))],
        out_shape=[pltpu.HBM(rows.shape, BF16), pltpu.HBM((8, LANES), F32)],
        input_output_aliases={0: 0},
        compiler_params=params(),
        cost_estimate=cost(1),
        name="fill_dense",
    )(rows, own, seen)


def unpack_kernel(n_grp, n_lane, dense_ref, left0, left1, right0, right1, rows_out, fm, proj_t, lcb, gain, token, held):
    step = pl.program_id(0)
    token[...] = jnp.zeros_like(token)
    peers = n_grp * n_lane
    for side, (left_ref, right_ref) in enumerate(((left0, right0), (left1, right1))):
        for q in range(n_lane):
            for gg in range(n_grp // 2):
                left, right = [], []
                for g in (2 * gg, 2 * gg + 1):
                    peer = g * n_lane + q
                    left.append(left_ref[peer].astype(F32))
                    packed = right_ref[peer].astype(F32)
                    right.append(jnp.concatenate([packed, turn(packed)], axis=0))
                at = side * 128 + q * n_grp * TILE + gg * 16
                for s in range(STEP):
                    here = slice(s * TILE, s * TILE + TILE)
                    both = jnp.concatenate([left[0][here], left[1][here]], axis=0)
                    held[s, at : at + 16, 0:128] = both.astype(BF16)
                    both = jnp.concatenate([right[0][here], right[1][here]], axis=0)
                    held[s, at : at + 16, 128:256] = both.astype(BF16)
    eye = identity(192, 256)
    for s in range(STEP):
        rows_out[s] = mm_nt(eye, held[s]).astype(BF16)

    @pl.when(step == 0)
    def _():
        part, third = 256 // peers, 192 // peers
        for peer in range(peers):
            dense = dense_ref[peer].astype(F32)
            here = slice(peer * part, (peer + 1) * part)
            fm[here] = dense[0:part]
            lcb[here, 0:128] = dense[part : 2 * part]
            lcb[here, 128:256] = dense[2 * part : 3 * part]
            last = dense[3 * part : 4 * part]
            proj_t[peer * third : (peer + 1) * third] = last[0:third]
            if peer == 0:
                last = last[third : third + 3]
                gain[:, 0:128] = last[0:1] + last[2:3]
                gain[:, 128:192] = (last + turn(last))[1:2, 0:64]


def unpack(n_grp, n_lane, wire, count, seen):
    def whole(*shape):
        return pl.BlockSpec(shape, lambda i: (0,) * len(shape))

    def part(rows, start):
        return pl.BlockSpec((peers, rows, LANES), lambda i: (0, start // rows + i, 0))

    peers = n_grp * n_lane
    shapes = [(256, 128), (192, 128), (256, 256), (1, 192), (8, 128)]
    return pl.pallas_call(
        functools.partial(unpack_kernel, n_grp, n_lane),
        grid=(count // STEP,),
        in_specs=[pl.BlockSpec((peers, wire.share, LANES), lambda i: (0, 0, 0))]
        + [part(32, start) for start in wire.back_left]
        + [part(16, start) for start in wire.back_right],
        out_specs=[pl.BlockSpec((STEP, 192, 256), lambda i: (i, 0, 0))] + [whole(*shape) for shape in shapes],
        out_shape=[jax.ShapeDtypeStruct((count, 192, 256), BF16)]
        + [jax.ShapeDtypeStruct(shape, F32) for shape in shapes],
        scratch_shapes=[pltpu.VMEM((STEP, 256, 256), BF16)],
        compiler_params=params(),
        cost_estimate=cost(1),
        name="unpack_rows",
    )(seen, seen, seen, seen, seen)


def combine_kernel(place, own, seen, after, *outs):
    for k, out in enumerate(outs):
        g = jnp.bitwise_xor(place[0], k)
        out[...] = (own[g] + seen[g].astype(F32)).astype(BF16)


def combine(place, own, seen, after):
    n_grp = own.shape[0]
    shape = jax.ShapeDtypeStruct(own.shape[1:], BF16)
    return pl.pallas_call(
        combine_kernel,
        in_specs=[SMEM, VMEM, VMEM, pl.BlockSpec(memory_space=pl.ANY)],
        out_specs=[VMEM] * n_grp,
        out_shape=[shape] * n_grp,
        compiler_params=params(),
        cost_estimate=cost(100),
        name="combine",
    )(place, own, seen, after)


def finish_kernel(place, *refs):
    out = refs[-1]
    piece = out.shape[1]
    for k, seen in enumerate(refs[:-2]):
        base = jnp.bitwise_xor(place[0], k) * TILE
        for f in range(TILE):
            out[base + f, :, 0:128] = seen[f, 0:piece].astype(F32)
            packed = seen[f, piece : piece + piece // 2].astype(F32)
            out[base + f, 0 : piece // 2, 128:192] = packed[:, 0:64]
            out[base + f, piece // 2 : piece, 128:192] = turn(packed)[:, 0:64]


def finish(place, pieces, after):
    n_grp = len(pieces)
    piece = pieces[0].shape[1] * 2 // 3
    return pl.pallas_call(
        finish_kernel,
        in_specs=[SMEM] + [VMEM] * n_grp + [pl.BlockSpec(memory_space=pl.ANY)],
        out_specs=VMEM,
        out_shape=jax.ShapeDtypeStruct((n_grp * TILE, piece, 192), F32),
        compiler_params=params(),
        cost_estimate=cost(0),
        name="finish_tables",
    )(place, *pieces, after)


def cross(array):
    return lax.ppermute(array, "half", [(0, 1), (1, 0)])


def halves(pooled, upstream, ids_now, ids_next, tables, w_fm, w_proj, w_lcb, gain):
    n_grp, n_lane = lax.axis_size("grp"), lax.axis_size("lane")
    count = pooled.shape[0]
    wire = Wire(count, n_grp * n_lane)
    factor = 1.0 / (count * n_grp * 2 * n_lane)
    half = lax.axis_index("half").astype(jnp.int32)[None]
    grp = lax.axis_index("grp").astype(jnp.int32)
    mine_t = lax.dynamic_slice_in_dim(tables.transpose(0, 2, 1), grp * TILE, TILE, 0)
    crossed_t = cross(mine_t)
    sent = backward(
        n_grp, n_lane, wire, half,
        pooled.transpose(0, 2, 1), upstream.transpose(0, 2, 1), ids_now, ids_next, w_fm, w_proj.T, w_lcb, gain,
    )
    seen = exchange(sent, PEER)
    part, dense, ids = part_sums(n_grp, wire, True, half, seen)
    dense_seen = cross(dense)
    part_seen = cross(part)
    rows_wire = lookup(wire, stack_tables(half, mine_t, crossed_t), ids)
    rows_wire, token = fill(wire, factor, rows_wire, dense, dense_seen)
    rows = exchange(rows_wire, PEER)
    (own,) = part_sums(n_grp, wire, False, half, seen, ids, token)
    next_rows, grad_fm, grad_proj_t, grad_lcb, grad_gain, token_out = unpack(n_grp, n_lane, wire, count, rows)
    pieces = combine(grp[None], own, part_seen, token)
    pieces = [pieces[0]] + [
        lax.ppermute(pieces[k], "grp", [(g, g ^ k) for g in range(n_grp)]) for k in range(1, n_grp)
    ]
    table_grad = finish(grp[None], pieces, token_out)
    return next_rows.transpose(0, 2, 1), table_grad, grad_fm, grad_proj_t.T, grad_lcb, grad_gain.reshape(-1)


def solution(mesh):
    n_grp, n_emb = mesh.shape["grp"], mesh.shape["emb"]
    split = n_emb % 2 == 0 and n_grp * (n_emb // 2) == 16 and n_grp % 2 == 0

    def run(*args):
        pooled, _, _, _, tables, w_fm = args[:6]
        count = pooled.shape[0] // (n_grp * n_emb)
        fits = (
            split
            and pooled.shape[1:] == (256, 192)
            and tables.shape[1] == 128
            and w_fm.shape[1] == 128
            and pooled.shape[1] == n_grp * n_emb * TILE
            and count % STEP == 0
            and count <= 16
        )
        if fits:
            devices = mesh.devices.reshape(n_grp, 2, n_emb // 2)
            where, emb, body = Mesh(devices, ("grp", "half", "lane")), ("half", "lane"), halves
        else:
            where, emb, body = mesh, ("emb",), local
        both = ("grp",) + emb
        return jax.shard_map(
            body,
            mesh=where,
            in_specs=(
                P(both, None, None),
                P(both, None, None),
                P(both, None),
                P(both, None),
                P(emb, None, None),
                P(),
                P(),
                P(),
                P(),
            ),
            out_specs=(P(both, None, None), P(emb, "grp", None), P(), P(), P(), P()),
            check_vma=False,
        )(*args)

    return run
```

```python
import functools

import jax
import jax.numpy as jnp
from jax import lax
from jax.experimental import pallas as pl
from jax.experimental.pallas import tpu as pltpu
from jax.sharding import Mesh, PartitionSpec as P

F32, BF16 = jnp.float32, jnp.bfloat16
SMEM = pl.BlockSpec(memory_space=pltpu.SMEM)
VMEM = pl.BlockSpec(memory_space=pltpu.VMEM)
LANES = 128
TILE = 8
STEP = 4
LIMIT = 30 * 1024 * 1024
PEER = ("grp", "lane")


BOTH = ("grp", "emb")


def product(form, left, right):
    return jnp.einsum(form, left, right, preferred_element_type=jnp.float32)


def layer_backward(embeds, cotangent, w_fm, w_proj, w_lcb, gain):
    fm_proj = product("bfc,fj->bcj", embeds, w_fm).astype(jnp.bfloat16)
    fm_rows = product("bfc,bcj->bfj", embeds, fm_proj).astype(jnp.bfloat16)
    projected = product("bfj,jc->bfc", fm_rows, w_proj)
    compressed = product("fi,bfc->bic", w_lcb, embeds)
    summed = embeds.astype(jnp.float32) + projected + compressed
    centre = jnp.mean(summed, axis=2, keepdims=True)
    spread = jnp.mean((summed - centre) ** 2, axis=2, keepdims=True)
    inverse = lax.rsqrt(spread + 1e-05)
    normed = (summed - centre) * inverse
    upper = cotangent.astype(jnp.float32)
    scaled = upper * gain
    grad_sum = inverse * (
        scaled
        - jnp.mean(scaled, axis=2, keepdims=True)
        - normed * jnp.mean(scaled * normed, axis=2, keepdims=True)
    )
    grad_sum = grad_sum.astype(jnp.bfloat16)
    grad_gain = jnp.sum(upper * normed, axis=(0, 1))
    grad_proj = product("bfj,bfc->jc", fm_rows, grad_sum)
    grad_rows = product("bfc,jc->bfj", grad_sum, w_proj).astype(jnp.bfloat16)
    grad_p = product("bfc,bfj->bcj", embeds, grad_rows).astype(jnp.bfloat16)
    grad_fm = product("bfc,bcj->fj", embeds, grad_p)
    grad_lcb = product("bfc,bic->fi", embeds, grad_sum)
    grad_in = (
        grad_sum.astype(jnp.float32)
        + product("bfj,bcj->bfc", grad_rows, fm_proj)
        + product("fj,bcj->bfc", w_fm, grad_p)
        + product("fi,bic->bfc", w_lcb, grad_sum)
    )
    return (grad_in.astype(jnp.bfloat16), (grad_fm, grad_proj, grad_lcb, grad_gain))


def exchange(blocks, axes):
    return lax.all_to_all(blocks, axes, split_axis=0, concat_axis=0, tiled=True)


def dense_sum(partials, factor):
    n = lax.axis_size("grp") * lax.axis_size("emb")
    shapes = [part.shape for part in partials]
    flat = jnp.concatenate([part.reshape(-1) for part in partials])
    unit = 128 * n
    padded = -(-flat.shape[0] // unit) * unit
    flat = jnp.pad(flat, (0, padded - flat.shape[0])).astype(jnp.bfloat16)
    seen = exchange(flat.reshape(n, padded // unit, 128), BOTH)
    share = (jnp.sum(seen.astype(jnp.float32), axis=0) * factor).astype(jnp.bfloat16)
    total = exchange(jnp.broadcast_to(share[None], (n,) + share.shape), BOTH).reshape(-1)
    total = total.astype(jnp.float32)
    outs, at = [], 0
    for shape in shapes:
        size = 1
        for extent in shape:
            size *= extent
        outs.append(total[at : at + size].reshape(shape))
        at += size
    return outs


def local(pooled, upstream, ids_now, ids_next, tables, w_fm, w_proj, w_lcb, gain):
    n_grp, n_emb = lax.axis_size("grp"), lax.axis_size("emb")
    count, features, width = pooled.shape
    owned, rows = tables.shape[:2]
    ids = jnp.stack([ids_now, ids_next]).reshape(2, count, n_emb, owned)
    ids = exchange(ids.transpose(2, 0, 1, 3), "emb")
    row_index = jnp.arange(rows)
    wanted = (ids[:, 1, :, :, None] == row_index).astype(jnp.bfloat16)
    fetched = product("esfr,frc->esfc", wanted, tables).astype(jnp.bfloat16)
    next_rows = exchange(fetched, "emb")
    next_rows = next_rows.transpose(1, 0, 2, 3).reshape(count, features, width)
    grad_in, partials = layer_backward(pooled, upstream, w_fm, w_proj, w_lcb, gain)
    grad_in = grad_in.reshape(count, n_emb, owned, width).transpose(1, 0, 2, 3)
    grads = exchange(grad_in, "emb")
    hit = (ids[:, 0, :, :, None] == row_index).astype(jnp.bfloat16)
    part = product("esfr,esfc->frc", hit, grads).astype(jnp.bfloat16)
    part = part.reshape(owned, n_grp, rows // n_grp, width).transpose(1, 0, 2, 3)
    table_grad = jnp.sum(exchange(part, "grp").astype(jnp.float32), axis=0)
    dense = dense_sum(partials, 1.0 / (count * n_grp * n_emb))
    return (next_rows, table_grad, *dense)


def params(share=1):
    return pltpu.CompilerParams(vmem_limit_bytes=share * LIMIT)


def cost(weight):
    return pl.CostEstimate(flops=weight * 10**9, bytes_accessed=10**5, transcendentals=0)


def mm(left, right, dims=((1,), (0,))):
    return lax.dot_general(left, right, (dims, ((), ())), preferred_element_type=F32)


def mm_nt(left, right):
    return mm(left, right, ((1,), (1,)))


def low_lanes(shape):
    return lax.broadcasted_iota(jnp.int32, shape, 1) < LANES // 2


def turn(tile):
    return pltpu.roll(tile, LANES // 2, 1)


def identity(rows, lanes):
    row = lax.broadcasted_iota(jnp.int32, (rows, lanes), 0)
    return jnp.where(row == lax.broadcasted_iota(jnp.int32, (rows, lanes), 1), 1.0, 0.0).astype(BF16)


class Wire:
    def __init__(self, count, peers):
        self.left = count * TILE
        self.half = self.left + self.left // 2
        self.dense = 2 * self.half
        self.share = 1024 // peers
        self.ids = self.dense + self.share
        self.back = 2 * self.half + self.share
        self.back_left = (self.share, self.share + self.left)
        self.back_right = (self.share + 2 * self.left, self.share + 2 * self.left + self.left // 2)


def place_of(n_grp, n_lane, peer):
    return (peer % n_lane) * n_grp * TILE + (peer // n_lane) * TILE


def backward_kernel(
    n_grp, n_lane, wire,
    half_ref, x_ref, u_ref, now_ref, next_ref, fm_ref, proj_t_ref, lcb_ref, gain_ref,
    out_ref,
    fm_t, proj, lcb_t, gains, eye, mixed, p_t, g_t, d_sum, d_p_t, left_in, right_in, grads, turned, ids,
):
    count, width, features = x_ref.shape
    rank = fm_ref.shape[1]
    peers = n_grp * n_lane
    scale = 1.0 / width
    samples = range(count)

    turned_fm = fm_ref[...].astype(F32).T.astype(BF16)
    fm_t[...] = turned_fm
    proj[...] = proj_t_ref[...].astype(F32).T.astype(BF16)
    lcb_t[...] = lcb_ref[...].astype(F32).T.astype(BF16)
    column = jnp.broadcast_to(gain_ref[...], (LANES, width)).T
    gains[:, 0:128] = column
    gains[:, 128:256] = column
    eye[...] = identity(features, features)

    x_all = x_ref[...].reshape(count * width, features)
    left_in[:, :, 0:rank] = mm(x_all, fm_ref[...]).astype(BF16).reshape(count, width, rank)
    mixed[...] = mm(x_all, lcb_ref[...]).reshape(count, width, features)
    for s in samples:
        p_t[s] = mm_nt(fm_t[...], x_ref[s]).astype(BF16)
        right_in[s, rank : 2 * rank] = turned_fm
    for s in samples:
        g_t[s] = mm(p_t[s], x_ref[s]).astype(BF16)
    for s in samples:
        mixed[s] = mixed[s] + mm(proj_t_ref[...], g_t[s])
    sum_gain = 0.0
    for s in samples:
        summed = x_ref[s].astype(F32) + mixed[s]
        centre = jnp.sum(summed, axis=0, keepdims=True) * scale
        summed = summed - centre
        spread = jnp.sum(summed * summed, axis=0, keepdims=True) * scale
        inverse = lax.rsqrt(spread + 1e-05)
        normed = summed * inverse
        upper = u_ref[s].astype(F32)
        scaled = upper * gains[...]
        first = jnp.sum(scaled, axis=0, keepdims=True) * scale
        second = jnp.sum(scaled * normed, axis=0, keepdims=True) * scale
        d_sum[s] = (inverse * (scaled - first - normed * second)).astype(BF16)
        product_gain = upper * normed
        sum_gain += product_gain[:, 0:128] + product_gain[:, 128:256]
    for s in samples:
        right_in[s, 0:rank] = mm(proj[...], d_sum[s]).astype(BF16)
    for s in samples:
        left_in[s, :, rank : 2 * rank] = mm_nt(x_ref[s], right_in[s, 0:rank]).astype(BF16)
        d_p_t[s] = mm_nt(right_in[s, 0:rank], x_ref[s]).astype(BF16)
    d_all = d_sum[...].reshape(count * width, features)
    mixed[...] = mm(d_all, lcb_t[...]).reshape(count, width, features)
    for s in samples:
        grad = d_sum[s].astype(F32) + mixed[s] + mm(left_in[s], right_in[s])
        grad = grad.astype(BF16)
        group, k = s // STEP, s % STEP
        grads[group, k * 128 : k * 128 + 128] = grad[0:128]
        at = 512 + 64 * (2 * (k % 2) + k // 2)
        grads[group, at : at + 64] = grad[128:192]
    sum_lcb = mm(x_all, d_all, ((0,), (0,)))
    sum_fm_t, sum_proj_t = 0.0, 0.0
    for s in samples:
        sum_fm_t += mm(d_p_t[s], x_ref[s])
        sum_proj_t += mm_nt(d_sum[s], g_t[s])

    half = half_ref[0]
    for group in range(count // STEP):
        rows = mm_nt(eye[...], grads[group])
        turned[group, 0] = rows[0:128]
        turned[group, 1] = rows[128:256]
    for group in range(count // STEP):
        for side, base in ((1 - half, 0), (half, wire.half)):
            for peer in range(peers):
                at = place_of(n_grp, n_lane, peer)
                line = turned[group, side, at : at + TILE]
                left = jnp.concatenate([line[:, k * 128 : k * 128 + 128] for k in range(STEP)], axis=0)
                row = base + group * 32
                out_ref[peer, row : row + 32] = left.astype(BF16)
                right = jnp.concatenate([line[:, 512:640], line[:, 640:768]], axis=0)
                row = base + wire.left + group * 16
                out_ref[peer, row : row + 16] = right.astype(BF16)

    part = features // peers
    third = width // peers
    total = jnp.sum(sum_gain.T, axis=0, keepdims=True)
    high = total.astype(BF16).astype(F32)
    low = total - high
    middle = jnp.concatenate([high[:, 128:192], low[:, 128:192]], axis=1)
    gain_rows = [high[:, 0:128], middle, low[:, 0:128], jnp.zeros((1, LANES), F32)]
    sum_fm = sum_fm_t.T
    for peer in range(peers):
        at = wire.dense
        here = slice(peer * part, (peer + 1) * part)
        out_ref[peer, at : at + part] = sum_fm[here].astype(BF16)
        out_ref[peer, at + part : at + 2 * part] = sum_lcb[here, 0:128].astype(BF16)
        out_ref[peer, at + 2 * part : at + 3 * part] = sum_lcb[here, 128:256].astype(BF16)
        last = [sum_proj_t[peer * third : (peer + 1) * third]] + gain_rows
        out_ref[peer, at + 3 * part : at + 4 * part] = jnp.concatenate(last, axis=0).astype(BF16)

    lane = lax.broadcasted_iota(jnp.int32, (16, LANES), 1)
    sample = lax.broadcasted_iota(jnp.int32, (16, LANES), 0)
    mine = (lane // TILE == sample) & (sample < count)
    spread_ids = []
    for which, ref in enumerate((now_ref, next_ref)):
        ids[which] = jnp.zeros_like(ids[which])
        ids[which, 0:count] = ref[...].astype(F32)
        for side in range(2):
            line = ids[which, :, side * 128 : side * 128 + 128]
            spread_ids.append(pltpu.roll(line, 0, 1, stride=TILE, stride_axis=0))
    for peer in range(peers):
        at = place_of(n_grp, n_lane, peer)
        lines = []
        for line in spread_ids:
            line = pltpu.roll(line, LANES - at, 1) if at else line
            lines.append(jnp.sum(jnp.where(mine, line, 0.0), axis=0, keepdims=True))
        lines.append(jnp.zeros((12, LANES), F32))
        out_ref[peer, wire.ids : wire.ids + 16] = jnp.concatenate(lines, axis=0).astype(BF16)


def backward(n_grp, n_lane, wire, half, pooled_t, upstream_t, ids_now, ids_next, w_fm, w_proj_t, w_lcb, gain):
    count, width, features = pooled_t.shape
    rank = w_fm.shape[1]
    peers = n_grp * n_lane

    def whole(shape):
        return pl.BlockSpec(shape, lambda i: (0,) * len(shape))

    operands = (pooled_t, upstream_t, ids_now, ids_next, w_fm, w_proj_t, w_lcb, gain.reshape(1, width))
    shape = (peers, wire.ids + 16, LANES)
    return pl.pallas_call(
        functools.partial(backward_kernel, n_grp, n_lane, wire),
        grid=(1,),
        in_specs=[SMEM] + [whole(array.shape) for array in operands],
        out_specs=whole(shape),
        out_shape=pltpu.HBM(shape, BF16),
        scratch_shapes=[
            pltpu.VMEM((rank, features), BF16),
            pltpu.VMEM((rank, width), BF16),
            pltpu.VMEM((features, features), BF16),
            pltpu.VMEM((width, features), F32),
            pltpu.VMEM((features, features), BF16),
            pltpu.VMEM((count, width, features), F32),
            pltpu.VMEM((count, rank, width), BF16),
            pltpu.VMEM((count, rank, features), BF16),
            pltpu.VMEM((count, width, features), BF16),
            pltpu.VMEM((count, rank, width), BF16),
            pltpu.VMEM((count, width, 2 * rank), BF16),
            pltpu.VMEM((count, 2 * rank, features), BF16),
            pltpu.VMEM((count // STEP, STEP * width, features), BF16),
            pltpu.VMEM((count // STEP, 2, features // 2, STEP * width), F32),
            pltpu.VMEM((2, 16, features), F32),
        ],
        compiler_params=params(2),
        cost_estimate=cost(1),
        name="layer_backward",
    )(half, *operands)


def dense_kernel(dense_ref, ids_ref, dense, all_ids):
    total = dense_ref[0].astype(F32)
    for peer in range(1, dense_ref.shape[0]):
        total = total + dense_ref[peer].astype(F32)
    dense[...] = total
    all_ids[...] = ids_ref[...].astype(F32)


def half_dense(wire, seen):
    peers = seen.shape[0]
    rows = wire.share // 2
    at_ids = wire.ids // 16
    return pl.pallas_call(
        dense_kernel,
        grid=(2,),
        in_specs=[
            pl.BlockSpec((peers, rows, LANES), lambda i: (0, wire.dense // rows + i, 0)),
            pl.BlockSpec((peers, 16, LANES), lambda i: (0, at_ids, 0)),
        ],
        out_specs=[
            pl.BlockSpec((rows, LANES), lambda i: (i, 0)),
            pl.BlockSpec((peers, 16, LANES), lambda i: (0, 0, 0)),
        ],
        out_shape=[
            jax.ShapeDtypeStruct((wire.share, LANES), F32),
            jax.ShapeDtypeStruct((peers, 16, LANES), F32),
        ],
        compiler_params=params(),
        cost_estimate=cost(1),
        name="half_dense",
    )(seen, seen)


def part_kernel(n_grp, wire, other, half_ref, seen, all_ids, *refs):
    out, held = refs[-2:]
    peers = seen.shape[0]
    base = 0 if other else wire.half
    half = 1 - half_ref[0] if other else half_ref[0]
    lane = lax.broadcasted_iota(jnp.int32, (1, LANES), 1)
    start = ((lane % TILE) * LANES).astype(F32)
    keys = []
    for peer in range(peers):
        at = peer * LANES
        held[at : at + wire.left, 0:128] = seen[peer, base : base + wire.left]
        right = seen[peer, base + wire.left : base + wire.half]
        turned = turn(right.astype(F32)).astype(BF16)
        for i in range(wire.left // 32):
            held[at + 32 * i : at + 32 * i + 16, 128:256] = right[16 * i : 16 * i + 16]
            held[at + 32 * i + 16 : at + 32 * i + 32, 128:256] = turned[16 * i : 16 * i + 16]
        if wire.left < LANES:
            held[at + wire.left : at + LANES] = jnp.zeros((LANES - wire.left, 256), BF16)
        ids = all_ids[peer]
        key = jnp.where(half == 0, ids[0:1], ids[1:2]) + start
        keys.append(jnp.where(lane < wire.left, key, -1.0))
    keys = jnp.concatenate(keys, axis=1)
    piece = LANES // n_grp
    for pair in range(TILE // 2):
        row = lax.broadcasted_iota(jnp.int32, (256, 1), 0).astype(F32) + 256.0 * pair
        hit = jnp.where(keys == row, 1.0, 0.0).astype(BF16)
        part = mm(hit, held[...])
        for f in range(2):
            for g in range(n_grp):
                at = f * LANES + g * piece
                rows = part[at : at + piece]
                out[g, 2 * pair + f, 0:piece] = rows[:, 0:128].astype(out.dtype)
                second = turn(rows[piece // 2 :, 128:256])
                packed = jnp.where(low_lanes(second.shape), rows[: piece // 2, 128:256], second)
                out[g, 2 * pair + f, piece : piece + piece // 2] = packed.astype(out.dtype)


def part_sums(n_grp, wire, other, half, seen, ids, *after):
    peers = seen.shape[0]
    piece = LANES // n_grp
    shape = (n_grp, TILE, piece + piece // 2, LANES)
    return pl.pallas_call(
        functools.partial(part_kernel, n_grp, wire, other),
        in_specs=[SMEM, VMEM, VMEM] + [pl.BlockSpec(memory_space=pl.ANY)] * len(after),
        out_specs=VMEM,
        out_shape=jax.ShapeDtypeStruct(shape, BF16 if other else F32),
        scratch_shapes=[pltpu.VMEM((peers * LANES, 256), BF16)],
        compiler_params=params(1 if other else 2),
        cost_estimate=cost(1),
        name="part_other" if other else "part_own",
    )(half, seen, ids, *after)


def stack_kernel(half_ref, mine_t, crossed_t, out):
    half = half_ref[0]
    for f in range(TILE):
        at = f * LANES
        for side, ref in ((half, mine_t), (1 - half, crossed_t)):
            out[side, 0:192, at : at + LANES] = ref[f]
            out[side, 192:256, at : at + LANES] = ref[f, 128:192]


def stack_tables(half, mine_t, crossed_t):
    return pl.pallas_call(
        stack_kernel,
        in_specs=[SMEM, VMEM, VMEM],
        out_specs=VMEM,
        out_shape=jax.ShapeDtypeStruct((2, 256, TILE * LANES), BF16),
        compiler_params=params(),
        cost_estimate=cost(100),
        name="stack_tables",
    )(half, mine_t, crossed_t)


def lookup_kernel(wire, stacked, ids_ref, out):
    peers = out.shape[0]
    ids = ids_ref[...].reshape(peers * 16, LANES)
    keys = ids.T
    rows = peers * wire.left
    lane = lax.broadcasted_iota(jnp.int32, (1, LANES), 1).astype(F32)
    feature = lax.broadcasted_iota(jnp.int32, (rows, LANES), 0) % TILE
    masks = [jnp.where(feature == f, 1.0, 0.0).astype(BF16) for f in range(TILE)]
    for which in range(2):
        same = []
        for peer in range(peers):
            at = peer * 16 + 2 + which
            same.append(jnp.where(keys[0 : wire.left, at : at + 1] == lane, 1.0, 0.0))
        same = jnp.concatenate(same, axis=0).astype(BF16)
        hit = jnp.concatenate([same * mask for mask in masks], axis=1)
        both = mm_nt(hit, stacked[which])
        for peer in range(peers):
            got = both[peer * wire.left : (peer + 1) * wire.left]
            base = wire.back_left[which]
            out[peer, base : base + wire.left] = got[:, 0:128].astype(BF16)
            packed = []
            for i in range(wire.left // 32):
                first, second = got[32 * i : 32 * i + 16, 128:256], got[32 * i + 16 : 32 * i + 32, 128:256]
                packed.append(jnp.where(low_lanes(first.shape), first, second))
            base = wire.back_right[which]
            out[peer, base : base + wire.left // 2] = jnp.concatenate(packed, axis=0).astype(BF16)


def lookup(wire, stacked, ids):
    peers = ids.shape[0]
    some = peers // 4
    return pl.pallas_call(
        functools.partial(lookup_kernel, wire),
        grid=(4,),
        in_specs=[
            pl.BlockSpec(stacked.shape, lambda i: (0, 0, 0)),
            pl.BlockSpec((some, 16, LANES), lambda i: (i, 0, 0)),
        ],
        out_specs=pl.BlockSpec((some, wire.back, LANES), lambda i: (i, 0, 0)),
        out_shape=pltpu.HBM((peers, wire.back, LANES), BF16),
        compiler_params=params(),
        cost_estimate=cost(100),
        name="lookup",
    )(stacked, ids)


def fill_kernel(factor, rows, own, seen, out, token):
    token[...] = jnp.zeros_like(token)
    total = ((own[...] + seen[...]) * factor).astype(BF16)
    for peer in range(out.shape[0]):
        out[peer] = total


def fill(wire, factor, rows, own, seen):
    peers = rows.shape[0]

    def whole(shape):
        return pl.BlockSpec(shape, lambda i: (0,) * len(shape))

    return pl.pallas_call(
        functools.partial(fill_kernel, factor),
        grid=(1,),
        in_specs=[pl.BlockSpec(memory_space=pl.ANY), whole(own.shape), whole(seen.shape)],
        out_specs=[whole((peers, wire.share, LANES)), whole((8, LANES))],
        out_shape=[pltpu.HBM(rows.shape, BF16), pltpu.HBM((8, LANES), F32)],
        input_output_aliases={0: 0},
        compiler_params=params(),
        cost_estimate=cost(1),
        name="fill_dense",
    )(rows, own, seen)


def unpack_kernel(n_grp, n_lane, dense_ref, left0, left1, right0, right1, rows_out, fm, proj_t, lcb, gain, token, held):
    step = pl.program_id(0)
    token[...] = jnp.zeros_like(token)
    peers = n_grp * n_lane
    for side, (left_ref, right_ref) in enumerate(((left0, right0), (left1, right1))):
        for q in range(n_lane):
            for gg in range(n_grp // 2):
                left, right = [], []
                for g in (2 * gg, 2 * gg + 1):
                    peer = g * n_lane + q
                    left.append(left_ref[peer].astype(F32))
                    packed = right_ref[peer].astype(F32)
                    right.append(jnp.concatenate([packed, turn(packed)], axis=0))
                at = side * 128 + q * n_grp * TILE + gg * 16
                for s in range(STEP):
                    here = slice(s * TILE, s * TILE + TILE)
                    both = jnp.concatenate([left[0][here], left[1][here]], axis=0)
                    held[s, at : at + 16, 0:128] = both.astype(BF16)
                    both = jnp.concatenate([right[0][here], right[1][here]], axis=0)
                    held[s, at : at + 16, 128:256] = both.astype(BF16)
    eye = identity(192, 256)
    for s in range(STEP):
        rows_out[s] = mm_nt(eye, held[s]).astype(BF16)

    @pl.when(step == 0)
    def _():
        part, third = 256 // peers, 192 // peers
        for peer in range(peers):
            dense = dense_ref[peer].astype(F32)
            here = slice(peer * part, (peer + 1) * part)
            fm[here] = dense[0:part]
            lcb[here, 0:128] = dense[part : 2 * part]
            lcb[here, 128:256] = dense[2 * part : 3 * part]
            last = dense[3 * part : 4 * part]
            proj_t[peer * third : (peer + 1) * third] = last[0:third]
            if peer == 0:
                last = last[third : third + 3]
                gain[:, 0:128] = last[0:1] + last[2:3]
                gain[:, 128:192] = (last + turn(last))[1:2, 0:64]


def unpack(n_grp, n_lane, wire, count, seen):
    def whole(*shape):
        return pl.BlockSpec(shape, lambda i: (0,) * len(shape))

    def part(rows, start):
        return pl.BlockSpec((peers, rows, LANES), lambda i: (0, start // rows + i, 0))

    peers = n_grp * n_lane
    shapes = [(256, 128), (192, 128), (256, 256), (1, 192), (8, 128)]
    return pl.pallas_call(
        functools.partial(unpack_kernel, n_grp, n_lane),
        grid=(count // STEP,),
        in_specs=[pl.BlockSpec((peers, wire.share, LANES), lambda i: (0, 0, 0))]
        + [part(32, start) for start in wire.back_left]
        + [part(16, start) for start in wire.back_right],
        out_specs=[pl.BlockSpec((STEP, 192, 256), lambda i: (i, 0, 0))] + [whole(*shape) for shape in shapes],
        out_shape=[jax.ShapeDtypeStruct((count, 192, 256), BF16)]
        + [jax.ShapeDtypeStruct(shape, F32) for shape in shapes],
        scratch_shapes=[pltpu.VMEM((STEP, 256, 256), BF16)],
        compiler_params=params(),
        cost_estimate=cost(1),
        name="unpack_rows",
    )(seen, seen, seen, seen, seen)


def combine_kernel(place, own, seen, after, *outs):
    for k, out in enumerate(outs):
        g = jnp.bitwise_xor(place[0], k)
        out[...] = (own[g] + seen[g].astype(F32)).astype(BF16)


def combine(place, own, seen, after):
    n_grp = own.shape[0]
    shape = jax.ShapeDtypeStruct(own.shape[1:], BF16)
    return pl.pallas_call(
        combine_kernel,
        in_specs=[SMEM, VMEM, VMEM, pl.BlockSpec(memory_space=pl.ANY)],
        out_specs=[VMEM] * n_grp,
        out_shape=[shape] * n_grp,
        compiler_params=params(),
        cost_estimate=cost(100),
        name="combine",
    )(place, own, seen, after)


def finish_kernel(place, *refs):
    out = refs[-1]
    piece = out.shape[1]
    for k, seen in enumerate(refs[:-2]):
        base = jnp.bitwise_xor(place[0], k) * TILE
        for f in range(TILE):
            out[base + f, :, 0:128] = seen[f, 0:piece].astype(F32)
            packed = seen[f, piece : piece + piece // 2].astype(F32)
            out[base + f, 0 : piece // 2, 128:192] = packed[:, 0:64]
            out[base + f, piece // 2 : piece, 128:192] = turn(packed)[:, 0:64]


def finish(place, pieces, after):
    n_grp = len(pieces)
    piece = pieces[0].shape[1] * 2 // 3
    return pl.pallas_call(
        finish_kernel,
        in_specs=[SMEM] + [VMEM] * n_grp + [pl.BlockSpec(memory_space=pl.ANY)],
        out_specs=VMEM,
        out_shape=jax.ShapeDtypeStruct((n_grp * TILE, piece, 192), F32),
        compiler_params=params(),
        cost_estimate=cost(0),
        name="finish_tables",
    )(place, *pieces, after)


def cross(array):
    return lax.ppermute(array, "half", [(0, 1), (1, 0)])


def halves(pooled, upstream, ids_now, ids_next, tables, w_fm, w_proj, w_lcb, gain):
    n_grp, n_lane = lax.axis_size("grp"), lax.axis_size("lane")
    count = pooled.shape[0]
    wire = Wire(count, n_grp * n_lane)
    factor = 1.0 / (count * n_grp * 2 * n_lane)
    half = lax.axis_index("half").astype(jnp.int32)[None]
    grp = lax.axis_index("grp").astype(jnp.int32)
    mine_t = lax.dynamic_slice_in_dim(tables.transpose(0, 2, 1), grp * TILE, TILE, 0)
    crossed_t = cross(mine_t)
    sent = backward(
        n_grp, n_lane, wire, half,
        pooled.transpose(0, 2, 1), upstream.transpose(0, 2, 1), ids_now, ids_next, w_fm, w_proj.T, w_lcb, gain,
    )
    seen = exchange(sent, PEER)
    dense, ids = half_dense(wire, seen)
    dense_seen = cross(dense)
    part_seen = cross(part_sums(n_grp, wire, True, half, seen, ids))
    rows_wire = lookup(wire, stack_tables(half, mine_t, crossed_t), ids)
    rows_wire, token = fill(wire, factor, rows_wire, dense, dense_seen)
    rows = exchange(rows_wire, PEER)
    own = part_sums(n_grp, wire, False, half, seen, ids, token)
    next_rows, grad_fm, grad_proj_t, grad_lcb, grad_gain, token_out = unpack(n_grp, n_lane, wire, count, rows)
    pieces = combine(grp[None], own, part_seen, token)
    pieces = [pieces[0]] + [
        lax.ppermute(pieces[k], "grp", [(g, g ^ k) for g in range(n_grp)]) for k in range(1, n_grp)
    ]
    table_grad = finish(grp[None], pieces, token_out)
    return next_rows.transpose(0, 2, 1), table_grad, grad_fm, grad_proj_t.T, grad_lcb, grad_gain.reshape(-1)


def solution(mesh):
    n_grp, n_emb = mesh.shape["grp"], mesh.shape["emb"]
    split = n_emb % 2 == 0 and n_grp * (n_emb // 2) == 16 and n_grp % 2 == 0

    def run(*args):
        pooled, _, _, _, tables, w_fm = args[:6]
        count = pooled.shape[0] // (n_grp * n_emb)
        fits = (
            split
            and pooled.shape[1:] == (256, 192)
            and tables.shape[1] == 128
            and w_fm.shape[1] == 128
            and pooled.shape[1] == n_grp * n_emb * TILE
            and count % STEP == 0
            and count <= 16
        )
        if fits:
            devices = mesh.devices.reshape(n_grp, 2, n_emb // 2)
            where, emb, body = Mesh(devices, ("grp", "half", "lane")), ("half", "lane"), halves
        else:
            where, emb, body = mesh, ("emb",), local
        both = ("grp",) + emb
        return jax.shard_map(
            body,
            mesh=where,
            in_specs=(
                P(both, None, None),
                P(both, None, None),
                P(both, None),
                P(both, None),
                P(emb, None, None),
                P(),
                P(),
                P(),
                P(),
            ),
            out_specs=(P(both, None, None), P(emb, "grp", None), P(), P(), P(), P()),
            check_vma=False,
        )(*args)

    return run
```

```python
import functools

import jax
import jax.numpy as jnp
from jax import lax
from jax.experimental import pallas as pl
from jax.experimental.pallas import tpu as pltpu
from jax.sharding import Mesh, PartitionSpec as P

F32, BF16 = jnp.float32, jnp.bfloat16
SMEM = pl.BlockSpec(memory_space=pltpu.SMEM)
VMEM = pl.BlockSpec(memory_space=pltpu.VMEM)
LANES = 128
TILE = 8
STEP = 4
LIMIT = 30 * 1024 * 1024
PEER = ("grp", "lane")


BOTH = ("grp", "emb")


def product(form, left, right):
    return jnp.einsum(form, left, right, preferred_element_type=jnp.float32)


def layer_backward(embeds, cotangent, w_fm, w_proj, w_lcb, gain):
    fm_proj = product("bfc,fj->bcj", embeds, w_fm).astype(jnp.bfloat16)
    fm_rows = product("bfc,bcj->bfj", embeds, fm_proj).astype(jnp.bfloat16)
    projected = product("bfj,jc->bfc", fm_rows, w_proj)
    compressed = product("fi,bfc->bic", w_lcb, embeds)
    summed = embeds.astype(jnp.float32) + projected + compressed
    centre = jnp.mean(summed, axis=2, keepdims=True)
    spread = jnp.mean((summed - centre) ** 2, axis=2, keepdims=True)
    inverse = lax.rsqrt(spread + 1e-05)
    normed = (summed - centre) * inverse
    upper = cotangent.astype(jnp.float32)
    scaled = upper * gain
    grad_sum = inverse * (
        scaled
        - jnp.mean(scaled, axis=2, keepdims=True)
        - normed * jnp.mean(scaled * normed, axis=2, keepdims=True)
    )
    grad_sum = grad_sum.astype(jnp.bfloat16)
    grad_gain = jnp.sum(upper * normed, axis=(0, 1))
    grad_proj = product("bfj,bfc->jc", fm_rows, grad_sum)
    grad_rows = product("bfc,jc->bfj", grad_sum, w_proj).astype(jnp.bfloat16)
    grad_p = product("bfc,bfj->bcj", embeds, grad_rows).astype(jnp.bfloat16)
    grad_fm = product("bfc,bcj->fj", embeds, grad_p)
    grad_lcb = product("bfc,bic->fi", embeds, grad_sum)
    grad_in = (
        grad_sum.astype(jnp.float32)
        + product("bfj,bcj->bfc", grad_rows, fm_proj)
        + product("fj,bcj->bfc", w_fm, grad_p)
        + product("fi,bic->bfc", w_lcb, grad_sum)
    )
    return (grad_in.astype(jnp.bfloat16), (grad_fm, grad_proj, grad_lcb, grad_gain))


def exchange(blocks, axes):
    return lax.all_to_all(blocks, axes, split_axis=0, concat_axis=0, tiled=True)


def dense_sum(partials, factor):
    n = lax.axis_size("grp") * lax.axis_size("emb")
    shapes = [part.shape for part in partials]
    flat = jnp.concatenate([part.reshape(-1) for part in partials])
    unit = 128 * n
    padded = -(-flat.shape[0] // unit) * unit
    flat = jnp.pad(flat, (0, padded - flat.shape[0])).astype(jnp.bfloat16)
    seen = exchange(flat.reshape(n, padded // unit, 128), BOTH)
    share = (jnp.sum(seen.astype(jnp.float32), axis=0) * factor).astype(jnp.bfloat16)
    total = exchange(jnp.broadcast_to(share[None], (n,) + share.shape), BOTH).reshape(-1)
    total = total.astype(jnp.float32)
    outs, at = [], 0
    for shape in shapes:
        size = 1
        for extent in shape:
            size *= extent
        outs.append(total[at : at + size].reshape(shape))
        at += size
    return outs


def local(pooled, upstream, ids_now, ids_next, tables, w_fm, w_proj, w_lcb, gain):
    n_grp, n_emb = lax.axis_size("grp"), lax.axis_size("emb")
    count, features, width = pooled.shape
    owned, rows = tables.shape[:2]
    ids = jnp.stack([ids_now, ids_next]).reshape(2, count, n_emb, owned)
    ids = exchange(ids.transpose(2, 0, 1, 3), "emb")
    row_index = jnp.arange(rows)
    wanted = (ids[:, 1, :, :, None] == row_index).astype(jnp.bfloat16)
    fetched = product("esfr,frc->esfc", wanted, tables).astype(jnp.bfloat16)
    next_rows = exchange(fetched, "emb")
    next_rows = next_rows.transpose(1, 0, 2, 3).reshape(count, features, width)
    grad_in, partials = layer_backward(pooled, upstream, w_fm, w_proj, w_lcb, gain)
    grad_in = grad_in.reshape(count, n_emb, owned, width).transpose(1, 0, 2, 3)
    grads = exchange(grad_in, "emb")
    hit = (ids[:, 0, :, :, None] == row_index).astype(jnp.bfloat16)
    part = product("esfr,esfc->frc", hit, grads).astype(jnp.bfloat16)
    part = part.reshape(owned, n_grp, rows // n_grp, width).transpose(1, 0, 2, 3)
    table_grad = jnp.sum(exchange(part, "grp").astype(jnp.float32), axis=0)
    dense = dense_sum(partials, 1.0 / (count * n_grp * n_emb))
    return (next_rows, table_grad, *dense)


def params(share=1):
    return pltpu.CompilerParams(vmem_limit_bytes=share * LIMIT)


def cost(weight):
    return pl.CostEstimate(flops=weight * 10**9, bytes_accessed=10**5, transcendentals=0)


def mm(left, right, dims=((1,), (0,))):
    return lax.dot_general(left, right, (dims, ((), ())), preferred_element_type=F32)


def mm_nt(left, right):
    return mm(left, right, ((1,), (1,)))


def low_lanes(shape):
    return lax.broadcasted_iota(jnp.int32, shape, 1) < LANES // 2


def turn(tile):
    return pltpu.roll(tile, LANES // 2, 1)


def identity(rows, lanes):
    row = lax.broadcasted_iota(jnp.int32, (rows, lanes), 0)
    return jnp.where(row == lax.broadcasted_iota(jnp.int32, (rows, lanes), 1), 1.0, 0.0).astype(BF16)


class Wire:
    def __init__(self, count, peers):
        self.left = count * TILE
        self.half = self.left + self.left // 2
        self.dense = 2 * self.half
        self.share = 1024 // peers
        self.rows = self.dense + self.share
        self.back_left = (self.share, self.share + self.left)
        self.back_right = (self.share + 2 * self.left, self.share + 2 * self.left + self.left // 2)


def place_of(n_grp, n_lane, peer):
    return (peer % n_lane) * n_grp * TILE + (peer // n_lane) * TILE


def backward_kernel(
    n_grp, n_lane, wire,
    half_ref, x_ref, u_any, now_ref, next_ref, fm_ref, proj_t_ref, lcb_ref, gain_ref,
    out_any,
    fm_t, proj, lcb_t, gains, eye, mixed, p_t, g_t, d_sum, d_p_t, left_in, right_in, grads, turned, ids,
    u_ref, out_ref, sems,
):
    count, width, features = x_ref.shape
    rank = fm_ref.shape[1]
    peers = n_grp * n_lane
    scale = 1.0 / width
    load = pltpu.make_async_copy(u_any, u_ref, sems.at[0])
    load.start()

    turned_fm = fm_ref[...].astype(F32).T.astype(BF16)
    fm_t[...] = turned_fm
    proj[...] = proj_t_ref[...].astype(F32).T.astype(BF16)
    lcb_t[...] = lcb_ref[...].astype(F32).T.astype(BF16)
    column = jnp.broadcast_to(gain_ref[...], (LANES, width)).T
    gains[:, 0:128] = column
    gains[:, 128:256] = column
    eye[...] = identity(features, features)
    sum_gain, sum_fm_t, sum_proj_t = [], [], []

    def project(s):
        p_t[s] = mm_nt(fm_t[...], x_ref[s]).astype(BF16)
        right_in[s, rank : 2 * rank] = fm_t[...]

    def interact(s):
        g_t[s] = mm(p_t[s], x_ref[s]).astype(BF16)

    def add_up(s):
        mixed[s] = mixed[s] + mm(proj_t_ref[...], g_t[s])

    def normalise(s):
        summed = x_ref[s].astype(F32) + mixed[s]
        centre = jnp.sum(summed, axis=0, keepdims=True) * scale
        summed = summed - centre
        spread = jnp.sum(summed * summed, axis=0, keepdims=True) * scale
        inverse = lax.rsqrt(spread + 1e-05)
        normed = summed * inverse
        upper = u_ref[s].astype(F32)
        scaled = upper * gains[...]
        first = jnp.sum(scaled, axis=0, keepdims=True) * scale
        second = jnp.sum(scaled * normed, axis=0, keepdims=True) * scale
        d_sum[s] = (inverse * (scaled - first - normed * second)).astype(BF16)
        product_gain = upper * normed
        sum_gain.append(product_gain[:, 0:128] + product_gain[:, 128:256])

    def back_rows(s):
        right_in[s, 0:rank] = mm(proj[...], d_sum[s]).astype(BF16)

    def back_project(s):
        left_in[s, :, rank : 2 * rank] = mm_nt(x_ref[s], right_in[s, 0:rank]).astype(BF16)
        d_p_t[s] = mm_nt(right_in[s, 0:rank], x_ref[s]).astype(BF16)

    def gather(s):
        grad = d_sum[s].astype(F32) + mm(d_sum[s], lcb_t[...]) + mm(left_in[s], right_in[s])
        grad = grad.astype(BF16)
        group, k = s // STEP, s % STEP
        grads[group, k * 128 : k * 128 + 128] = grad[0:128]
        at = 512 + 64 * (2 * (k % 2) + k // 2)
        grads[group, at : at + 64] = grad[128:192]
        sum_fm_t.append(mm(d_p_t[s], x_ref[s]))
        sum_proj_t.append(mm_nt(d_sum[s], g_t[s]))

    x_all = x_ref[...].reshape(count * width, features)
    left_in[:, :, 0:rank] = mm(x_all, fm_ref[...]).astype(BF16).reshape(count, width, rank)
    mixed[...] = mm(x_all, lcb_ref[...]).reshape(count, width, features)
    ahead, behind = range(count // 2), range(count // 2, count)
    for stage in (project, interact, add_up):
        for s in ahead:
            stage(s)
    load.wait()
    for one, other in zip(ahead, behind):
        normalise(one)
        project(other)
    for one, other in zip(ahead, behind):
        back_rows(one)
        interact(other)
    for one, other in zip(ahead, behind):
        back_project(one)
        add_up(other)
    for one, other in zip(ahead, behind):
        gather(one)
        normalise(other)
    for stage in (back_rows, back_project, gather):
        for s in behind:
            stage(s)
    sum_gain, sum_fm_t, sum_proj_t = sum(sum_gain), sum(sum_fm_t), sum(sum_proj_t)

    half = half_ref[0]
    for group in range(count // STEP):
        rows = mm_nt(eye[...], grads[group])
        turned[group, 0] = rows[0:128]
        turned[group, 1] = rows[128:256]
    for group in range(count // STEP):
        for side, base in ((1 - half, 0), (half, wire.half)):
            for peer in range(peers):
                at = place_of(n_grp, n_lane, peer)
                line = turned[group, side, at : at + TILE]
                left = jnp.concatenate([line[:, k * 128 : k * 128 + 128] for k in range(STEP)], axis=0)
                row = base + group * 32
                out_ref[peer, row : row + 32] = left.astype(BF16)
                right = jnp.concatenate([line[:, 512:640], line[:, 640:768]], axis=0)
                row = base + wire.left + group * 16
                out_ref[peer, row : row + 16] = right.astype(BF16)

    first_store = pltpu.make_async_copy(
        out_ref.at[:, 0 : wire.dense], out_any.at[:, 0 : wire.dense], sems.at[1]
    )
    first_store.start()

    sum_lcb = mm(x_all, d_sum[...].reshape(count * width, features), ((0,), (0,)))
    part = features // peers
    third = width // peers
    total = jnp.sum(sum_gain.T, axis=0, keepdims=True)
    high = total.astype(BF16).astype(F32)
    shares = jnp.concatenate([high, total - high, jnp.zeros((2, width), F32)], axis=0)
    shares = jnp.concatenate([shares, jnp.zeros((4, 256 - width), F32)], axis=1)

    lane = lax.broadcasted_iota(jnp.int32, (16, LANES), 1)
    sample = lax.broadcasted_iota(jnp.int32, (16, LANES), 0)
    mine = (lane // TILE == sample) & (sample < count)
    behind_ids = (lane[0:4] >= wire.left) & (lane[0:4] < wire.left + third)
    spread_ids = []
    for which, ref in enumerate((now_ref, next_ref)):
        ids[which] = jnp.zeros_like(ids[which])
        ids[which, 0:count] = ref[...].astype(F32)
        for side in range(2):
            line = ids[which, :, side * 128 : side * 128 + 128]
            spread_ids.append(pltpu.roll(line, 0, 1, stride=TILE, stride_axis=0))
    sum_fm = sum_fm_t.T
    for peer in range(peers):
        at = wire.dense
        here = slice(peer * part, (peer + 1) * part)
        out_ref[peer, at : at + part] = sum_fm[here].astype(BF16)
        out_ref[peer, at + part : at + 2 * part] = sum_lcb[here, 0:128].astype(BF16)
        out_ref[peer, at + 2 * part : at + 3 * part] = sum_lcb[here, 128:256].astype(BF16)
        place = place_of(n_grp, n_lane, peer)
        lines = []
        for line in spread_ids:
            line = pltpu.roll(line, LANES - place, 1) if place else line
            lines.append(jnp.sum(jnp.where(mine, line, 0.0), axis=0, keepdims=True))
        share = pltpu.roll(shares, (wire.left - peer * third) % 256, 1)[:, 0:128]
        lines = jnp.where(behind_ids, share, jnp.concatenate(lines, axis=0))
        last = jnp.concatenate([sum_proj_t[peer * third : (peer + 1) * third], lines], axis=0)
        out_ref[peer, at + 3 * part : at + 4 * part] = last.astype(BF16)
    second_store = pltpu.make_async_copy(
        out_ref.at[:, wire.dense : wire.rows], out_any.at[:, wire.dense : wire.rows], sems.at[2]
    )
    second_store.start()
    first_store.wait()
    second_store.wait()


def backward(n_grp, n_lane, wire, half, pooled_t, upstream_t, ids_now, ids_next, w_fm, w_proj_t, w_lcb, gain):
    count, width, features = pooled_t.shape
    rank = w_fm.shape[1]
    peers = n_grp * n_lane

    def whole(shape):
        return pl.BlockSpec(shape, lambda i: (0,) * len(shape))

    operands = (pooled_t, upstream_t, ids_now, ids_next, w_fm, w_proj_t, w_lcb, gain.reshape(1, width))
    shape = (peers, wire.rows, LANES)
    free = pl.BlockSpec(memory_space=pl.ANY)
    return pl.pallas_call(
        functools.partial(backward_kernel, n_grp, n_lane, wire),
        grid=(1,),
        in_specs=[SMEM, whole(pooled_t.shape), free] + [whole(array.shape) for array in operands[2:]],
        out_specs=free,
        out_shape=pltpu.HBM(shape, BF16),
        scratch_shapes=[
            pltpu.VMEM((rank, features), BF16),
            pltpu.VMEM((rank, width), BF16),
            pltpu.VMEM((features, features), BF16),
            pltpu.VMEM((width, features), F32),
            pltpu.VMEM((features, features), BF16),
            pltpu.VMEM((count, width, features), F32),
            pltpu.VMEM((count, rank, width), BF16),
            pltpu.VMEM((count, rank, features), BF16),
            pltpu.VMEM((count, width, features), BF16),
            pltpu.VMEM((count, rank, width), BF16),
            pltpu.VMEM((count, width, 2 * rank), BF16),
            pltpu.VMEM((count, 2 * rank, features), BF16),
            pltpu.VMEM((count // STEP, STEP * width, features), BF16),
            pltpu.VMEM((count // STEP, 2, features // 2, STEP * width), F32),
            pltpu.VMEM((2, 16, features), F32),
            pltpu.VMEM(upstream_t.shape, BF16),
            pltpu.VMEM(shape, BF16),
            pltpu.SemaphoreType.DMA((3,)),
        ],
        compiler_params=params(2),
        cost_estimate=cost(1),
        name="layer_backward",
    )(half, *operands)


def dense_kernel(dense_ref, ids_ref, dense, all_ids):
    total = dense_ref[0].astype(F32)
    for peer in range(1, dense_ref.shape[0]):
        total = total + dense_ref[peer].astype(F32)
    dense[...] = total
    all_ids[...] = ids_ref[...].astype(F32)


def half_dense(wire, seen):
    peers = seen.shape[0]
    rows = wire.share // 2
    at_ids = wire.rows // 16 - 1
    return pl.pallas_call(
        dense_kernel,
        grid=(2,),
        in_specs=[
            pl.BlockSpec((peers, rows, LANES), lambda i: (0, wire.dense // rows + i, 0)),
            pl.BlockSpec((peers, 16, LANES), lambda i: (0, at_ids, 0)),
        ],
        out_specs=[
            pl.BlockSpec((rows, LANES), lambda i: (i, 0)),
            pl.BlockSpec((peers, 16, LANES), lambda i: (0, 0, 0)),
        ],
        out_shape=[
            jax.ShapeDtypeStruct((wire.share, LANES), F32),
            jax.ShapeDtypeStruct((peers, 16, LANES), F32),
        ],
        compiler_params=params(),
        cost_estimate=cost(1),
        name="half_dense",
    )(seen, seen)


def part_kernel(n_grp, wire, other, half_ref, seen, all_ids, *refs):
    out, held = refs[-2:]
    peers = seen.shape[0]
    half = 1 - half_ref[0] if other else half_ref[0]
    lane = lax.broadcasted_iota(jnp.int32, (1, LANES), 1)
    start = ((lane % TILE) * LANES).astype(F32)
    keys = []
    for peer in range(peers):
        at = peer * LANES
        held[at : at + wire.left, 0:128] = seen[peer, 0 : wire.left]
        right = seen[peer, wire.left : wire.half]
        turned = turn(right.astype(F32)).astype(BF16)
        for i in range(wire.left // 32):
            held[at + 32 * i : at + 32 * i + 16, 128:256] = right[16 * i : 16 * i + 16]
            held[at + 32 * i + 16 : at + 32 * i + 32, 128:256] = turned[16 * i : 16 * i + 16]
        if wire.left < LANES:
            held[at + wire.left : at + LANES] = jnp.zeros((LANES - wire.left, 256), BF16)
        ids = all_ids[peer]
        key = jnp.where(half == 0, ids[12:13], ids[13:14]) + start
        keys.append(jnp.where(lane < wire.left, key, -1.0))
    keys = jnp.concatenate(keys, axis=1)
    piece = LANES // n_grp
    for pair in range(TILE // 2):
        row = lax.broadcasted_iota(jnp.int32, (256, 1), 0).astype(F32) + 256.0 * pair
        hit = jnp.where(keys == row, 1.0, 0.0).astype(BF16)
        part = mm(hit, held[...])
        for f in range(2):
            for g in range(n_grp):
                at = f * LANES + g * piece
                rows = part[at : at + piece]
                out[g, 2 * pair + f, 0:piece] = rows[:, 0:128].astype(out.dtype)
                second = turn(rows[piece // 2 :, 128:256])
                packed = jnp.where(low_lanes(second.shape), rows[: piece // 2, 128:256], second)
                out[g, 2 * pair + f, piece : piece + piece // 2] = packed.astype(out.dtype)


def part_sums(n_grp, wire, other, half, seen, ids, *after):
    peers = seen.shape[0]
    piece = LANES // n_grp
    shape = (n_grp, TILE, piece + piece // 2, LANES)
    which = 0 if other else 1
    return pl.pallas_call(
        functools.partial(part_kernel, n_grp, wire, other),
        grid=(1,),
        in_specs=[
            SMEM,
            pl.BlockSpec((peers, wire.half, LANES), lambda i: (0, which, 0)),
            pl.BlockSpec(ids.shape, lambda i: (0, 0, 0)),
        ]
        + [pl.BlockSpec(memory_space=pl.ANY)] * len(after),
        out_specs=pl.BlockSpec(shape, lambda i: (0, 0, 0, 0)),
        out_shape=jax.ShapeDtypeStruct(shape, BF16 if other else F32),
        scratch_shapes=[pltpu.VMEM((peers * LANES, 256), BF16)],
        compiler_params=params(1 if other else 2),
        cost_estimate=cost(1),
        name="part_other" if other else "part_own",
    )(half, seen, ids, *after)


def take_kernel(place, tables, out, sem):
    copy = pltpu.make_async_copy(tables.at[pl.ds(place[0] * TILE, TILE)], out, sem)
    copy.start()
    copy.wait()


def take_tables(place, tables_t):
    return pl.pallas_call(
        take_kernel,
        in_specs=[SMEM, pl.BlockSpec(memory_space=pl.ANY)],
        out_specs=pl.BlockSpec(memory_space=pl.ANY),
        out_shape=pltpu.HBM((TILE,) + tables_t.shape[1:], BF16),
        scratch_shapes=[pltpu.SemaphoreType.DMA],
        compiler_params=params(2),
        cost_estimate=cost(1),
        name="take_tables",
    )(place, tables_t)


def stack_kernel(half_ref, mine_t, crossed_t, out):
    half = half_ref[0]
    for f in range(TILE):
        at = f * LANES
        for side, ref in ((half, mine_t), (1 - half, crossed_t)):
            out[side, 0:192, at : at + LANES] = ref[f]
            out[side, 192:256, at : at + LANES] = ref[f, 128:192]


def stack_tables(half, mine_t, crossed_t):
    return pl.pallas_call(
        stack_kernel,
        in_specs=[SMEM, VMEM, VMEM],
        out_specs=VMEM,
        out_shape=jax.ShapeDtypeStruct((2, 256, TILE * LANES), BF16),
        compiler_params=params(),
        cost_estimate=cost(100),
        name="stack_tables",
    )(half, mine_t, crossed_t)


def lookup_kernel(wire, stacked, ids_ref, out):
    peers = out.shape[0]
    ids = ids_ref[...].reshape(peers * 16, LANES)
    keys = ids.T
    rows = peers * wire.left
    lane = lax.broadcasted_iota(jnp.int32, (1, LANES), 1).astype(F32)
    feature = lax.broadcasted_iota(jnp.int32, (rows, LANES), 0) % TILE
    masks = [jnp.where(feature == f, 1.0, 0.0).astype(BF16) for f in range(TILE)]
    for which in range(2):
        same = []
        for peer in range(peers):
            at = peer * 16 + 14 + which
            same.append(jnp.where(keys[0 : wire.left, at : at + 1] == lane, 1.0, 0.0))
        same = jnp.concatenate(same, axis=0).astype(BF16)
        hit = jnp.concatenate([same * mask for mask in masks], axis=1)
        both = mm_nt(hit, stacked[which])
        for peer in range(peers):
            got = both[peer * wire.left : (peer + 1) * wire.left]
            base = wire.back_left[which]
            out[peer, base : base + wire.left] = got[:, 0:128].astype(BF16)
            packed = []
            for i in range(wire.left // 32):
                first, second = got[32 * i : 32 * i + 16, 128:256], got[32 * i + 16 : 32 * i + 32, 128:256]
                packed.append(jnp.where(low_lanes(first.shape), first, second))
            base = wire.back_right[which]
            out[peer, base : base + wire.left // 2] = jnp.concatenate(packed, axis=0).astype(BF16)


def lookup(wire, stacked, ids):
    peers = ids.shape[0]
    some = peers // 4
    return pl.pallas_call(
        functools.partial(lookup_kernel, wire),
        grid=(4,),
        in_specs=[
            pl.BlockSpec(stacked.shape, lambda i: (0, 0, 0)),
            pl.BlockSpec((some, 16, LANES), lambda i: (i, 0, 0)),
        ],
        out_specs=pl.BlockSpec((some, wire.rows, LANES), lambda i: (i, 0, 0)),
        out_shape=pltpu.HBM((peers, wire.rows, LANES), BF16),
        compiler_params=params(),
        cost_estimate=cost(100),
        name="lookup",
    )(stacked, ids)


def fill_kernel(factor, rows, own, seen, out, token):
    token[...] = jnp.zeros_like(token)
    total = ((own[...] + seen[...]) * factor).astype(BF16)
    for peer in range(out.shape[0]):
        out[peer] = total


def fill(wire, factor, rows, own, seen):
    peers = rows.shape[0]

    def whole(shape):
        return pl.BlockSpec(shape, lambda i: (0,) * len(shape))

    return pl.pallas_call(
        functools.partial(fill_kernel, factor),
        grid=(1,),
        in_specs=[pl.BlockSpec(memory_space=pl.ANY), whole(own.shape), whole(seen.shape)],
        out_specs=[whole((peers, wire.share, LANES)), whole((8, LANES))],
        out_shape=[pltpu.HBM(rows.shape, BF16), pltpu.HBM((8, LANES), F32)],
        input_output_aliases={0: 0},
        compiler_params=params(),
        cost_estimate=cost(1),
        name="fill_dense",
    )(rows, own, seen)


def finish_pieces(grp, pieces, out):
    piece = out.shape[1]
    for k, seen in enumerate(pieces):
        base = jnp.bitwise_xor(grp, k) * TILE
        for f in range(TILE):
            out[base + f, :, 0:128] = seen[f, 0:piece].astype(F32)
            packed = seen[f, piece : piece + piece // 2].astype(F32)
            out[base + f, 0 : piece // 2, 128:192] = packed[:, 0:64]
            out[base + f, piece // 2 : piece, 128:192] = turn(packed)[:, 0:64]


def unpack_kernel(n_grp, n_lane, wire, place, dense_ref, left0, left1, right0, right1, *refs):
    pieces, refs = refs[:n_grp], refs[n_grp:]
    rows_out, table_grad, fm, proj_t, lcb, gain, held = refs
    step = pl.program_id(0)
    peers = n_grp * n_lane
    for side, (left_ref, right_ref) in enumerate(((left0, right0), (left1, right1))):
        for q in range(n_lane):
            for gg in range(n_grp // 2):
                left, right = [], []
                for g in (2 * gg, 2 * gg + 1):
                    peer = g * n_lane + q
                    left.append(left_ref[peer].astype(F32))
                    packed = right_ref[peer].astype(F32)
                    right.append(jnp.concatenate([packed, turn(packed)], axis=0))
                at = side * 128 + q * n_grp * TILE + gg * 16
                for s in range(STEP):
                    here = slice(s * TILE, s * TILE + TILE)
                    both = jnp.concatenate([left[0][here], left[1][here]], axis=0)
                    held[s, at : at + 16, 0:128] = both.astype(BF16)
                    both = jnp.concatenate([right[0][here], right[1][here]], axis=0)
                    held[s, at : at + 16, 128:256] = both.astype(BF16)
    eye = identity(192, 256)
    for s in range(STEP):
        rows_out[s] = mm_nt(eye, held[s]).astype(BF16)

    @pl.when(step == 0)
    def _():
        part, third = 256 // peers, 192 // peers
        lane = lax.broadcasted_iota(jnp.int32, (1, LANES), 1)
        behind_ids = (lane >= wire.left) & (lane < wire.left + third)
        total = jnp.zeros((1, 256), F32)
        for peer in range(peers):
            dense = dense_ref[peer].astype(F32)
            here = slice(peer * part, (peer + 1) * part)
            fm[here] = dense[0:part]
            lcb[here, 0:128] = dense[part : 2 * part]
            lcb[here, 128:256] = dense[2 * part : 3 * part]
            last = dense[3 * part : 4 * part]
            proj_t[peer * third : (peer + 1) * third] = last[0:third]
            share = jnp.where(behind_ids, last[third : third + 1] + last[third + 1 : third + 2], 0.0)
            share = jnp.concatenate([share, jnp.zeros((1, LANES), F32)], axis=1)
            total += pltpu.roll(share, (peer * third - wire.left) % 256, 1)
        gain[...] = total[:, 0:192]

    @pl.when(step == pl.num_programs(0) - 1)
    def _():
        finish_pieces(place[0], pieces, table_grad)


def unpack(n_grp, n_lane, wire, count, place, seen, pieces):
    def whole(*shape):
        return pl.BlockSpec(shape, lambda i: (0,) * len(shape))

    def part(rows, start):
        return pl.BlockSpec((peers, rows, LANES), lambda i: (0, start // rows + i, 0))

    peers = n_grp * n_lane
    shapes = [(n_grp * TILE, pieces[0].shape[1] * 2 // 3, 192), (256, 128), (192, 128), (256, 256), (1, 192)]
    return pl.pallas_call(
        functools.partial(unpack_kernel, n_grp, n_lane, wire),
        grid=(count // STEP,),
        in_specs=[SMEM, pl.BlockSpec((peers, wire.share, LANES), lambda i: (0, 0, 0))]
        + [part(32, start) for start in wire.back_left]
        + [part(16, start) for start in wire.back_right]
        + [whole(*piece.shape) for piece in pieces],
        out_specs=[pl.BlockSpec((STEP, 192, 256), lambda i: (i, 0, 0))] + [whole(*shape) for shape in shapes],
        out_shape=[jax.ShapeDtypeStruct((count, 192, 256), BF16)]
        + [jax.ShapeDtypeStruct(shape, F32) for shape in shapes],
        scratch_shapes=[pltpu.VMEM((STEP, 256, 256), BF16)],
        compiler_params=params(),
        cost_estimate=cost(1),
        name="unpack",
    )(place, seen, seen, seen, seen, seen, *pieces)


def combine_kernel(place, own, seen, after, *outs):
    for k, out in enumerate(outs):
        g = jnp.bitwise_xor(place[0], k)
        out[...] = (own[g] + seen[g].astype(F32)).astype(BF16)


def combine(place, own, seen, after):
    n_grp = own.shape[0]
    shape = jax.ShapeDtypeStruct(own.shape[1:], BF16)
    return pl.pallas_call(
        combine_kernel,
        in_specs=[SMEM, VMEM, VMEM, pl.BlockSpec(memory_space=pl.ANY)],
        out_specs=[VMEM] * n_grp,
        out_shape=[shape] * n_grp,
        compiler_params=params(),
        cost_estimate=cost(100),
        name="combine",
    )(place, own, seen, after)


def cross(array):
    return lax.ppermute(array, "half", [(0, 1), (1, 0)])


def halves(pooled, upstream, ids_now, ids_next, tables, w_fm, w_proj, w_lcb, gain):
    n_grp, n_lane = lax.axis_size("grp"), lax.axis_size("lane")
    count = pooled.shape[0]
    wire = Wire(count, n_grp * n_lane)
    factor = 1.0 / (count * n_grp * 2 * n_lane)
    half = lax.axis_index("half").astype(jnp.int32)[None]
    grp = lax.axis_index("grp").astype(jnp.int32)
    mine_t = take_tables(grp[None], tables.transpose(0, 2, 1))
    crossed_t = cross(mine_t)
    sent = backward(
        n_grp, n_lane, wire, half,
        pooled.transpose(0, 2, 1), upstream.transpose(0, 2, 1), ids_now, ids_next, w_fm, w_proj.T, w_lcb, gain,
    )
    seen = exchange(sent, PEER)
    dense, ids = half_dense(wire, seen)
    dense_seen = cross(dense)
    part_seen = cross(part_sums(n_grp, wire, True, half, seen, ids))
    rows_wire = lookup(wire, stack_tables(half, mine_t, crossed_t), ids)
    rows_wire, token = fill(wire, factor, rows_wire, dense, dense_seen)
    rows = exchange(rows_wire, PEER)
    own = part_sums(n_grp, wire, False, half, seen, ids, token)
    pieces = combine(grp[None], own, part_seen, token)
    pieces = [pieces[0]] + [
        lax.ppermute(pieces[k], "grp", [(g, g ^ k) for g in range(n_grp)]) for k in range(1, n_grp)
    ]
    next_rows, table_grad, grad_fm, grad_proj_t, grad_lcb, grad_gain = unpack(
        n_grp, n_lane, wire, count, grp[None], rows, pieces
    )
    return next_rows.transpose(0, 2, 1), table_grad, grad_fm, grad_proj_t.T, grad_lcb, grad_gain.reshape(-1)


def solution(mesh):
    n_grp, n_emb = mesh.shape["grp"], mesh.shape["emb"]
    split = n_emb % 2 == 0 and n_grp * (n_emb // 2) == 16 and n_grp % 2 == 0

    def run(*args):
        pooled, _, _, _, tables, w_fm = args[:6]
        count = pooled.shape[0] // (n_grp * n_emb)
        fits = (
            split
            and pooled.shape[1:] == (256, 192)
            and tables.shape[1] == 128
            and w_fm.shape[1] == 128
            and pooled.shape[1] == n_grp * n_emb * TILE
            and count % STEP == 0
            and count <= 12
        )
        if fits:
            devices = mesh.devices.reshape(n_grp, 2, n_emb // 2)
            where, emb, body = Mesh(devices, ("grp", "half", "lane")), ("half", "lane"), halves
        else:
            where, emb, body = mesh, ("emb",), local
        both = ("grp",) + emb
        return jax.shard_map(
            body,
            mesh=where,
            in_specs=(
                P(both, None, None),
                P(both, None, None),
                P(both, None),
                P(both, None),
                P(emb, None, None),
                P(),
                P(),
                P(),
                P(),
            ),
            out_specs=(P(both, None, None), P(emb, "grp", None), P(), P(), P(), P()),
            check_vma=False,
        )(*args)

    return run
```

```python
import functools

import jax
import jax.numpy as jnp
from jax import lax
from jax.experimental import pallas as pl
from jax.experimental.pallas import tpu as pltpu
from jax.sharding import Mesh, PartitionSpec as P

F32, BF16 = jnp.float32, jnp.bfloat16
SMEM = pl.BlockSpec(memory_space=pltpu.SMEM)
VMEM = pl.BlockSpec(memory_space=pltpu.VMEM)
LANES = 128
TILE = 8
STEP = 4
LIMIT = 30 * 1024 * 1024
PEER = ("grp", "lane")


BOTH = ("grp", "emb")


def product(form, left, right):
    return jnp.einsum(form, left, right, preferred_element_type=jnp.float32)


def layer_backward(embeds, cotangent, w_fm, w_proj, w_lcb, gain):
    fm_proj = product("bfc,fj->bcj", embeds, w_fm).astype(jnp.bfloat16)
    fm_rows = product("bfc,bcj->bfj", embeds, fm_proj).astype(jnp.bfloat16)
    projected = product("bfj,jc->bfc", fm_rows, w_proj)
    compressed = product("fi,bfc->bic", w_lcb, embeds)
    summed = embeds.astype(jnp.float32) + projected + compressed
    centre = jnp.mean(summed, axis=2, keepdims=True)
    spread = jnp.mean((summed - centre) ** 2, axis=2, keepdims=True)
    inverse = lax.rsqrt(spread + 1e-05)
    normed = (summed - centre) * inverse
    upper = cotangent.astype(jnp.float32)
    scaled = upper * gain
    grad_sum = inverse * (
        scaled
        - jnp.mean(scaled, axis=2, keepdims=True)
        - normed * jnp.mean(scaled * normed, axis=2, keepdims=True)
    )
    grad_sum = grad_sum.astype(jnp.bfloat16)
    grad_gain = jnp.sum(upper * normed, axis=(0, 1))
    grad_proj = product("bfj,bfc->jc", fm_rows, grad_sum)
    grad_rows = product("bfc,jc->bfj", grad_sum, w_proj).astype(jnp.bfloat16)
    grad_p = product("bfc,bfj->bcj", embeds, grad_rows).astype(jnp.bfloat16)
    grad_fm = product("bfc,bcj->fj", embeds, grad_p)
    grad_lcb = product("bfc,bic->fi", embeds, grad_sum)
    grad_in = (
        grad_sum.astype(jnp.float32)
        + product("bfj,bcj->bfc", grad_rows, fm_proj)
        + product("fj,bcj->bfc", w_fm, grad_p)
        + product("fi,bic->bfc", w_lcb, grad_sum)
    )
    return (grad_in.astype(jnp.bfloat16), (grad_fm, grad_proj, grad_lcb, grad_gain))


def exchange(blocks, axes):
    return lax.all_to_all(blocks, axes, split_axis=0, concat_axis=0, tiled=True)


def dense_sum(partials, factor):
    n = lax.axis_size("grp") * lax.axis_size("emb")
    shapes = [part.shape for part in partials]
    flat = jnp.concatenate([part.reshape(-1) for part in partials])
    unit = 128 * n
    padded = -(-flat.shape[0] // unit) * unit
    flat = jnp.pad(flat, (0, padded - flat.shape[0])).astype(jnp.bfloat16)
    seen = exchange(flat.reshape(n, padded // unit, 128), BOTH)
    share = (jnp.sum(seen.astype(jnp.float32), axis=0) * factor).astype(jnp.bfloat16)
    total = exchange(jnp.broadcast_to(share[None], (n,) + share.shape), BOTH).reshape(-1)
    total = total.astype(jnp.float32)
    outs, at = [], 0
    for shape in shapes:
        size = 1
        for extent in shape:
            size *= extent
        outs.append(total[at : at + size].reshape(shape))
        at += size
    return outs


def local(pooled, upstream, ids_now, ids_next, tables, w_fm, w_proj, w_lcb, gain):
    n_grp, n_emb = lax.axis_size("grp"), lax.axis_size("emb")
    count, features, width = pooled.shape
    owned, rows = tables.shape[:2]
    ids = jnp.stack([ids_now, ids_next]).reshape(2, count, n_emb, owned)
    ids = exchange(ids.transpose(2, 0, 1, 3), "emb")
    row_index = jnp.arange(rows)
    wanted = (ids[:, 1, :, :, None] == row_index).astype(jnp.bfloat16)
    fetched = product("esfr,frc->esfc", wanted, tables).astype(jnp.bfloat16)
    next_rows = exchange(fetched, "emb")
    next_rows = next_rows.transpose(1, 0, 2, 3).reshape(count, features, width)
    grad_in, partials = layer_backward(pooled, upstream, w_fm, w_proj, w_lcb, gain)
    grad_in = grad_in.reshape(count, n_emb, owned, width).transpose(1, 0, 2, 3)
    grads = exchange(grad_in, "emb")
    hit = (ids[:, 0, :, :, None] == row_index).astype(jnp.bfloat16)
    part = product("esfr,esfc->frc", hit, grads).astype(jnp.bfloat16)
    part = part.reshape(owned, n_grp, rows // n_grp, width).transpose(1, 0, 2, 3)
    table_grad = jnp.sum(exchange(part, "grp").astype(jnp.float32), axis=0)
    dense = dense_sum(partials, 1.0 / (count * n_grp * n_emb))
    return (next_rows, table_grad, *dense)


def params(share=1):
    return pltpu.CompilerParams(vmem_limit_bytes=share * LIMIT)


def cost(weight):
    return pl.CostEstimate(flops=weight * 10**9, bytes_accessed=10**5, transcendentals=0)


def mm(left, right, dims=((1,), (0,))):
    return lax.dot_general(left, right, (dims, ((), ())), preferred_element_type=F32)


def mm_nt(left, right):
    return mm(left, right, ((1,), (1,)))


def low_lanes(shape):
    return lax.broadcasted_iota(jnp.int32, shape, 1) < LANES // 2


def turn(tile):
    return pltpu.roll(tile, LANES // 2, 1)


def identity(rows, lanes):
    row = lax.broadcasted_iota(jnp.int32, (rows, lanes), 0)
    return jnp.where(row == lax.broadcasted_iota(jnp.int32, (rows, lanes), 1), 1.0, 0.0).astype(BF16)


class Wire:
    def __init__(self, count, peers):
        self.left = count * TILE
        self.half = self.left + self.left // 2
        self.dense = 2 * self.half
        self.share = 1024 // peers
        self.rows = self.dense + self.share
        self.back_left = (self.share, self.share + self.left)
        self.back_right = (self.share + 2 * self.left, self.share + 2 * self.left + self.left // 2)


def place_of(n_grp, n_lane, peer):
    return (peer % n_lane) * n_grp * TILE + (peer // n_lane) * TILE


def backward_kernel(
    n_grp, n_lane, wire,
    half_ref, x_ref, u_any, now_ref, next_ref, fm_ref, proj_t_ref, lcb_ref, gain_ref,
    out_any,
    fm_t, proj, lcb_t, gains, eye, mixed, p_t, g_t, d_sum, d_p_t, left_in, right_in, grads, turned, ids,
    u_ref, out_ref, sems,
):
    count, width, features = x_ref.shape
    rank = fm_ref.shape[1]
    peers = n_grp * n_lane
    scale = 1.0 / width
    load = pltpu.make_async_copy(u_any, u_ref, sems.at[0])
    load.start()

    turned_fm = fm_ref[...].astype(F32).T.astype(BF16)
    fm_t[...] = turned_fm
    proj[...] = proj_t_ref[...].astype(F32).T.astype(BF16)
    lcb_t[...] = lcb_ref[...].astype(F32).T.astype(BF16)
    column = jnp.broadcast_to(gain_ref[...], (LANES, width)).T
    gains[:, 0:128] = column
    gains[:, 128:256] = column
    eye[...] = identity(features, features)
    sum_gain, sum_fm_t, sum_proj_t = [], [], []

    def project(s):
        p_t[s] = mm_nt(fm_t[...], x_ref[s]).astype(BF16)
        right_in[s, rank : 2 * rank] = fm_t[...]

    def interact(s):
        g_t[s] = mm(p_t[s], x_ref[s]).astype(BF16)

    def add_up(s):
        mixed[s] = mixed[s] + mm(proj_t_ref[...], g_t[s])

    def normalise(s):
        summed = x_ref[s].astype(F32) + mixed[s]
        centre = jnp.sum(summed, axis=0, keepdims=True) * scale
        summed = summed - centre
        spread = jnp.sum(summed * summed, axis=0, keepdims=True) * scale
        inverse = lax.rsqrt(spread + 1e-05)
        normed = summed * inverse
        upper = u_ref[s].astype(F32)
        scaled = upper * gains[...]
        first = jnp.sum(scaled, axis=0, keepdims=True) * scale
        second = jnp.sum(scaled * normed, axis=0, keepdims=True) * scale
        d_sum[s] = (inverse * (scaled - first - normed * second)).astype(BF16)
        product_gain = upper * normed
        sum_gain.append(product_gain[:, 0:128] + product_gain[:, 128:256])

    def back_rows(s):
        right_in[s, 0:rank] = mm(proj[...], d_sum[s]).astype(BF16)

    def back_project(s):
        left_in[s, :, rank : 2 * rank] = mm_nt(x_ref[s], right_in[s, 0:rank]).astype(BF16)
        d_p_t[s] = mm_nt(right_in[s, 0:rank], x_ref[s]).astype(BF16)

    def gather(s):
        grad = d_sum[s].astype(F32) + mm(d_sum[s], lcb_t[...]) + mm(left_in[s], right_in[s])
        grad = grad.astype(BF16)
        group, k = s // STEP, s % STEP
        grads[group, k * 128 : k * 128 + 128] = grad[0:128]
        at = 512 + 64 * (2 * (k % 2) + k // 2)
        grads[group, at : at + 64] = grad[128:192]
        sum_fm_t.append(mm(d_p_t[s], x_ref[s]))
        sum_proj_t.append(mm_nt(d_sum[s], g_t[s]))

    x_all = x_ref[...].reshape(count * width, features)
    left_in[:, :, 0:rank] = mm(x_all, fm_ref[...]).astype(BF16).reshape(count, width, rank)
    mixed[...] = mm(x_all, lcb_ref[...]).reshape(count, width, features)
    ahead, behind = range(count // 2), range(count // 2, count)
    for stage in (project, interact, add_up):
        for s in ahead:
            stage(s)
    load.wait()
    for one, other in zip(ahead, behind):
        normalise(one)
        project(other)
    for one, other in zip(ahead, behind):
        back_rows(one)
        interact(other)
    for one, other in zip(ahead, behind):
        back_project(one)
        add_up(other)
    for one, other in zip(ahead, behind):
        gather(one)
        normalise(other)
    for stage in (back_rows, back_project, gather):
        for s in behind:
            stage(s)
    sum_gain, sum_fm_t, sum_proj_t = sum(sum_gain), sum(sum_fm_t), sum(sum_proj_t)

    half = half_ref[0]
    for group in range(count // STEP):
        rows = mm_nt(eye[...], grads[group])
        turned[group, 0] = rows[0:128]
        turned[group, 1] = rows[128:256]
    for group in range(count // STEP):
        for side, base in ((1 - half, 0), (half, wire.half)):
            for peer in range(peers):
                at = place_of(n_grp, n_lane, peer)
                line = turned[group, side, at : at + TILE]
                left = jnp.concatenate([line[:, k * 128 : k * 128 + 128] for k in range(STEP)], axis=0)
                row = base + group * 32
                out_ref[peer, row : row + 32] = left.astype(BF16)
                right = jnp.concatenate([line[:, 512:640], line[:, 640:768]], axis=0)
                row = base + wire.left + group * 16
                out_ref[peer, row : row + 16] = right.astype(BF16)

    first_store = pltpu.make_async_copy(
        out_ref.at[:, 0 : wire.dense], out_any.at[:, 0 : wire.dense], sems.at[1]
    )
    first_store.start()

    sum_lcb = mm(x_all, d_sum[...].reshape(count * width, features), ((0,), (0,)))
    part = features // peers
    third = width // peers
    total = jnp.sum(sum_gain.T, axis=0, keepdims=True)
    high = total.astype(BF16).astype(F32)
    shares = jnp.concatenate([high, total - high, jnp.zeros((2, width), F32)], axis=0)
    shares = jnp.concatenate([shares, jnp.zeros((4, 256 - width), F32)], axis=1)

    lane = lax.broadcasted_iota(jnp.int32, (16, LANES), 1)
    sample = lax.broadcasted_iota(jnp.int32, (16, LANES), 0)
    mine = (lane // TILE == sample) & (sample < count)
    behind_ids = (lane[0:4] >= wire.left) & (lane[0:4] < wire.left + third)
    spread_ids = []
    for which, ref in enumerate((now_ref, next_ref)):
        ids[which] = jnp.zeros_like(ids[which])
        ids[which, 0:count] = ref[...].astype(F32)
        for side in range(2):
            line = ids[which, :, side * 128 : side * 128 + 128]
            spread_ids.append(pltpu.roll(line, 0, 1, stride=TILE, stride_axis=0))
    sum_fm = sum_fm_t.T
    for peer in range(peers):
        at = wire.dense
        here = slice(peer * part, (peer + 1) * part)
        out_ref[peer, at : at + part] = sum_fm[here].astype(BF16)
        out_ref[peer, at + part : at + 2 * part] = sum_lcb[here, 0:128].astype(BF16)
        out_ref[peer, at + 2 * part : at + 3 * part] = sum_lcb[here, 128:256].astype(BF16)
        place = place_of(n_grp, n_lane, peer)
        lines = []
        for line in spread_ids:
            line = pltpu.roll(line, LANES - place, 1) if place else line
            lines.append(jnp.sum(jnp.where(mine, line, 0.0), axis=0, keepdims=True))
        share = pltpu.roll(shares, (wire.left - peer * third) % 256, 1)[:, 0:128]
        lines = jnp.where(behind_ids, share, jnp.concatenate(lines, axis=0))
        last = jnp.concatenate([sum_proj_t[peer * third : (peer + 1) * third], lines], axis=0)
        out_ref[peer, at + 3 * part : at + 4 * part] = last.astype(BF16)
    second_store = pltpu.make_async_copy(
        out_ref.at[:, wire.dense : wire.rows], out_any.at[:, wire.dense : wire.rows], sems.at[2]
    )
    second_store.start()
    first_store.wait()
    second_store.wait()


def backward(n_grp, n_lane, wire, half, pooled_t, upstream_t, ids_now, ids_next, w_fm, w_proj_t, w_lcb, gain):
    count, width, features = pooled_t.shape
    rank = w_fm.shape[1]
    peers = n_grp * n_lane

    def whole(shape):
        return pl.BlockSpec(shape, lambda i: (0,) * len(shape))

    operands = (pooled_t, upstream_t, ids_now, ids_next, w_fm, w_proj_t, w_lcb, gain.reshape(1, width))
    shape = (peers, wire.rows, LANES)
    free = pl.BlockSpec(memory_space=pl.ANY)
    return pl.pallas_call(
        functools.partial(backward_kernel, n_grp, n_lane, wire),
        grid=(1,),
        in_specs=[SMEM, whole(pooled_t.shape), free] + [whole(array.shape) for array in operands[2:]],
        out_specs=free,
        out_shape=pltpu.HBM(shape, BF16),
        scratch_shapes=[
            pltpu.VMEM((rank, features), BF16),
            pltpu.VMEM((rank, width), BF16),
            pltpu.VMEM((features, features), BF16),
            pltpu.VMEM((width, features), F32),
            pltpu.VMEM((features, features), BF16),
            pltpu.VMEM((count, width, features), F32),
            pltpu.VMEM((count, rank, width), BF16),
            pltpu.VMEM((count, rank, features), BF16),
            pltpu.VMEM((count, width, features), BF16),
            pltpu.VMEM((count, rank, width), BF16),
            pltpu.VMEM((count, width, 2 * rank), BF16),
            pltpu.VMEM((count, 2 * rank, features), BF16),
            pltpu.VMEM((count // STEP, STEP * width, features), BF16),
            pltpu.VMEM((count // STEP, 2, features // 2, STEP * width), F32),
            pltpu.VMEM((2, 16, features), F32),
            pltpu.VMEM(upstream_t.shape, BF16),
            pltpu.VMEM(shape, BF16),
            pltpu.SemaphoreType.DMA((3,)),
        ],
        compiler_params=params(2),
        cost_estimate=cost(1),
        name="layer_backward",
    )(half, *operands)


def dense_kernel(dense_ref, ids_ref, dense, all_ids):
    total = dense_ref[0].astype(F32)
    for peer in range(1, dense_ref.shape[0]):
        total = total + dense_ref[peer].astype(F32)
    dense[...] = total
    all_ids[...] = ids_ref[...].astype(F32)


def half_dense(wire, seen):
    peers = seen.shape[0]
    rows = wire.share // 2
    at_ids = wire.rows // 16 - 1
    return pl.pallas_call(
        dense_kernel,
        grid=(2,),
        in_specs=[
            pl.BlockSpec((peers, rows, LANES), lambda i: (0, wire.dense // rows + i, 0)),
            pl.BlockSpec((peers, 16, LANES), lambda i: (0, at_ids, 0)),
        ],
        out_specs=[
            pl.BlockSpec((rows, LANES), lambda i: (i, 0)),
            pl.BlockSpec((peers, 16, LANES), lambda i: (0, 0, 0)),
        ],
        out_shape=[
            jax.ShapeDtypeStruct((wire.share, LANES), F32),
            jax.ShapeDtypeStruct((peers, 16, LANES), F32),
        ],
        compiler_params=params(),
        cost_estimate=cost(1),
        name="half_dense",
    )(seen, seen)


def part_kernel(n_grp, wire, other, half_ref, seen, all_ids, *refs):
    out, held = refs[-2:]
    peers = seen.shape[0]
    half = 1 - half_ref[0] if other else half_ref[0]
    lane = lax.broadcasted_iota(jnp.int32, (1, LANES), 1)
    start = ((lane % TILE) * LANES).astype(F32)
    keys = []
    for peer in range(peers):
        at = peer * LANES
        held[at : at + wire.left, 0:128] = seen[peer, 0 : wire.left]
        right = seen[peer, wire.left : wire.half]
        turned = turn(right.astype(F32)).astype(BF16)
        for i in range(wire.left // 32):
            held[at + 32 * i : at + 32 * i + 16, 128:256] = right[16 * i : 16 * i + 16]
            held[at + 32 * i + 16 : at + 32 * i + 32, 128:256] = turned[16 * i : 16 * i + 16]
        if wire.left < LANES:
            held[at + wire.left : at + LANES] = jnp.zeros((LANES - wire.left, 256), BF16)
        ids = all_ids[peer]
        key = jnp.where(half == 0, ids[12:13], ids[13:14]) + start
        keys.append(jnp.where(lane < wire.left, key, -1.0))
    keys = jnp.concatenate(keys, axis=1)
    piece = LANES // n_grp
    for pair in range(TILE // 2):
        row = lax.broadcasted_iota(jnp.int32, (256, 1), 0).astype(F32) + 256.0 * pair
        hit = jnp.where(keys == row, 1.0, 0.0).astype(BF16)
        part = mm(hit, held[...])
        for f in range(2):
            for g in range(n_grp):
                at = f * LANES + g * piece
                rows = part[at : at + piece]
                out[g, 2 * pair + f, 0:piece] = rows[:, 0:128].astype(out.dtype)
                second = turn(rows[piece // 2 :, 128:256])
                packed = jnp.where(low_lanes(second.shape), rows[: piece // 2, 128:256], second)
                out[g, 2 * pair + f, piece : piece + piece // 2] = packed.astype(out.dtype)


def part_sums(n_grp, wire, other, half, seen, ids, *after):
    peers = seen.shape[0]
    piece = LANES // n_grp
    shape = (n_grp, TILE, piece + piece // 2, LANES)
    which = 0 if other else 1
    return pl.pallas_call(
        functools.partial(part_kernel, n_grp, wire, other),
        grid=(1,),
        in_specs=[
            SMEM,
            pl.BlockSpec((peers, wire.half, LANES), lambda i: (0, which, 0)),
            pl.BlockSpec(ids.shape, lambda i: (0, 0, 0)),
        ]
        + [pl.BlockSpec(memory_space=pl.ANY)] * len(after),
        out_specs=pl.BlockSpec(shape, lambda i: (0, 0, 0, 0)),
        out_shape=jax.ShapeDtypeStruct(shape, BF16 if other else F32),
        scratch_shapes=[pltpu.VMEM((peers * LANES, 256), BF16)],
        compiler_params=params(),
        cost_estimate=cost(1),
        name="part_other" if other else "part_own",
    )(half, seen, ids, *after)


def take_kernel(place, tables, out):
    out[...] = tables[...]


def take_tables(place, tables_t):
    rows, lanes = tables_t.shape[1:]
    return pl.pallas_call(
        take_kernel,
        grid_spec=pltpu.PrefetchScalarGridSpec(
            num_scalar_prefetch=1,
            grid=(1,),
            in_specs=[pl.BlockSpec((TILE, rows, lanes), lambda i, place: (place[0], 0, 0))],
            out_specs=pl.BlockSpec((TILE, rows, lanes), lambda i, place: (0, 0, 0)),
        ),
        out_shape=jax.ShapeDtypeStruct((TILE, rows, lanes), BF16),
        compiler_params=params(2),
        cost_estimate=cost(1),
        name="take_tables",
    )(place, tables_t)


def stack_kernel(half_ref, mine_t, crossed_t, out):
    half = half_ref[0]
    for f in range(TILE):
        at = f * LANES
        for side, ref in ((half, mine_t), (1 - half, crossed_t)):
            out[side, 0:192, at : at + LANES] = ref[f]
            out[side, 192:256, at : at + LANES] = ref[f, 128:192]


def stack_tables(half, mine_t, crossed_t):
    return pl.pallas_call(
        stack_kernel,
        in_specs=[SMEM, VMEM, VMEM],
        out_specs=VMEM,
        out_shape=jax.ShapeDtypeStruct((2, 256, TILE * LANES), BF16),
        compiler_params=params(),
        cost_estimate=cost(100),
        name="stack_tables",
    )(half, mine_t, crossed_t)


def lookup_kernel(wire, stacked, ids_ref, out):
    peers = out.shape[0]
    ids = ids_ref[...].reshape(peers * 16, LANES)
    keys = ids.T
    rows = peers * wire.left
    lane = lax.broadcasted_iota(jnp.int32, (1, LANES), 1).astype(F32)
    feature = lax.broadcasted_iota(jnp.int32, (rows, LANES), 0) % TILE
    masks = [jnp.where(feature == f, 1.0, 0.0).astype(BF16) for f in range(TILE)]
    for which in range(2):
        same = []
        for peer in range(peers):
            at = peer * 16 + 14 + which
            same.append(jnp.where(keys[0 : wire.left, at : at + 1] == lane, 1.0, 0.0))
        same = jnp.concatenate(same, axis=0).astype(BF16)
        hit = jnp.concatenate([same * mask for mask in masks], axis=1)
        both = mm_nt(hit, stacked[which])
        for peer in range(peers):
            got = both[peer * wire.left : (peer + 1) * wire.left]
            base = wire.back_left[which]
            out[peer, base : base + wire.left] = got[:, 0:128].astype(BF16)
            packed = []
            for i in range(wire.left // 32):
                first, second = got[32 * i : 32 * i + 16, 128:256], got[32 * i + 16 : 32 * i + 32, 128:256]
                packed.append(jnp.where(low_lanes(first.shape), first, second))
            base = wire.back_right[which]
            out[peer, base : base + wire.left // 2] = jnp.concatenate(packed, axis=0).astype(BF16)


def lookup(wire, stacked, ids):
    peers = ids.shape[0]
    some = peers // 2
    return pl.pallas_call(
        functools.partial(lookup_kernel, wire),
        grid=(2,),
        in_specs=[
            pl.BlockSpec(stacked.shape, lambda i: (0, 0, 0)),
            pl.BlockSpec((some, 16, LANES), lambda i: (i, 0, 0)),
        ],
        out_specs=pl.BlockSpec((some, wire.rows, LANES), lambda i: (i, 0, 0)),
        out_shape=pltpu.HBM((peers, wire.rows, LANES), BF16),
        compiler_params=params(),
        cost_estimate=cost(100),
        name="lookup",
    )(stacked, ids)


def fill_kernel(factor, rows, own, seen, out, token):
    token[...] = jnp.zeros_like(token)
    total = ((own[...] + seen[...]) * factor).astype(BF16)
    for peer in range(out.shape[0]):
        out[peer] = total


def fill(wire, factor, rows, own, seen):
    peers = rows.shape[0]

    def whole(shape):
        return pl.BlockSpec(shape, lambda i: (0,) * len(shape))

    return pl.pallas_call(
        functools.partial(fill_kernel, factor),
        grid=(1,),
        in_specs=[pl.BlockSpec(memory_space=pl.ANY), whole(own.shape), whole(seen.shape)],
        out_specs=[whole((peers, wire.share, LANES)), whole((8, LANES))],
        out_shape=[pltpu.HBM(rows.shape, BF16), pltpu.HBM((8, LANES), F32)],
        input_output_aliases={0: 0},
        compiler_params=params(),
        cost_estimate=cost(1),
        name="fill_dense",
    )(rows, own, seen)


def finish_pieces(grp, pieces, out):
    piece = out.shape[1]
    for k, seen in enumerate(pieces):
        base = jnp.bitwise_xor(grp, k) * TILE
        for f in range(TILE):
            out[base + f, :, 0:128] = seen[f, 0:piece].astype(F32)
            packed = seen[f, piece : piece + piece // 2].astype(F32)
            out[base + f, 0 : piece // 2, 128:192] = packed[:, 0:64]
            out[base + f, piece // 2 : piece, 128:192] = turn(packed)[:, 0:64]


def unpack_kernel(n_grp, n_lane, wire, place, dense_ref, left0, left1, right0, right1, *refs):
    pieces, refs = refs[:n_grp], refs[n_grp:]
    rows_out, table_grad, fm, proj_t, lcb, gain, held = refs
    step = pl.program_id(0)
    peers = n_grp * n_lane
    for side, (left_ref, right_ref) in enumerate(((left0, right0), (left1, right1))):
        for q in range(n_lane):
            for gg in range(n_grp // 2):
                left, right = [], []
                for g in (2 * gg, 2 * gg + 1):
                    peer = g * n_lane + q
                    left.append(left_ref[peer].astype(F32))
                    packed = right_ref[peer].astype(F32)
                    right.append(jnp.concatenate([packed, turn(packed)], axis=0))
                at = side * 128 + q * n_grp * TILE + gg * 16
                for s in range(STEP):
                    here = slice(s * TILE, s * TILE + TILE)
                    both = jnp.concatenate([left[0][here], left[1][here]], axis=0)
                    held[s, at : at + 16, 0:128] = both.astype(BF16)
                    both = jnp.concatenate([right[0][here], right[1][here]], axis=0)
                    held[s, at : at + 16, 128:256] = both.astype(BF16)
    eye = identity(192, 256)
    for s in range(STEP):
        rows_out[s] = mm_nt(eye, held[s]).astype(BF16)

    @pl.when(step == 0)
    def _():
        part, third = 256 // peers, 192 // peers
        lane = lax.broadcasted_iota(jnp.int32, (1, LANES), 1)
        behind_ids = (lane >= wire.left) & (lane < wire.left + third)
        total = jnp.zeros((1, 256), F32)
        for peer in range(peers):
            dense = dense_ref[peer].astype(F32)
            here = slice(peer * part, (peer + 1) * part)
            fm[here] = dense[0:part]
            lcb[here, 0:128] = dense[part : 2 * part]
            lcb[here, 128:256] = dense[2 * part : 3 * part]
            last = dense[3 * part : 4 * part]
            proj_t[peer * third : (peer + 1) * third] = last[0:third]
            share = jnp.where(behind_ids, last[third : third + 1] + last[third + 1 : third + 2], 0.0)
            share = jnp.concatenate([share, jnp.zeros((1, LANES), F32)], axis=1)
            total += pltpu.roll(share, (peer * third - wire.left) % 256, 1)
        gain[...] = total[:, 0:192]

    @pl.when(step == pl.num_programs(0) - 1)
    def _():
        finish_pieces(place[0], pieces, table_grad)


def unpack(n_grp, n_lane, wire, count, place, seen, pieces):
    def whole(*shape):
        return pl.BlockSpec(shape, lambda i: (0,) * len(shape))

    def part(rows, start):
        return pl.BlockSpec((peers, rows, LANES), lambda i: (0, start // rows + i, 0))

    peers = n_grp * n_lane
    shapes = [(n_grp * TILE, pieces[0].shape[1] * 2 // 3, 192), (256, 128), (192, 128), (256, 256), (1, 192)]
    return pl.pallas_call(
        functools.partial(unpack_kernel, n_grp, n_lane, wire),
        grid=(count // STEP,),
        in_specs=[SMEM, pl.BlockSpec((peers, wire.share, LANES), lambda i: (0, 0, 0))]
        + [part(32, start) for start in wire.back_left]
        + [part(16, start) for start in wire.back_right]
        + [whole(*piece.shape) for piece in pieces],
        out_specs=[pl.BlockSpec((STEP, 192, 256), lambda i: (i, 0, 0))] + [whole(*shape) for shape in shapes],
        out_shape=[jax.ShapeDtypeStruct((count, 192, 256), BF16)]
        + [jax.ShapeDtypeStruct(shape, F32) for shape in shapes],
        scratch_shapes=[pltpu.VMEM((STEP, 256, 256), BF16)],
        compiler_params=params(),
        cost_estimate=cost(1),
        name="unpack",
    )(place, seen, seen, seen, seen, seen, *pieces)


def combine_kernel(place, own, seen, after, *outs):
    for k, out in enumerate(outs):
        g = jnp.bitwise_xor(place[0], k)
        out[...] = (own[g] + seen[g].astype(F32)).astype(BF16)


def combine(place, own, seen, after):
    n_grp = own.shape[0]
    shape = jax.ShapeDtypeStruct(own.shape[1:], BF16)
    return pl.pallas_call(
        combine_kernel,
        in_specs=[SMEM, VMEM, VMEM, pl.BlockSpec(memory_space=pl.ANY)],
        out_specs=[VMEM] * n_grp,
        out_shape=[shape] * n_grp,
        compiler_params=params(),
        cost_estimate=cost(100),
        name="combine",
    )(place, own, seen, after)


def cross(array):
    return lax.ppermute(array, "half", [(0, 1), (1, 0)])


def halves(pooled, upstream, ids_now, ids_next, tables, w_fm, w_proj, w_lcb, gain):
    n_grp, n_lane = lax.axis_size("grp"), lax.axis_size("lane")
    count = pooled.shape[0]
    wire = Wire(count, n_grp * n_lane)
    factor = 1.0 / (count * n_grp * 2 * n_lane)
    half = lax.axis_index("half").astype(jnp.int32)[None]
    grp = lax.axis_index("grp").astype(jnp.int32)
    mine_t = take_tables(grp[None], tables.transpose(0, 2, 1))
    crossed_t = cross(mine_t)
    sent = backward(
        n_grp, n_lane, wire, half,
        pooled.transpose(0, 2, 1), upstream.transpose(0, 2, 1), ids_now, ids_next, w_fm, w_proj.T, w_lcb, gain,
    )
    seen = exchange(sent, PEER)
    dense, ids = half_dense(wire, seen)
    dense_seen = cross(dense)
    part_seen = cross(part_sums(n_grp, wire, True, half, seen, ids))
    rows_wire = lookup(wire, stack_tables(half, mine_t, crossed_t), ids)
    rows_wire, token = fill(wire, factor, rows_wire, dense, dense_seen)
    rows = exchange(rows_wire, PEER)
    own = part_sums(n_grp, wire, False, half, seen, ids, token)
    pieces = combine(grp[None], own, part_seen, token)
    pieces = [pieces[0]] + [
        lax.ppermute(pieces[k], "grp", [(g, g ^ k) for g in range(n_grp)]) for k in range(1, n_grp)
    ]
    next_rows, table_grad, grad_fm, grad_proj_t, grad_lcb, grad_gain = unpack(
        n_grp, n_lane, wire, count, grp[None], rows, pieces
    )
    return next_rows.transpose(0, 2, 1), table_grad, grad_fm, grad_proj_t.T, grad_lcb, grad_gain.reshape(-1)


def solution(mesh):
    n_grp, n_emb = mesh.shape["grp"], mesh.shape["emb"]
    split = n_emb % 2 == 0 and n_grp * (n_emb // 2) == 16 and n_grp % 2 == 0

    def run(*args):
        pooled, _, _, _, tables, w_fm = args[:6]
        count = pooled.shape[0] // (n_grp * n_emb)
        fits = (
            split
            and pooled.shape[1:] == (256, 192)
            and tables.shape[1] == 128
            and w_fm.shape[1] == 128
            and pooled.shape[1] == n_grp * n_emb * TILE
            and count % STEP == 0
            and count <= 12
        )
        if fits:
            devices = mesh.devices.reshape(n_grp, 2, n_emb // 2)
            where, emb, body = Mesh(devices, ("grp", "half", "lane")), ("half", "lane"), halves
        else:
            where, emb, body = mesh, ("emb",), local
        both = ("grp",) + emb
        return jax.shard_map(
            body,
            mesh=where,
            in_specs=(
                P(both, None, None),
                P(both, None, None),
                P(both, None),
                P(both, None),
                P(emb, None, None),
                P(),
                P(),
                P(),
                P(),
            ),
            out_specs=(P(both, None, None), P(emb, "grp", None), P(), P(), P(), P()),
            check_vma=False,
        )(*args)

    return run
```

```python
import functools

import jax
import jax.numpy as jnp
from jax import lax
from jax.experimental import pallas as pl
from jax.experimental.pallas import tpu as pltpu
from jax.sharding import Mesh, PartitionSpec as P

F32, BF16 = jnp.float32, jnp.bfloat16
SMEM = pl.BlockSpec(memory_space=pltpu.SMEM)
VMEM = pl.BlockSpec(memory_space=pltpu.VMEM)
LANES = 128
TILE = 8
STEP = 4
LIMIT = 30 * 1024 * 1024
PEER = ("lane", "grp")


BOTH = ("grp", "emb")


def product(form, left, right):
    return jnp.einsum(form, left, right, preferred_element_type=jnp.float32)


def layer_backward(embeds, cotangent, w_fm, w_proj, w_lcb, gain):
    fm_proj = product("bfc,fj->bcj", embeds, w_fm).astype(jnp.bfloat16)
    fm_rows = product("bfc,bcj->bfj", embeds, fm_proj).astype(jnp.bfloat16)
    projected = product("bfj,jc->bfc", fm_rows, w_proj)
    compressed = product("fi,bfc->bic", w_lcb, embeds)
    summed = embeds.astype(jnp.float32) + projected + compressed
    centre = jnp.mean(summed, axis=2, keepdims=True)
    spread = jnp.mean((summed - centre) ** 2, axis=2, keepdims=True)
    inverse = lax.rsqrt(spread + 1e-05)
    normed = (summed - centre) * inverse
    upper = cotangent.astype(jnp.float32)
    scaled = upper * gain
    grad_sum = inverse * (
        scaled
        - jnp.mean(scaled, axis=2, keepdims=True)
        - normed * jnp.mean(scaled * normed, axis=2, keepdims=True)
    )
    grad_sum = grad_sum.astype(jnp.bfloat16)
    grad_gain = jnp.sum(upper * normed, axis=(0, 1))
    grad_proj = product("bfj,bfc->jc", fm_rows, grad_sum)
    grad_rows = product("bfc,jc->bfj", grad_sum, w_proj).astype(jnp.bfloat16)
    grad_p = product("bfc,bfj->bcj", embeds, grad_rows).astype(jnp.bfloat16)
    grad_fm = product("bfc,bcj->fj", embeds, grad_p)
    grad_lcb = product("bfc,bic->fi", embeds, grad_sum)
    grad_in = (
        grad_sum.astype(jnp.float32)
        + product("bfj,bcj->bfc", grad_rows, fm_proj)
        + product("fj,bcj->bfc", w_fm, grad_p)
        + product("fi,bic->bfc", w_lcb, grad_sum)
    )
    return (grad_in.astype(jnp.bfloat16), (grad_fm, grad_proj, grad_lcb, grad_gain))


def exchange(blocks, axes):
    return lax.all_to_all(blocks, axes, split_axis=0, concat_axis=0, tiled=True)


def dense_sum(partials, factor):
    n = lax.axis_size("grp") * lax.axis_size("emb")
    shapes = [part.shape for part in partials]
    flat = jnp.concatenate([part.reshape(-1) for part in partials])
    unit = 128 * n
    padded = -(-flat.shape[0] // unit) * unit
    flat = jnp.pad(flat, (0, padded - flat.shape[0])).astype(jnp.bfloat16)
    seen = exchange(flat.reshape(n, padded // unit, 128), BOTH)
    share = (jnp.sum(seen.astype(jnp.float32), axis=0) * factor).astype(jnp.bfloat16)
    total = exchange(jnp.broadcast_to(share[None], (n,) + share.shape), BOTH).reshape(-1)
    total = total.astype(jnp.float32)
    outs, at = [], 0
    for shape in shapes:
        size = 1
        for extent in shape:
            size *= extent
        outs.append(total[at : at + size].reshape(shape))
        at += size
    return outs


def local(pooled, upstream, ids_now, ids_next, tables, w_fm, w_proj, w_lcb, gain):
    n_grp, n_emb = lax.axis_size("grp"), lax.axis_size("emb")
    count, features, width = pooled.shape
    owned, rows = tables.shape[:2]
    ids = jnp.stack([ids_now, ids_next]).reshape(2, count, n_emb, owned)
    ids = exchange(ids.transpose(2, 0, 1, 3), "emb")
    row_index = jnp.arange(rows)
    wanted = (ids[:, 1, :, :, None] == row_index).astype(jnp.bfloat16)
    fetched = product("esfr,frc->esfc", wanted, tables).astype(jnp.bfloat16)
    next_rows = exchange(fetched, "emb")
    next_rows = next_rows.transpose(1, 0, 2, 3).reshape(count, features, width)
    grad_in, partials = layer_backward(pooled, upstream, w_fm, w_proj, w_lcb, gain)
    grad_in = grad_in.reshape(count, n_emb, owned, width).transpose(1, 0, 2, 3)
    grads = exchange(grad_in, "emb")
    hit = (ids[:, 0, :, :, None] == row_index).astype(jnp.bfloat16)
    part = product("esfr,esfc->frc", hit, grads).astype(jnp.bfloat16)
    part = part.reshape(owned, n_grp, rows // n_grp, width).transpose(1, 0, 2, 3)
    table_grad = jnp.sum(exchange(part, "grp").astype(jnp.float32), axis=0)
    dense = dense_sum(partials, 1.0 / (count * n_grp * n_emb))
    return (next_rows, table_grad, *dense)


def params(share=1):
    return pltpu.CompilerParams(vmem_limit_bytes=share * LIMIT)


def cost(weight):
    return pl.CostEstimate(flops=weight * 10**9, bytes_accessed=10**5, transcendentals=0)


def mm(left, right, dims=((1,), (0,))):
    return lax.dot_general(left, right, (dims, ((), ())), preferred_element_type=F32)


def mm_nt(left, right):
    return mm(left, right, ((1,), (1,)))


def low_lanes(shape):
    return lax.broadcasted_iota(jnp.int32, shape, 1) < LANES // 2


def turn(tile):
    return pltpu.roll(tile, LANES // 2, 1)


def identity(rows, lanes):
    row = lax.broadcasted_iota(jnp.int32, (rows, lanes), 0)
    return jnp.where(row == lax.broadcasted_iota(jnp.int32, (rows, lanes), 1), 1.0, 0.0).astype(BF16)


class Wire:
    def __init__(self, count, peers):
        self.left = count * TILE
        self.half = self.left + self.left // 2
        self.dense = 2 * self.half
        self.share = 1024 // peers
        self.rows = self.dense + self.share
        self.back_left = (self.share, self.share + self.left)
        self.back_right = (self.share + 2 * self.left, self.share + 2 * self.left + self.left // 2)


def place_of(peer):
    return peer * TILE


def backward_kernel(
    n_grp, n_lane, wire,
    half_ref, x_ref, u_any, now_ref, next_ref, fm_ref, proj_t_ref, lcb_ref, gain_ref,
    out_any,
    fm_t, proj, lcb_t, gains, eye, mixed, p_t, g_t, d_sum, d_p_t, left_in, right_in, grads, turned, ids,
    u_ref, out_ref, sems,
):
    count, width, features = x_ref.shape
    rank = fm_ref.shape[1]
    peers = n_grp * n_lane
    scale = 1.0 / width
    load = pltpu.make_async_copy(u_any, u_ref, sems.at[0])
    load.start()

    turned_fm = fm_ref[...].astype(F32).T.astype(BF16)
    fm_t[...] = turned_fm
    proj[...] = proj_t_ref[...].astype(F32).T.astype(BF16)
    lcb_t[...] = lcb_ref[...].astype(F32).T.astype(BF16)
    column = jnp.broadcast_to(gain_ref[...], (LANES, width)).T
    gains[:, 0:128] = column
    gains[:, 128:256] = column
    eye[...] = identity(features, features)
    sum_gain, sum_fm_t, sum_proj_t = [], [], []

    def project(s):
        p_t[s] = mm_nt(fm_t[...], x_ref[s]).astype(BF16)
        right_in[s, rank : 2 * rank] = fm_t[...]

    def interact(s):
        g_t[s] = mm(p_t[s], x_ref[s]).astype(BF16)

    def add_up(s):
        mixed[s] = mixed[s] + mm(proj_t_ref[...], g_t[s])

    def normalise(s):
        summed = x_ref[s].astype(F32) + mixed[s]
        centre = jnp.sum(summed, axis=0, keepdims=True) * scale
        summed = summed - centre
        spread = jnp.sum(summed * summed, axis=0, keepdims=True) * scale
        inverse = lax.rsqrt(spread + 1e-05)
        normed = summed * inverse
        upper = u_ref[s].astype(F32)
        scaled = upper * gains[...]
        first = jnp.sum(scaled, axis=0, keepdims=True) * scale
        second = jnp.sum(scaled * normed, axis=0, keepdims=True) * scale
        d_sum[s] = (inverse * (scaled - first - normed * second)).astype(BF16)
        product_gain = upper * normed
        sum_gain.append(product_gain[:, 0:128] + product_gain[:, 128:256])

    def back_rows(s):
        right_in[s, 0:rank] = mm(proj[...], d_sum[s]).astype(BF16)

    def back_project(s):
        left_in[s, :, rank : 2 * rank] = mm_nt(x_ref[s], right_in[s, 0:rank]).astype(BF16)
        d_p_t[s] = mm_nt(right_in[s, 0:rank], x_ref[s]).astype(BF16)

    def gather(s):
        grad = d_sum[s].astype(F32) + mm(d_sum[s], lcb_t[...]) + mm(left_in[s], right_in[s])
        grad = grad.astype(BF16)
        group, k = s // STEP, s % STEP
        grads[group, k * 128 : k * 128 + 128] = grad[0:128]
        at = 512 + 64 * (2 * (k % 2) + k // 2)
        grads[group, at : at + 64] = grad[128:192]
        sum_fm_t.append(mm(d_p_t[s], x_ref[s]))
        sum_proj_t.append(mm_nt(d_sum[s], g_t[s]))

    x_all = x_ref[...].reshape(count * width, features)
    left_in[:, :, 0:rank] = mm(x_all, fm_ref[...]).astype(BF16).reshape(count, width, rank)
    mixed[...] = mm(x_all, lcb_ref[...]).reshape(count, width, features)
    ahead, behind = range(count // 2), range(count // 2, count)
    for stage in (project, interact, add_up):
        for s in ahead:
            stage(s)
    load.wait()
    for one, other in zip(ahead, behind):
        normalise(one)
        project(other)
    for one, other in zip(ahead, behind):
        back_rows(one)
        interact(other)
    for one, other in zip(ahead, behind):
        back_project(one)
        add_up(other)
    for one, other in zip(ahead, behind):
        gather(one)
        normalise(other)
    for stage in (back_rows, back_project, gather):
        for s in behind:
            stage(s)
    sum_gain, sum_fm_t, sum_proj_t = sum(sum_gain), sum(sum_fm_t), sum(sum_proj_t)

    half = half_ref[0]
    for group in range(count // STEP):
        rows = mm_nt(eye[...], grads[group])
        turned[group, 0] = rows[0:128]
        turned[group, 1] = rows[128:256]
    for group in range(count // STEP):
        for side, base in ((1 - half, 0), (half, wire.half)):
            for peer in range(peers):
                at = place_of(peer)
                line = turned[group, side, at : at + TILE]
                left = jnp.concatenate([line[:, k * 128 : k * 128 + 128] for k in range(STEP)], axis=0)
                row = base + group * 32
                out_ref[peer, row : row + 32] = left.astype(BF16)
                right = jnp.concatenate([line[:, 512:640], line[:, 640:768]], axis=0)
                row = base + wire.left + group * 16
                out_ref[peer, row : row + 16] = right.astype(BF16)

    first_store = pltpu.make_async_copy(
        out_ref.at[:, 0 : wire.dense], out_any.at[:, 0 : wire.dense], sems.at[1]
    )
    first_store.start()

    sum_lcb = mm(x_all, d_sum[...].reshape(count * width, features), ((0,), (0,)))
    part = features // peers
    third = width // peers
    total = jnp.sum(sum_gain.T, axis=0, keepdims=True)
    high = total.astype(BF16).astype(F32)
    shares = jnp.concatenate([high, total - high, jnp.zeros((2, width), F32)], axis=0)
    shares = jnp.concatenate([shares, jnp.zeros((4, 256 - width), F32)], axis=1)

    lane = lax.broadcasted_iota(jnp.int32, (16, LANES), 1)
    sample = lax.broadcasted_iota(jnp.int32, (16, LANES), 0)
    mine = (lane // TILE == sample) & (sample < count)
    behind_ids = (lane[0:4] >= wire.left) & (lane[0:4] < wire.left + third)
    spread_ids = []
    for which, ref in enumerate((now_ref, next_ref)):
        ids[which] = jnp.zeros_like(ids[which])
        ids[which, 0:count] = ref[...].astype(F32)
        for side in range(2):
            line = ids[which, :, side * 128 : side * 128 + 128]
            spread_ids.append(pltpu.roll(line, 0, 1, stride=TILE, stride_axis=0))
    sum_fm = sum_fm_t.T
    for peer in range(peers):
        at = wire.dense
        here = slice(peer * part, (peer + 1) * part)
        out_ref[peer, at : at + part] = sum_fm[here].astype(BF16)
        out_ref[peer, at + part : at + 2 * part] = sum_lcb[here, 0:128].astype(BF16)
        out_ref[peer, at + 2 * part : at + 3 * part] = sum_lcb[here, 128:256].astype(BF16)
        place = place_of(peer)
        lines = []
        for line in spread_ids:
            line = pltpu.roll(line, LANES - place, 1) if place else line
            lines.append(jnp.sum(jnp.where(mine, line, 0.0), axis=0, keepdims=True))
        share = pltpu.roll(shares, (wire.left - peer * third) % 256, 1)[:, 0:128]
        lines = jnp.where(behind_ids, share, jnp.concatenate(lines, axis=0))
        last = jnp.concatenate([sum_proj_t[peer * third : (peer + 1) * third], lines], axis=0)
        out_ref[peer, at + 3 * part : at + 4 * part] = last.astype(BF16)
    second_store = pltpu.make_async_copy(
        out_ref.at[:, wire.dense : wire.rows], out_any.at[:, wire.dense : wire.rows], sems.at[2]
    )
    second_store.start()
    first_store.wait()
    second_store.wait()


def backward(n_grp, n_lane, wire, half, pooled_t, upstream_t, ids_now, ids_next, w_fm, w_proj_t, w_lcb, gain):
    count, width, features = pooled_t.shape
    rank = w_fm.shape[1]
    peers = n_grp * n_lane

    def whole(shape):
        return pl.BlockSpec(shape, lambda i: (0,) * len(shape))

    operands = (pooled_t, upstream_t, ids_now, ids_next, w_fm, w_proj_t, w_lcb, gain.reshape(1, width))
    shape = (peers, wire.rows, LANES)
    free = pl.BlockSpec(memory_space=pl.ANY)
    return pl.pallas_call(
        functools.partial(backward_kernel, n_grp, n_lane, wire),
        grid=(1,),
        in_specs=[SMEM, whole(pooled_t.shape), free] + [whole(array.shape) for array in operands[2:]],
        out_specs=free,
        out_shape=pltpu.HBM(shape, BF16),
        scratch_shapes=[
            pltpu.VMEM((rank, features), BF16),
            pltpu.VMEM((rank, width), BF16),
            pltpu.VMEM((features, features), BF16),
            pltpu.VMEM((width, features), F32),
            pltpu.VMEM((features, features), BF16),
            pltpu.VMEM((count, width, features), F32),
            pltpu.VMEM((count, rank, width), BF16),
            pltpu.VMEM((count, rank, features), BF16),
            pltpu.VMEM((count, width, features), BF16),
            pltpu.VMEM((count, rank, width), BF16),
            pltpu.VMEM((count, width, 2 * rank), BF16),
            pltpu.VMEM((count, 2 * rank, features), BF16),
            pltpu.VMEM((count // STEP, STEP * width, features), BF16),
            pltpu.VMEM((count // STEP, 2, features // 2, STEP * width), F32),
            pltpu.VMEM((2, 16, features), F32),
            pltpu.VMEM(upstream_t.shape, BF16),
            pltpu.VMEM(shape, BF16),
            pltpu.SemaphoreType.DMA((3,)),
        ],
        compiler_params=params(2),
        cost_estimate=cost(1),
        name="layer_backward",
    )(half, *operands)


def dense_kernel(dense_ref, ids_ref, dense, all_ids):
    total = dense_ref[0].astype(F32)
    for peer in range(1, dense_ref.shape[0]):
        total = total + dense_ref[peer].astype(F32)
    dense[...] = total
    all_ids[...] = ids_ref[...].astype(F32)


def half_dense(wire, seen):
    peers = seen.shape[0]
    rows = wire.share // 2
    at_ids = wire.rows // 16 - 1
    return pl.pallas_call(
        dense_kernel,
        grid=(2,),
        in_specs=[
            pl.BlockSpec((peers, rows, LANES), lambda i: (0, wire.dense // rows + i, 0)),
            pl.BlockSpec((peers, 16, LANES), lambda i: (0, at_ids, 0)),
        ],
        out_specs=[
            pl.BlockSpec((rows, LANES), lambda i: (i, 0)),
            pl.BlockSpec((peers, 16, LANES), lambda i: (0, 0, 0)),
        ],
        out_shape=[
            jax.ShapeDtypeStruct((wire.share, LANES), F32),
            jax.ShapeDtypeStruct((peers, 16, LANES), F32),
        ],
        compiler_params=params(),
        cost_estimate=cost(1),
        name="half_dense",
    )(seen, seen)


def part_kernel(n_grp, wire, other, half_ref, seen, all_ids, *refs):
    out, held = refs[-2:]
    peers = seen.shape[0]
    half = 1 - half_ref[0] if other else half_ref[0]
    lane = lax.broadcasted_iota(jnp.int32, (1, LANES), 1)
    start = ((lane % TILE) * LANES).astype(F32)
    keys = []
    for peer in range(peers):
        at = peer * LANES
        held[at : at + wire.left, 0:128] = seen[peer, 0 : wire.left]
        right = seen[peer, wire.left : wire.half]
        turned = turn(right.astype(F32)).astype(BF16)
        for i in range(wire.left // 32):
            held[at + 32 * i : at + 32 * i + 16, 128:256] = right[16 * i : 16 * i + 16]
            held[at + 32 * i + 16 : at + 32 * i + 32, 128:256] = turned[16 * i : 16 * i + 16]
        if wire.left < LANES:
            held[at + wire.left : at + LANES] = jnp.zeros((LANES - wire.left, 256), BF16)
        ids = all_ids[peer]
        key = jnp.where(half == 0, ids[12:13], ids[13:14]) + start
        keys.append(jnp.where(lane < wire.left, key, -1.0))
    keys = jnp.concatenate(keys, axis=1)
    piece = LANES // n_grp
    for pair in range(TILE // 2):
        row = lax.broadcasted_iota(jnp.int32, (256, 1), 0).astype(F32) + 256.0 * pair
        hit = jnp.where(keys == row, 1.0, 0.0).astype(BF16)
        part = mm(hit, held[...])
        for f in range(2):
            for g in range(n_grp):
                at = f * LANES + g * piece
                rows = part[at : at + piece]
                out[g, 2 * pair + f, 0:piece] = rows[:, 0:128].astype(out.dtype)
                second = turn(rows[piece // 2 :, 128:256])
                packed = jnp.where(low_lanes(second.shape), rows[: piece // 2, 128:256], second)
                out[g, 2 * pair + f, piece : piece + piece // 2] = packed.astype(out.dtype)


def part_sums(n_grp, wire, other, half, seen, ids, *after):
    peers = seen.shape[0]
    piece = LANES // n_grp
    shape = (n_grp, TILE, piece + piece // 2, LANES)
    which = 0 if other else 1
    return pl.pallas_call(
        functools.partial(part_kernel, n_grp, wire, other),
        grid=(1,),
        in_specs=[
            SMEM,
            pl.BlockSpec((peers, wire.half, LANES), lambda i: (0, which, 0)),
            pl.BlockSpec(ids.shape, lambda i: (0, 0, 0)),
        ]
        + [pl.BlockSpec(memory_space=pl.ANY)] * len(after),
        out_specs=pl.BlockSpec(shape, lambda i: (0, 0, 0, 0)),
        out_shape=jax.ShapeDtypeStruct(shape, BF16 if other else F32),
        scratch_shapes=[pltpu.VMEM((peers * LANES, 256), BF16)],
        compiler_params=params(),
        cost_estimate=cost(1),
        name="part_other" if other else "part_own",
    )(half, seen, ids, *after)


def take_kernel(place, tables, out):
    out[...] = tables[...]


def take_tables(place, tables_t):
    rows, lanes = tables_t.shape[1:]
    return pl.pallas_call(
        take_kernel,
        grid_spec=pltpu.PrefetchScalarGridSpec(
            num_scalar_prefetch=1,
            grid=(1,),
            in_specs=[pl.BlockSpec((TILE, rows, lanes), lambda i, place: (place[0], 0, 0))],
            out_specs=pl.BlockSpec((TILE, rows, lanes), lambda i, place: (0, 0, 0)),
        ),
        out_shape=jax.ShapeDtypeStruct((TILE, rows, lanes), BF16),
        compiler_params=params(2),
        cost_estimate=cost(1),
        name="take_tables",
    )(place, tables_t)


def stack_kernel(half_ref, mine_t, crossed_t, out):
    half = half_ref[0]
    for f in range(TILE):
        at = f * LANES
        for side, ref in ((half, mine_t), (1 - half, crossed_t)):
            out[side, 0:192, at : at + LANES] = ref[f]
            out[side, 192:256, at : at + LANES] = ref[f, 128:192]


def stack_tables(half, mine_t, crossed_t):
    return pl.pallas_call(
        stack_kernel,
        in_specs=[SMEM, VMEM, VMEM],
        out_specs=VMEM,
        out_shape=jax.ShapeDtypeStruct((2, 256, TILE * LANES), BF16),
        compiler_params=params(),
        cost_estimate=cost(100),
        name="stack_tables",
    )(half, mine_t, crossed_t)


def lookup_kernel(wire, stacked, ids_ref, out):
    peers = out.shape[0]
    ids = ids_ref[...].reshape(peers * 16, LANES)
    keys = ids.T
    rows = peers * wire.left
    lane = lax.broadcasted_iota(jnp.int32, (1, LANES), 1).astype(F32)
    feature = lax.broadcasted_iota(jnp.int32, (rows, LANES), 0) % TILE
    masks = [jnp.where(feature == f, 1.0, 0.0).astype(BF16) for f in range(TILE)]
    for which in range(2):
        same = []
        for peer in range(peers):
            at = peer * 16 + 14 + which
            same.append(jnp.where(keys[0 : wire.left, at : at + 1] == lane, 1.0, 0.0))
        same = jnp.concatenate(same, axis=0).astype(BF16)
        hit = jnp.concatenate([same * mask for mask in masks], axis=1)
        both = mm_nt(hit, stacked[which])
        for peer in range(peers):
            got = both[peer * wire.left : (peer + 1) * wire.left]
            base = wire.back_left[which]
            out[peer, base : base + wire.left] = got[:, 0:128].astype(BF16)
            packed = []
            for i in range(wire.left // 32):
                first, second = got[32 * i : 32 * i + 16, 128:256], got[32 * i + 16 : 32 * i + 32, 128:256]
                packed.append(jnp.where(low_lanes(first.shape), first, second))
            base = wire.back_right[which]
            out[peer, base : base + wire.left // 2] = jnp.concatenate(packed, axis=0).astype(BF16)


def lookup(wire, stacked, ids):
    peers = ids.shape[0]
    some = peers // 2
    return pl.pallas_call(
        functools.partial(lookup_kernel, wire),
        grid=(2,),
        in_specs=[
            pl.BlockSpec(stacked.shape, lambda i: (0, 0, 0)),
            pl.BlockSpec((some, 16, LANES), lambda i: (i, 0, 0)),
        ],
        out_specs=pl.BlockSpec((some, wire.rows, LANES), lambda i: (i, 0, 0)),
        out_shape=pltpu.HBM((peers, wire.rows, LANES), BF16),
        compiler_params=params(),
        cost_estimate=cost(100),
        name="lookup",
    )(stacked, ids)


def fill_kernel(factor, rows, own, seen, out, token):
    token[...] = jnp.zeros_like(token)
    total = ((own[...] + seen[...]) * factor).astype(BF16)
    for peer in range(out.shape[0]):
        out[peer] = total


def fill(wire, factor, rows, own, seen):
    peers = rows.shape[0]

    def whole(shape):
        return pl.BlockSpec(shape, lambda i: (0,) * len(shape))

    return pl.pallas_call(
        functools.partial(fill_kernel, factor),
        grid=(1,),
        in_specs=[pl.BlockSpec(memory_space=pl.ANY), whole(own.shape), whole(seen.shape)],
        out_specs=[whole((peers, wire.share, LANES)), whole((8, LANES))],
        out_shape=[pltpu.HBM(rows.shape, BF16), pltpu.HBM((8, LANES), F32)],
        input_output_aliases={0: 0},
        compiler_params=params(),
        cost_estimate=cost(1),
        name="fill_dense",
    )(rows, own, seen)


def finish_pieces(grp, pieces, out):
    piece = out.shape[1]
    for k, seen in enumerate(pieces):
        base = jnp.bitwise_xor(grp, k) * TILE
        for f in range(TILE):
            out[base + f, :, 0:128] = seen[f, 0:piece].astype(F32)
            packed = seen[f, piece : piece + piece // 2].astype(F32)
            out[base + f, 0 : piece // 2, 128:192] = packed[:, 0:64]
            out[base + f, piece // 2 : piece, 128:192] = turn(packed)[:, 0:64]


def unpack_kernel(n_grp, n_lane, wire, place, dense_ref, left0, left1, right0, right1, *refs):
    pieces, refs = refs[:n_grp], refs[n_grp:]
    rows_out, table_grad, fm, proj_t, lcb, gain, held = refs
    step = pl.program_id(0)
    peers = n_grp * n_lane
    for side, (left_ref, right_ref) in enumerate(((left0, right0), (left1, right1))):
        for q in range(n_lane):
            for gg in range(n_grp // 2):
                left, right = [], []
                for g in (2 * gg, 2 * gg + 1):
                    peer = q * n_grp + g
                    left.append(left_ref[peer].astype(F32))
                    packed = right_ref[peer].astype(F32)
                    right.append(jnp.concatenate([packed, turn(packed)], axis=0))
                at = side * 128 + q * n_grp * TILE + gg * 16
                for s in range(STEP):
                    here = slice(s * TILE, s * TILE + TILE)
                    both = jnp.concatenate([left[0][here], left[1][here]], axis=0)
                    held[s, at : at + 16, 0:128] = both.astype(BF16)
                    both = jnp.concatenate([right[0][here], right[1][here]], axis=0)
                    held[s, at : at + 16, 128:256] = both.astype(BF16)
    eye = identity(192, 256)
    for s in range(STEP):
        rows_out[s] = mm_nt(eye, held[s]).astype(BF16)

    @pl.when(step == 0)
    def _():
        part, third = 256 // peers, 192 // peers
        lane = lax.broadcasted_iota(jnp.int32, (1, LANES), 1)
        behind_ids = (lane >= wire.left) & (lane < wire.left + third)
        total = jnp.zeros((1, 256), F32)
        for peer in range(peers):
            dense = dense_ref[peer].astype(F32)
            here = slice(peer * part, (peer + 1) * part)
            fm[here] = dense[0:part]
            lcb[here, 0:128] = dense[part : 2 * part]
            lcb[here, 128:256] = dense[2 * part : 3 * part]
            last = dense[3 * part : 4 * part]
            proj_t[peer * third : (peer + 1) * third] = last[0:third]
            share = jnp.where(behind_ids, last[third : third + 1] + last[third + 1 : third + 2], 0.0)
            share = jnp.concatenate([share, jnp.zeros((1, LANES), F32)], axis=1)
            total += pltpu.roll(share, (peer * third - wire.left) % 256, 1)
        gain[...] = total[:, 0:192]

    @pl.when(step == pl.num_programs(0) - 1)
    def _():
        finish_pieces(place[0], pieces, table_grad)


def unpack(n_grp, n_lane, wire, count, place, seen, pieces):
    def whole(*shape):
        return pl.BlockSpec(shape, lambda i: (0,) * len(shape))

    def part(rows, start):
        return pl.BlockSpec((peers, rows, LANES), lambda i: (0, start // rows + i, 0))

    peers = n_grp * n_lane
    shapes = [(n_grp * TILE, pieces[0].shape[1] * 2 // 3, 192), (256, 128), (192, 128), (256, 256), (1, 192)]
    return pl.pallas_call(
        functools.partial(unpack_kernel, n_grp, n_lane, wire),
        grid=(count // STEP,),
        in_specs=[SMEM, pl.BlockSpec((peers, wire.share, LANES), lambda i: (0, 0, 0))]
        + [part(32, start) for start in wire.back_left]
        + [part(16, start) for start in wire.back_right]
        + [whole(*piece.shape) for piece in pieces],
        out_specs=[pl.BlockSpec((STEP, 192, 256), lambda i: (i, 0, 0))] + [whole(*shape) for shape in shapes],
        out_shape=[jax.ShapeDtypeStruct((count, 192, 256), BF16)]
        + [jax.ShapeDtypeStruct(shape, F32) for shape in shapes],
        scratch_shapes=[pltpu.VMEM((STEP, 256, 256), BF16)],
        compiler_params=params(),
        cost_estimate=cost(1),
        name="unpack",
    )(place, seen, seen, seen, seen, seen, *pieces)


def combine_kernel(place, own, seen, after, *outs):
    for k, out in enumerate(outs):
        g = jnp.bitwise_xor(place[0], k)
        out[...] = (own[g] + seen[g].astype(F32)).astype(BF16)


def combine(place, own, seen, after):
    n_grp = own.shape[0]
    shape = jax.ShapeDtypeStruct(own.shape[1:], BF16)
    return pl.pallas_call(
        combine_kernel,
        in_specs=[SMEM, VMEM, VMEM, pl.BlockSpec(memory_space=pl.ANY)],
        out_specs=[VMEM] * n_grp,
        out_shape=[shape] * n_grp,
        compiler_params=params(),
        cost_estimate=cost(100),
        name="combine",
    )(place, own, seen, after)


def cross(array):
    return lax.ppermute(array, "half", [(0, 1), (1, 0)])


def halves(pooled, upstream, ids_now, ids_next, tables, w_fm, w_proj, w_lcb, gain):
    n_grp, n_lane = lax.axis_size("grp"), lax.axis_size("lane")
    count = pooled.shape[0]
    wire = Wire(count, n_grp * n_lane)
    factor = 1.0 / (count * n_grp * 2 * n_lane)
    half = lax.axis_index("half").astype(jnp.int32)[None]
    grp = lax.axis_index("grp").astype(jnp.int32)
    mine_t = take_tables(grp[None], tables.transpose(0, 2, 1))
    crossed_t = cross(mine_t)
    sent = backward(
        n_grp, n_lane, wire, half,
        pooled.transpose(0, 2, 1), upstream.transpose(0, 2, 1), ids_now, ids_next, w_fm, w_proj.T, w_lcb, gain,
    )
    seen = exchange(sent, PEER)
    dense, ids = half_dense(wire, seen)
    dense_seen = cross(dense)
    part_seen = cross(part_sums(n_grp, wire, True, half, seen, ids))
    rows_wire = lookup(wire, stack_tables(half, mine_t, crossed_t), ids)
    rows_wire, token = fill(wire, factor, rows_wire, dense, dense_seen)
    rows = exchange(rows_wire, PEER)
    own = part_sums(n_grp, wire, False, half, seen, ids, token)
    pieces = combine(grp[None], own, part_seen, token)
    pieces = [pieces[0]] + [
        lax.ppermute(pieces[k], "grp", [(g, g ^ k) for g in range(n_grp)]) for k in range(1, n_grp)
    ]
    next_rows, table_grad, grad_fm, grad_proj_t, grad_lcb, grad_gain = unpack(
        n_grp, n_lane, wire, count, grp[None], rows, pieces
    )
    return next_rows.transpose(0, 2, 1), table_grad, grad_fm, grad_proj_t.T, grad_lcb, grad_gain.reshape(-1)


def solution(mesh):
    n_grp, n_emb = mesh.shape["grp"], mesh.shape["emb"]
    split = n_emb % 2 == 0 and n_grp * (n_emb // 2) == 16 and n_grp % 2 == 0

    def run(*args):
        pooled, _, _, _, tables, w_fm = args[:6]
        count = pooled.shape[0] // (n_grp * n_emb)
        fits = (
            split
            and pooled.shape[1:] == (256, 192)
            and tables.shape[1] == 128
            and w_fm.shape[1] == 128
            and pooled.shape[1] == n_grp * n_emb * TILE
            and count % STEP == 0
            and count <= 12
        )
        if fits:
            devices = mesh.devices.reshape(n_grp, 2, n_emb // 2)
            where, emb, body = Mesh(devices, ("grp", "half", "lane")), ("half", "lane"), halves
        else:
            where, emb, body = mesh, ("emb",), local
        both = ("grp",) + emb
        return jax.shard_map(
            body,
            mesh=where,
            in_specs=(
                P(both, None, None),
                P(both, None, None),
                P(both, None),
                P(both, None),
                P(emb, None, None),
                P(),
                P(),
                P(),
                P(),
            ),
            out_specs=(P(both, None, None), P(emb, "grp", None), P(), P(), P(), P()),
            check_vma=False,
        )(*args)

    return run
```

```python
import functools

import jax
import jax.numpy as jnp
from jax import lax
from jax.experimental import pallas as pl
from jax.experimental.pallas import tpu as pltpu
from jax.sharding import Mesh, PartitionSpec as P

F32, BF16 = jnp.float32, jnp.bfloat16
SMEM = pl.BlockSpec(memory_space=pltpu.SMEM)
VMEM = pl.BlockSpec(memory_space=pltpu.VMEM)
LANES = 128
TILE = 8
STEP = 4
LIMIT = 30 * 1024 * 1024
LANE = ("deep", "core")
PEER = ("core", "deep", "grp")


BOTH = ("grp", "emb")


def product(form, left, right):
    return jnp.einsum(form, left, right, preferred_element_type=jnp.float32)


def layer_backward(embeds, cotangent, w_fm, w_proj, w_lcb, gain):
    fm_proj = product("bfc,fj->bcj", embeds, w_fm).astype(jnp.bfloat16)
    fm_rows = product("bfc,bcj->bfj", embeds, fm_proj).astype(jnp.bfloat16)
    projected = product("bfj,jc->bfc", fm_rows, w_proj)
    compressed = product("fi,bfc->bic", w_lcb, embeds)
    summed = embeds.astype(jnp.float32) + projected + compressed
    centre = jnp.mean(summed, axis=2, keepdims=True)
    spread = jnp.mean((summed - centre) ** 2, axis=2, keepdims=True)
    inverse = lax.rsqrt(spread + 1e-05)
    normed = (summed - centre) * inverse
    upper = cotangent.astype(jnp.float32)
    scaled = upper * gain
    grad_sum = inverse * (
        scaled
        - jnp.mean(scaled, axis=2, keepdims=True)
        - normed * jnp.mean(scaled * normed, axis=2, keepdims=True)
    )
    grad_sum = grad_sum.astype(jnp.bfloat16)
    grad_gain = jnp.sum(upper * normed, axis=(0, 1))
    grad_proj = product("bfj,bfc->jc", fm_rows, grad_sum)
    grad_rows = product("bfc,jc->bfj", grad_sum, w_proj).astype(jnp.bfloat16)
    grad_p = product("bfc,bfj->bcj", embeds, grad_rows).astype(jnp.bfloat16)
    grad_fm = product("bfc,bcj->fj", embeds, grad_p)
    grad_lcb = product("bfc,bic->fi", embeds, grad_sum)
    grad_in = (
        grad_sum.astype(jnp.float32)
        + product("bfj,bcj->bfc", grad_rows, fm_proj)
        + product("fj,bcj->bfc", w_fm, grad_p)
        + product("fi,bic->bfc", w_lcb, grad_sum)
    )
    return (grad_in.astype(jnp.bfloat16), (grad_fm, grad_proj, grad_lcb, grad_gain))


def exchange(blocks, axes):
    return lax.all_to_all(blocks, axes, split_axis=0, concat_axis=0, tiled=True)


def dense_sum(partials, factor):
    n = lax.axis_size("grp") * lax.axis_size("emb")
    shapes = [part.shape for part in partials]
    flat = jnp.concatenate([part.reshape(-1) for part in partials])
    unit = 128 * n
    padded = -(-flat.shape[0] // unit) * unit
    flat = jnp.pad(flat, (0, padded - flat.shape[0])).astype(jnp.bfloat16)
    seen = exchange(flat.reshape(n, padded // unit, 128), BOTH)
    share = (jnp.sum(seen.astype(jnp.float32), axis=0) * factor).astype(jnp.bfloat16)
    total = exchange(jnp.broadcast_to(share[None], (n,) + share.shape), BOTH).reshape(-1)
    total = total.astype(jnp.float32)
    outs, at = [], 0
    for shape in shapes:
        size = 1
        for extent in shape:
            size *= extent
        outs.append(total[at : at + size].reshape(shape))
        at += size
    return outs


def local(pooled, upstream, ids_now, ids_next, tables, w_fm, w_proj, w_lcb, gain):
    n_grp, n_emb = lax.axis_size("grp"), lax.axis_size("emb")
    count, features, width = pooled.shape
    owned, rows = tables.shape[:2]
    ids = jnp.stack([ids_now, ids_next]).reshape(2, count, n_emb, owned)
    ids = exchange(ids.transpose(2, 0, 1, 3), "emb")
    row_index = jnp.arange(rows)
    wanted = (ids[:, 1, :, :, None] == row_index).astype(jnp.bfloat16)
    fetched = product("esfr,frc->esfc", wanted, tables).astype(jnp.bfloat16)
    next_rows = exchange(fetched, "emb")
    next_rows = next_rows.transpose(1, 0, 2, 3).reshape(count, features, width)
    grad_in, partials = layer_backward(pooled, upstream, w_fm, w_proj, w_lcb, gain)
    grad_in = grad_in.reshape(count, n_emb, owned, width).transpose(1, 0, 2, 3)
    grads = exchange(grad_in, "emb")
    hit = (ids[:, 0, :, :, None] == row_index).astype(jnp.bfloat16)
    part = product("esfr,esfc->frc", hit, grads).astype(jnp.bfloat16)
    part = part.reshape(owned, n_grp, rows // n_grp, width).transpose(1, 0, 2, 3)
    table_grad = jnp.sum(exchange(part, "grp").astype(jnp.float32), axis=0)
    dense = dense_sum(partials, 1.0 / (count * n_grp * n_emb))
    return (next_rows, table_grad, *dense)


def params(share=1):
    return pltpu.CompilerParams(vmem_limit_bytes=share * LIMIT)


def cost(weight):
    return pl.CostEstimate(flops=weight * 10**9, bytes_accessed=10**5, transcendentals=0)


def mm(left, right, dims=((1,), (0,))):
    return lax.dot_general(left, right, (dims, ((), ())), preferred_element_type=F32)


def mm_nt(left, right):
    return mm(left, right, ((1,), (1,)))


def low_lanes(shape):
    return lax.broadcasted_iota(jnp.int32, shape, 1) < LANES // 2


def turn(tile):
    return pltpu.roll(tile, LANES // 2, 1)


def identity(rows, lanes):
    row = lax.broadcasted_iota(jnp.int32, (rows, lanes), 0)
    return jnp.where(row == lax.broadcasted_iota(jnp.int32, (rows, lanes), 1), 1.0, 0.0).astype(BF16)


class Wire:
    def __init__(self, count, peers):
        self.left = count * TILE
        self.half = self.left + self.left // 2
        self.dense = 2 * self.half
        self.share = 1024 // peers
        self.rows = self.dense + self.share
        self.back_left = (self.share, self.share + self.left)
        self.back_right = (self.share + 2 * self.left, self.share + 2 * self.left + self.left // 2)


def place_of(n_grp, n_lane, peer):
    core, deep, g = peer // (n_grp * n_lane // 2), peer // n_grp % (n_lane // 2), peer % n_grp
    return ((deep * 2 + core) * n_grp + g) * TILE


def backward_kernel(
    n_grp, n_lane, wire,
    half_ref, x_ref, u_any, now_ref, next_ref, fm_ref, proj_t_ref, lcb_ref, gain_ref,
    out_any,
    fm_t, proj, lcb_t, gains, eye, mixed, p_t, g_t, d_sum, d_p_t, left_in, right_in, grads, turned, ids,
    u_ref, out_ref, sems,
):
    count, width, features = x_ref.shape
    rank = fm_ref.shape[1]
    peers = n_grp * n_lane
    scale = 1.0 / width
    load = pltpu.make_async_copy(u_any, u_ref, sems.at[0])
    load.start()

    turned_fm = fm_ref[...].astype(F32).T.astype(BF16)
    fm_t[...] = turned_fm
    proj[...] = proj_t_ref[...].astype(F32).T.astype(BF16)
    lcb_t[...] = lcb_ref[...].astype(F32).T.astype(BF16)
    column = jnp.broadcast_to(gain_ref[...], (LANES, width)).T
    gains[:, 0:128] = column
    gains[:, 128:256] = column
    eye[...] = identity(features, features)
    sum_gain, sum_fm_t, sum_proj_t = [], [], []

    def project(s):
        p_t[s] = mm_nt(fm_t[...], x_ref[s]).astype(BF16)
        right_in[s, rank : 2 * rank] = fm_t[...]

    def interact(s):
        g_t[s] = mm(p_t[s], x_ref[s]).astype(BF16)

    def add_up(s):
        mixed[s] = mixed[s] + mm(proj_t_ref[...], g_t[s])

    def normalise(s):
        summed = x_ref[s].astype(F32) + mixed[s]
        centre = jnp.sum(summed, axis=0, keepdims=True) * scale
        summed = summed - centre
        spread = jnp.sum(summed * summed, axis=0, keepdims=True) * scale
        inverse = lax.rsqrt(spread + 1e-05)
        normed = summed * inverse
        upper = u_ref[s].astype(F32)
        scaled = upper * gains[...]
        first = jnp.sum(scaled, axis=0, keepdims=True) * scale
        second = jnp.sum(scaled * normed, axis=0, keepdims=True) * scale
        d_sum[s] = (inverse * (scaled - first - normed * second)).astype(BF16)
        product_gain = upper * normed
        sum_gain.append(product_gain[:, 0:128] + product_gain[:, 128:256])

    def back_rows(s):
        right_in[s, 0:rank] = mm(proj[...], d_sum[s]).astype(BF16)

    def back_project(s):
        left_in[s, :, rank : 2 * rank] = mm_nt(x_ref[s], right_in[s, 0:rank]).astype(BF16)
        d_p_t[s] = mm_nt(right_in[s, 0:rank], x_ref[s]).astype(BF16)

    def gather(s):
        grad = d_sum[s].astype(F32) + mm(d_sum[s], lcb_t[...]) + mm(left_in[s], right_in[s])
        grad = grad.astype(BF16)
        group, k = s // STEP, s % STEP
        grads[group, k * 128 : k * 128 + 128] = grad[0:128]
        at = 512 + 64 * (2 * (k % 2) + k // 2)
        grads[group, at : at + 64] = grad[128:192]
        sum_fm_t.append(mm(d_p_t[s], x_ref[s]))
        sum_proj_t.append(mm_nt(d_sum[s], g_t[s]))

    x_all = x_ref[...].reshape(count * width, features)
    left_in[:, :, 0:rank] = mm(x_all, fm_ref[...]).astype(BF16).reshape(count, width, rank)
    mixed[...] = mm(x_all, lcb_ref[...]).reshape(count, width, features)
    ahead, behind = range(count // 2), range(count // 2, count)
    for stage in (project, interact, add_up):
        for s in ahead:
            stage(s)
    load.wait()
    for one, other in zip(ahead, behind):
        normalise(one)
        project(other)
    for one, other in zip(ahead, behind):
        back_rows(one)
        interact(other)
    for one, other in zip(ahead, behind):
        back_project(one)
        add_up(other)
    for one, other in zip(ahead, behind):
        gather(one)
        normalise(other)
    for stage in (back_rows, back_project, gather):
        for s in behind:
            stage(s)
    sum_gain, sum_fm_t, sum_proj_t = sum(sum_gain), sum(sum_fm_t), sum(sum_proj_t)

    half = half_ref[0]
    for group in range(count // STEP):
        rows = mm_nt(eye[...], grads[group])
        turned[group, 0] = rows[0:128]
        turned[group, 1] = rows[128:256]
    for group in range(count // STEP):
        for side, base in ((1 - half, 0), (half, wire.half)):
            for peer in range(peers):
                at = place_of(n_grp, n_lane, peer)
                line = turned[group, side, at : at + TILE]
                left = jnp.concatenate([line[:, k * 128 : k * 128 + 128] for k in range(STEP)], axis=0)
                row = base + group * 32
                out_ref[peer, row : row + 32] = left.astype(BF16)
                right = jnp.concatenate([line[:, 512:640], line[:, 640:768]], axis=0)
                row = base + wire.left + group * 16
                out_ref[peer, row : row + 16] = right.astype(BF16)

    first_store = pltpu.make_async_copy(
        out_ref.at[:, 0 : wire.dense], out_any.at[:, 0 : wire.dense], sems.at[1]
    )
    first_store.start()

    sum_lcb = mm(x_all, d_sum[...].reshape(count * width, features), ((0,), (0,)))
    part = features // peers
    third = width // peers
    total = jnp.sum(sum_gain.T, axis=0, keepdims=True)
    high = total.astype(BF16).astype(F32)
    shares = jnp.concatenate([high, total - high, jnp.zeros((2, width), F32)], axis=0)
    shares = jnp.concatenate([shares, jnp.zeros((4, 256 - width), F32)], axis=1)

    lane = lax.broadcasted_iota(jnp.int32, (16, LANES), 1)
    sample = lax.broadcasted_iota(jnp.int32, (16, LANES), 0)
    mine = (lane // TILE == sample) & (sample < count)
    behind_ids = (lane[0:4] >= wire.left) & (lane[0:4] < wire.left + third)
    spread_ids = []
    for which, ref in enumerate((now_ref, next_ref)):
        ids[which] = jnp.zeros_like(ids[which])
        ids[which, 0:count] = ref[...].astype(F32)
        for side in range(2):
            line = ids[which, :, side * 128 : side * 128 + 128]
            spread_ids.append(pltpu.roll(line, 0, 1, stride=TILE, stride_axis=0))
    sum_fm = sum_fm_t.T
    for peer in range(peers):
        at = wire.dense
        here = slice(peer * part, (peer + 1) * part)
        out_ref[peer, at : at + part] = sum_fm[here].astype(BF16)
        out_ref[peer, at + part : at + 2 * part] = sum_lcb[here, 0:128].astype(BF16)
        out_ref[peer, at + 2 * part : at + 3 * part] = sum_lcb[here, 128:256].astype(BF16)
        place = place_of(n_grp, n_lane, peer)
        lines = []
        for line in spread_ids:
            line = pltpu.roll(line, LANES - place, 1) if place else line
            lines.append(jnp.sum(jnp.where(mine, line, 0.0), axis=0, keepdims=True))
        share = pltpu.roll(shares, (wire.left - peer * third) % 256, 1)[:, 0:128]
        lines = jnp.where(behind_ids, share, jnp.concatenate(lines, axis=0))
        last = jnp.concatenate([sum_proj_t[peer * third : (peer + 1) * third], lines], axis=0)
        out_ref[peer, at + 3 * part : at + 4 * part] = last.astype(BF16)
    second_store = pltpu.make_async_copy(
        out_ref.at[:, wire.dense : wire.rows], out_any.at[:, wire.dense : wire.rows], sems.at[2]
    )
    second_store.start()
    first_store.wait()
    second_store.wait()


def backward(n_grp, n_lane, wire, half, pooled_t, upstream_t, ids_now, ids_next, w_fm, w_proj_t, w_lcb, gain):
    count, width, features = pooled_t.shape
    rank = w_fm.shape[1]
    peers = n_grp * n_lane

    def whole(shape):
        return pl.BlockSpec(shape, lambda i: (0,) * len(shape))

    operands = (pooled_t, upstream_t, ids_now, ids_next, w_fm, w_proj_t, w_lcb, gain.reshape(1, width))
    shape = (peers, wire.rows, LANES)
    free = pl.BlockSpec(memory_space=pl.ANY)
    return pl.pallas_call(
        functools.partial(backward_kernel, n_grp, n_lane, wire),
        grid=(1,),
        in_specs=[SMEM, whole(pooled_t.shape), free] + [whole(array.shape) for array in operands[2:]],
        out_specs=free,
        out_shape=pltpu.HBM(shape, BF16),
        scratch_shapes=[
            pltpu.VMEM((rank, features), BF16),
            pltpu.VMEM((rank, width), BF16),
            pltpu.VMEM((features, features), BF16),
            pltpu.VMEM((width, features), F32),
            pltpu.VMEM((features, features), BF16),
            pltpu.VMEM((count, width, features), F32),
            pltpu.VMEM((count, rank, width), BF16),
            pltpu.VMEM((count, rank, features), BF16),
            pltpu.VMEM((count, width, features), BF16),
            pltpu.VMEM((count, rank, width), BF16),
            pltpu.VMEM((count, width, 2 * rank), BF16),
            pltpu.VMEM((count, 2 * rank, features), BF16),
            pltpu.VMEM((count // STEP, STEP * width, features), BF16),
            pltpu.VMEM((count // STEP, 2, features // 2, STEP * width), F32),
            pltpu.VMEM((2, 16, features), F32),
            pltpu.VMEM(upstream_t.shape, BF16),
            pltpu.VMEM(shape, BF16),
            pltpu.SemaphoreType.DMA((3,)),
        ],
        compiler_params=params(2),
        cost_estimate=cost(1),
        name="layer_backward",
    )(half, *operands)


def dense_kernel(dense_ref, ids_ref, dense, all_ids):
    total = dense_ref[0].astype(F32)
    for peer in range(1, dense_ref.shape[0]):
        total = total + dense_ref[peer].astype(F32)
    dense[...] = total
    all_ids[...] = ids_ref[...].astype(F32)


def half_dense(wire, seen):
    peers = seen.shape[0]
    rows = wire.share // 2
    at_ids = wire.rows // 16 - 1
    return pl.pallas_call(
        dense_kernel,
        grid=(2,),
        in_specs=[
            pl.BlockSpec((peers, rows, LANES), lambda i: (0, wire.dense // rows + i, 0)),
            pl.BlockSpec((peers, 16, LANES), lambda i: (0, at_ids, 0)),
        ],
        out_specs=[
            pl.BlockSpec((rows, LANES), lambda i: (i, 0)),
            pl.BlockSpec((peers, 16, LANES), lambda i: (0, 0, 0)),
        ],
        out_shape=[
            jax.ShapeDtypeStruct((wire.share, LANES), F32),
            jax.ShapeDtypeStruct((peers, 16, LANES), F32),
        ],
        compiler_params=params(),
        cost_estimate=cost(1),
        name="half_dense",
    )(seen, seen)


def part_kernel(n_grp, wire, other, half_ref, seen, all_ids, *refs):
    out, held = refs[-2:]
    peers = seen.shape[0]
    half = 1 - half_ref[0] if other else half_ref[0]
    lane = lax.broadcasted_iota(jnp.int32, (1, LANES), 1)
    start = ((lane % TILE) * LANES).astype(F32)
    keys = []
    for peer in range(peers):
        at = peer * LANES
        held[at : at + wire.left, 0:128] = seen[peer, 0 : wire.left]
        right = seen[peer, wire.left : wire.half]
        turned = turn(right.astype(F32)).astype(BF16)
        for i in range(wire.left // 32):
            held[at + 32 * i : at + 32 * i + 16, 128:256] = right[16 * i : 16 * i + 16]
            held[at + 32 * i + 16 : at + 32 * i + 32, 128:256] = turned[16 * i : 16 * i + 16]
        if wire.left < LANES:
            held[at + wire.left : at + LANES] = jnp.zeros((LANES - wire.left, 256), BF16)
        ids = all_ids[peer]
        key = jnp.where(half == 0, ids[12:13], ids[13:14]) + start
        keys.append(jnp.where(lane < wire.left, key, -1.0))
    keys = jnp.concatenate(keys, axis=1)
    piece = LANES // n_grp
    for pair in range(TILE // 2):
        row = lax.broadcasted_iota(jnp.int32, (256, 1), 0).astype(F32) + 256.0 * pair
        hit = jnp.where(keys == row, 1.0, 0.0).astype(BF16)
        part = mm(hit, held[...])
        for f in range(2):
            for g in range(n_grp):
                at = f * LANES + g * piece
                rows = part[at : at + piece]
                out[g, 2 * pair + f, 0:piece] = rows[:, 0:128].astype(out.dtype)
                second = turn(rows[piece // 2 :, 128:256])
                packed = jnp.where(low_lanes(second.shape), rows[: piece // 2, 128:256], second)
                out[g, 2 * pair + f, piece : piece + piece // 2] = packed.astype(out.dtype)


def part_sums(n_grp, wire, other, half, seen, ids, *after):
    peers = seen.shape[0]
    piece = LANES // n_grp
    shape = (n_grp, TILE, piece + piece // 2, LANES)
    which = 0 if other else 1
    return pl.pallas_call(
        functools.partial(part_kernel, n_grp, wire, other),
        grid=(1,),
        in_specs=[
            SMEM,
            pl.BlockSpec((peers, wire.half, LANES), lambda i: (0, which, 0)),
            pl.BlockSpec(ids.shape, lambda i: (0, 0, 0)),
        ]
        + [pl.BlockSpec(memory_space=pl.ANY)] * len(after),
        out_specs=pl.BlockSpec(shape, lambda i: (0, 0, 0, 0)),
        out_shape=jax.ShapeDtypeStruct(shape, BF16 if other else F32),
        scratch_shapes=[pltpu.VMEM((peers * LANES, 256), BF16)],
        compiler_params=params(),
        cost_estimate=cost(1),
        name="part_other" if other else "part_own",
    )(half, seen, ids, *after)


def take_kernel(place, tables, out):
    out[...] = tables[...]


def take_tables(place, tables_t):
    rows, lanes = tables_t.shape[1:]
    return pl.pallas_call(
        take_kernel,
        grid_spec=pltpu.PrefetchScalarGridSpec(
            num_scalar_prefetch=1,
            grid=(1,),
            in_specs=[pl.BlockSpec((TILE, rows, lanes), lambda i, place: (place[0], 0, 0))],
            out_specs=pl.BlockSpec((TILE, rows, lanes), lambda i, place: (0, 0, 0)),
        ),
        out_shape=jax.ShapeDtypeStruct((TILE, rows, lanes), BF16),
        compiler_params=params(2),
        cost_estimate=cost(1),
        name="take_tables",
    )(place, tables_t)


def stack_kernel(half_ref, mine_t, crossed_t, out):
    half = half_ref[0]
    for f in range(TILE):
        at = f * LANES
        for side, ref in ((half, mine_t), (1 - half, crossed_t)):
            out[side, 0:192, at : at + LANES] = ref[f]
            out[side, 192:256, at : at + LANES] = ref[f, 128:192]


def stack_tables(half, mine_t, crossed_t):
    return pl.pallas_call(
        stack_kernel,
        in_specs=[SMEM, VMEM, VMEM],
        out_specs=VMEM,
        out_shape=jax.ShapeDtypeStruct((2, 256, TILE * LANES), BF16),
        compiler_params=params(),
        cost_estimate=cost(100),
        name="stack_tables",
    )(half, mine_t, crossed_t)


def lookup_kernel(wire, stacked, ids_ref, out):
    peers = out.shape[0]
    ids = ids_ref[...].reshape(peers * 16, LANES)
    keys = ids.T
    rows = peers * wire.left
    lane = lax.broadcasted_iota(jnp.int32, (1, LANES), 1).astype(F32)
    feature = lax.broadcasted_iota(jnp.int32, (rows, LANES), 0) % TILE
    masks = [jnp.where(feature == f, 1.0, 0.0).astype(BF16) for f in range(TILE)]
    for which in range(2):
        same = []
        for peer in range(peers):
            at = peer * 16 + 14 + which
            same.append(jnp.where(keys[0 : wire.left, at : at + 1] == lane, 1.0, 0.0))
        same = jnp.concatenate(same, axis=0).astype(BF16)
        hit = jnp.concatenate([same * mask for mask in masks], axis=1)
        both = mm_nt(hit, stacked[which])
        for peer in range(peers):
            got = both[peer * wire.left : (peer + 1) * wire.left]
            base = wire.back_left[which]
            out[peer, base : base + wire.left] = got[:, 0:128].astype(BF16)
            packed = []
            for i in range(wire.left // 32):
                first, second = got[32 * i : 32 * i + 16, 128:256], got[32 * i + 16 : 32 * i + 32, 128:256]
                packed.append(jnp.where(low_lanes(first.shape), first, second))
            base = wire.back_right[which]
            out[peer, base : base + wire.left // 2] = jnp.concatenate(packed, axis=0).astype(BF16)


def lookup(wire, stacked, ids):
    peers = ids.shape[0]
    some = peers // 2
    return pl.pallas_call(
        functools.partial(lookup_kernel, wire),
        grid=(2,),
        in_specs=[
            pl.BlockSpec(stacked.shape, lambda i: (0, 0, 0)),
            pl.BlockSpec((some, 16, LANES), lambda i: (i, 0, 0)),
        ],
        out_specs=pl.BlockSpec((some, wire.rows, LANES), lambda i: (i, 0, 0)),
        out_shape=pltpu.HBM((peers, wire.rows, LANES), BF16),
        compiler_params=params(),
        cost_estimate=cost(100),
        name="lookup",
    )(stacked, ids)


def fill_kernel(factor, rows, own, seen, out, token):
    token[...] = jnp.zeros_like(token)
    total = ((own[...] + seen[...]) * factor).astype(BF16)
    for peer in range(out.shape[0]):
        out[peer] = total


def fill(wire, factor, rows, own, seen):
    peers = rows.shape[0]

    def whole(shape):
        return pl.BlockSpec(shape, lambda i: (0,) * len(shape))

    return pl.pallas_call(
        functools.partial(fill_kernel, factor),
        grid=(1,),
        in_specs=[pl.BlockSpec(memory_space=pl.ANY), whole(own.shape), whole(seen.shape)],
        out_specs=[whole((peers, wire.share, LANES)), whole((8, LANES))],
        out_shape=[pltpu.HBM(rows.shape, BF16), pltpu.HBM((8, LANES), F32)],
        input_output_aliases={0: 0},
        compiler_params=params(),
        cost_estimate=cost(1),
        name="fill_dense",
    )(rows, own, seen)


def finish_pieces(grp, pieces, out):
    piece = out.shape[1]
    for k, seen in enumerate(pieces):
        base = jnp.bitwise_xor(grp, k) * TILE
        for f in range(TILE):
            out[base + f, :, 0:128] = seen[f, 0:piece].astype(F32)
            packed = seen[f, piece : piece + piece // 2].astype(F32)
            out[base + f, 0 : piece // 2, 128:192] = packed[:, 0:64]
            out[base + f, piece // 2 : piece, 128:192] = turn(packed)[:, 0:64]


def unpack_kernel(n_grp, n_lane, wire, place, dense_ref, left0, left1, right0, right1, *refs):
    pieces, refs = refs[:n_grp], refs[n_grp:]
    rows_out, table_grad, fm, proj_t, lcb, gain, held = refs
    step = pl.program_id(0)
    peers = n_grp * n_lane
    for side, (left_ref, right_ref) in enumerate(((left0, right0), (left1, right1))):
        for q in range(n_lane):
            for gg in range(n_grp // 2):
                left, right = [], []
                for g in (2 * gg, 2 * gg + 1):
                    peer = (q % 2 * (n_lane // 2) + q // 2) * n_grp + g
                    left.append(left_ref[peer].astype(F32))
                    packed = right_ref[peer].astype(F32)
                    right.append(jnp.concatenate([packed, turn(packed)], axis=0))
                at = side * 128 + q * n_grp * TILE + gg * 16
                for s in range(STEP):
                    here = slice(s * TILE, s * TILE + TILE)
                    both = jnp.concatenate([left[0][here], left[1][here]], axis=0)
                    held[s, at : at + 16, 0:128] = both.astype(BF16)
                    both = jnp.concatenate([right[0][here], right[1][here]], axis=0)
                    held[s, at : at + 16, 128:256] = both.astype(BF16)
    eye = identity(192, 256)
    for s in range(STEP):
        rows_out[s] = mm_nt(eye, held[s]).astype(BF16)

    @pl.when(step == 0)
    def _():
        part, third = 256 // peers, 192 // peers
        lane = lax.broadcasted_iota(jnp.int32, (1, LANES), 1)
        behind_ids = (lane >= wire.left) & (lane < wire.left + third)
        total = jnp.zeros((1, 256), F32)
        for peer in range(peers):
            dense = dense_ref[peer].astype(F32)
            here = slice(peer * part, (peer + 1) * part)
            fm[here] = dense[0:part]
            lcb[here, 0:128] = dense[part : 2 * part]
            lcb[here, 128:256] = dense[2 * part : 3 * part]
            last = dense[3 * part : 4 * part]
            proj_t[peer * third : (peer + 1) * third] = last[0:third]
            share = jnp.where(behind_ids, last[third : third + 1] + last[third + 1 : third + 2], 0.0)
            share = jnp.concatenate([share, jnp.zeros((1, LANES), F32)], axis=1)
            total += pltpu.roll(share, (peer * third - wire.left) % 256, 1)
        gain[...] = total[:, 0:192]

    @pl.when(step == pl.num_programs(0) - 1)
    def _():
        finish_pieces(place[0], pieces, table_grad)


def unpack(n_grp, n_lane, wire, count, place, seen, pieces):
    def whole(*shape):
        return pl.BlockSpec(shape, lambda i: (0,) * len(shape))

    def part(rows, start):
        return pl.BlockSpec((peers, rows, LANES), lambda i: (0, start // rows + i, 0))

    peers = n_grp * n_lane
    shapes = [(n_grp * TILE, pieces[0].shape[1] * 2 // 3, 192), (256, 128), (192, 128), (256, 256), (1, 192)]
    return pl.pallas_call(
        functools.partial(unpack_kernel, n_grp, n_lane, wire),
        grid=(count // STEP,),
        in_specs=[SMEM, pl.BlockSpec((peers, wire.share, LANES), lambda i: (0, 0, 0))]
        + [part(32, start) for start in wire.back_left]
        + [part(16, start) for start in wire.back_right]
        + [whole(*piece.shape) for piece in pieces],
        out_specs=[pl.BlockSpec((STEP, 192, 256), lambda i: (i, 0, 0))] + [whole(*shape) for shape in shapes],
        out_shape=[jax.ShapeDtypeStruct((count, 192, 256), BF16)]
        + [jax.ShapeDtypeStruct(shape, F32) for shape in shapes],
        scratch_shapes=[pltpu.VMEM((STEP, 256, 256), BF16)],
        compiler_params=params(),
        cost_estimate=cost(1),
        name="unpack",
    )(place, seen, seen, seen, seen, seen, *pieces)


def combine_kernel(place, own, seen, after, *outs):
    for k, out in enumerate(outs):
        g = jnp.bitwise_xor(place[0], k)
        out[...] = (own[g] + seen[g].astype(F32)).astype(BF16)


def combine(place, own, seen, after):
    n_grp = own.shape[0]
    shape = jax.ShapeDtypeStruct(own.shape[1:], BF16)
    return pl.pallas_call(
        combine_kernel,
        in_specs=[SMEM, VMEM, VMEM, pl.BlockSpec(memory_space=pl.ANY)],
        out_specs=[VMEM] * n_grp,
        out_shape=[shape] * n_grp,
        compiler_params=params(),
        cost_estimate=cost(100),
        name="combine",
    )(place, own, seen, after)


def cross(array):
    return lax.ppermute(array, "half", [(0, 1), (1, 0)])


def halves(pooled, upstream, ids_now, ids_next, tables, w_fm, w_proj, w_lcb, gain):
    n_grp, n_lane = lax.axis_size("grp"), lax.axis_size(LANE)
    count = pooled.shape[0]
    wire = Wire(count, n_grp * n_lane)
    factor = 1.0 / (count * n_grp * 2 * n_lane)
    half = lax.axis_index("half").astype(jnp.int32)[None]
    grp = lax.axis_index("grp").astype(jnp.int32)
    mine_t = take_tables(grp[None], tables.transpose(0, 2, 1))
    crossed_t = cross(mine_t)
    sent = backward(
        n_grp, n_lane, wire, half,
        pooled.transpose(0, 2, 1), upstream.transpose(0, 2, 1), ids_now, ids_next, w_fm, w_proj.T, w_lcb, gain,
    )
    seen = exchange(sent, PEER)
    dense, ids = half_dense(wire, seen)
    dense_seen = cross(dense)
    part_seen = cross(part_sums(n_grp, wire, True, half, seen, ids))
    rows_wire = lookup(wire, stack_tables(half, mine_t, crossed_t), ids)
    rows_wire, token = fill(wire, factor, rows_wire, dense, dense_seen)
    rows = exchange(rows_wire, PEER)
    own = part_sums(n_grp, wire, False, half, seen, ids, token)
    pieces = combine(grp[None], own, part_seen, token)
    pieces = [pieces[0]] + [
        lax.ppermute(pieces[k], "grp", [(g, g ^ k) for g in range(n_grp)]) for k in range(1, n_grp)
    ]
    next_rows, table_grad, grad_fm, grad_proj_t, grad_lcb, grad_gain = unpack(
        n_grp, n_lane, wire, count, grp[None], rows, pieces
    )
    return next_rows.transpose(0, 2, 1), table_grad, grad_fm, grad_proj_t.T, grad_lcb, grad_gain.reshape(-1)


def solution(mesh):
    n_grp, n_emb = mesh.shape["grp"], mesh.shape["emb"]
    split = n_emb % 4 == 0 and n_grp * (n_emb // 2) == 16 and n_grp % 2 == 0

    def run(*args):
        pooled, _, _, _, tables, w_fm = args[:6]
        count = pooled.shape[0] // (n_grp * n_emb)
        fits = (
            split
            and pooled.shape[1:] == (256, 192)
            and tables.shape[1] == 128
            and w_fm.shape[1] == 128
            and pooled.shape[1] == n_grp * n_emb * TILE
            and count % STEP == 0
            and count <= 12
        )
        if fits:
            devices = mesh.devices.reshape(n_grp, 2, n_emb // 4, 2)
            where, emb, body = Mesh(devices, ("grp", "half", "deep", "core")), ("half",) + LANE, halves
        else:
            where, emb, body = mesh, ("emb",), local
        both = ("grp",) + emb
        return jax.shard_map(
            body,
            mesh=where,
            in_specs=(
                P(both, None, None),
                P(both, None, None),
                P(both, None),
                P(both, None),
                P(emb, None, None),
                P(),
                P(),
                P(),
                P(),
            ),
            out_specs=(P(both, None, None), P(emb, "grp", None), P(), P(), P(), P()),
            check_vma=False,
        )(*args)

    return run
```

```python
import functools

import jax
import jax.numpy as jnp
from jax import lax
from jax.experimental import pallas as pl
from jax.experimental.pallas import tpu as pltpu
from jax.sharding import Mesh, PartitionSpec as P

F32, BF16 = jnp.float32, jnp.bfloat16
SMEM = pl.BlockSpec(memory_space=pltpu.SMEM)
VMEM = pl.BlockSpec(memory_space=pltpu.VMEM)
LANES = 128
TILE = 8
STEP = 4
LIMIT = 30 * 1024 * 1024
LANE = ("deep", "core")
PEER = ("core", "deep", "grp")


BOTH = ("grp", "emb")


def product(form, left, right):
    return jnp.einsum(form, left, right, preferred_element_type=jnp.float32)


def layer_backward(embeds, cotangent, w_fm, w_proj, w_lcb, gain):
    fm_proj = product("bfc,fj->bcj", embeds, w_fm).astype(jnp.bfloat16)
    fm_rows = product("bfc,bcj->bfj", embeds, fm_proj).astype(jnp.bfloat16)
    projected = product("bfj,jc->bfc", fm_rows, w_proj)
    compressed = product("fi,bfc->bic", w_lcb, embeds)
    summed = embeds.astype(jnp.float32) + projected + compressed
    centre = jnp.mean(summed, axis=2, keepdims=True)
    spread = jnp.mean((summed - centre) ** 2, axis=2, keepdims=True)
    inverse = lax.rsqrt(spread + 1e-05)
    normed = (summed - centre) * inverse
    upper = cotangent.astype(jnp.float32)
    scaled = upper * gain
    grad_sum = inverse * (
        scaled
        - jnp.mean(scaled, axis=2, keepdims=True)
        - normed * jnp.mean(scaled * normed, axis=2, keepdims=True)
    )
    grad_sum = grad_sum.astype(jnp.bfloat16)
    grad_gain = jnp.sum(upper * normed, axis=(0, 1))
    grad_proj = product("bfj,bfc->jc", fm_rows, grad_sum)
    grad_rows = product("bfc,jc->bfj", grad_sum, w_proj).astype(jnp.bfloat16)
    grad_p = product("bfc,bfj->bcj", embeds, grad_rows).astype(jnp.bfloat16)
    grad_fm = product("bfc,bcj->fj", embeds, grad_p)
    grad_lcb = product("bfc,bic->fi", embeds, grad_sum)
    grad_in = (
        grad_sum.astype(jnp.float32)
        + product("bfj,bcj->bfc", grad_rows, fm_proj)
        + product("fj,bcj->bfc", w_fm, grad_p)
        + product("fi,bic->bfc", w_lcb, grad_sum)
    )
    return (grad_in.astype(jnp.bfloat16), (grad_fm, grad_proj, grad_lcb, grad_gain))


def exchange(blocks, axes):
    return lax.all_to_all(blocks, axes, split_axis=0, concat_axis=0, tiled=True)


def dense_sum(partials, factor):
    n = lax.axis_size("grp") * lax.axis_size("emb")
    shapes = [part.shape for part in partials]
    flat = jnp.concatenate([part.reshape(-1) for part in partials])
    unit = 128 * n
    padded = -(-flat.shape[0] // unit) * unit
    flat = jnp.pad(flat, (0, padded - flat.shape[0])).astype(jnp.bfloat16)
    seen = exchange(flat.reshape(n, padded // unit, 128), BOTH)
    share = (jnp.sum(seen.astype(jnp.float32), axis=0) * factor).astype(jnp.bfloat16)
    total = exchange(jnp.broadcast_to(share[None], (n,) + share.shape), BOTH).reshape(-1)
    total = total.astype(jnp.float32)
    outs, at = [], 0
    for shape in shapes:
        size = 1
        for extent in shape:
            size *= extent
        outs.append(total[at : at + size].reshape(shape))
        at += size
    return outs


def local(pooled, upstream, ids_now, ids_next, tables, w_fm, w_proj, w_lcb, gain):
    n_grp, n_emb = lax.axis_size("grp"), lax.axis_size("emb")
    count, features, width = pooled.shape
    owned, rows = tables.shape[:2]
    ids = jnp.stack([ids_now, ids_next]).reshape(2, count, n_emb, owned)
    ids = exchange(ids.transpose(2, 0, 1, 3), "emb")
    row_index = jnp.arange(rows)
    wanted = (ids[:, 1, :, :, None] == row_index).astype(jnp.bfloat16)
    fetched = product("esfr,frc->esfc", wanted, tables).astype(jnp.bfloat16)
    next_rows = exchange(fetched, "emb")
    next_rows = next_rows.transpose(1, 0, 2, 3).reshape(count, features, width)
    grad_in, partials = layer_backward(pooled, upstream, w_fm, w_proj, w_lcb, gain)
    grad_in = grad_in.reshape(count, n_emb, owned, width).transpose(1, 0, 2, 3)
    grads = exchange(grad_in, "emb")
    hit = (ids[:, 0, :, :, None] == row_index).astype(jnp.bfloat16)
    part = product("esfr,esfc->frc", hit, grads).astype(jnp.bfloat16)
    part = part.reshape(owned, n_grp, rows // n_grp, width).transpose(1, 0, 2, 3)
    table_grad = jnp.sum(exchange(part, "grp").astype(jnp.float32), axis=0)
    dense = dense_sum(partials, 1.0 / (count * n_grp * n_emb))
    return (next_rows, table_grad, *dense)


def params(share=1):
    return pltpu.CompilerParams(vmem_limit_bytes=share * LIMIT)


def cost(weight):
    return pl.CostEstimate(flops=weight * 10**9, bytes_accessed=10**5, transcendentals=0)


def mm(left, right, dims=((1,), (0,))):
    return lax.dot_general(left, right, (dims, ((), ())), preferred_element_type=F32)


def mm_nt(left, right):
    return mm(left, right, ((1,), (1,)))


def low_lanes(shape):
    return lax.broadcasted_iota(jnp.int32, shape, 1) < LANES // 2


def turn(tile):
    return pltpu.roll(tile, LANES // 2, 1)


def identity(rows, lanes):
    row = lax.broadcasted_iota(jnp.int32, (rows, lanes), 0)
    return jnp.where(row == lax.broadcasted_iota(jnp.int32, (rows, lanes), 1), 1.0, 0.0).astype(BF16)


class Wire:
    def __init__(self, count, peers):
        self.left = count * TILE
        self.half = self.left + self.left // 2
        self.dense = 2 * self.half
        self.share = 1024 // peers
        self.rows = self.dense + self.share
        self.back_left = (self.share, self.share + self.left)
        self.back_right = (self.share + 2 * self.left, self.share + 2 * self.left + self.left // 2)


def place_of(n_grp, n_lane, peer):
    core, deep, g = peer // (n_grp * n_lane // 2), peer // n_grp % (n_lane // 2), peer % n_grp
    return ((deep * 2 + core) * n_grp + g) * TILE


def backward_kernel(
    n_grp, n_lane, wire,
    half_ref, x_ref, u_any, now_ref, next_ref, fm_ref, proj_t_ref, lcb_ref, gain_ref,
    out_any,
    fm_t, proj, lcb_t, gains, eye, mixed, p_t, g_t, d_sum, d_p_t, left_in, right_in, grads, turned, ids,
    u_ref, out_ref, sems,
):
    count, width, features = x_ref.shape
    rank = fm_ref.shape[1]
    peers = n_grp * n_lane
    scale = 1.0 / width
    load = pltpu.make_async_copy(u_any, u_ref, sems.at[0])
    load.start()

    turned_fm = fm_ref[...].astype(F32).T.astype(BF16)
    fm_t[...] = turned_fm
    proj[...] = proj_t_ref[...].astype(F32).T.astype(BF16)
    lcb_t[...] = lcb_ref[...].astype(F32).T.astype(BF16)
    column = jnp.broadcast_to(gain_ref[...], (LANES, width)).T
    gains[:, 0:128] = column
    gains[:, 128:256] = column
    eye[...] = identity(features, features)
    sum_gain, sum_fm_t, sum_proj_t = [], [], []

    def project(s):
        p_t[s] = mm_nt(fm_t[...], x_ref[s]).astype(BF16)
        right_in[s, rank : 2 * rank] = fm_t[...]

    def interact(s):
        g_t[s] = mm(p_t[s], x_ref[s]).astype(BF16)

    def add_up(s):
        mixed[s] = mixed[s] + mm(proj_t_ref[...], g_t[s])

    def normalise(s):
        summed = x_ref[s].astype(F32) + mixed[s]
        centre = jnp.sum(summed, axis=0, keepdims=True) * scale
        summed = summed - centre
        spread = jnp.sum(summed * summed, axis=0, keepdims=True) * scale
        inverse = lax.rsqrt(spread + 1e-05)
        normed = summed * inverse
        upper = u_ref[s].astype(F32)
        scaled = upper * gains[...]
        first = jnp.sum(scaled, axis=0, keepdims=True) * scale
        second = jnp.sum(scaled * normed, axis=0, keepdims=True) * scale
        d_sum[s] = (inverse * (scaled - first - normed * second)).astype(BF16)
        product_gain = upper * normed
        sum_gain.append(product_gain[:, 0:128] + product_gain[:, 128:256])

    def back_rows(s):
        right_in[s, 0:rank] = mm(proj[...], d_sum[s]).astype(BF16)

    def back_project(s):
        left_in[s, :, rank : 2 * rank] = mm_nt(x_ref[s], right_in[s, 0:rank]).astype(BF16)
        d_p_t[s] = mm_nt(right_in[s, 0:rank], x_ref[s]).astype(BF16)

    def gather(s):
        grad = d_sum[s].astype(F32) + mm(d_sum[s], lcb_t[...]) + mm(left_in[s], right_in[s])
        grad = grad.astype(BF16)
        group, k = s // STEP, s % STEP
        grads[group, k * 128 : k * 128 + 128] = grad[0:128]
        at = 512 + 64 * (2 * (k % 2) + k // 2)
        grads[group, at : at + 64] = grad[128:192]
        sum_fm_t.append(mm(d_p_t[s], x_ref[s]))
        sum_proj_t.append(mm_nt(d_sum[s], g_t[s]))

    x_all = x_ref[...].reshape(count * width, features)
    left_in[:, :, 0:rank] = mm(x_all, fm_ref[...]).astype(BF16).reshape(count, width, rank)
    mixed[...] = mm(x_all, lcb_ref[...]).reshape(count, width, features)
    ahead, behind = range(count // 2), range(count // 2, count)
    for stage in (project, interact, add_up):
        for s in ahead:
            stage(s)
    load.wait()
    for one, other in zip(ahead, behind):
        normalise(one)
        project(other)
    for one, other in zip(ahead, behind):
        back_rows(one)
        interact(other)
    for one, other in zip(ahead, behind):
        back_project(one)
        add_up(other)
    for one, other in zip(ahead, behind):
        gather(one)
        normalise(other)
    for stage in (back_rows, back_project, gather):
        for s in behind:
            stage(s)
    sum_gain, sum_fm_t, sum_proj_t = sum(sum_gain), sum(sum_fm_t), sum(sum_proj_t)

    half = half_ref[0]
    for group in range(count // STEP):
        rows = mm_nt(eye[...], grads[group])
        turned[group, 0] = rows[0:128]
        turned[group, 1] = rows[128:256]
    for group in range(count // STEP):
        for side, base in ((1 - half, 0), (half, wire.half)):
            for peer in range(peers):
                at = place_of(n_grp, n_lane, peer)
                line = turned[group, side, at : at + TILE]
                left = jnp.concatenate([line[:, k * 128 : k * 128 + 128] for k in range(STEP)], axis=0)
                row = base + group * 32
                out_ref[peer, row : row + 32] = left.astype(BF16)
                right = jnp.concatenate([line[:, 512:640], line[:, 640:768]], axis=0)
                row = base + wire.left + group * 16
                out_ref[peer, row : row + 16] = right.astype(BF16)

    first_store = pltpu.make_async_copy(
        out_ref.at[:, 0 : wire.dense], out_any.at[:, 0 : wire.dense], sems.at[1]
    )
    first_store.start()

    sum_lcb = mm(x_all, d_sum[...].reshape(count * width, features), ((0,), (0,)))
    part = features // peers
    third = width // peers
    total = jnp.sum(sum_gain.T, axis=0, keepdims=True)
    high = total.astype(BF16).astype(F32)
    shares = jnp.concatenate([high, total - high, jnp.zeros((2, width), F32)], axis=0)
    shares = jnp.concatenate([shares, jnp.zeros((4, 256 - width), F32)], axis=1)

    lane = lax.broadcasted_iota(jnp.int32, (16, LANES), 1)
    sample = lax.broadcasted_iota(jnp.int32, (16, LANES), 0)
    mine = (lane // TILE == sample) & (sample < count)
    behind_ids = (lane[0:4] >= wire.left) & (lane[0:4] < wire.left + third)
    spread_ids = []
    for which, ref in enumerate((now_ref, next_ref)):
        ids[which] = jnp.zeros_like(ids[which])
        ids[which, 0:count] = ref[...].astype(F32)
        for side in range(2):
            line = ids[which, :, side * 128 : side * 128 + 128]
            spread_ids.append(pltpu.roll(line, 0, 1, stride=TILE, stride_axis=0))
    sum_fm = sum_fm_t.T
    for peer in range(peers):
        at = wire.dense
        here = slice(peer * part, (peer + 1) * part)
        out_ref[peer, at : at + part] = sum_fm[here].astype(BF16)
        out_ref[peer, at + part : at + 2 * part] = sum_lcb[here, 0:128].astype(BF16)
        out_ref[peer, at + 2 * part : at + 3 * part] = sum_lcb[here, 128:256].astype(BF16)
        place = place_of(n_grp, n_lane, peer)
        lines = []
        for line in spread_ids:
            line = pltpu.roll(line, LANES - place, 1) if place else line
            lines.append(jnp.sum(jnp.where(mine, line, 0.0), axis=0, keepdims=True))
        share = pltpu.roll(shares, (wire.left - peer * third) % 256, 1)[:, 0:128]
        lines = jnp.where(behind_ids, share, jnp.concatenate(lines, axis=0))
        last = jnp.concatenate([sum_proj_t[peer * third : (peer + 1) * third], lines], axis=0)
        out_ref[peer, at + 3 * part : at + 4 * part] = last.astype(BF16)
    second_store = pltpu.make_async_copy(
        out_ref.at[:, wire.dense : wire.rows], out_any.at[:, wire.dense : wire.rows], sems.at[2]
    )
    second_store.start()
    first_store.wait()
    second_store.wait()


def backward(n_grp, n_lane, wire, half, pooled_t, upstream_t, ids_now, ids_next, w_fm, w_proj_t, w_lcb, gain):
    count, width, features = pooled_t.shape
    rank = w_fm.shape[1]
    peers = n_grp * n_lane

    def whole(shape):
        return pl.BlockSpec(shape, lambda i: (0,) * len(shape))

    operands = (pooled_t, upstream_t, ids_now, ids_next, w_fm, w_proj_t, w_lcb, gain.reshape(1, width))
    shape = (peers, wire.rows, LANES)
    free = pl.BlockSpec(memory_space=pl.ANY)
    return pl.pallas_call(
        functools.partial(backward_kernel, n_grp, n_lane, wire),
        grid=(1,),
        in_specs=[SMEM, whole(pooled_t.shape), free] + [whole(array.shape) for array in operands[2:]],
        out_specs=free,
        out_shape=pltpu.HBM(shape, BF16),
        scratch_shapes=[
            pltpu.VMEM((rank, features), BF16),
            pltpu.VMEM((rank, width), BF16),
            pltpu.VMEM((features, features), BF16),
            pltpu.VMEM((width, features), F32),
            pltpu.VMEM((features, features), BF16),
            pltpu.VMEM((count, width, features), F32),
            pltpu.VMEM((count, rank, width), BF16),
            pltpu.VMEM((count, rank, features), BF16),
            pltpu.VMEM((count, width, features), BF16),
            pltpu.VMEM((count, rank, width), BF16),
            pltpu.VMEM((count, width, 2 * rank), BF16),
            pltpu.VMEM((count, 2 * rank, features), BF16),
            pltpu.VMEM((count // STEP, STEP * width, features), BF16),
            pltpu.VMEM((count // STEP, 2, features // 2, STEP * width), F32),
            pltpu.VMEM((2, 16, features), F32),
            pltpu.VMEM(upstream_t.shape, BF16),
            pltpu.VMEM(shape, BF16),
            pltpu.SemaphoreType.DMA((3,)),
        ],
        compiler_params=params(2),
        cost_estimate=cost(1),
        name="layer_backward",
    )(half, *operands)


def dense_kernel(dense_ref, ids_ref, dense, all_ids):
    total = dense_ref[0].astype(F32)
    for peer in range(1, dense_ref.shape[0]):
        total = total + dense_ref[peer].astype(F32)
    dense[...] = total
    all_ids[...] = ids_ref[...].astype(F32)


def half_dense(wire, seen):
    peers = seen.shape[0]
    rows = wire.share // 2
    at_ids = wire.rows // 16 - 1
    return pl.pallas_call(
        dense_kernel,
        grid=(2,),
        in_specs=[
            pl.BlockSpec((peers, rows, LANES), lambda i: (0, wire.dense // rows + i, 0)),
            pl.BlockSpec((peers, 16, LANES), lambda i: (0, at_ids, 0)),
        ],
        out_specs=[
            pl.BlockSpec((rows, LANES), lambda i: (i, 0)),
            pl.BlockSpec((peers, 16, LANES), lambda i: (0, 0, 0)),
        ],
        out_shape=[
            jax.ShapeDtypeStruct((wire.share, LANES), F32),
            jax.ShapeDtypeStruct((peers, 16, LANES), F32),
        ],
        compiler_params=params(),
        cost_estimate=cost(1),
        name="half_dense",
    )(seen, seen)


def part_kernel(n_grp, wire, other, half_ref, seen, all_ids, *refs):
    out, held = refs[-2:]
    peers = seen.shape[0]
    half = 1 - half_ref[0] if other else half_ref[0]
    lane = lax.broadcasted_iota(jnp.int32, (1, LANES), 1)
    start = ((lane % TILE) * LANES).astype(F32)
    keys = []
    for peer in range(peers):
        at = peer * LANES
        held[at : at + wire.left, 0:128] = seen[peer, 0 : wire.left]
        right = seen[peer, wire.left : wire.half]
        turned = turn(right.astype(F32)).astype(BF16)
        for i in range(wire.left // 32):
            held[at + 32 * i : at + 32 * i + 16, 128:256] = right[16 * i : 16 * i + 16]
            held[at + 32 * i + 16 : at + 32 * i + 32, 128:256] = turned[16 * i : 16 * i + 16]
        if wire.left < LANES:
            held[at + wire.left : at + LANES] = jnp.zeros((LANES - wire.left, 256), BF16)
        ids = all_ids[peer]
        key = jnp.where(half == 0, ids[12:13], ids[13:14]) + start
        keys.append(jnp.where(lane < wire.left, key, -1.0))
    keys = jnp.concatenate(keys, axis=1)
    piece = LANES // n_grp
    for pair in range(TILE // 2):
        row = lax.broadcasted_iota(jnp.int32, (256, 1), 0).astype(F32) + 256.0 * pair
        hit = jnp.where(keys == row, 1.0, 0.0).astype(BF16)
        part = mm(hit, held[...])
        for f in range(2):
            for g in range(n_grp):
                at = f * LANES + g * piece
                rows = part[at : at + piece]
                out[g, 2 * pair + f, 0:piece] = rows[:, 0:128].astype(out.dtype)
                second = turn(rows[piece // 2 :, 128:256])
                packed = jnp.where(low_lanes(second.shape), rows[: piece // 2, 128:256], second)
                out[g, 2 * pair + f, piece : piece + piece // 2] = packed.astype(out.dtype)


def part_sums(n_grp, wire, other, half, seen, ids, *after):
    peers = seen.shape[0]
    piece = LANES // n_grp
    shape = (n_grp, TILE, piece + piece // 2, LANES)
    which = 0 if other else 1
    return pl.pallas_call(
        functools.partial(part_kernel, n_grp, wire, other),
        grid=(1,),
        in_specs=[
            SMEM,
            pl.BlockSpec((peers, wire.half, LANES), lambda i: (0, which, 0)),
            pl.BlockSpec(ids.shape, lambda i: (0, 0, 0)),
        ]
        + [pl.BlockSpec(memory_space=pl.ANY)] * len(after),
        out_specs=pl.BlockSpec(shape, lambda i: (0, 0, 0, 0)),
        out_shape=jax.ShapeDtypeStruct(shape, BF16 if other else F32),
        scratch_shapes=[pltpu.VMEM((peers * LANES, 256), BF16)],
        compiler_params=params(),
        cost_estimate=cost(1),
        name="part_other" if other else "part_own",
    )(half, seen, ids, *after)


def take_kernel(place, tables, out):
    out[...] = tables[...]


def take_tables(place, tables_t):
    rows, lanes = tables_t.shape[1:]
    return pl.pallas_call(
        take_kernel,
        grid_spec=pltpu.PrefetchScalarGridSpec(
            num_scalar_prefetch=1,
            grid=(1,),
            in_specs=[pl.BlockSpec((TILE, rows, lanes), lambda i, place: (place[0], 0, 0))],
            out_specs=pl.BlockSpec((TILE, rows, lanes), lambda i, place: (0, 0, 0)),
        ),
        out_shape=jax.ShapeDtypeStruct((TILE, rows, lanes), BF16),
        compiler_params=params(2),
        cost_estimate=cost(1),
        name="take_tables",
    )(place, tables_t)


def stack_kernel(half_ref, mine_t, crossed_t, out):
    half = half_ref[0]
    for f in range(TILE):
        at = f * LANES
        for side, ref in ((half, mine_t), (1 - half, crossed_t)):
            out[side, 0:192, at : at + LANES] = ref[f]
            out[side, 192:256, at : at + LANES] = ref[f, 128:192]


def stack_tables(half, mine_t, crossed_t):
    return pl.pallas_call(
        stack_kernel,
        in_specs=[SMEM, VMEM, VMEM],
        out_specs=VMEM,
        out_shape=jax.ShapeDtypeStruct((2, 256, TILE * LANES), BF16),
        compiler_params=params(),
        cost_estimate=cost(100),
        name="stack_tables",
    )(half, mine_t, crossed_t)


def lookup_kernel(wire, stacked, ids_ref, out):
    peers = out.shape[0]
    ids = ids_ref[...].reshape(peers * 16, LANES)
    keys = ids.T
    rows = peers * wire.left
    lane = lax.broadcasted_iota(jnp.int32, (1, LANES), 1).astype(F32)
    feature = lax.broadcasted_iota(jnp.int32, (rows, LANES), 0) % TILE
    masks = [jnp.where(feature == f, 1.0, 0.0).astype(BF16) for f in range(TILE)]
    for which in range(2):
        same = []
        for peer in range(peers):
            at = peer * 16 + 14 + which
            same.append(jnp.where(keys[0 : wire.left, at : at + 1] == lane, 1.0, 0.0))
        same = jnp.concatenate(same, axis=0).astype(BF16)
        hit = jnp.concatenate([same * mask for mask in masks], axis=1)
        both = mm_nt(hit, stacked[which])
        for peer in range(peers):
            got = both[peer * wire.left : (peer + 1) * wire.left]
            base = wire.back_left[which]
            out[peer, base : base + wire.left] = got[:, 0:128].astype(BF16)
            packed = []
            for i in range(wire.left // 32):
                first, second = got[32 * i : 32 * i + 16, 128:256], got[32 * i + 16 : 32 * i + 32, 128:256]
                packed.append(jnp.where(low_lanes(first.shape), first, second))
            base = wire.back_right[which]
            out[peer, base : base + wire.left // 2] = jnp.concatenate(packed, axis=0).astype(BF16)


def lookup(wire, stacked, ids):
    peers = ids.shape[0]
    some = peers // 2
    return pl.pallas_call(
        functools.partial(lookup_kernel, wire),
        grid=(2,),
        in_specs=[
            pl.BlockSpec(stacked.shape, lambda i: (0, 0, 0)),
            pl.BlockSpec((some, 16, LANES), lambda i: (i, 0, 0)),
        ],
        out_specs=pl.BlockSpec((some, wire.rows, LANES), lambda i: (i, 0, 0)),
        out_shape=pltpu.HBM((peers, wire.rows, LANES), BF16),
        compiler_params=params(),
        cost_estimate=cost(100),
        name="lookup",
    )(stacked, ids)


def fill_kernel(factor, rows, own, seen, out, token):
    token[...] = jnp.zeros_like(token)
    total = ((own[...] + seen[...]) * factor).astype(BF16)
    for peer in range(out.shape[0]):
        out[peer] = total


def fill(wire, factor, rows, own, seen):
    peers = rows.shape[0]

    def whole(shape):
        return pl.BlockSpec(shape, lambda i: (0,) * len(shape))

    return pl.pallas_call(
        functools.partial(fill_kernel, factor),
        grid=(1,),
        in_specs=[pl.BlockSpec(memory_space=pl.ANY), whole(own.shape), whole(seen.shape)],
        out_specs=[whole((peers, wire.share, LANES)), whole((8, LANES))],
        out_shape=[pltpu.HBM(rows.shape, BF16), pltpu.HBM((8, LANES), F32)],
        input_output_aliases={0: 0},
        compiler_params=params(),
        cost_estimate=cost(1),
        name="fill_dense",
    )(rows, own, seen)


def far_first(n_grp):
    return [0] + list(range(n_grp - 1, 0, -1))


def finish_pieces(grp, pieces, out):
    piece = out.shape[1]
    for k, seen in zip(far_first(len(pieces)), pieces):
        base = jnp.bitwise_xor(grp, k) * TILE
        for f in range(TILE):
            out[base + f, :, 0:128] = seen[f, 0:piece].astype(F32)
            packed = seen[f, piece : piece + piece // 2].astype(F32)
            out[base + f, 0 : piece // 2, 128:192] = packed[:, 0:64]
            out[base + f, piece // 2 : piece, 128:192] = turn(packed)[:, 0:64]


def unpack_kernel(n_grp, n_lane, wire, place, dense_ref, left0, left1, right0, right1, *refs):
    pieces, refs = refs[:n_grp], refs[n_grp:]
    rows_out, table_grad, fm, proj_t, lcb, gain, held = refs
    step = pl.program_id(0)
    peers = n_grp * n_lane
    for side, (left_ref, right_ref) in enumerate(((left0, right0), (left1, right1))):
        for q in range(n_lane):
            for gg in range(n_grp // 2):
                left, right = [], []
                for g in (2 * gg, 2 * gg + 1):
                    peer = (q % 2 * (n_lane // 2) + q // 2) * n_grp + g
                    left.append(left_ref[peer].astype(F32))
                    packed = right_ref[peer].astype(F32)
                    right.append(jnp.concatenate([packed, turn(packed)], axis=0))
                at = side * 128 + q * n_grp * TILE + gg * 16
                for s in range(STEP):
                    here = slice(s * TILE, s * TILE + TILE)
                    both = jnp.concatenate([left[0][here], left[1][here]], axis=0)
                    held[s, at : at + 16, 0:128] = both.astype(BF16)
                    both = jnp.concatenate([right[0][here], right[1][here]], axis=0)
                    held[s, at : at + 16, 128:256] = both.astype(BF16)
    eye = identity(192, 256)
    for s in range(STEP):
        rows_out[s] = mm_nt(eye, held[s]).astype(BF16)

    @pl.when(step == 0)
    def _():
        part, third = 256 // peers, 192 // peers
        lane = lax.broadcasted_iota(jnp.int32, (1, LANES), 1)
        behind_ids = (lane >= wire.left) & (lane < wire.left + third)
        total = jnp.zeros((1, 256), F32)
        for peer in range(peers):
            dense = dense_ref[peer].astype(F32)
            here = slice(peer * part, (peer + 1) * part)
            fm[here] = dense[0:part]
            lcb[here, 0:128] = dense[part : 2 * part]
            lcb[here, 128:256] = dense[2 * part : 3 * part]
            last = dense[3 * part : 4 * part]
            proj_t[peer * third : (peer + 1) * third] = last[0:third]
            share = jnp.where(behind_ids, last[third : third + 1] + last[third + 1 : third + 2], 0.0)
            share = jnp.concatenate([share, jnp.zeros((1, LANES), F32)], axis=1)
            total += pltpu.roll(share, (peer * third - wire.left) % 256, 1)
        gain[...] = total[:, 0:192]

    @pl.when(step == pl.num_programs(0) - 1)
    def _():
        finish_pieces(place[0], pieces, table_grad)


def unpack(n_grp, n_lane, wire, count, place, seen, pieces):
    def whole(*shape):
        return pl.BlockSpec(shape, lambda i: (0,) * len(shape))

    def part(rows, start):
        return pl.BlockSpec((peers, rows, LANES), lambda i: (0, start // rows + i, 0))

    peers = n_grp * n_lane
    shapes = [(n_grp * TILE, pieces[0].shape[1] * 2 // 3, 192), (256, 128), (192, 128), (256, 256), (1, 192)]
    return pl.pallas_call(
        functools.partial(unpack_kernel, n_grp, n_lane, wire),
        grid=(count // STEP,),
        in_specs=[SMEM, pl.BlockSpec((peers, wire.share, LANES), lambda i: (0, 0, 0))]
        + [part(32, start) for start in wire.back_left]
        + [part(16, start) for start in wire.back_right]
        + [whole(*piece.shape) for piece in pieces],
        out_specs=[pl.BlockSpec((STEP, 192, 256), lambda i: (i, 0, 0))] + [whole(*shape) for shape in shapes],
        out_shape=[jax.ShapeDtypeStruct((count, 192, 256), BF16)]
        + [jax.ShapeDtypeStruct(shape, F32) for shape in shapes],
        scratch_shapes=[pltpu.VMEM((STEP, 256, 256), BF16)],
        compiler_params=params(),
        cost_estimate=cost(1),
        name="unpack",
    )(place, seen, seen, seen, seen, seen, *pieces)


def combine_kernel(place, own, seen, after, *outs):
    for k, out in zip(far_first(len(outs)), outs):
        g = jnp.bitwise_xor(place[0], k)
        out[...] = (own[g] + seen[g].astype(F32)).astype(BF16)


def combine(place, own, seen, after):
    n_grp = own.shape[0]
    shape = jax.ShapeDtypeStruct(own.shape[1:], BF16)
    return pl.pallas_call(
        combine_kernel,
        in_specs=[SMEM, VMEM, VMEM, pl.BlockSpec(memory_space=pl.ANY)],
        out_specs=[VMEM] * n_grp,
        out_shape=[shape] * n_grp,
        compiler_params=params(),
        cost_estimate=cost(100),
        name="combine",
    )(place, own, seen, after)


def cross(array):
    return lax.ppermute(array, "half", [(0, 1), (1, 0)])


def halves(pooled, upstream, ids_now, ids_next, tables, w_fm, w_proj, w_lcb, gain):
    n_grp, n_lane = lax.axis_size("grp"), lax.axis_size(LANE)
    count = pooled.shape[0]
    wire = Wire(count, n_grp * n_lane)
    factor = 1.0 / (count * n_grp * 2 * n_lane)
    half = lax.axis_index("half").astype(jnp.int32)[None]
    grp = lax.axis_index("grp").astype(jnp.int32)
    mine_t = take_tables(grp[None], tables.transpose(0, 2, 1))
    crossed_t = cross(mine_t)
    sent = backward(
        n_grp, n_lane, wire, half,
        pooled.transpose(0, 2, 1), upstream.transpose(0, 2, 1), ids_now, ids_next, w_fm, w_proj.T, w_lcb, gain,
    )
    seen = exchange(sent, PEER)
    dense, ids = half_dense(wire, seen)
    dense_seen = cross(dense)
    part_seen = cross(part_sums(n_grp, wire, True, half, seen, ids))
    rows_wire = lookup(wire, stack_tables(half, mine_t, crossed_t), ids)
    rows_wire, token = fill(wire, factor, rows_wire, dense, dense_seen)
    rows = exchange(rows_wire, PEER)
    own = part_sums(n_grp, wire, False, half, seen, ids, token)
    pieces = list(combine(grp[None], own, part_seen, token))
    for at, k in list(enumerate(far_first(n_grp)))[1:]:
        pieces[at] = lax.ppermute(pieces[at], "grp", [(g, g ^ k) for g in range(n_grp)])
    next_rows, table_grad, grad_fm, grad_proj_t, grad_lcb, grad_gain = unpack(
        n_grp, n_lane, wire, count, grp[None], rows, pieces
    )
    return next_rows.transpose(0, 2, 1), table_grad, grad_fm, grad_proj_t.T, grad_lcb, grad_gain.reshape(-1)


def solution(mesh):
    n_grp, n_emb = mesh.shape["grp"], mesh.shape["emb"]
    split = n_emb % 4 == 0 and n_grp * (n_emb // 2) == 16 and n_grp % 2 == 0

    def run(*args):
        pooled, _, _, _, tables, w_fm = args[:6]
        count = pooled.shape[0] // (n_grp * n_emb)
        fits = (
            split
            and pooled.shape[1:] == (256, 192)
            and tables.shape[1] == 128
            and w_fm.shape[1] == 128
            and pooled.shape[1] == n_grp * n_emb * TILE
            and count % STEP == 0
            and count <= 12
        )
        if fits:
            devices = mesh.devices.reshape(n_grp, 2, n_emb // 4, 2)
            where, emb, body = Mesh(devices, ("grp", "half", "deep", "core")), ("half",) + LANE, halves
        else:
            where, emb, body = mesh, ("emb",), local
        both = ("grp",) + emb
        return jax.shard_map(
            body,
            mesh=where,
            in_specs=(
                P(both, None, None),
                P(both, None, None),
                P(both, None),
                P(both, None),
                P(emb, None, None),
                P(),
                P(),
                P(),
                P(),
            ),
            out_specs=(P(both, None, None), P(emb, "grp", None), P(), P(), P(), P()),
            check_vma=False,
        )(*args)

    return run
```

```python
import functools

import jax
import jax.numpy as jnp
from jax import lax
from jax.experimental import pallas as pl
from jax.experimental.pallas import tpu as pltpu
from jax.sharding import Mesh, PartitionSpec as P

F32, BF16 = jnp.float32, jnp.bfloat16
SMEM = pl.BlockSpec(memory_space=pltpu.SMEM)
VMEM = pl.BlockSpec(memory_space=pltpu.VMEM)
LANES = 128
TILE = 8
STEP = 4
LIMIT = 30 * 1024 * 1024
LANE = ("deep", "core")
PEER = ("deep", "grp", "core")


BOTH = ("grp", "emb")


def product(form, left, right):
    return jnp.einsum(form, left, right, preferred_element_type=jnp.float32)


def layer_backward(embeds, cotangent, w_fm, w_proj, w_lcb, gain):
    fm_proj = product("bfc,fj->bcj", embeds, w_fm).astype(jnp.bfloat16)
    fm_rows = product("bfc,bcj->bfj", embeds, fm_proj).astype(jnp.bfloat16)
    projected = product("bfj,jc->bfc", fm_rows, w_proj)
    compressed = product("fi,bfc->bic", w_lcb, embeds)
    summed = embeds.astype(jnp.float32) + projected + compressed
    centre = jnp.mean(summed, axis=2, keepdims=True)
    spread = jnp.mean((summed - centre) ** 2, axis=2, keepdims=True)
    inverse = lax.rsqrt(spread + 1e-05)
    normed = (summed - centre) * inverse
    upper = cotangent.astype(jnp.float32)
    scaled = upper * gain
    grad_sum = inverse * (
        scaled
        - jnp.mean(scaled, axis=2, keepdims=True)
        - normed * jnp.mean(scaled * normed, axis=2, keepdims=True)
    )
    grad_sum = grad_sum.astype(jnp.bfloat16)
    grad_gain = jnp.sum(upper * normed, axis=(0, 1))
    grad_proj = product("bfj,bfc->jc", fm_rows, grad_sum)
    grad_rows = product("bfc,jc->bfj", grad_sum, w_proj).astype(jnp.bfloat16)
    grad_p = product("bfc,bfj->bcj", embeds, grad_rows).astype(jnp.bfloat16)
    grad_fm = product("bfc,bcj->fj", embeds, grad_p)
    grad_lcb = product("bfc,bic->fi", embeds, grad_sum)
    grad_in = (
        grad_sum.astype(jnp.float32)
        + product("bfj,bcj->bfc", grad_rows, fm_proj)
        + product("fj,bcj->bfc", w_fm, grad_p)
        + product("fi,bic->bfc", w_lcb, grad_sum)
    )
    return (grad_in.astype(jnp.bfloat16), (grad_fm, grad_proj, grad_lcb, grad_gain))


def exchange(blocks, axes):
    return lax.all_to_all(blocks, axes, split_axis=0, concat_axis=0, tiled=True)


def dense_sum(partials, factor):
    n = lax.axis_size("grp") * lax.axis_size("emb")
    shapes = [part.shape for part in partials]
    flat = jnp.concatenate([part.reshape(-1) for part in partials])
    unit = 128 * n
    padded = -(-flat.shape[0] // unit) * unit
    flat = jnp.pad(flat, (0, padded - flat.shape[0])).astype(jnp.bfloat16)
    seen = exchange(flat.reshape(n, padded // unit, 128), BOTH)
    share = (jnp.sum(seen.astype(jnp.float32), axis=0) * factor).astype(jnp.bfloat16)
    total = exchange(jnp.broadcast_to(share[None], (n,) + share.shape), BOTH).reshape(-1)
    total = total.astype(jnp.float32)
    outs, at = [], 0
    for shape in shapes:
        size = 1
        for extent in shape:
            size *= extent
        outs.append(total[at : at + size].reshape(shape))
        at += size
    return outs


def local(pooled, upstream, ids_now, ids_next, tables, w_fm, w_proj, w_lcb, gain):
    n_grp, n_emb = lax.axis_size("grp"), lax.axis_size("emb")
    count, features, width = pooled.shape
    owned, rows = tables.shape[:2]
    ids = jnp.stack([ids_now, ids_next]).reshape(2, count, n_emb, owned)
    ids = exchange(ids.transpose(2, 0, 1, 3), "emb")
    row_index = jnp.arange(rows)
    wanted = (ids[:, 1, :, :, None] == row_index).astype(jnp.bfloat16)
    fetched = product("esfr,frc->esfc", wanted, tables).astype(jnp.bfloat16)
    next_rows = exchange(fetched, "emb")
    next_rows = next_rows.transpose(1, 0, 2, 3).reshape(count, features, width)
    grad_in, partials = layer_backward(pooled, upstream, w_fm, w_proj, w_lcb, gain)
    grad_in = grad_in.reshape(count, n_emb, owned, width).transpose(1, 0, 2, 3)
    grads = exchange(grad_in, "emb")
    hit = (ids[:, 0, :, :, None] == row_index).astype(jnp.bfloat16)
    part = product("esfr,esfc->frc", hit, grads).astype(jnp.bfloat16)
    part = part.reshape(owned, n_grp, rows // n_grp, width).transpose(1, 0, 2, 3)
    table_grad = jnp.sum(exchange(part, "grp").astype(jnp.float32), axis=0)
    dense = dense_sum(partials, 1.0 / (count * n_grp * n_emb))
    return (next_rows, table_grad, *dense)


def params(share=1):
    return pltpu.CompilerParams(vmem_limit_bytes=share * LIMIT)


def cost(weight):
    return pl.CostEstimate(flops=weight * 10**9, bytes_accessed=10**5, transcendentals=0)


def mm(left, right, dims=((1,), (0,))):
    return lax.dot_general(left, right, (dims, ((), ())), preferred_element_type=F32)


def mm_nt(left, right):
    return mm(left, right, ((1,), (1,)))


def low_lanes(shape):
    return lax.broadcasted_iota(jnp.int32, shape, 1) < LANES // 2


def turn(tile):
    return pltpu.roll(tile, LANES // 2, 1)


def identity(rows, lanes):
    row = lax.broadcasted_iota(jnp.int32, (rows, lanes), 0)
    return jnp.where(row == lax.broadcasted_iota(jnp.int32, (rows, lanes), 1), 1.0, 0.0).astype(BF16)


class Wire:
    def __init__(self, count, peers):
        self.left = count * TILE
        self.half = self.left + self.left // 2
        self.dense = 2 * self.half
        self.share = 1024 // peers
        self.rows = self.dense + self.share
        self.back_left = (self.share, self.share + self.left)
        self.back_right = (self.share + 2 * self.left, self.share + 2 * self.left + self.left // 2)


def place_of(n_grp, n_lane, peer):
    deep, g, core = peer // (2 * n_grp), peer // 2 % n_grp, peer % 2
    return ((deep * 2 + core) * n_grp + g) * TILE


def backward_kernel(
    n_grp, n_lane, wire,
    half_ref, x_ref, u_any, now_ref, next_ref, fm_ref, proj_t_ref, lcb_ref, gain_ref,
    out_any,
    fm_t, proj, lcb_t, gains, eye, mixed, p_t, g_t, d_sum, d_p_t, left_in, right_in, grads, turned, ids,
    u_ref, out_ref, sems,
):
    count, width, features = x_ref.shape
    rank = fm_ref.shape[1]
    peers = n_grp * n_lane
    scale = 1.0 / width
    load = pltpu.make_async_copy(u_any, u_ref, sems.at[0])
    load.start()

    turned_fm = fm_ref[...].astype(F32).T.astype(BF16)
    fm_t[...] = turned_fm
    proj[...] = proj_t_ref[...].astype(F32).T.astype(BF16)
    lcb_t[...] = lcb_ref[...].astype(F32).T.astype(BF16)
    column = jnp.broadcast_to(gain_ref[...], (LANES, width)).T
    gains[:, 0:128] = column
    gains[:, 128:256] = column
    eye[...] = identity(features, features)
    sum_gain, sum_fm_t, sum_proj_t = [], [], []

    def project(s):
        p_t[s] = mm_nt(fm_t[...], x_ref[s]).astype(BF16)
        right_in[s, rank : 2 * rank] = fm_t[...]

    def interact(s):
        g_t[s] = mm(p_t[s], x_ref[s]).astype(BF16)

    def add_up(s):
        mixed[s] = mixed[s] + mm(proj_t_ref[...], g_t[s])

    def normalise(s):
        summed = x_ref[s].astype(F32) + mixed[s]
        centre = jnp.sum(summed, axis=0, keepdims=True) * scale
        summed = summed - centre
        spread = jnp.sum(summed * summed, axis=0, keepdims=True) * scale
        inverse = lax.rsqrt(spread + 1e-05)
        normed = summed * inverse
        upper = u_ref[s].astype(F32)
        scaled = upper * gains[...]
        first = jnp.sum(scaled, axis=0, keepdims=True) * scale
        second = jnp.sum(scaled * normed, axis=0, keepdims=True) * scale
        d_sum[s] = (inverse * (scaled - first - normed * second)).astype(BF16)
        product_gain = upper * normed
        sum_gain.append(product_gain[:, 0:128] + product_gain[:, 128:256])

    def back_rows(s):
        right_in[s, 0:rank] = mm(proj[...], d_sum[s]).astype(BF16)

    def back_project(s):
        left_in[s, :, rank : 2 * rank] = mm_nt(x_ref[s], right_in[s, 0:rank]).astype(BF16)
        d_p_t[s] = mm_nt(right_in[s, 0:rank], x_ref[s]).astype(BF16)

    def gather(s):
        grad = d_sum[s].astype(F32) + mm(d_sum[s], lcb_t[...]) + mm(left_in[s], right_in[s])
        grad = grad.astype(BF16)
        group, k = s // STEP, s % STEP
        grads[group, k * 128 : k * 128 + 128] = grad[0:128]
        at = 512 + 64 * (2 * (k % 2) + k // 2)
        grads[group, at : at + 64] = grad[128:192]
        sum_fm_t.append(mm(d_p_t[s], x_ref[s]))
        sum_proj_t.append(mm_nt(d_sum[s], g_t[s]))

    x_all = x_ref[...].reshape(count * width, features)
    left_in[:, :, 0:rank] = mm(x_all, fm_ref[...]).astype(BF16).reshape(count, width, rank)
    mixed[...] = mm(x_all, lcb_ref[...]).reshape(count, width, features)
    ahead, behind = range(count // 2), range(count // 2, count)
    for stage in (project, interact, add_up):
        for s in ahead:
            stage(s)
    load.wait()
    for one, other in zip(ahead, behind):
        normalise(one)
        project(other)
    for one, other in zip(ahead, behind):
        back_rows(one)
        interact(other)
    for one, other in zip(ahead, behind):
        back_project(one)
        add_up(other)
    for one, other in zip(ahead, behind):
        gather(one)
        normalise(other)
    for stage in (back_rows, back_project, gather):
        for s in behind:
            stage(s)
    sum_gain, sum_fm_t, sum_proj_t = sum(sum_gain), sum(sum_fm_t), sum(sum_proj_t)

    half = half_ref[0]
    for group in range(count // STEP):
        rows = mm_nt(eye[...], grads[group])
        turned[group, 0] = rows[0:128]
        turned[group, 1] = rows[128:256]
    for group in range(count // STEP):
        for side, base in ((1 - half, 0), (half, wire.half)):
            for peer in range(peers):
                at = place_of(n_grp, n_lane, peer)
                line = turned[group, side, at : at + TILE]
                left = jnp.concatenate([line[:, k * 128 : k * 128 + 128] for k in range(STEP)], axis=0)
                row = base + group * 32
                out_ref[peer, row : row + 32] = left.astype(BF16)
                right = jnp.concatenate([line[:, 512:640], line[:, 640:768]], axis=0)
                row = base + wire.left + group * 16
                out_ref[peer, row : row + 16] = right.astype(BF16)

    first_store = pltpu.make_async_copy(
        out_ref.at[:, 0 : wire.dense], out_any.at[:, 0 : wire.dense], sems.at[1]
    )
    first_store.start()

    sum_lcb = mm(x_all, d_sum[...].reshape(count * width, features), ((0,), (0,)))
    part = features // peers
    third = width // peers
    total = jnp.sum(sum_gain.T, axis=0, keepdims=True)
    high = total.astype(BF16).astype(F32)
    shares = jnp.concatenate([high, total - high, jnp.zeros((2, width), F32)], axis=0)
    shares = jnp.concatenate([shares, jnp.zeros((4, 256 - width), F32)], axis=1)

    lane = lax.broadcasted_iota(jnp.int32, (16, LANES), 1)
    sample = lax.broadcasted_iota(jnp.int32, (16, LANES), 0)
    mine = (lane // TILE == sample) & (sample < count)
    behind_ids = (lane[0:4] >= wire.left) & (lane[0:4] < wire.left + third)
    spread_ids = []
    for which, ref in enumerate((now_ref, next_ref)):
        ids[which] = jnp.zeros_like(ids[which])
        ids[which, 0:count] = ref[...].astype(F32)
        for side in range(2):
            line = ids[which, :, side * 128 : side * 128 + 128]
            spread_ids.append(pltpu.roll(line, 0, 1, stride=TILE, stride_axis=0))
    sum_fm = sum_fm_t.T
    for peer in range(peers):
        at = wire.dense
        here = slice(peer * part, (peer + 1) * part)
        out_ref[peer, at : at + part] = sum_fm[here].astype(BF16)
        out_ref[peer, at + part : at + 2 * part] = sum_lcb[here, 0:128].astype(BF16)
        out_ref[peer, at + 2 * part : at + 3 * part] = sum_lcb[here, 128:256].astype(BF16)
        place = place_of(n_grp, n_lane, peer)
        lines = []
        for line in spread_ids:
            line = pltpu.roll(line, LANES - place, 1) if place else line
            lines.append(jnp.sum(jnp.where(mine, line, 0.0), axis=0, keepdims=True))
        share = pltpu.roll(shares, (wire.left - peer * third) % 256, 1)[:, 0:128]
        lines = jnp.where(behind_ids, share, jnp.concatenate(lines, axis=0))
        last = jnp.concatenate([sum_proj_t[peer * third : (peer + 1) * third], lines], axis=0)
        out_ref[peer, at + 3 * part : at + 4 * part] = last.astype(BF16)
    second_store = pltpu.make_async_copy(
        out_ref.at[:, wire.dense : wire.rows], out_any.at[:, wire.dense : wire.rows], sems.at[2]
    )
    second_store.start()
    first_store.wait()
    second_store.wait()


def backward(n_grp, n_lane, wire, half, pooled_t, upstream_t, ids_now, ids_next, w_fm, w_proj_t, w_lcb, gain):
    count, width, features = pooled_t.shape
    rank = w_fm.shape[1]
    peers = n_grp * n_lane

    def whole(shape):
        return pl.BlockSpec(shape, lambda i: (0,) * len(shape))

    operands = (pooled_t, upstream_t, ids_now, ids_next, w_fm, w_proj_t, w_lcb, gain.reshape(1, width))
    shape = (peers, wire.rows, LANES)
    free = pl.BlockSpec(memory_space=pl.ANY)
    return pl.pallas_call(
        functools.partial(backward_kernel, n_grp, n_lane, wire),
        grid=(1,),
        in_specs=[SMEM, whole(pooled_t.shape), free] + [whole(array.shape) for array in operands[2:]],
        out_specs=free,
        out_shape=pltpu.HBM(shape, BF16),
        scratch_shapes=[
            pltpu.VMEM((rank, features), BF16),
            pltpu.VMEM((rank, width), BF16),
            pltpu.VMEM((features, features), BF16),
            pltpu.VMEM((width, features), F32),
            pltpu.VMEM((features, features), BF16),
            pltpu.VMEM((count, width, features), F32),
            pltpu.VMEM((count, rank, width), BF16),
            pltpu.VMEM((count, rank, features), BF16),
            pltpu.VMEM((count, width, features), BF16),
            pltpu.VMEM((count, rank, width), BF16),
            pltpu.VMEM((count, width, 2 * rank), BF16),
            pltpu.VMEM((count, 2 * rank, features), BF16),
            pltpu.VMEM((count // STEP, STEP * width, features), BF16),
            pltpu.VMEM((count // STEP, 2, features // 2, STEP * width), F32),
            pltpu.VMEM((2, 16, features), F32),
            pltpu.VMEM(upstream_t.shape, BF16),
            pltpu.VMEM(shape, BF16),
            pltpu.SemaphoreType.DMA((3,)),
        ],
        compiler_params=params(2),
        cost_estimate=cost(1),
        name="layer_backward",
    )(half, *operands)


def dense_kernel(dense_ref, ids_ref, dense, all_ids):
    total = dense_ref[0].astype(F32)
    for peer in range(1, dense_ref.shape[0]):
        total = total + dense_ref[peer].astype(F32)
    dense[...] = total
    all_ids[...] = ids_ref[...].astype(F32)


def half_dense(wire, seen):
    peers = seen.shape[0]
    rows = wire.share // 2
    at_ids = wire.rows // 16 - 1
    return pl.pallas_call(
        dense_kernel,
        grid=(2,),
        in_specs=[
            pl.BlockSpec((peers, rows, LANES), lambda i: (0, wire.dense // rows + i, 0)),
            pl.BlockSpec((peers, 16, LANES), lambda i: (0, at_ids, 0)),
        ],
        out_specs=[
            pl.BlockSpec((rows, LANES), lambda i: (i, 0)),
            pl.BlockSpec((peers, 16, LANES), lambda i: (0, 0, 0)),
        ],
        out_shape=[
            jax.ShapeDtypeStruct((wire.share, LANES), F32),
            jax.ShapeDtypeStruct((peers, 16, LANES), F32),
        ],
        compiler_params=params(),
        cost_estimate=cost(1),
        name="half_dense",
    )(seen, seen)


def part_kernel(n_grp, wire, other, half_ref, seen, all_ids, *refs):
    out, held = refs[-2:]
    peers = seen.shape[0]
    half = 1 - half_ref[0] if other else half_ref[0]
    lane = lax.broadcasted_iota(jnp.int32, (1, LANES), 1)
    start = ((lane % TILE) * LANES).astype(F32)
    keys = []
    for peer in range(peers):
        at = peer * LANES
        held[at : at + wire.left, 0:128] = seen[peer, 0 : wire.left]
        right = seen[peer, wire.left : wire.half]
        turned = turn(right.astype(F32)).astype(BF16)
        for i in range(wire.left // 32):
            held[at + 32 * i : at + 32 * i + 16, 128:256] = right[16 * i : 16 * i + 16]
            held[at + 32 * i + 16 : at + 32 * i + 32, 128:256] = turned[16 * i : 16 * i + 16]
        if wire.left < LANES:
            held[at + wire.left : at + LANES] = jnp.zeros((LANES - wire.left, 256), BF16)
        ids = all_ids[peer]
        key = jnp.where(half == 0, ids[12:13], ids[13:14]) + start
        keys.append(jnp.where(lane < wire.left, key, -1.0))
    keys = jnp.concatenate(keys, axis=1)
    piece = LANES // n_grp
    for pair in range(TILE // 2):
        row = lax.broadcasted_iota(jnp.int32, (256, 1), 0).astype(F32) + 256.0 * pair
        hit = jnp.where(keys == row, 1.0, 0.0).astype(BF16)
        part = mm(hit, held[...])
        for f in range(2):
            for g in range(n_grp):
                at = f * LANES + g * piece
                rows = part[at : at + piece]
                out[g, 2 * pair + f, 0:piece] = rows[:, 0:128].astype(out.dtype)
                second = turn(rows[piece // 2 :, 128:256])
                packed = jnp.where(low_lanes(second.shape), rows[: piece // 2, 128:256], second)
                out[g, 2 * pair + f, piece : piece + piece // 2] = packed.astype(out.dtype)


def part_sums(n_grp, wire, other, half, seen, ids, *after):
    peers = seen.shape[0]
    piece = LANES // n_grp
    shape = (n_grp, TILE, piece + piece // 2, LANES)
    which = 0 if other else 1
    return pl.pallas_call(
        functools.partial(part_kernel, n_grp, wire, other),
        grid=(1,),
        in_specs=[
            SMEM,
            pl.BlockSpec((peers, wire.half, LANES), lambda i: (0, which, 0)),
            pl.BlockSpec(ids.shape, lambda i: (0, 0, 0)),
        ]
        + [pl.BlockSpec(memory_space=pl.ANY)] * len(after),
        out_specs=pl.BlockSpec(shape, lambda i: (0, 0, 0, 0)),
        out_shape=jax.ShapeDtypeStruct(shape, BF16 if other else F32),
        scratch_shapes=[pltpu.VMEM((peers * LANES, 256), BF16)],
        compiler_params=params(),
        cost_estimate=cost(1),
        name="part_other" if other else "part_own",
    )(half, seen, ids, *after)


def take_kernel(place, tables, out):
    out[...] = tables[...]


def take_tables(place, tables_t):
    rows, lanes = tables_t.shape[1:]
    return pl.pallas_call(
        take_kernel,
        grid_spec=pltpu.PrefetchScalarGridSpec(
            num_scalar_prefetch=1,
            grid=(1,),
            in_specs=[pl.BlockSpec((TILE, rows, lanes), lambda i, place: (place[0], 0, 0))],
            out_specs=pl.BlockSpec((TILE, rows, lanes), lambda i, place: (0, 0, 0)),
        ),
        out_shape=jax.ShapeDtypeStruct((TILE, rows, lanes), BF16),
        compiler_params=params(2),
        cost_estimate=cost(1),
        name="take_tables",
    )(place, tables_t)


def stack_kernel(half_ref, mine_t, crossed_t, out):
    half = half_ref[0]
    for f in range(TILE):
        at = f * LANES
        for side, ref in ((half, mine_t), (1 - half, crossed_t)):
            out[side, 0:192, at : at + LANES] = ref[f]
            out[side, 192:256, at : at + LANES] = ref[f, 128:192]


def stack_tables(half, mine_t, crossed_t):
    return pl.pallas_call(
        stack_kernel,
        in_specs=[SMEM, VMEM, VMEM],
        out_specs=VMEM,
        out_shape=jax.ShapeDtypeStruct((2, 256, TILE * LANES), BF16),
        compiler_params=params(),
        cost_estimate=cost(100),
        name="stack_tables",
    )(half, mine_t, crossed_t)


def lookup_kernel(wire, stacked, ids_ref, out):
    peers = out.shape[0]
    ids = ids_ref[...].reshape(peers * 16, LANES)
    keys = ids.T
    rows = peers * wire.left
    lane = lax.broadcasted_iota(jnp.int32, (1, LANES), 1).astype(F32)
    feature = lax.broadcasted_iota(jnp.int32, (rows, LANES), 0) % TILE
    masks = [jnp.where(feature == f, 1.0, 0.0).astype(BF16) for f in range(TILE)]
    for which in range(2):
        same = []
        for peer in range(peers):
            at = peer * 16 + 14 + which
            same.append(jnp.where(keys[0 : wire.left, at : at + 1] == lane, 1.0, 0.0))
        same = jnp.concatenate(same, axis=0).astype(BF16)
        hit = jnp.concatenate([same * mask for mask in masks], axis=1)
        both = mm_nt(hit, stacked[which])
        for peer in range(peers):
            got = both[peer * wire.left : (peer + 1) * wire.left]
            base = wire.back_left[which]
            out[peer, base : base + wire.left] = got[:, 0:128].astype(BF16)
            packed = []
            for i in range(wire.left // 32):
                first, second = got[32 * i : 32 * i + 16, 128:256], got[32 * i + 16 : 32 * i + 32, 128:256]
                packed.append(jnp.where(low_lanes(first.shape), first, second))
            base = wire.back_right[which]
            out[peer, base : base + wire.left // 2] = jnp.concatenate(packed, axis=0).astype(BF16)


def lookup(wire, stacked, ids):
    peers = ids.shape[0]
    some = peers // 2
    return pl.pallas_call(
        functools.partial(lookup_kernel, wire),
        grid=(2,),
        in_specs=[
            pl.BlockSpec(stacked.shape, lambda i: (0, 0, 0)),
            pl.BlockSpec((some, 16, LANES), lambda i: (i, 0, 0)),
        ],
        out_specs=pl.BlockSpec((some, wire.rows, LANES), lambda i: (i, 0, 0)),
        out_shape=pltpu.HBM((peers, wire.rows, LANES), BF16),
        compiler_params=params(),
        cost_estimate=cost(100),
        name="lookup",
    )(stacked, ids)


def fill_kernel(factor, rows, own, seen, out, token):
    token[...] = jnp.zeros_like(token)
    total = ((own[...] + seen[...]) * factor).astype(BF16)
    for peer in range(out.shape[0]):
        out[peer] = total


def fill(wire, factor, rows, own, seen):
    peers = rows.shape[0]

    def whole(shape):
        return pl.BlockSpec(shape, lambda i: (0,) * len(shape))

    return pl.pallas_call(
        functools.partial(fill_kernel, factor),
        grid=(1,),
        in_specs=[pl.BlockSpec(memory_space=pl.ANY), whole(own.shape), whole(seen.shape)],
        out_specs=[whole((peers, wire.share, LANES)), whole((8, LANES))],
        out_shape=[pltpu.HBM(rows.shape, BF16), pltpu.HBM((8, LANES), F32)],
        input_output_aliases={0: 0},
        compiler_params=params(),
        cost_estimate=cost(1),
        name="fill_dense",
    )(rows, own, seen)


def far_first(n_grp):
    return [0] + list(range(n_grp - 1, 0, -1))


def finish_pieces(grp, pieces, out):
    piece = out.shape[1]
    for k, seen in zip(far_first(len(pieces)), pieces):
        base = jnp.bitwise_xor(grp, k) * TILE
        for f in range(TILE):
            out[base + f, :, 0:128] = seen[f, 0:piece].astype(F32)
            packed = seen[f, piece : piece + piece // 2].astype(F32)
            out[base + f, 0 : piece // 2, 128:192] = packed[:, 0:64]
            out[base + f, piece // 2 : piece, 128:192] = turn(packed)[:, 0:64]


def unpack_kernel(n_grp, n_lane, wire, place, dense_ref, left0, left1, right0, right1, *refs):
    pieces, refs = refs[:n_grp], refs[n_grp:]
    rows_out, table_grad, fm, proj_t, lcb, gain, held = refs
    step = pl.program_id(0)
    peers = n_grp * n_lane
    for side, (left_ref, right_ref) in enumerate(((left0, right0), (left1, right1))):
        for q in range(n_lane):
            for gg in range(n_grp // 2):
                left, right = [], []
                for g in (2 * gg, 2 * gg + 1):
                    peer = (q // 2 * n_grp + g) * 2 + q % 2
                    left.append(left_ref[peer].astype(F32))
                    packed = right_ref[peer].astype(F32)
                    right.append(jnp.concatenate([packed, turn(packed)], axis=0))
                at = side * 128 + q * n_grp * TILE + gg * 16
                for s in range(STEP):
                    here = slice(s * TILE, s * TILE + TILE)
                    both = jnp.concatenate([left[0][here], left[1][here]], axis=0)
                    held[s, at : at + 16, 0:128] = both.astype(BF16)
                    both = jnp.concatenate([right[0][here], right[1][here]], axis=0)
                    held[s, at : at + 16, 128:256] = both.astype(BF16)
    eye = identity(192, 256)
    for s in range(STEP):
        rows_out[s] = mm_nt(eye, held[s]).astype(BF16)

    @pl.when(step == 0)
    def _():
        part, third = 256 // peers, 192 // peers
        lane = lax.broadcasted_iota(jnp.int32, (1, LANES), 1)
        behind_ids = (lane >= wire.left) & (lane < wire.left + third)
        total = jnp.zeros((1, 256), F32)
        for peer in range(peers):
            dense = dense_ref[peer].astype(F32)
            here = slice(peer * part, (peer + 1) * part)
            fm[here] = dense[0:part]
            lcb[here, 0:128] = dense[part : 2 * part]
            lcb[here, 128:256] = dense[2 * part : 3 * part]
            last = dense[3 * part : 4 * part]
            proj_t[peer * third : (peer + 1) * third] = last[0:third]
            share = jnp.where(behind_ids, last[third : third + 1] + last[third + 1 : third + 2], 0.0)
            share = jnp.concatenate([share, jnp.zeros((1, LANES), F32)], axis=1)
            total += pltpu.roll(share, (peer * third - wire.left) % 256, 1)
        gain[...] = total[:, 0:192]

    @pl.when(step == pl.num_programs(0) - 1)
    def _():
        finish_pieces(place[0], pieces, table_grad)


def unpack(n_grp, n_lane, wire, count, place, seen, pieces):
    def whole(*shape):
        return pl.BlockSpec(shape, lambda i: (0,) * len(shape))

    def part(rows, start):
        return pl.BlockSpec((peers, rows, LANES), lambda i: (0, start // rows + i, 0))

    peers = n_grp * n_lane
    shapes = [(n_grp * TILE, pieces[0].shape[1] * 2 // 3, 192), (256, 128), (192, 128), (256, 256), (1, 192)]
    return pl.pallas_call(
        functools.partial(unpack_kernel, n_grp, n_lane, wire),
        grid=(count // STEP,),
        in_specs=[SMEM, pl.BlockSpec((peers, wire.share, LANES), lambda i: (0, 0, 0))]
        + [part(32, start) for start in wire.back_left]
        + [part(16, start) for start in wire.back_right]
        + [whole(*piece.shape) for piece in pieces],
        out_specs=[pl.BlockSpec((STEP, 192, 256), lambda i: (i, 0, 0))] + [whole(*shape) for shape in shapes],
        out_shape=[jax.ShapeDtypeStruct((count, 192, 256), BF16)]
        + [jax.ShapeDtypeStruct(shape, F32) for shape in shapes],
        scratch_shapes=[pltpu.VMEM((STEP, 256, 256), BF16)],
        compiler_params=params(),
        cost_estimate=cost(1),
        name="unpack",
    )(place, seen, seen, seen, seen, seen, *pieces)


def combine_kernel(place, own, seen, after, *outs):
    for k, out in zip(far_first(len(outs)), outs):
        g = jnp.bitwise_xor(place[0], k)
        out[...] = (own[g] + seen[g].astype(F32)).astype(BF16)


def combine(place, own, seen, after):
    n_grp = own.shape[0]
    shape = jax.ShapeDtypeStruct(own.shape[1:], BF16)
    return pl.pallas_call(
        combine_kernel,
        in_specs=[SMEM, VMEM, VMEM, pl.BlockSpec(memory_space=pl.ANY)],
        out_specs=[VMEM] * n_grp,
        out_shape=[shape] * n_grp,
        compiler_params=params(),
        cost_estimate=cost(100),
        name="combine",
    )(place, own, seen, after)


def cross(array):
    return lax.ppermute(array, "half", [(0, 1), (1, 0)])


def halves(pooled, upstream, ids_now, ids_next, tables, w_fm, w_proj, w_lcb, gain):
    n_grp, n_lane = lax.axis_size("grp"), lax.axis_size(LANE)
    count = pooled.shape[0]
    wire = Wire(count, n_grp * n_lane)
    factor = 1.0 / (count * n_grp * 2 * n_lane)
    half = lax.axis_index("half").astype(jnp.int32)[None]
    grp = lax.axis_index("grp").astype(jnp.int32)
    mine_t = take_tables(grp[None], tables.transpose(0, 2, 1))
    crossed_t = cross(mine_t)
    sent = backward(
        n_grp, n_lane, wire, half,
        pooled.transpose(0, 2, 1), upstream.transpose(0, 2, 1), ids_now, ids_next, w_fm, w_proj.T, w_lcb, gain,
    )
    seen = exchange(sent, PEER)
    dense, ids = half_dense(wire, seen)
    dense_seen = cross(dense)
    part_seen = cross(part_sums(n_grp, wire, True, half, seen, ids))
    rows_wire = lookup(wire, stack_tables(half, mine_t, crossed_t), ids)
    rows_wire, token = fill(wire, factor, rows_wire, dense, dense_seen)
    rows = exchange(rows_wire, PEER)
    own = part_sums(n_grp, wire, False, half, seen, ids, token)
    pieces = list(combine(grp[None], own, part_seen, token))
    for at, k in list(enumerate(far_first(n_grp)))[1:]:
        pieces[at] = lax.ppermute(pieces[at], "grp", [(g, g ^ k) for g in range(n_grp)])
    next_rows, table_grad, grad_fm, grad_proj_t, grad_lcb, grad_gain = unpack(
        n_grp, n_lane, wire, count, grp[None], rows, pieces
    )
    return next_rows.transpose(0, 2, 1), table_grad, grad_fm, grad_proj_t.T, grad_lcb, grad_gain.reshape(-1)


def solution(mesh):
    n_grp, n_emb = mesh.shape["grp"], mesh.shape["emb"]
    split = n_emb % 4 == 0 and n_grp * (n_emb // 2) == 16 and n_grp % 2 == 0

    def run(*args):
        pooled, _, _, _, tables, w_fm = args[:6]
        count = pooled.shape[0] // (n_grp * n_emb)
        fits = (
            split
            and pooled.shape[1:] == (256, 192)
            and tables.shape[1] == 128
            and w_fm.shape[1] == 128
            and pooled.shape[1] == n_grp * n_emb * TILE
            and count % STEP == 0
            and count <= 12
        )
        if fits:
            devices = mesh.devices.reshape(n_grp, 2, n_emb // 4, 2)
            where, emb, body = Mesh(devices, ("grp", "half", "deep", "core")), ("half",) + LANE, halves
        else:
            where, emb, body = mesh, ("emb",), local
        both = ("grp",) + emb
        return jax.shard_map(
            body,
            mesh=where,
            in_specs=(
                P(both, None, None),
                P(both, None, None),
                P(both, None),
                P(both, None),
                P(emb, None, None),
                P(),
                P(),
                P(),
                P(),
            ),
            out_specs=(P(both, None, None), P(emb, "grp", None), P(), P(), P(), P()),
            check_vma=False,
        )(*args)

    return run
```
